128 devices in a mesh: section: 2 (over core), seq: 16 (over y, z), wsh: 4 (over x).
Axes of the slice: x: 4, y: 4, z: 4, core: 2. Of those that a mesh axis runs over, the one named last changes fastest.
Arguments:
- block_input: bfloat16 [4, 2, 2048, 1536], P('wsh', None, 'seq'), may hold values from -6 to 6
- cotangent: bfloat16 [4, 2, 2048, 1536], P('wsh', None, 'seq'), may hold values from -6 to 6
- seg_groups: int32 [4, 2], P('wsh'), may hold values from 6 to 8, as said below
- norm_gain: bfloat16 [2, 1536], P('section', ('seq', 'wsh')), may hold values from 0.5 to 1.5
- w_gate: bfloat16 [2, 1536, 3072], P('section', ('seq', 'wsh')), may hold values from -0.15625 to 0.15625
- w_inner: bfloat16 [2, 1536, 3072], P('section', ('seq', 'wsh')), may hold values from -0.15625 to 0.15625
- w_bc: bfloat16 [2, 1536, 256], P('section', ('seq', 'wsh')), may hold values from -0.15625 to 0.15625
- w_step: bfloat16 [2, 1536, 48], P('section', ('seq', 'wsh')), may hold values from -0.15625 to 0.15625
- conv_inner: bfloat16 [2, 5, 3072], P('section', None, ('seq', 'wsh')), may hold values from -0.5 to 0.5
- conv_bc: bfloat16 [2, 5, 256], P('section', None, ('seq', 'wsh')), may hold values from -0.5 to 0.5
- head_params: float32 [2, 3, 48], P('section', None, 'seq'), as said below
- inner_gain: bfloat16 [2, 3072], P('section', ('seq', 'wsh')), may hold values from 0.5 to 1.5
- w_out: bfloat16 [2, 3072, 1536], P('section', ('seq', 'wsh')), may hold values from -0.109375 to 0.109375
Outputs:
- block_out: bfloat16 [2, 4, 2, 2048, 1536], P('section', 'wsh', None, 'seq')
- input_grad: bfloat16 [2, 4, 2, 2048, 1536], P('section', 'wsh', None, 'seq')
- grad_norm_gain: float32 [2, 1536], P('section', ('seq', 'wsh'))
- grad_w_gate: float32 [2, 1536, 3072], P('section', ('seq', 'wsh'))
- grad_w_inner: float32 [2, 1536, 3072], P('section', ('seq', 'wsh'))
- grad_w_bc: float32 [2, 1536, 256], P('section', ('seq', 'wsh'))
- grad_w_step: float32 [2, 1536, 48], P('section', ('seq', 'wsh'))
- grad_conv_inner: float32 [2, 5, 3072], P('section', None, ('seq', 'wsh'))
- grad_conv_bc: float32 [2, 5, 256], P('section', None, ('seq', 'wsh'))
- grad_head_params: float32 [2, 3, 48], P('section', None, 'seq')
- grad_inner_gain: float32 [2, 3072], P('section', ('seq', 'wsh'))
- grad_w_out: float32 [2, 3072, 1536], P('section', ('seq', 'wsh'))
The draws below stay inside these ranges and needn't reach their ends.
Inputs may be any that keep to these rules, and one draw needn't show every extreme that they name: `seg_groups`: each sequence's 2 segment lengths add up to 14 blocks; in each sequence one segment has 8 blocks and the others share the rest as evenly as possible. `head_params`: row 0 is the step bias, row 1 the logarithm of the decay factor, row 2 the skip factor.
All inputs are finite; a program needn't handle non-finite values.
Results may differ from the reference program's by a relative error of at most 0.02.
Values may be sent and summed in bfloat16 or wider, within the bound.
A program may use at most 320 MiB of HBM per device.

```python
import math
import jax
import jax.numpy as jnp
from jax import lax

D = 1536
INNER = 3072
HEADS = 48
HDIM = 64
STATE = 128
BLOCK_LEN = 256
MICRO = 2
SEG = 2048
CAP = 8
TOTAL_CH = 14
SEQS = 4


def draw_seg_groups(key, part):
    key = jax.random.fold_in(key, 11)
    rest = TOTAL_CH - CAP
    others = MICRO - 1
    base = rest // others
    extra = rest - base * others
    long_pos = jax.random.randint(key, (SEQS,), 0, MICRO).astype(jnp.int32)
    slots = jnp.arange(MICRO, dtype=jnp.int32)
    other_rank = slots[None, :] - (slots[None, :] > long_pos[:, None]).astype(jnp.int32)
    shared = base + (other_rank < extra).astype(jnp.int32)
    return jnp.where(slots[None, :] == long_pos[:, None], CAP, shared).astype(jnp.int32)


def draw_head_params(key, part):
    key = jax.random.fold_in(key, 7)
    key_decay, key_level, key_skip = jax.random.split(key, 3)
    fast_log = math.log(8.0 / BLOCK_LEN)
    slow_log = math.log(1.0 / (MICRO * SEG))
    level = jax.random.uniform(key_level, (2, HEADS), minval=0.0, maxval=1.0)
    skip_factor = jax.random.uniform(key_skip, (2, HEADS), minval=0.5, maxval=1.5)
    decay_log = jax.random.uniform(key_decay, (2, HEADS), minval=0.0, maxval=math.log(16.0))
    rate_target = jnp.exp(slow_log + level * (fast_log - slow_log))
    step_target = rate_target * jnp.exp(-decay_log)
    step_bias = jnp.log(jnp.expm1(step_target))
    return jnp.stack([step_bias, decay_log, skip_factor], axis=1).astype(jnp.float32)


def block_scale(stream_key, extent, cuts, least, largest):
    level = 1.0
    for position, blocks in cuts:
        steps = jax.random.uniform(jax.random.fold_in(jax.random.fold_in(stream_key, 6), position), (blocks,), jnp.float32, least / len(cuts), largest / len(cuts))
        level = level * jnp.repeat(jnp.exp(steps), extent[position] // blocks).reshape((-1,) + (1,) * (len(extent) - 1 - position))
    return level


def scatter_about(own_key, dims, scale, limit, cuts=(), kind=jnp.bfloat16):
    result = scale * jax.random.normal(own_key, dims, jnp.float32)
    if cuts:
        result = result * block_scale(own_key, dims, cuts, -0.22, 0.18)
    return jnp.clip(result, -limit, limit).astype(kind)


def setup_inputs(seed: int = 0) -> dict:
    splits = jax.random.split(jax.random.key(seed), 14)
    return {
        "block_input": scatter_about(splits[0], (SEQS, MICRO, SEG, D), 1.0, 6.0, ((0, 4), (2, 16))),
        "cotangent": scatter_about(splits[1], (SEQS, MICRO, SEG, D), 1.0, 6.0, ((0, 4), (2, 16))),
        "seg_groups": draw_seg_groups(jax.random.fold_in(splits[13], 71), 0),
        "norm_gain": jnp.clip(1.0 + 0.1 * jax.random.normal(splits[3], (2, D), jnp.float32), 0.5, 1.5).astype(jnp.bfloat16),
        "w_gate": scatter_about(splits[4], (2, D, INNER), D ** -0.5, 0.15625, ((0, 2), (1, 64))),
        "w_inner": scatter_about(splits[5], (2, D, INNER), D ** -0.5, 0.15625, ((0, 2), (1, 64))),
        "w_bc": scatter_about(splits[6], (2, D, 2 * STATE), D ** -0.5, 0.15625, ((0, 2), (1, 64))),
        "w_step": scatter_about(splits[7], (2, D, HEADS), D ** -0.5, 0.15625, ((0, 2), (1, 64))),
        "conv_inner": jnp.clip(jax.random.uniform(splits[8], (2, 5, INNER), jnp.float32, -0.5, 0.5) * block_scale(splits[8], (2, 5, INNER), ((0, 2), (2, 64)), -0.4, 0.0), -0.5, 0.5).astype(jnp.bfloat16),
        "conv_bc": jnp.clip(jax.random.uniform(splits[9], (2, 5, 2 * STATE), jnp.float32, -0.5, 0.5) * block_scale(splits[9], (2, 5, 2 * STATE), ((0, 2), (2, 64)), -0.4, 0.0), -0.5, 0.5).astype(jnp.bfloat16),
        "head_params": draw_head_params(jax.random.fold_in(splits[13], 71), 0),
        "inner_gain": jnp.clip(1.0 + 0.1 * jax.random.normal(splits[11], (2, INNER), jnp.float32), 0.5, 1.5).astype(jnp.bfloat16),
        "w_out": scatter_about(splits[12], (2, INNER, D), INNER ** -0.5, 0.109375, ((0, 2), (1, 64))),
    }


EPS = 1e-05
HIGH = lax.Precision.HIGHEST

@jax.custom_vjp
def low(v):
    return lax.optimization_barrier(v.astype(jnp.bfloat16)).astype(jnp.float32)

@jax.custom_vjp
def low_back(v):
    return v

def low_keep(v):
    return (low(v), None)

def low_pass(kept, grad):
    return (grad,)

def back_keep(v):
    return (v, None)

def back_low(kept, grad):
    return (low(grad),)
low.defvjp(low_keep, low_pass)
low_back.defvjp(back_keep, back_low)

def normed(value, gain):
    return value * lax.rsqrt(lax.optimization_barrier(jnp.mean(value * value, axis=-1, keepdims=True)) + EPS) * gain

def product(left, right):
    return jnp.dot(left, right, precision=HIGH)

def block_step(carried, pieces):
    inner_act, step_size, log_decay, b_rows, c_rows = pieces
    span = log_decay.shape[0]
    cum_rate = jnp.cumsum(log_decay, axis=0)
    rate_gap = cum_rate[:, None, :] - cum_rate[None, :, :]
    causal = (jnp.arange(span)[:, None] >= jnp.arange(span)[None, :])[:, :, None]
    decay_mat = jnp.where(causal, jnp.exp(jnp.where(causal, rate_gap, 0.0)), 0.0)
    scores = jnp.dot(c_rows, b_rows.T, precision=HIGH)
    mix_weights = scores[:, :, None] * decay_mat * step_size[None, :, :]
    mixed_out = jnp.einsum('tsh,shp->thp', mix_weights, inner_act, precision=HIGH)
    mixed_out = mixed_out + jnp.exp(cum_rate)[:, :, None] * jnp.einsum('tn,hpn->thp', c_rows, carried, precision=HIGH)
    last_rate = cum_rate[-1]
    carry_w = jnp.exp(last_rate[None, :] - cum_rate) * step_size
    carried = jnp.exp(last_rate)[:, None, None] * carried + jnp.einsum('sh,shp,sn->hpn', carry_w, inner_act, b_rows, precision=HIGH)
    return (carried, mixed_out)

def scan_states(inner_act, step_size, log_decay, b_rows, c_rows, carried):
    length = inner_act.shape[0]
    count = length // BLOCK_LEN
    head_count = inner_act.shape[1]
    pieces = (inner_act.reshape(count, BLOCK_LEN, head_count, HDIM), step_size.reshape(count, BLOCK_LEN, head_count), log_decay.reshape(count, BLOCK_LEN, head_count), b_rows.reshape(count, BLOCK_LEN, STATE), c_rows.reshape(count, BLOCK_LEN, STATE))
    carried, outs = lax.scan(jax.checkpoint(block_step), carried, pieces)
    return (outs.reshape(length, head_count, HDIM), carried)

def apply_block(residual, weights):
    norm_w, gate_w, inner_w, shared_w, step_w, conv_inner_w, conv_shared_w, head_vals, mid_gain, out_w = weights
    length = residual.shape[0]
    hidden = low(normed(residual, norm_w))
    gate_pre = low_back(product(hidden, gate_w))
    inner_pre = low_back(low(product(hidden, inner_w)))
    shared_pre = low_back(low(product(hidden, shared_w)))
    step_pre = low_back(low(product(hidden, step_w)))
    pre_conv = jnp.concatenate([inner_pre, shared_pre], axis=1)
    conv_taps = jnp.concatenate([conv_inner_w, conv_shared_w], axis=1)
    padded_rows = jnp.concatenate([jnp.zeros((3, pre_conv.shape[1]), jnp.float32), pre_conv], axis=0)
    summed = conv_taps[4] + conv_taps[0] * padded_rows[0:length] + conv_taps[1] * padded_rows[1:length + 1]
    summed = summed + conv_taps[2] * padded_rows[2:length + 2] + conv_taps[3] * padded_rows[3:length + 3]
    activated = jax.nn.silu(summed)
    inner_act = activated[:, :INNER].reshape(length, HEADS, HDIM)
    b_rows = activated[:, INNER:INNER + STATE]
    c_rows = activated[:, INNER + STATE:]
    step_size = jax.nn.softplus(step_pre + head_vals[0])
    log_decay = -step_size * jnp.exp(head_vals[1])
    mixed_out, unused = scan_states(inner_act, step_size, log_decay, b_rows, c_rows, jnp.zeros((HEADS, HDIM, STATE), jnp.float32))
    mixed_out = mixed_out + head_vals[2][None, :, None] * inner_act
    mixer_y = low_back(low(mixed_out.reshape(length, INNER)))
    gated = low(normed(mixer_y * jax.nn.silu(gate_pre), mid_gain))
    branch = low_back(product(gated, out_w))
    return residual + branch

def reference(block_input, cotangent, seg_groups, norm_gain, w_gate, w_inner, w_bc, w_step, conv_inner, conv_bc, head_params, inner_gain, w_out):
    params = tuple((weight.astype(jnp.float32) for weight in (norm_gain, w_gate, w_inner, w_bc, w_step, conv_inner, conv_bc, head_params, inner_gain, w_out)))
    seq_cells = jnp.arange(TOTAL_CH * BLOCK_LEN, dtype=jnp.int32)
    first_outs, second_outs, first_grads, second_grads = ([], [], [], [])
    totals = None
    for seq_no in range(SEQS):
        lengths = (seg_groups[seq_no] * BLOCK_LEN).astype(jnp.int32)
        seg_ends = jnp.cumsum(lengths).astype(jnp.int32)
        which_seg = lax.optimization_barrier(jnp.sum((seq_cells[:, None] >= seg_ends[None, :]).astype(jnp.int32), axis=1)).astype(jnp.int32)
        begins = (seg_ends - lengths).astype(jnp.int32)
        live_place = (which_seg * SEG + SEG - lengths[which_seg] + seq_cells - begins[which_seg]).astype(jnp.int32)

        def forward(entering, zero_probe, weights):
            flat_rows = entering.reshape(MICRO * SEG, D)
            first_section = tuple((weight[0] for weight in weights))
            second_section = tuple((weight[1] for weight in weights))
            middle = low(flat_rows.at[live_place].set(apply_block(flat_rows[live_place], first_section)))
            shifted = low_back(middle + zero_probe.reshape(MICRO * SEG, D))
            final_rows = shifted.at[live_place].set(apply_block(shifted[live_place], second_section))
            return (final_rows.reshape(MICRO, SEG, D), middle.reshape(MICRO, SEG, D))
        entering = block_input[seq_no].astype(jnp.float32)
        zero_probe = jnp.zeros((MICRO, SEG, D), jnp.float32)
        final_rows, back_fn, middle = jax.vjp(forward, entering, zero_probe, params, has_aux=True)
        grad_entering, grad_probe, weight_grads = back_fn(cotangent[seq_no].astype(jnp.float32))
        first_outs.append(middle)
        second_outs.append(final_rows)
        first_grads.append(grad_entering)
        second_grads.append(grad_probe)
        if totals is None:
            totals = weight_grads
        else:
            totals = tuple((left + right for left, right in zip(totals, weight_grads)))
    block_out = jnp.stack([jnp.stack(first_outs), jnp.stack(second_outs)]).astype(jnp.bfloat16)
    input_grad = jnp.stack([jnp.stack(first_grads), jnp.stack(second_grads)]).astype(jnp.bfloat16)
    return (block_out, input_grad, totals[0], totals[1], totals[2], totals[3], totals[4], totals[5], totals[6], totals[7], totals[8], totals[9])
```

```python
import functools

import jax
import jax.numpy as jnp
from jax import lax
from jax.experimental import pallas as pl
from jax.experimental.pallas import tpu as pltpu
from jax.sharding import PartitionSpec as P

D = 1536
INNER = 3072
HEADS = 48
STATE = 128
BLOCK_LEN = 256
BLOCKS = 8
TOK = 128
CONV = INNER + 2 * STATE
STEP0 = CONV
SMALL0 = STEP0 + 128
WIN = SMALL0 + 128
HALF = (WIN + INNER) // 2
OWNERS = 16
OWN = 192
EPS = 1e-05
F32 = jnp.float32
BF16 = jnp.bfloat16
MESH = pl.DeviceIdType.MESH
VMEM_LIMIT = 58 * 1024 * 1024
LANES = (0, 1, 2, 8, 9, 10)
ROWS_ALL = ("seq", "wsh")


def dot32(left, right, dims=((1,), (0,))):
    return lax.dot_general(left, right, (dims, ((), ())), preferred_element_type=F32)


def split_left(exact, value, terms):
    total = None
    for _ in range(terms):
        part = value.astype(BF16)
        value = value - part.astype(F32)
        term = dot32(exact, part)
        total = term if total is None else total + term
    return total


def split_right(value, exact, terms, dims=((1,), (0,))):
    total = None
    for _ in range(terms):
        part = value.astype(BF16)
        value = value - part.astype(F32)
        term = dot32(part, exact, dims)
        total = term if total is None else total + term
    return total


def vmem():
    return pl.BlockSpec(memory_space=pltpu.VMEM)


def smem():
    return pl.BlockSpec(memory_space=pltpu.SMEM)


def layer_block(layer, rows, cols):
    return pl.BlockSpec((None, rows, cols), lambda i: (layer, 0, 0))


def whole(*dims):
    return pl.BlockSpec(dims, lambda i: (0,) * len(dims))


def pair_cols(tile, q):
    lane = lax.broadcasted_iota(jnp.int32, (TOK, 128), 1)
    a = jnp.broadcast_to(tile[:, LANES[2 * q] : LANES[2 * q] + 1], (TOK, 128))
    b = jnp.broadcast_to(tile[:, LANES[2 * q + 1] : LANES[2 * q + 1] + 1], (TOK, 128))
    return a, b, jnp.where(lane < 64, a, b)


def pair_row(row, q):
    lane = lax.broadcasted_iota(jnp.int32, (1, 128), 1)
    a = jnp.broadcast_to(row[:, LANES[2 * q] : LANES[2 * q] + 1], (1, 128))
    b = jnp.broadcast_to(row[:, LANES[2 * q + 1] : LANES[2 * q + 1] + 1], (1, 128))
    return jnp.where(lane < 64, a, b)


def to_front(tile, i):
    return pltpu.roll(tile, lax.rem(128 - 16 * i, 128), 1)


def conv_of(cat, taps):
    total = taps[4:5] + taps[3:4] * cat[8 : 8 + TOK]
    for k in range(3):
        total = total + taps[k : k + 1] * cat[5 + k : 5 + k + TOK]
    return total


def tri_of(lower):
    row = lax.broadcasted_iota(jnp.int32, (TOK, TOK), 0)
    col = lax.broadcasted_iota(jnp.int32, (TOK, TOK), 1)
    return row >= col if lower else row <= col


def head_lanes():
    lane = lax.broadcasted_iota(jnp.int32, (TOK, 128), 1)
    return (lane % 8) < 3


def states_body(live_ref, pre_ref, halo_ref, taps_ref, heads_ref, act_ref, dact_ref, dt_ref, cum_ref, ds_ref, dec_ref):
    live = live_ref[0]
    heads = heads_ref[...]
    step = pre_ref[:, STEP0 : STEP0 + 128].astype(F32) + heads[0:1]
    dt = jnp.maximum(step, 0.0) + jnp.log1p(jnp.exp(-jnp.abs(step)))
    dt = jnp.where(head_lanes(), dt, 0.0) * live
    rate = -dt * jnp.exp(heads[1:2])
    cum = split_left(tri_of(True).astype(F32).astype(BF16), rate, 3)
    dt_ref[...] = dt
    cum_ref[...] = cum
    last = jnp.broadcast_to(cum[TOK - 1 : TOK], (TOK, 128))
    dec_ref[...] = jnp.exp(last).T
    weight = dt * jnp.exp(last - cum)

    def conv_tile(cols):
        blk = pre_ref[:, cols].astype(F32)
        cat = jnp.concatenate([halo_ref[:, cols].astype(F32), blk], axis=0)
        summed = conv_of(cat, taps_ref[:, cols])
        sig = 1.0 / (1.0 + jnp.exp(-summed))
        act = summed * sig
        act_ref[:, cols] = act
        dact_ref[:, cols] = sig * (1.0 + summed * (1.0 - sig))
        return act

    b = conv_tile(pl.ds(INNER, 128)).astype(BF16)
    conv_tile(pl.ds(INNER + 128, 128))

    def group(i, carry):
        wt = to_front(weight, i)
        for q in range(3):
            base = pl.multiple_of(i * 384 + q * 128, 128)
            x = conv_tile(pl.ds(base, 128))
            scaled = (x * pair_cols(wt, q)[2]).astype(BF16)
            ds_ref[pl.ds(base, 128), :] = dot32(scaled, b, ((0,), (0,))).astype(BF16)
        return carry

    lax.fori_loop(0, 8, group, 0)


def local_states(live, pre, halo, taps, heads):
    return pl.pallas_call(
        states_body,
        out_shape=(
            jax.ShapeDtypeStruct((TOK, CONV), F32),
            jax.ShapeDtypeStruct((TOK, CONV), F32),
            jax.ShapeDtypeStruct((TOK, 128), F32),
            jax.ShapeDtypeStruct((TOK, 128), F32),
            jax.ShapeDtypeStruct((INNER, STATE), BF16),
            jax.ShapeDtypeStruct((TOK, 128), F32),
        ),
        in_specs=[smem()] + [vmem()] * 4,
        out_specs=(vmem(),) * 6,
        compiler_params=pltpu.CompilerParams(vmem_limit_bytes=VMEM_LIMIT),
        name="local_states",
    )(live, pre, halo, taps, heads)


def scan_body(
    backward, ds_ref, dec_ref, out_ref,
    got, got_dec, kept, fade, ready, final, other,
    send_a, recv_a, send_d, recv_d, send_b, recv_b, send_f, recv_f, own_a, own_d, own_b,
):
    me = lax.axis_index("seq")
    section = lax.axis_index("section")
    barrier = pltpu.get_barrier_semaphore()
    for d in range(1, OWNERS):
        pl.semaphore_signal(
            barrier, inc=1, device_id={"seq": lax.rem(me + d, OWNERS)}, device_id_type=MESH
        )
    pl.semaphore_signal(barrier, inc=1, device_id={"section": 1 - section}, device_id_type=MESH)
    pl.semaphore_wait(barrier, OWNERS)

    def out_copies(d):
        peer = lax.rem(me + d, OWNERS)
        return (
            pltpu.make_async_remote_copy(
                src_ref=ds_ref.at[peer], dst_ref=got.at[me], send_sem=send_a.at[d], recv_sem=recv_a.at[d],
                device_id={"seq": peer}, device_id_type=MESH,
            ),
            pltpu.make_async_remote_copy(
                src_ref=dec_ref.at[peer], dst_ref=got_dec.at[me], send_sem=send_d.at[d], recv_sem=recv_d.at[d],
                device_id={"seq": peer}, device_id_type=MESH,
            ),
        )

    firsts = [out_copies(d) for d in range(1, OWNERS)]
    for one, two in firsts:
        one.start()
        two.start()
    mine = pltpu.make_async_copy(ds_ref.at[me], got.at[me], own_a)
    mine.start()
    mine_dec = pltpu.make_async_copy(dec_ref.at[me], got_dec.at[me], own_d)
    mine_dec.start()
    mine.wait()
    mine_dec.wait()
    for one, two in firsts:
        one.wait()
        two.wait()

    def rows_of(dec):
        return jnp.concatenate([jnp.broadcast_to(dec[h : h + 1], (64, 128)) for h in range(3)], axis=0)

    final[...] = jnp.zeros((OWN, STATE), F32)
    fade[0] = jnp.ones((8, 128), F32)

    def step(n, carry):
        c = OWNERS - 1 - n if backward else n
        state = final[...]
        kept[c] = state
        dec = got_dec[c]
        final[...] = rows_of(dec) * state + got[c].astype(F32)
        fade[n + 1] = fade[n] * dec
        return carry

    lax.fori_loop(0, OWNERS, step, 0)
    swap = pltpu.make_async_remote_copy(
        src_ref=final, dst_ref=other, send_sem=send_f, recv_sem=recv_f,
        device_id={"section": 1 - section}, device_id_type=MESH,
    )
    swap.start()
    swap.wait()
    takes = 0 if backward else 1
    begin = jnp.where(section == takes, other[...], 0.0)

    def finish(n, carry):
        c = OWNERS - 1 - n if backward else n
        ready[c] = (kept[c] + rows_of(fade[n]) * begin).astype(BF16)
        return carry

    lax.fori_loop(0, OWNERS, finish, 0)

    def back_copy(d):
        peer = lax.rem(me + d, OWNERS)
        return pltpu.make_async_remote_copy(
            src_ref=ready.at[peer], dst_ref=out_ref.at[me], send_sem=send_b.at[d], recv_sem=recv_b.at[d],
            device_id={"seq": peer}, device_id_type=MESH,
        )

    seconds = [back_copy(d) for d in range(1, OWNERS)]
    for one in seconds:
        one.start()
    mine = pltpu.make_async_copy(ready.at[me], out_ref.at[me], own_b)
    mine.start()
    mine.wait()
    for one in seconds:
        one.wait()


def scan_states(ds, dec, backward):
    any_spec = pl.BlockSpec(memory_space=pl.ANY)
    sems = pltpu.SemaphoreType.DMA((OWNERS,))
    one = pltpu.SemaphoreType.DMA
    out = pl.pallas_call(
        functools.partial(scan_body, backward),
        out_shape=jax.ShapeDtypeStruct((OWNERS, OWN, STATE), BF16),
        in_specs=[any_spec, any_spec],
        out_specs=any_spec,
        scratch_shapes=[
            pltpu.VMEM((OWNERS, OWN, STATE), BF16),
            pltpu.VMEM((OWNERS, 8, 128), F32),
            pltpu.VMEM((OWNERS, OWN, STATE), F32),
            pltpu.VMEM((OWNERS + 1, 8, 128), F32),
            pltpu.VMEM((OWNERS, OWN, STATE), BF16),
            pltpu.VMEM((OWN, STATE), F32),
            pltpu.VMEM((OWN, STATE), F32),
            sems, sems, sems, sems, sems, sems, one, one, one, one, one,
        ],
        compiler_params=pltpu.CompilerParams(
            collective_id=2 if backward else 1, has_side_effects=True, vmem_limit_bytes=VMEM_LIMIT
        ),
        name="scan_backward" if backward else "scan_forward",
    )(ds.reshape(OWNERS, OWN, STATE), dec.reshape(OWNERS, 8, 128))
    return out.reshape(INNER, STATE)


def mix_body(
    live_ref, act_ref, dt_ref, cum_ref, state_ref, gate_ref, heads_ref, gain_ref, wout_ref, x_ref,
    raw_ref, y_ref, gated_ref, inv_ref, out_ref,
    z_s, cumt_s, square_s,
):
    live = live_ref[0]
    heads = heads_ref[...]
    b = act_ref[:, INNER : INNER + 128].astype(BF16)
    c = act_ref[:, INNER + 128 : CONV].astype(BF16)
    dt = dt_ref[...]
    cum = cum_ref[...]
    cumt_s[...] = cum.T
    causal = tri_of(True)
    scores = dot32(c, b, ((1,), (1,)))
    lane = lax.broadcasted_iota(jnp.int32, (TOK, 128), 1)
    square_s[...] = jnp.zeros((TOK, 128), F32)

    def group(i, carry):
        cum_i = to_front(cum, i)
        dt_i = to_front(dt, i)
        skip_i = pltpu.roll(heads, lax.rem(128 - 16 * i, 128), 1)[2:3]
        rows = cumt_s[pl.ds(pl.multiple_of(16 * i, 16), 16), :]
        for q in range(3):
            base = pl.multiple_of(i * 384 + q * 128, 128)
            cols = pl.ds(base, 128)
            x = act_ref[:, cols]
            cum_a, cum_b, cum_x = pair_cols(cum_i, q)
            u = x * pair_cols(dt_i, q)[2]
            mixes = []
            for cum_h, off in ((cum_a, LANES[2 * q]), (cum_b, LANES[2 * q + 1])):
                gap = cum_h - rows[off : off + 1]
                mixes.append((scores * jnp.exp(jnp.where(causal, gap, -1e30))).astype(BF16))
            terms = jnp.concatenate(
                [jnp.where(lane < 64, u, 0.0).astype(BF16), jnp.where(lane < 64, 0.0, u).astype(BF16)], axis=0
            )
            raw = dot32(jnp.concatenate(mixes, axis=1), terms)
            raw = raw + jnp.exp(cum_x) * dot32(c, state_ref[cols, :], ((1,), (1,)))
            raw_ref[:, cols] = raw
            y = (raw + pair_row(skip_i, q) * x).astype(BF16)
            y_ref[:, cols] = y
            gate = gate_ref[:, cols]
            z = y.astype(F32) * (gate / (1.0 + jnp.exp(-gate)))
            z_s[:, cols] = z
            square_s[...] += z * z
        return carry

    lax.fori_loop(0, 8, group, 0)
    total = jnp.sum(square_s[...], axis=1, keepdims=True)
    inv = jnp.broadcast_to(lax.rsqrt(total / INNER + EPS), (TOK, 128))
    inv_ref[...] = inv

    def scale(i, carry):
        cols = pl.ds(pl.multiple_of(i * 128, 128), 128)
        gated_ref[:, cols] = (z_s[:, cols] * inv * gain_ref[0:1, cols]).astype(BF16)
        return carry

    lax.fori_loop(0, 24, scale, 0)

    def project(n, carry):
        cols = pl.ds(pl.multiple_of(n * 256, 256), 256)
        branch = dot32(gated_ref[...], wout_ref[:, cols])
        out_ref[:, cols] = (x_ref[:, cols].astype(F32) + live * branch).astype(BF16)
        return carry

    lax.fori_loop(0, D // 256, project, 0)


def mix_forward(layer, live, act, dt, cum, states, gate, heads, gain, w_out, x):
    return pl.pallas_call(
        mix_body,
        grid=(1,),
        out_shape=(
            jax.ShapeDtypeStruct((TOK, INNER), F32),
            jax.ShapeDtypeStruct((TOK, INNER), BF16),
            jax.ShapeDtypeStruct((TOK, INNER), BF16),
            jax.ShapeDtypeStruct((TOK, 128), F32),
            jax.ShapeDtypeStruct((TOK, D), BF16),
        ),
        in_specs=[
            smem(), whole(TOK, CONV), whole(TOK, 128), whole(TOK, 128), whole(INNER, STATE), whole(TOK, INNER),
            whole(8, 128), whole(8, INNER), layer_block(layer, INNER, D), whole(TOK, D),
        ],
        out_specs=(
            whole(TOK, INNER), whole(TOK, INNER), whole(TOK, INNER), whole(TOK, 128), whole(TOK, D),
        ),
        scratch_shapes=[
            pltpu.VMEM((TOK, INNER), F32),
            pltpu.VMEM((TOK, 128), F32),
            pltpu.VMEM((TOK, 128), F32),
        ],
        compiler_params=pltpu.CompilerParams(vmem_limit_bytes=VMEM_LIMIT),
        name="mix_forward",
    )(live, act, dt, cum, states, gate, heads, gain, w_out, x)


def gate_back_body(
    live_ref, g_ref, wout_ref, gate_ref, y_ref, gain_ref, inv_ref, act_ref, cum_ref,
    gb_ref, dy_ref, dgate_ref, ggain_ref, ds_ref,
    gg_s, dots_s,
):
    live = live_ref[0]
    gb = (g_ref[...].astype(F32) * live).astype(BF16)
    gb_ref[...] = gb
    inv = inv_ref[...]
    c = act_ref[:, INNER + 128 : CONV].astype(BF16)
    cum = cum_ref[...]
    dots_s[...] = jnp.zeros((TOK, 128), F32)

    def first(i, carry):
        rows = pl.ds(pl.multiple_of(i * 384, 384), 384)
        gg = dot32(gb, wout_ref[rows, :], ((1,), (1,)))
        gg_s[:, rows] = gg
        for q in range(3):
            cols = pl.ds(pl.multiple_of(i * 384 + q * 128, 128), 128)
            gate = gate_ref[:, cols]
            z = y_ref[:, cols].astype(F32) * (gate / (1.0 + jnp.exp(-gate)))
            dots_s[...] += gg[:, 128 * q : 128 * q + 128] * gain_ref[0:1, cols] * z
        return carry

    lax.fori_loop(0, 8, first, 0)
    total = jnp.broadcast_to(jnp.sum(dots_s[...], axis=1, keepdims=True), (TOK, 128))
    shift = total * inv * inv * inv / INNER

    def second(i, carry):
        cum_i = to_front(cum, i)
        for q in range(3):
            cols = pl.ds(pl.multiple_of(i * 384 + q * 128, 128), 128)
            gate = gate_ref[:, cols]
            y = y_ref[:, cols].astype(F32)
            gg = gg_s[:, cols]
            sig = 1.0 / (1.0 + jnp.exp(-gate))
            act = gate * sig
            z = y * act
            dz = gg * gain_ref[0:1, cols] * inv - z * shift
            dy = (dz * act).astype(BF16)
            dy_ref[:, cols] = dy
            dgate_ref[:, cols] = (dz * y * (sig * (1.0 + gate * (1.0 - sig)))).astype(BF16)
            ggain_ref[:, cols] = jnp.broadcast_to(
                jnp.sum(gg * z * inv, axis=0, keepdims=True), (8, 128)
            )
            far = (dy.astype(F32) * jnp.exp(pair_cols(cum_i, q)[2])).astype(BF16)
            ds_ref[cols, :] = dot32(far, c, ((0,), (0,))).astype(BF16)
        return carry

    lax.fori_loop(0, 8, second, 0)


def gate_backward(layer, live, g, w_out, gate, y, gain, inv, act, cum):
    return pl.pallas_call(
        gate_back_body,
        grid=(1,),
        out_shape=(
            jax.ShapeDtypeStruct((TOK, D), BF16),
            jax.ShapeDtypeStruct((TOK, INNER), BF16),
            jax.ShapeDtypeStruct((TOK, INNER), BF16),
            jax.ShapeDtypeStruct((8, INNER), F32),
            jax.ShapeDtypeStruct((INNER, STATE), BF16),
        ),
        in_specs=[
            smem(), whole(TOK, D), layer_block(layer, INNER, D), whole(TOK, INNER), whole(TOK, INNER),
            whole(8, INNER), whole(TOK, 128), whole(TOK, CONV), whole(TOK, 128),
        ],
        out_specs=(
            whole(TOK, D), whole(TOK, INNER), whole(TOK, INNER), whole(8, INNER), whole(INNER, STATE),
        ),
        scratch_shapes=[pltpu.VMEM((TOK, INNER), F32), pltpu.VMEM((TOK, 128), F32)],
        compiler_params=pltpu.CompilerParams(vmem_limit_bytes=VMEM_LIMIT),
        name="gate_backward",
    )(live, g, w_out, gate, y, gain, inv, act, cum)


def mix_back_body(
    live_ref, pre_ref, halo_ref, taps_ref, heads_ref, act_ref, dact_ref, dt_ref, cum_ref, raw_ref, state_ref, dstate_ref, dy_ref,
    gsum_ref, dstep_ref, gtaps_ref, ghead_ref,
    cumt_s, edge_s, dscore_s, gb_s, gc_s, xdu_s, dyy_s, row_s,
):
    live = live_ref[0]
    heads = heads_ref[...]
    b = act_ref[:, INNER : INNER + 128].astype(BF16)
    c = act_ref[:, INNER + 128 : CONV].astype(BF16)
    dt = dt_ref[...]
    cum = cum_ref[...]
    cumt_s[...] = cum.T
    causal = tri_of(True)
    scores = dot32(c, b, ((1,), (1,)))
    lane = lax.broadcasted_iota(jnp.int32, (TOK, 128), 1)
    pick_row = lax.broadcasted_iota(jnp.int32, (128, 128), 0)
    pick_col = lax.broadcasted_iota(jnp.int32, (128, 128), 1)
    picks = []
    for q in range(3):
        target = jnp.where(pick_row < 64, LANES[2 * q], LANES[2 * q + 1])
        picks.append((pick_col == target).astype(F32).astype(BF16))
    for ref in (dscore_s, gb_s, gc_s, xdu_s, dyy_s, row_s, gtaps_ref):
        ref[...] = jnp.zeros_like(ref)

    def conv_back(cols, gact):
        gsum = gact * dact_ref[:, cols]
        gsum_ref[:, cols] = gsum
        blk = pre_ref[:, cols].astype(F32)
        cat = jnp.concatenate([halo_ref[:, cols].astype(F32), blk], axis=0)
        sums = [jnp.sum(gsum * cat[5 + k : 5 + k + TOK], axis=0, keepdims=True) for k in range(4)]
        sums.append(jnp.sum(gsum, axis=0, keepdims=True))
        gtaps_ref[:, cols] = jnp.concatenate(sums + [jnp.zeros((3, 128), F32)], axis=0)

    def group(i, carry):
        back = lax.rem(128 - 16 * i, 128)
        cum_i = to_front(cum, i)
        dt_i = to_front(dt, i)
        skip_i = pltpu.roll(heads, back, 1)[2:3]
        rows = cumt_s[pl.ds(pl.multiple_of(16 * i, 16), 16), :]
        x_du = jnp.zeros((TOK, 128), F32)
        dy_y = jnp.zeros((TOK, 128), F32)
        thin = jnp.zeros((16, 128), F32)
        edges = {}
        for q in range(3):
            cols = pl.ds(pl.multiple_of(i * 384 + q * 128, 128), 128)
            x = act_ref[:, cols]
            cum_a, cum_b, cum_x = pair_cols(cum_i, q)
            dt_x = pair_cols(dt_i, q)[2]
            last_x = cum_x[TOK - 1 : TOK]
            fade = jnp.exp(last_x - cum_x)
            u = x * dt_x
            u16 = u.astype(BF16)
            dy16 = dy_ref[:, cols]
            dy = dy16.astype(F32)
            nil = jnp.zeros_like(dy16)
            dys = jnp.concatenate([jnp.where(lane < 64, dy16, nil), jnp.where(lane < 64, nil, dy16)], axis=0)
            both = dot32(dys, u16, ((1,), (1,)))
            mixes = []
            for n, (cum_h, off) in enumerate(((cum_a, LANES[2 * q]), (cum_b, LANES[2 * q + 1]))):
                gap = cum_h - rows[off : off + 1]
                decay = jnp.exp(jnp.where(causal, gap, -1e30))
                mixes.append((scores * decay).astype(BF16))
                dscore_s[...] += both[n * TOK : n * TOK + TOK] * decay
            du = dot32(jnp.concatenate(mixes, axis=0), dys, ((0,), (0,)))
            state16 = state_ref[cols, :]
            dstate16 = dstate_ref[cols, :]
            du_far = fade * dot32(b, dstate16, ((1,), (1,)))
            du = du + du_far
            gc_s[...] += dot32((dy * jnp.exp(cum_x)).astype(BF16), state16)
            gb_s[...] += dot32((u * fade).astype(BF16), dstate16)
            overlap = state16.astype(F32) * dstate16.astype(F32)
            edges[LANES[2 * q]] = jnp.sum(overlap[:64], axis=0, keepdims=True)
            edges[LANES[2 * q + 1]] = jnp.sum(overlap[64:], axis=0, keepdims=True)
            x_du = x_du + split_right(x * du, picks[q], 2)
            dy_y = dy_y + split_right(dy * raw_ref[:, cols], picks[q], 2)
            thin = thin + split_right(
                jnp.concatenate(
                    [
                        jnp.broadcast_to(jnp.sum(u * du_far, axis=0, keepdims=True), (8, 128)),
                        jnp.broadcast_to(jnp.sum(dy * x, axis=0, keepdims=True), (8, 128)),
                    ],
                    axis=0,
                ),
                picks[q],
                3,
            )
            conv_back(cols, du * dt_x + pair_row(skip_i, q) * dy)
        nothing = jnp.zeros((1, 128), F32)
        edge_s[pl.ds(pl.multiple_of(16 * i, 16), 16), :] = jnp.concatenate(
            [edges.get(k, nothing) for k in range(16)], axis=0
        )
        xdu_s[...] += pltpu.roll(x_du, 16 * i, 1)
        dyy_s[...] += pltpu.roll(dy_y, 16 * i, 1)
        row_s[...] += pltpu.roll(thin, 16 * i, 1)
        return carry

    lax.fori_loop(0, 8, group, 0)
    dscore16 = dscore_s[...].astype(BF16)
    conv_back(pl.ds(INNER, 128), gb_s[...] + dot32(dscore16, c, ((0,), (0,))))
    conv_back(pl.ds(INNER + 128, 128), gc_s[...] + dot32(dscore16, b))
    ones = jnp.ones((128, 128), BF16)
    edge = split_right(edge_s[...], ones, 3).T[0:1] * jnp.exp(cum[TOK - 1 : TOK]) + row_s[0:1]
    x_du = xdu_s[...]
    drate = split_left(tri_of(False).astype(F32).astype(BF16), dyy_s[...] - dt * x_du, 3) + edge
    speed = jnp.exp(heads[1:2])
    ddt = x_du - drate * speed
    step = pre_ref[:, STEP0 : STEP0 + 128].astype(F32) + heads[0:1]
    dstep = jnp.where(head_lanes(), ddt / (1.0 + jnp.exp(-step)), 0.0) * live
    dstep_ref[...] = dstep
    ghead_ref[...] = jnp.concatenate(
        [
            jnp.sum(dstep, axis=0, keepdims=True),
            jnp.sum(-drate * dt * speed, axis=0, keepdims=True),
            row_s[8:9],
            jnp.zeros((5, 128), F32),
        ],
        axis=0,
    )


def mix_backward(live, pre, halo, taps, heads, act, dact, dt, cum, raw, states, dstates, dy):
    tile = pltpu.VMEM((TOK, 128), F32)
    return pl.pallas_call(
        mix_back_body,
        out_shape=(
            jax.ShapeDtypeStruct((TOK, CONV), F32),
            jax.ShapeDtypeStruct((TOK, 128), F32),
            jax.ShapeDtypeStruct((8, CONV), F32),
            jax.ShapeDtypeStruct((8, 128), F32),
        ),
        in_specs=[smem()] + [vmem()] * 12,
        out_specs=(vmem(),) * 4,
        scratch_shapes=[tile, tile, tile, tile, tile, tile, tile, pltpu.VMEM((16, 128), F32)],
        compiler_params=pltpu.CompilerParams(vmem_limit_bytes=VMEM_LIMIT),
        name="mix_backward",
    )(live, pre, halo, taps, heads, act, dact, dt, cum, raw, states, dstates, dy)


def input_back_body(
    gsum_ref, next_ref, dstep_ref, taps_ref, dgate_ref, win_ref, wgate_ref, x_ref, g_ref, gain_ref,
    gpre_ref, out_ref, ggain_ref,
    hid_s,
):
    def conv_tile(i, carry):
        cols = pl.ds(pl.multiple_of(i * 128, 128), 128)
        cat = jnp.concatenate([gsum_ref[:, cols], next_ref[:, cols]], axis=0)
        taps = taps_ref[:, cols]
        total = taps[3:4] * cat[:TOK]
        for k in range(3):
            total = total + taps[k : k + 1] * cat[3 - k : 3 - k + TOK]
        gpre_ref[:, cols] = total.astype(BF16)
        return carry

    lax.fori_loop(0, CONV // 128, conv_tile, 0)
    gpre_ref[:, STEP0 : STEP0 + 128] = dstep_ref[...].astype(BF16)
    gpre_ref[:, SMALL0:WIN] = jnp.zeros((TOK, 128), BF16)

    def project(n, carry):
        rows = pl.ds(pl.multiple_of(n * 256, 256), 256)
        hid_s[:, rows] = dot32(gpre_ref[...], win_ref[rows, :], ((1,), (1,))) + dot32(
            dgate_ref[...], wgate_ref[rows, :], ((1,), (1,))
        )
        return carry

    lax.fori_loop(0, D // 256, project, 0)
    x = x_ref[...].astype(F32)
    grad = hid_s[...]
    inv = lax.rsqrt(jnp.sum(x * x, axis=1, keepdims=True) / D + EPS)
    scaled = grad * gain_ref[0:1, :]
    dots = jnp.sum(scaled * x, axis=1, keepdims=True)
    dx = scaled * inv - x * (dots * inv * inv * inv / D)
    out_ref[...] = (g_ref[...].astype(F32) + dx).astype(BF16)
    ggain_ref[...] = jnp.broadcast_to(jnp.sum(grad * x * inv, axis=0, keepdims=True), (8, D))


def input_backward(layer, gsum, after, dstep, taps, dgate, w_in, w_gate, x, g, gain):
    return pl.pallas_call(
        input_back_body,
        grid=(1,),
        out_shape=(
            jax.ShapeDtypeStruct((TOK, WIN), BF16),
            jax.ShapeDtypeStruct((TOK, D), BF16),
            jax.ShapeDtypeStruct((8, D), F32),
        ),
        in_specs=[
            whole(TOK, CONV), whole(8, CONV), whole(TOK, 128), whole(8, CONV), whole(TOK, INNER),
            layer_block(layer, D, WIN), layer_block(layer, D, INNER), whole(TOK, D), whole(TOK, D), whole(8, D),
        ],
        out_specs=(whole(TOK, WIN), whole(TOK, D), whole(8, D)),
        scratch_shapes=[pltpu.VMEM((TOK, D), F32)],
        compiler_params=pltpu.CompilerParams(vmem_limit_bytes=VMEM_LIMIT),
        name="input_backward",
    )(gsum, after, dstep, taps, dgate, w_in, w_gate, x, g, gain)


def exact_parts(value):
    parts = []
    for _ in range(3):
        part = lax.reduce_precision(value, 8, 7)
        parts.append(part.astype(BF16))
        value = value - part
    return jnp.stack(parts)


def rows8(vector):
    return jnp.broadcast_to(vector[None, :], (8, vector.shape[0]))


def step_lanes(step):
    lead = step.shape[0]
    return jnp.pad(step.reshape(lead, OWNERS, 3), ((0, 0), (0, 0), (0, 5))).reshape(lead, 128)


def pack_small(norm_gain, inner_gain, conv_inner, conv_bc, heads):
    flat = jnp.concatenate(
        [norm_gain, inner_gain, conv_inner.reshape(-1), conv_bc.reshape(-1), exact_parts(heads).reshape(-1)]
    )
    return jnp.pad(flat, (0, 24 * 128 - flat.shape[0])).reshape(24, 128)


def unpack_small(cells):
    rows = cells.reshape(64, 24 * 128)
    norm_gain = rows[:, :24].reshape(D).astype(F32)
    inner_gain = rows[:, 24:72].reshape(INNER).astype(F32)
    conv_inner = rows[:, 72:312].reshape(64, 5, 48).transpose(1, 0, 2).reshape(5, INNER)
    conv_bc = rows[:, 312:332].reshape(64, 5, 4).transpose(1, 0, 2).reshape(5, 2 * STATE)
    taps = jnp.concatenate([conv_inner, conv_bc], axis=1).astype(F32)
    taps = jnp.pad(taps, ((0, 3), (0, 0)))
    heads = rows[::4, 332:359].reshape(OWNERS, 3, 3, 3).astype(F32).sum(axis=1)
    heads = jnp.pad(heads.transpose(1, 0, 2), ((0, 5), (0, 0), (0, 5))).reshape(8, 128)
    return rows8(norm_gain), rows8(inner_gain), taps, heads


def small_grads(norm_gain, inner_gain, taps, heads, seq_pos):
    conv_inner = taps[:5, :INNER].reshape(5, 64, 48).transpose(1, 0, 2).reshape(64, 240)
    conv_bc = taps[:5, INNER:].reshape(5, 64, 4).transpose(1, 0, 2).reshape(64, 20)
    head = heads[:3].reshape(3, OWNERS, 8)[:, :, :3].transpose(1, 0, 2).reshape(OWNERS, 9)
    head = jnp.repeat(head, 4, axis=0)
    flat = jnp.concatenate(
        [norm_gain.reshape(64, 24), inner_gain.reshape(64, 48), conv_inner, conv_bc, head], axis=1
    )
    return jnp.pad(flat, ((0, 0), (0, 24 * 128 - flat.shape[1]))).reshape(D, 128)


def swap_cores(value):
    return lax.ppermute(value, "section", [(0, 1), (1, 0)])


def per_device(
    block_input, cotangent, seg_groups, norm_gain, w_gate, w_inner, w_bc, w_step, conv_inner, conv_bc, head_params,
    inner_gain, w_out,
):
    section = lax.axis_index("section")
    seq_pos = lax.axis_index("seq")
    shard = jnp.concatenate(
        [
            w_inner[0],
            w_bc[0],
            step_lanes(w_step[0]),
            pack_small(norm_gain[0], inner_gain[0], conv_inner[0], conv_bc[0], head_params[0]),
        ],
        axis=1,
    )
    w_in = lax.all_gather(lax.all_gather(shard, ROWS_ALL, axis=0, tiled=True), "section", axis=0)
    w_gates = lax.all_gather(lax.all_gather(w_gate[0], ROWS_ALL, axis=0, tiled=True), "section", axis=0)
    w_outs = lax.all_gather(lax.all_gather(w_out[0], ROWS_ALL, axis=0, tiled=True), "section", axis=0)
    firsts = (BLOCKS - seg_groups[0]) * (BLOCK_LEN // TOK)
    first = jnp.where(section == 0, firsts[0], firsts[1])
    live = (seq_pos >= first).astype(F32).reshape(1)
    ring = [(s * 16 + i, s * 16 + i + 1) for s in range(2) for i in range(15)] + [(15, 16)]
    jump = [(15, 20)]
    unring = [(b, a) for a, b in ring]
    unjump = [(b, a) for a, b in jump]
    axes = ("section", "seq")

    x = lax.dynamic_index_in_dim(block_input[0], section, 0, keepdims=False)
    kept = []
    outs = []
    for layer in range(2):
        gain, mid_gain, taps, heads = unpack_small(w_in[layer, :, SMALL0:])
        x32 = x.astype(F32)
        hidden = (x32 * lax.rsqrt(jnp.mean(x32 * x32, axis=-1, keepdims=True) + EPS) * gain[0]).astype(BF16)
        pre = jnp.dot(hidden, w_in[layer], preferred_element_type=F32).astype(BF16)
        tail = pre[TOK - 8 :]
        near = lax.ppermute(tail, axes, ring)
        far = lax.ppermute(tail, axes, jump)
        halo = jnp.where(
            seq_pos == first,
            jnp.where(section == 0, jnp.zeros_like(near), jnp.where(first == 0, near, far)),
            near,
        )
        gate = jnp.dot(hidden, w_gates[layer], preferred_element_type=F32)
        act, dact, dt, cum, ds, dec = local_states(live, pre, halo, taps, heads)
        states = scan_states(ds, dec, False)
        raw, y, gated, inv, out = mix_forward(
            layer, live, act, dt, cum, states, gate, heads, mid_gain, w_outs, x
        )
        kept.append((x, hidden, pre, halo, gate, act, dact, dt, cum, dec, states, raw, y, gated, inv, gain, mid_gain, taps, heads))
        outs.append(out)
        x = out

    g = lax.dynamic_index_in_dim(cotangent[0], section, 0, keepdims=False)
    grads_in = [None, None]
    pieces = [None, None]
    for layer in (1, 0):
        (x, hidden, pre, halo, gate, act, dact, dt, cum, dec, states, raw, y, gated, inv, gain, mid_gain, taps, heads) = kept[layer]
        gb, dy, dgate, gmid, ds = gate_backward(layer, live, g, w_outs, gate, y, mid_gain, inv, act, cum)
        dstates = scan_states(ds, dec, True)
        gsum, dstep, gtaps, ghead = mix_backward(
            live, pre, halo, taps, heads, act, dact, dt, cum, raw, states, dstates, dy
        )
        head_rows = gsum[:8]
        near = lax.ppermute(head_rows, axes, unring)
        far = lax.ppermute(head_rows, axes, unjump)
        crossing = (section == 0) & (seq_pos == 15) & (firsts[1] != 0)
        after = jnp.where(crossing, far, near) * live
        gpre, g, ggain = input_backward(
            layer, gsum, after, dstep, taps, dgate, w_in, w_gates, x, g, gain
        )
        grads_in[layer] = g
        small = lax.psum(small_grads(ggain[0], gmid[0], gtaps, ghead, seq_pos), "section")
        both_hidden = lax.all_gather(hidden, "section", axis=0, tiled=True)
        both_gb = lax.all_gather(gb, "section", axis=0, tiled=True)
        both_gated = lax.all_gather(gated, "section", axis=0, tiled=True)
        both_g = lax.all_gather(jnp.concatenate([gpre, dgate], axis=1), "section", axis=0, tiled=True)
        own_g = lax.dynamic_slice_in_dim(both_g, section * HALF, HALF, 1)
        own_gb = lax.dynamic_slice_in_dim(both_gb, section * (D // 2), D // 2, 1)
        grad_in = dot32(both_hidden, own_g, ((0,), (0,))).astype(BF16)
        keep = jnp.where(section == 1, small.astype(BF16), grad_in[:, 128:256])
        grad_in = lax.dynamic_update_slice_in_dim(grad_in, keep, 128, 1)
        grad_out = dot32(both_gated, own_gb, ((0,), (0,))).astype(BF16)
        pieces[layer] = (
            lax.psum_scatter(
                lax.psum_scatter(grad_in, "seq", scatter_dimension=0, tiled=True), "wsh", scatter_dimension=0, tiled=True
            ),
            lax.psum_scatter(
                lax.psum_scatter(grad_out, "seq", scatter_dimension=0, tiled=True), "wsh", scatter_dimension=0, tiled=True
            ),
        )

    def settle(first_value, second_value):
        own = jnp.where(section == 0, first_value, second_value)
        got = swap_cores(jnp.where(section == 0, second_value, first_value))
        return jnp.where(section == 0, own, got), jnp.where(section == 0, got, own)

    out_a, out_b = settle(outs[0], outs[1])
    in_a, in_b = settle(grads_in[0], grads_in[1])
    left, right = settle(pieces[0][0], pieces[1][0])
    out_left, out_right = settle(pieces[0][1], pieces[1][1])
    grad = jnp.concatenate([left, right], axis=1).astype(F32)
    grad_out = jnp.concatenate([out_left, out_right], axis=1).astype(F32)
    cells = grad[:, SMALL0:WIN].reshape(-1)
    heads_own = cells[332:341].reshape(3, 3)
    heads_sum = lax.psum(jnp.where(lax.axis_index("wsh") == 0, heads_own, 0.0), "wsh")
    return (
        jnp.stack([out_a, out_b])[None, None],
        jnp.stack([in_a, in_b])[None, None],
        cells[:24][None],
        grad[:, WIN:][None],
        grad[:, :INNER][None],
        grad[:, INNER:CONV][None],
        grad[:, STEP0:SMALL0].reshape(24, OWNERS, 8)[:, :, :3].reshape(24, HEADS)[None],
        cells[72:312].reshape(5, 48)[None],
        cells[312:332].reshape(5, 4)[None],
        heads_sum[None],
        cells[24:72][None],
        grad_out[None],
    )


def solution(mesh):
    weight = P("section", ROWS_ALL, None)
    vector = P("section", ROWS_ALL)
    taps = P("section", None, ROWS_ALL)
    tokens = P("wsh", None, "seq", None)
    heads = P("section", None, "seq")
    result = P("section", "wsh", None, "seq", None)
    return jax.shard_map(
        per_device,
        mesh=mesh,
        in_specs=(
            tokens, tokens, P("wsh", None), vector, weight, weight, weight, weight, taps, taps, heads, vector, weight,
        ),
        out_specs=(
            result, result, vector, weight, weight, weight, weight, taps, taps, heads, vector, weight,
        ),
        check_vma=False,
    )
```

```python
import functools

import jax
import jax.numpy as jnp
from jax import lax
from jax.experimental import pallas as pl
from jax.experimental.pallas import tpu as pltpu
from jax.sharding import PartitionSpec as P

D = 1536
INNER = 3072
HEADS = 48
STATE = 128
BLOCK_LEN = 256
BLOCKS = 8
TOK = 128
CONV = INNER + 2 * STATE
HALF = CONV
GATE0 = 256
CUT = HALF // 2
WALF = D // 2
OWNERS = 16
OWN = 192
EPS = 1e-05
F32 = jnp.float32
BF16 = jnp.bfloat16
MESH = pl.DeviceIdType.MESH
VMEM_LIMIT = 58 * 1024 * 1024
LANES = (0, 1, 2, 8, 9, 10)
ROWS_ALL = ("seq", "wsh")


def dot32(left, right, dims=((1,), (0,))):
    return lax.dot_general(left, right, (dims, ((), ())), preferred_element_type=F32)


def split_left(exact, value, terms):
    total = None
    for _ in range(terms):
        part = value.astype(BF16)
        value = value - part.astype(F32)
        term = dot32(exact, part)
        total = term if total is None else total + term
    return total


def split_right(value, exact, terms, dims=((1,), (0,))):
    total = None
    for _ in range(terms):
        part = value.astype(BF16)
        value = value - part.astype(F32)
        term = dot32(part, exact, dims)
        total = term if total is None else total + term
    return total


def vmem():
    return pl.BlockSpec(memory_space=pltpu.VMEM)


def smem():
    return pl.BlockSpec(memory_space=pltpu.SMEM)


def whole(*dims):
    return pl.BlockSpec(dims, lambda i: (0,) * len(dims))


def pair_cols(tile, q):
    lane = lax.broadcasted_iota(jnp.int32, (TOK, 128), 1)
    a = jnp.broadcast_to(tile[:, LANES[2 * q] : LANES[2 * q] + 1], (TOK, 128))
    b = jnp.broadcast_to(tile[:, LANES[2 * q + 1] : LANES[2 * q + 1] + 1], (TOK, 128))
    return a, b, jnp.where(lane < 64, a, b)


def pair_row(row, q):
    lane = lax.broadcasted_iota(jnp.int32, (1, 128), 1)
    a = jnp.broadcast_to(row[:, LANES[2 * q] : LANES[2 * q] + 1], (1, 128))
    b = jnp.broadcast_to(row[:, LANES[2 * q + 1] : LANES[2 * q + 1] + 1], (1, 128))
    return jnp.where(lane < 64, a, b)


def to_front(tile, i):
    return pltpu.roll(tile, lax.rem(128 - 16 * i, 128), 1)


def conv_of(cat, taps):
    total = taps[4:5] + taps[3:4] * cat[8 : 8 + TOK]
    for k in range(3):
        total = total + taps[k : k + 1] * cat[5 + k : 5 + k + TOK]
    return total


def tri_of(lower):
    row = lax.broadcasted_iota(jnp.int32, (TOK, TOK), 0)
    col = lax.broadcasted_iota(jnp.int32, (TOK, TOK), 1)
    return row >= col if lower else row <= col


def head_lanes():
    lane = lax.broadcasted_iota(jnp.int32, (TOK, 128), 1)
    return (lane % 8) < 3


def input_back_body(
    gsum_ref, next_ref, dstep_ref, taps_ref, dgate_ref, w_ref, x_ref, g_ref, gain_ref,
    gpre_ref, gside_ref, out_ref, ggain_ref,
    hid_s,
):
    def conv_tile(i, carry):
        cols = pl.ds(pl.multiple_of(i * 128, 128), 128)
        cat = jnp.concatenate([gsum_ref[:, cols], next_ref[:, cols]], axis=0)
        taps = taps_ref[:, cols]
        total = taps[3:4] * cat[:TOK]
        for k in range(3):
            total = total + taps[k : k + 1] * cat[3 - k : 3 - k + TOK]
        gpre_ref[:, cols] = total.astype(BF16)
        return carry

    lax.fori_loop(0, CONV // 128, conv_tile, 0)
    gside_ref[:, :128] = dstep_ref[...].astype(BF16)
    gside_ref[:, 128:GATE0] = jnp.zeros((TOK, 128), BF16)
    gside_ref[:, GATE0:] = dgate_ref[...]

    def project(n, carry):
        rows = pl.ds(pl.multiple_of(n * 256, 256), 256)
        hid_s[:, rows] = dot32(gpre_ref[...], w_ref[0, rows, :], ((1,), (1,))) + dot32(
            gside_ref[...], w_ref[1, rows, :], ((1,), (1,))
        )
        return carry

    lax.fori_loop(0, D // 256, project, 0)
    x = x_ref[...].astype(F32)
    grad = hid_s[...]
    inv = lax.rsqrt(jnp.sum(x * x, axis=1, keepdims=True) / D + EPS)
    scaled = grad * gain_ref[0:1, :]
    dots = jnp.sum(scaled * x, axis=1, keepdims=True)
    dx = scaled * inv - x * (dots * inv * inv * inv / D)
    out_ref[...] = (g_ref[...].astype(F32) + dx).astype(BF16)
    ggain_ref[...] = jnp.broadcast_to(jnp.sum(grad * x * inv, axis=0, keepdims=True), (8, D))


def input_backward(gsum, after, dstep, taps, dgate, w_in, x, g, gain):
    return pl.pallas_call(
        input_back_body,
        grid=(1,),
        out_shape=(
            jax.ShapeDtypeStruct((TOK, HALF), BF16),
            jax.ShapeDtypeStruct((TOK, HALF), BF16),
            jax.ShapeDtypeStruct((TOK, D), BF16),
            jax.ShapeDtypeStruct((8, D), F32),
        ),
        in_specs=[
            whole(TOK, CONV), whole(8, CONV), whole(TOK, 128), whole(8, CONV), whole(TOK, INNER),
            whole(2, D, HALF), whole(TOK, D), whole(TOK, D), whole(8, D),
        ],
        out_specs=(whole(TOK, HALF), whole(TOK, HALF), whole(TOK, D), whole(8, D)),
        scratch_shapes=[pltpu.VMEM((TOK, D), F32)],
        compiler_params=pltpu.CompilerParams(vmem_limit_bytes=VMEM_LIMIT),
        name="input_backward",
    )(gsum, after, dstep, taps, dgate, w_in, x, g, gain)


def exact_parts(value):
    parts = []
    for _ in range(3):
        part = lax.reduce_precision(value, 8, 7)
        parts.append(part.astype(BF16))
        value = value - part
    return jnp.stack(parts)


def rows8(vector):
    return jnp.broadcast_to(vector[None, :], (8, vector.shape[0]))


def step_lanes(step):
    lead = step.shape[0]
    return jnp.pad(step.reshape(lead, OWNERS, 3), ((0, 0), (0, 0), (0, 5))).reshape(lead, 128)


def pack_small(norm_gain, inner_gain, conv_inner, conv_bc, heads):
    flat = jnp.concatenate(
        [norm_gain, inner_gain, conv_inner.reshape(-1), conv_bc.reshape(-1), exact_parts(heads).reshape(-1)]
    )
    return jnp.pad(flat, (0, 24 * 128 - flat.shape[0])).reshape(24, 128)


def unpack_small(cells):
    rows = cells.reshape(64, 24 * 128)
    norm_gain = rows[:, :24].reshape(D).astype(F32)
    inner_gain = rows[:, 24:72].reshape(INNER).astype(F32)
    conv_inner = rows[:, 72:312].reshape(64, 5, 48).transpose(1, 0, 2).reshape(5, INNER)
    conv_bc = rows[:, 312:332].reshape(64, 5, 4).transpose(1, 0, 2).reshape(5, 2 * STATE)
    taps = jnp.concatenate([conv_inner, conv_bc], axis=1).astype(F32)
    taps = jnp.pad(taps, ((0, 3), (0, 0)))
    heads = rows[::4, 332:359].reshape(OWNERS, 3, 3, 3).astype(F32).sum(axis=1)
    heads = jnp.pad(heads.transpose(1, 0, 2), ((0, 5), (0, 0), (0, 5))).reshape(8, 128)
    return rows8(norm_gain), rows8(inner_gain), taps, heads


def small_grads(norm_gain, inner_gain, taps, heads, seq_pos):
    conv_inner = taps[:5, :INNER].reshape(5, 64, 48).transpose(1, 0, 2).reshape(64, 240)
    conv_bc = taps[:5, INNER:].reshape(5, 64, 4).transpose(1, 0, 2).reshape(64, 20)
    head = heads[:3].reshape(3, OWNERS, 8)[:, :, :3].transpose(1, 0, 2).reshape(OWNERS, 9)
    head = jnp.repeat(head, 4, axis=0)
    flat = jnp.concatenate(
        [norm_gain.reshape(64, 24), inner_gain.reshape(64, 48), conv_inner, conv_bc, head], axis=1
    )
    return jnp.pad(flat, ((0, 0), (0, 24 * 128 - flat.shape[1]))).reshape(D, 128)


def swap_cores(value):
    return lax.ppermute(value, "section", [(0, 1), (1, 0)])


def places():
    section = lax.axis_index("section")
    seq = lax.axis_index("seq")
    return section, seq // 4, lax.rem(seq, 4), lax.axis_index("wsh")


def x_peer(k):
    return {"wsh": lax.rem(lax.axis_index("wsh") + k, 4)}


def z_peer(k):
    _, y, z, _ = places()
    return {"seq": y * 4 + lax.rem(z + k, 4)}


def y_peer(k):
    _, y, z, _ = places()
    return {"seq": lax.rem(y + k, 4) * 4 + z}


def greet(with_sibling):
    barrier = pltpu.get_barrier_semaphore()
    for k in range(1, 4):
        for peer in (x_peer(k), y_peer(k), z_peer(k)):
            pl.semaphore_signal(barrier, inc=1, device_id=peer, device_id_type=MESH)
    if with_sibling:
        section = lax.axis_index("section")
        pl.semaphore_signal(barrier, inc=1, device_id={"section": 1 - section}, device_id_type=MESH)
    pl.semaphore_wait(barrier, 10 if with_sibling else 9)


def remote(src, dst, sems, index, peer):
    copy = pltpu.make_async_remote_copy(
        src_ref=src, dst_ref=dst, send_sem=sems[0].at[index], recv_sem=sems[1].at[index],
        device_id=peer, device_id_type=MESH,
    )
    copy.start()
    return copy


def gather_body(p_ref, o_ref, p1_ref, o1_ref, w_ref, wo_ref, pa, pb, po, stage, rows_s, stage1, rows1, send_s, recv_s, own_s):
    c, y, z, x = places()
    sems = (send_s, recv_s)
    greet(True)
    started = []

    def go(src, dst, index, peer):
        copy = remote(src, dst, sems, index, peer)
        started.append(copy)
        return copy

    first = [go(p_ref, stage.at[x], k - 1, x_peer(k)) for k in range(1, 4)]
    out_z = [go(o_ref, wo_ref.at[c, y, z, x], 2 + k, z_peer(k)) for k in range(1, 4)]
    own_o = pltpu.make_async_copy(o_ref, wo_ref.at[c, y, z, x], own_s.at[0])
    own_o.start()
    first1 = [go(p1_ref, stage1.at[x], 99 + k, x_peer(k)) for k in range(1, 4)]
    out1_z = [go(o1_ref, po.at[y, z], 102 + k, z_peer(k)) for k in range(1, 4)]
    own_o1 = pltpu.make_async_copy(o1_ref, po.at[y, z], own_s.at[2])
    own_o1.start()
    stage[x] = p_ref[...]
    stage1[x] = p1_ref[...]
    for copy in first:
        copy.wait_recv()
    rows_s[...] = jnp.concatenate([stage[n].astype(F32)[:24] for n in range(4)], axis=0).astype(BF16)
    left = pl.ds(0, CUT)
    right = pl.ds(CUT, CUT)
    a_z = [go(rows_s.at[:, left], w_ref.at[c, y, z, :, left], 5 + k, z_peer(k)) for k in range(1, 4)]
    b_y = [go(rows_s.at[:, right], w_ref.at[c, y, z, :, right], 8 + k, y_peer(k)) for k in range(1, 4)]
    own_w = pltpu.make_async_copy(rows_s, w_ref.at[c, y, z], own_s.at[1])
    own_w.start()
    own_o.wait()
    own_w.wait()
    sibling = {"section": 1 - c}
    arrivals = []
    passed = []
    peers = (y_peer, z_peer, x_peer)

    def band(kind, n, moved):
        if kind == 0:
            return w_ref.at[c, lax.rem(y + 4 - moved, 4), lax.rem(z + 4 - n, 4), :, left]
        if kind == 1:
            return w_ref.at[c, lax.rem(y + 4 - n, 4), lax.rem(z + 4 - moved, 4), :, right]
        return wo_ref.at[c, lax.rem(y + 4 - n, 4), :, lax.rem(x + 4 - moved, 4)]

    def spread_out(j):
        for k in range(1, 4):
            for kind in range(3):
                part = band(kind, j, 0)
                arrivals.append((kind, j, k, go(part, part, 12 + 12 * kind + 3 * j + k - 1, peers[kind](k))))
        for kind in range(3):
            part = band(kind, j, 0)
            passed.append(go(part, part, 48 + 16 * kind + j, sibling))

    for copy in out_z:
        copy.wait_recv()
    out_y = [go(band(2, 0, 0), band(2, 0, 0), 96 + k, y_peer(k)) for k in range(1, 4)]
    spread_out(0)
    for j in range(1, 4):
        a_z[j - 1].wait_recv()
        b_y[j - 1].wait_recv()
        out_y[j - 1].wait_recv()
        spread_out(j)
    for copy in first1:
        copy.wait_recv()
    rows1[...] = jnp.concatenate([stage1[n].astype(F32)[:24] for n in range(4)], axis=0).astype(BF16)
    extra = [go(rows1.at[:, left], pa.at[z], 105 + k, z_peer(k)) for k in range(1, 4)]
    extra += [go(rows1.at[:, right], pb.at[y], 108 + k, y_peer(k)) for k in range(1, 4)]
    own_rows = [
        pltpu.make_async_copy(rows1.at[:, left], pa.at[z], own_s.at[3]),
        pltpu.make_async_copy(rows1.at[:, right], pb.at[y], own_s.at[4]),
    ]
    for copy in own_rows:
        copy.start()
    own_o1.wait()
    for copy in out1_z:
        copy.wait_recv()
    extra += [go(po.at[y], po.at[y], 111 + k, y_peer(k)) for k in range(1, 4)]
    for n, (kind, j, k, copy) in enumerate(arrivals):
        copy.wait_recv()
        part = band(kind, j, k)
        passed.append(go(part, part, 48 + 16 * kind + 4 + n // 3, sibling))
    for copy in passed + extra:
        copy.wait_recv()
    for copy in own_rows:
        copy.wait()
    for copy in started:
        copy.wait_send()


def gather_weights(p, o, p1, o1):
    w, wo, pa, pb, po = pl.pallas_call(
        gather_body,
        out_shape=(
            jax.ShapeDtypeStruct((2, 4, 4, 96, HALF), BF16),
            jax.ShapeDtypeStruct((2, 4, 4, 4, 48, WALF), BF16),
            jax.ShapeDtypeStruct((4, 96, CUT), BF16),
            jax.ShapeDtypeStruct((4, 96, CUT), BF16),
            jax.ShapeDtypeStruct((4, 4, 48, WALF), BF16),
        ),
        in_specs=[vmem()] * 4,
        out_specs=(any_spec(),) * 5,
        scratch_shapes=[
            pltpu.VMEM((4, 32, HALF), BF16),
            pltpu.VMEM((96, HALF), BF16),
            pltpu.VMEM((4, 32, HALF), BF16),
            pltpu.VMEM((96, HALF), BF16),
            pltpu.SemaphoreType.DMA((115,)),
            pltpu.SemaphoreType.DMA((115,)),
            pltpu.SemaphoreType.DMA((5,)),
        ],
        compiler_params=pltpu.CompilerParams(
            collective_id=3, has_side_effects=True, vmem_limit_bytes=VMEM_LIMIT
        ),
        name="gather_weights",
    )(p, o, p1, o1)
    return w, wo, (pa, pb, po)


def fetch(src, dst, sem):
    copy = pltpu.make_async_copy(src, dst, sem)
    copy.start()
    return copy


def greet_seq(with_x):
    me = lax.axis_index("seq")
    section = lax.axis_index("section")
    barrier = pltpu.get_barrier_semaphore()
    for d in range(1, OWNERS):
        pl.semaphore_signal(
            barrier, inc=1, device_id={"seq": lax.rem(me + d, OWNERS)}, device_id_type=MESH
        )
    pl.semaphore_signal(barrier, inc=1, device_id={"section": 1 - section}, device_id_type=MESH)
    if with_x:
        for k in range(1, 4):
            pl.semaphore_signal(barrier, inc=1, device_id=x_peer(k), device_id_type=MESH)
    pl.semaphore_wait(barrier, OWNERS + (3 if with_x else 0))


class Exchange:
    def __init__(self, backward, refs):
        (self.ds, self.got, self.back, self.kept, self.fade, self.final, self.other, self.begin, self.ready,
         self.send_a, self.recv_a, self.send_b, self.recv_b, self.swap_s, self.own_s) = refs
        self.backward = backward
        self.me = lax.axis_index("seq")
        self.section = lax.axis_index("section")

    def first_copy(self, peer, d):
        return pltpu.make_async_remote_copy(
            src_ref=self.ds.at[peer], dst_ref=self.got.at[self.me],
            send_sem=self.send_a.at[d], recv_sem=self.recv_a.at[d],
            device_id={"seq": peer}, device_id_type=MESH,
        )

    def send(self, peer):
        d = lax.rem(peer + OWNERS - self.me, OWNERS)

        @pl.when(d != 0)
        def _():
            self.first_copy(peer, d).start()

        @pl.when(d == 0)
        def _():
            self.got[self.me] = self.ds[self.me]

    def back_copy(self, d):
        peer = lax.rem(self.me + d, OWNERS)
        return pltpu.make_async_remote_copy(
            src_ref=self.ready.at[peer], dst_ref=self.back.at[self.me],
            send_sem=self.send_b.at[d], recv_sem=self.recv_b.at[d],
            device_id={"seq": peer}, device_id_type=MESH,
        )

    def scan(self, decays):
        def rows_of(dec):
            return jnp.concatenate([jnp.broadcast_to(dec[h : h + 1], (64, 128)) for h in range(3)], axis=0)

        for d in range(1, OWNERS):
            self.first_copy(lax.rem(self.me + d, OWNERS), d).wait_recv()
        final, fade, kept = self.final, self.fade, self.kept
        final[...] = jnp.zeros((OWN, STATE), F32)
        fade[0] = jnp.ones((8, 128), F32)

        def step(n, carry):
            c = OWNERS - 1 - n if self.backward else n
            state = final[...]
            kept[c] = state
            dec = decays[c]
            final[...] = rows_of(dec) * state + self.got[c].astype(F32)
            fade[n + 1] = fade[n] * dec
            return carry

        lax.fori_loop(0, OWNERS, step, 0)
        swap = pltpu.make_async_remote_copy(
            src_ref=final, dst_ref=self.other, send_sem=self.swap_s.at[0], recv_sem=self.swap_s.at[1],
            device_id={"section": 1 - self.section}, device_id_type=MESH,
        )
        swap.start()
        takes = 0 if self.backward else 1
        self.begin[...] = jnp.zeros((OWN, STATE), F32)

        @pl.when(self.section == takes)
        def _():
            swap.wait_recv()
            self.begin[...] = self.other[...]

        begin = self.begin[...]
        for d in range(OWNERS):
            c = lax.rem(self.me + d, OWNERS)
            n = OWNERS - 1 - c if self.backward else c
            value = (kept[c] + rows_of(fade[n]) * begin).astype(BF16)
            if d == 0:
                self.back[c] = value
            else:
                self.ready[c] = value
                self.back_copy(d).start()

        @pl.when(self.section != takes)
        def _():
            swap.wait_recv()

        swap.wait_send()

    def finish(self):
        for d in range(1, OWNERS):
            self.back_copy(d).wait_recv()

    def drain(self):
        for d in range(1, OWNERS):
            self.first_copy(lax.rem(self.me + d, OWNERS), d).wait_send()
            self.back_copy(d).wait_send()


def exchange_scratch():
    block = pltpu.VMEM((OWNERS, OWN, STATE), BF16)
    part = pltpu.VMEM((OWN, STATE), F32)
    sems = pltpu.SemaphoreType.DMA((OWNERS,))
    return [
        block, block, block, pltpu.VMEM((OWNERS, OWN, STATE), F32), pltpu.VMEM((OWNERS + 1, 8, 128), F32),
        part, part, part, block, sems, sems, sems, sems,
        pltpu.SemaphoreType.DMA((2,)), pltpu.SemaphoreType.DMA((2,)),
    ]


def head_rows_at(ref, i, q):
    parts = []
    for h in (2 * q, 2 * q + 1):
        parts.append(ref[2 * i + h // 3, pl.ds(64 * (h % 3), 64), :])
    return jnp.concatenate(parts, axis=0)


def store_heads(ref, i, q, value):
    for n, h in enumerate((2 * q, 2 * q + 1)):
        ref[2 * i + h // 3, pl.ds(64 * (h % 3), 64), :] = value[64 * n : 64 * n + 64]


def own_group(n):
    return lax.rem(lax.axis_index("seq") // 2 + n, 8)


class Spread:
    def __init__(self, pa, pb, po, w_ref, wo_ref, send_s, recv_s, own_s):
        self.parts = (pa, pb, po)
        self.w, self.wo = w_ref, wo_ref
        self.sems = (send_s, recv_s)
        self.own_s = own_s
        self.place = places()
        self.started = []
        self.passed = []
        self.arrivals = []
        self.left = pl.ds(0, CUT)
        self.right = pl.ds(CUT, CUT)

    def go(self, src, dst, index, peer):
        copy = remote(src, dst, self.sems, index, peer)
        self.started.append(copy)
        return copy

    def spot(self, kind, n, moved):
        c, y, z, x = self.place
        if kind == 0:
            return self.w.at[c, lax.rem(y + 4 - moved, 4), n, :, self.left]
        if kind == 1:
            return self.w.at[c, n, lax.rem(z + 4 - moved, 4), :, self.right]
        return self.wo.at[c, n, :, lax.rem(x + 4 - moved, 4)]

    def start(self):
        sibling = {"section": 1 - self.place[0]}
        peers = (y_peer, z_peer, x_peer)
        self.own = []
        for n in range(4):
            for k in range(1, 4):
                for kind in range(3):
                    src = self.parts[kind].at[n]
                    copy = self.go(src, self.spot(kind, n, 0), 12 * kind + 3 * n + k - 1, peers[kind](k))
                    self.arrivals.append((kind, n, k, copy))
            for kind in range(3):
                src = self.parts[kind].at[n]
                dst = self.spot(kind, n, 0)
                self.passed.append(self.go(src, dst, 36 + 4 * kind + n, sibling))
                self.own.append(fetch(src, dst, self.own_s.at[4 * kind + n]))

    def forward(self, begin, end):
        sibling = {"section": 1 - self.place[0]}
        for at in range(begin, end):
            kind, n, k, copy = self.arrivals[at]
            copy.wait_recv()
            dst = self.spot(kind, n, k)
            self.passed.append(self.go(dst, dst, 48 + at, sibling))

    def end(self):
        for copy in self.own:
            copy.wait()
        for copy in self.passed:
            copy.wait_recv()
        for copy in self.started:
            copy.wait_send()


def forward_body(rider, *refs):
    (live_ref, pre_ref, side_ref, halo_ref, taps_ref, heads_ref, gain_ref, x_ref, wo_ref) = refs[:9]
    at = 9
    if rider:
        bands = refs[at : at + 3]
        at += 3
    (act_ref, dact_ref, dt_ref, cum_ref, dec_ref, state_ref, raw_ref, y_ref, gated_ref, inv_ref, out_ref) = refs[at : at + 11]
    at += 11
    if rider:
        next_w, next_wo = refs[at : at + 2]
        at += 2
    wo_s, z_s, cumt_s, square_s, dec_s, dec_send, dec_recv, load_s = refs[at : at + 8]
    at += 8
    ex = Exchange(False, refs[at : at + 15])
    at += 15
    load = fetch(wo_ref, wo_s, load_s.at[0])
    greet_seq(rider)
    if rider:
        spread = Spread(*bands, next_w, next_wo, *refs[at : at + 3])
        spread.start()
    me = lax.axis_index("seq")
    live = live_ref[0]
    heads = heads_ref[...]
    step = side_ref[:, :128].astype(BF16).astype(F32) + heads[0:1]
    dt = jnp.maximum(step, 0.0) + jnp.log1p(jnp.exp(-jnp.abs(step)))
    dt = jnp.where(head_lanes(), dt, 0.0) * live
    rate = -dt * jnp.exp(heads[1:2])
    cum = split_left(tri_of(True).astype(F32).astype(BF16), rate, 3)
    dt_ref[...] = dt
    cum_ref[...] = cum
    last = jnp.broadcast_to(cum[TOK - 1 : TOK], (TOK, 128))
    dec_s[...] = jnp.exp(last).T.reshape(OWNERS, 8, 128)
    dec_ref[me] = dec_s[me]

    def dec_copy(d):
        peer = lax.rem(me + d, OWNERS)
        return pltpu.make_async_remote_copy(
            src_ref=dec_s.at[peer], dst_ref=dec_ref.at[me], send_sem=dec_send.at[d], recv_sem=dec_recv.at[d],
            device_id={"seq": peer}, device_id_type=MESH,
        )

    for d in range(1, OWNERS):
        dec_copy(d).start()
    weight = dt * jnp.exp(last - cum)

    def conv_tile(cols):
        blk = pre_ref[:, cols].astype(F32)
        cat = jnp.concatenate([halo_ref[:, cols].astype(F32), blk], axis=0)
        summed = conv_of(cat, taps_ref[:, cols])
        sig = 1.0 / (1.0 + jnp.exp(-summed))
        act = summed * sig
        act_ref[:, cols] = act
        dact_ref[:, cols] = sig * (1.0 + summed * (1.0 - sig))
        return act

    b = conv_tile(pl.ds(INNER, 128)).astype(BF16)
    c = conv_tile(pl.ds(INNER + 128, 128)).astype(BF16)

    def states(n, carry):
        i = own_group(n)
        wt = to_front(weight, i)
        for q in range(3):
            x = conv_tile(pl.ds(pl.multiple_of(i * 384 + q * 128, 128), 128))
            scaled = (x * pair_cols(wt, q)[2]).astype(BF16)
            store_heads(ex.ds, i, q, dot32(scaled, b, ((0,), (0,))).astype(BF16))
        ex.send(2 * i)
        ex.send(2 * i + 1)
        return carry

    lax.fori_loop(0, 8, states, 0)
    for d in range(1, OWNERS):
        dec_copy(d).wait_recv()
    ex.scan(dec_ref)
    if rider:
        spread.forward(0, 9)
    cumt_s[...] = cum.T
    causal = tri_of(True)
    scores = dot32(c, b, ((1,), (1,)))
    lane = lax.broadcasted_iota(jnp.int32, (TOK, 128), 1)
    square_s[...] = jnp.zeros((TOK, 128), F32)

    def inside(i, carry):
        cum_i = to_front(cum, i)
        dt_i = to_front(dt, i)
        rows = cumt_s[pl.ds(pl.multiple_of(16 * i, 16), 16), :]
        for q in range(3):
            cols = pl.ds(pl.multiple_of(i * 384 + q * 128, 128), 128)
            cum_a, cum_b, _ = pair_cols(cum_i, q)
            u = act_ref[:, cols] * pair_cols(dt_i, q)[2]
            mixes = []
            for cum_h, off in ((cum_a, LANES[2 * q]), (cum_b, LANES[2 * q + 1])):
                gap = cum_h - rows[off : off + 1]
                mixes.append((scores * jnp.exp(jnp.where(causal, gap, -1e30))).astype(BF16))
            terms = jnp.concatenate(
                [jnp.where(lane < 64, u, 0.0).astype(BF16), jnp.where(lane < 64, 0.0, u).astype(BF16)], axis=0
            )
            raw_ref[:, cols] = dot32(jnp.concatenate(mixes, axis=1), terms)
        return carry

    lax.fori_loop(0, 8, inside, 0)
    ex.finish()
    save = fetch(ex.back, state_ref, load_s.at[1])

    def across(i, carry):
        cum_i = to_front(cum, i)
        skip_i = pltpu.roll(heads, lax.rem(128 - 16 * i, 128), 1)[2:3]
        for q in range(3):
            cols = pl.ds(pl.multiple_of(i * 384 + q * 128, 128), 128)
            x = act_ref[:, cols]
            state = head_rows_at(ex.back, i, q)
            raw = raw_ref[:, cols] + jnp.exp(pair_cols(cum_i, q)[2]) * dot32(c, state, ((1,), (1,)))
            raw_ref[:, cols] = raw
            y = (raw + pair_row(skip_i, q) * x).astype(BF16)
            y_ref[:, cols] = y
            gate = side_ref[:, pl.ds(pl.multiple_of(GATE0 + i * 384 + q * 128, 128), 128)]
            z = y.astype(F32) * (gate / (1.0 + jnp.exp(-gate)))
            z_s[:, cols] = z
            square_s[...] += z * z
        return carry

    lax.fori_loop(0, 8, across, 0)
    if rider:
        spread.forward(9, 18)
    total = jnp.sum(square_s[...], axis=1, keepdims=True)
    inv = jnp.broadcast_to(lax.rsqrt(total / INNER + EPS), (TOK, 128))
    inv_ref[...] = inv

    def scale(i, carry):
        cols = pl.ds(pl.multiple_of(i * 128, 128), 128)
        gated_ref[:, cols] = (z_s[:, cols] * inv * gain_ref[0:1, cols]).astype(BF16)
        return carry

    lax.fori_loop(0, 24, scale, 0)
    load.wait()
    for half in range(2):

        def project(n, carry):
            cols = pl.ds(pl.multiple_of(n * 256, 256), 256)
            full = pl.ds(pl.multiple_of(half * WALF + n * 256, 256), 256)
            branch = dot32(gated_ref[...], wo_s[half, :, cols])
            out_ref[:, full] = (x_ref[:, full].astype(F32) + live * branch).astype(BF16)
            return carry

        lax.fori_loop(0, WALF // 256, project, 0)
    save.wait()
    if rider:
        spread.forward(18, 36)
        spread.end()
    for d in range(1, OWNERS):
        dec_copy(d).wait_send()
    ex.drain()


def any_spec():
    return pl.BlockSpec(memory_space=pl.ANY)


def block_forward(live, pre, side, halo, taps, heads, gain, x, w_o, bands):
    rider = bands is not None
    tile = pltpu.VMEM((TOK, 128), F32)
    out_shape = [
        jax.ShapeDtypeStruct((TOK, CONV), F32),
        jax.ShapeDtypeStruct((TOK, CONV), F32),
        jax.ShapeDtypeStruct((TOK, 128), F32),
        jax.ShapeDtypeStruct((TOK, 128), F32),
        jax.ShapeDtypeStruct((OWNERS, 8, 128), F32),
        jax.ShapeDtypeStruct((OWNERS, OWN, STATE), BF16),
        jax.ShapeDtypeStruct((TOK, INNER), F32),
        jax.ShapeDtypeStruct((TOK, INNER), BF16),
        jax.ShapeDtypeStruct((TOK, INNER), BF16),
        jax.ShapeDtypeStruct((TOK, 128), F32),
        jax.ShapeDtypeStruct((TOK, D), BF16),
    ]
    out_specs = [vmem()] * 5 + [any_spec()] + [vmem()] * 5
    scratch = [
        pltpu.VMEM((2, INNER, WALF), BF16), pltpu.VMEM((TOK, INNER), F32), tile, tile,
        pltpu.VMEM((OWNERS, 8, 128), F32), pltpu.SemaphoreType.DMA((OWNERS,)), pltpu.SemaphoreType.DMA((OWNERS,)),
        pltpu.SemaphoreType.DMA((2,)),
    ] + exchange_scratch()
    args = [live, pre, side, halo, taps, heads, gain, x, w_o]
    in_specs = [smem()] + [vmem()] * 7 + [any_spec()]
    if rider:
        args += list(bands)
        in_specs += [vmem()] * 3
        out_shape += [
            jax.ShapeDtypeStruct((2, 4, 4, 96, HALF), BF16),
            jax.ShapeDtypeStruct((2, 4, 4, 4, 48, WALF), BF16),
        ]
        out_specs += [any_spec()] * 2
        scratch += [
            pltpu.SemaphoreType.DMA((84,)), pltpu.SemaphoreType.DMA((84,)), pltpu.SemaphoreType.DMA((12,)),
        ]
    return pl.pallas_call(
        functools.partial(forward_body, rider),
        out_shape=tuple(out_shape),
        in_specs=in_specs,
        out_specs=tuple(out_specs),
        scratch_shapes=scratch,
        compiler_params=pltpu.CompilerParams(
            collective_id=1 if rider else 2, has_side_effects=True, vmem_limit_bytes=VMEM_LIMIT
        ),
        name="block_forward",
    )(*args)


class Fold:
    def __init__(self, gi, go, sa, sb, so, ra, rb, ro, send_s, recv_s, own_s):
        self.gi, self.go_ref = gi, go
        self.target = (sa, sb, so)
        self.buf = (ra, rb, ro)
        self.sems = (send_s, recv_s)
        self.own_s = own_s
        self.place = places()
        self.copies = []

    def start(self):
        _, y, z, x = self.place
        left = pl.ds(0, CUT)
        right = pl.ds(CUT, CUT)
        ra, rb, ro = self.buf
        for k in range(1, 4):
            self.copies += [
                remote(self.gi.at[lax.rem(y + k, 4), :, :, left], ra.at[k], self.sems, k - 1, y_peer(k)),
                remote(self.gi.at[:, lax.rem(z + k, 4), :, right], rb.at[k], self.sems, 2 + k, z_peer(k)),
                remote(self.go_ref.at[:, :, lax.rem(x + k, 4)], ro.at[k], self.sems, 5 + k, x_peer(k)),
            ]
        self.own = [
            fetch(self.gi.at[y, :, :, left], ra.at[0], self.own_s.at[0]),
            fetch(self.gi.at[:, z, :, right], rb.at[0], self.own_s.at[1]),
            fetch(self.go_ref.at[:, :, x], ro.at[0], self.own_s.at[2]),
        ]

    def end(self):
        for copy in self.own:
            copy.wait()
        for copy in self.copies:
            copy.wait_recv()
        for buf, target in zip(self.buf, self.target):
            add_blocks(buf, target)
        for copy in self.copies:
            copy.wait_send()


def add_blocks(parts, target):
    rows, cols = parts.shape[-2:]
    lead = parts.shape[1:-2]
    blocks = functools.reduce(lambda a, b: a * b, lead, 1)
    per = rows // 16

    def body(n, carry):
        b = n // per
        at = pl.ds(pl.multiple_of(lax.rem(n, per) * 16, 16), 16)
        spot = (b,) if len(lead) == 1 else (b // lead[1], lax.rem(b, lead[1]))
        total = parts[(0,) + spot + (at, slice(None))].astype(F32)
        for k in range(1, 4):
            total = total + parts[(k,) + spot + (at, slice(None))].astype(F32)
        target[spot + (at, slice(None))] = total.astype(target.dtype)
        return carry

    lax.fori_loop(0, blocks * per, body, 0)


def backward_body(rider, *refs):
    (live_ref, g_ref, side_ref, y_ref, gain_ref, inv_ref, act_ref, dact_ref, dt_ref, cum_ref, raw_ref, pre_ref,
     halo_ref, heads_ref, dec_ref, wo_ref, state_ref) = refs[:17]
    at = 17
    if rider:
        grads = refs[at : at + 2]
        at += 2
    (gb_ref, dgate_ref, gmid_ref, gsum_ref, dstep_ref, gtaps_ref, ghead_ref) = refs[at : at + 7]
    at += 7
    if rider:
        folded = refs[at : at + 3]
        at += 3
    (wo_s, gg_s, dots_s, dy_s, cumt_s, edge_s, dscore_s, gb_s, gc_s, xdu_s, dyy_s, row_s, state_s, load_s) = refs[at : at + 14]
    at += 14
    ex = Exchange(True, refs[at : at + 15])
    at += 15
    load = fetch(wo_ref, wo_s, load_s.at[0])
    load_state = fetch(state_ref, state_s, load_s.at[1])
    greet_seq(rider)
    if rider:
        fold = Fold(*grads, *folded, *refs[at : at + 6])
        fold.start()
    live = live_ref[0]
    heads = heads_ref[...]
    gb = (g_ref[...].astype(F32) * live).astype(BF16)
    gb_ref[...] = gb
    inv = inv_ref[...]
    b = act_ref[:, INNER : INNER + 128].astype(BF16)
    c = act_ref[:, INNER + 128 : CONV].astype(BF16)
    dt = dt_ref[...]
    cum = cum_ref[...]
    dots_s[...] = jnp.zeros((TOK, 128), F32)
    load.wait()

    def first(i, carry):
        rows = pl.ds(pl.multiple_of(i * 384, 384), 384)
        gg = dot32(gb[:, :WALF], wo_s[0, rows, :], ((1,), (1,)))
        gg = gg + dot32(gb[:, WALF:], wo_s[1, rows, :], ((1,), (1,)))
        gg_s[:, rows] = gg
        for q in range(3):
            cols = pl.ds(pl.multiple_of(i * 384 + q * 128, 128), 128)
            gate = side_ref[:, pl.ds(pl.multiple_of(GATE0 + i * 384 + q * 128, 128), 128)]
            z = y_ref[:, cols].astype(F32) * (gate / (1.0 + jnp.exp(-gate)))
            dots_s[...] += gg[:, 128 * q : 128 * q + 128] * gain_ref[0:1, cols] * z
        return carry

    lax.fori_loop(0, 8, first, 0)
    total = jnp.broadcast_to(jnp.sum(dots_s[...], axis=1, keepdims=True), (TOK, 128))
    shift = total * inv * inv * inv / INNER

    def second(n, carry):
        i = own_group(n)
        cum_i = to_front(cum, i)
        for q in range(3):
            cols = pl.ds(pl.multiple_of(i * 384 + q * 128, 128), 128)
            gate = side_ref[:, pl.ds(pl.multiple_of(GATE0 + i * 384 + q * 128, 128), 128)]
            y = y_ref[:, cols].astype(F32)
            gg = gg_s[:, cols]
            sig = 1.0 / (1.0 + jnp.exp(-gate))
            act = gate * sig
            z = y * act
            dz = gg * gain_ref[0:1, cols] * inv - z * shift
            dy = (dz * act).astype(BF16)
            dy_s[:, cols] = dy
            dgate_ref[:, cols] = (dz * y * (sig * (1.0 + gate * (1.0 - sig)))).astype(BF16)
            gmid_ref[:, cols] = jnp.broadcast_to(
                jnp.sum(gg * z * inv, axis=0, keepdims=True), (8, 128)
            )
            far = (dy.astype(F32) * jnp.exp(pair_cols(cum_i, q)[2])).astype(BF16)
            store_heads(ex.ds, i, q, dot32(far, c, ((0,), (0,))).astype(BF16))
        ex.send(2 * i)
        ex.send(2 * i + 1)
        return carry

    lax.fori_loop(0, 8, second, 0)
    ex.scan(dec_ref)
    load_state.wait()
    cumt_s[...] = cum.T
    causal = tri_of(True)
    scores = dot32(c, b, ((1,), (1,)))
    lane = lax.broadcasted_iota(jnp.int32, (TOK, 128), 1)
    pick_row = lax.broadcasted_iota(jnp.int32, (128, 128), 0)
    pick_col = lax.broadcasted_iota(jnp.int32, (128, 128), 1)
    picks = []
    for q in range(3):
        target = jnp.where(pick_row < 64, LANES[2 * q], LANES[2 * q + 1])
        picks.append((pick_col == target).astype(F32).astype(BF16))
    for ref in (dscore_s, gb_s, gc_s, xdu_s, dyy_s, row_s, gtaps_ref):
        ref[...] = jnp.zeros_like(ref)

    def inside(i, carry):
        cum_i = to_front(cum, i)
        dt_i = to_front(dt, i)
        rows = cumt_s[pl.ds(pl.multiple_of(16 * i, 16), 16), :]
        for q in range(3):
            cols = pl.ds(pl.multiple_of(i * 384 + q * 128, 128), 128)
            cum_a, cum_b, cum_x = pair_cols(cum_i, q)
            u16 = (act_ref[:, cols] * pair_cols(dt_i, q)[2]).astype(BF16)
            dy16 = dy_s[:, cols]
            nil = jnp.zeros_like(dy16)
            dys = jnp.concatenate([jnp.where(lane < 64, dy16, nil), jnp.where(lane < 64, nil, dy16)], axis=0)
            both = dot32(dys, u16, ((1,), (1,)))
            mixes = []
            for n, (cum_h, off) in enumerate(((cum_a, LANES[2 * q]), (cum_b, LANES[2 * q + 1]))):
                gap = cum_h - rows[off : off + 1]
                decay = jnp.exp(jnp.where(causal, gap, -1e30))
                mixes.append((scores * decay).astype(BF16))
                dscore_s[...] += both[n * TOK : n * TOK + TOK] * decay
            gg_s[:, cols] = dot32(jnp.concatenate(mixes, axis=0), dys, ((0,), (0,)))
            far = (dy16.astype(F32) * jnp.exp(cum_x)).astype(BF16)
            gc_s[...] += dot32(far, head_rows_at(state_s, i, q))
        return carry

    lax.fori_loop(0, 8, inside, 0)

    def conv_back(cols, gact):
        gsum = gact * dact_ref[:, cols]
        gsum_ref[:, cols] = gsum
        blk = pre_ref[:, cols].astype(F32)
        cat = jnp.concatenate([halo_ref[:, cols].astype(F32), blk], axis=0)
        sums = [jnp.sum(gsum * cat[5 + k : 5 + k + TOK], axis=0, keepdims=True) for k in range(4)]
        sums.append(jnp.sum(gsum, axis=0, keepdims=True))
        gtaps_ref[:, cols] = jnp.concatenate(sums + [jnp.zeros((3, 128), F32)], axis=0)

    ex.finish()

    def across(i, carry):
        cum_i = to_front(cum, i)
        dt_i = to_front(dt, i)
        skip_i = pltpu.roll(heads, lax.rem(128 - 16 * i, 128), 1)[2:3]
        x_du = jnp.zeros((TOK, 128), F32)
        dy_y = jnp.zeros((TOK, 128), F32)
        thin = jnp.zeros((16, 128), F32)
        edges = {}
        for q in range(3):
            cols = pl.ds(pl.multiple_of(i * 384 + q * 128, 128), 128)
            x = act_ref[:, cols]
            cum_x = pair_cols(cum_i, q)[2]
            dt_x = pair_cols(dt_i, q)[2]
            fade = jnp.exp(cum_x[TOK - 1 : TOK] - cum_x)
            u = x * dt_x
            dy = dy_s[:, cols].astype(F32)
            state16 = head_rows_at(state_s, i, q)
            dstate16 = head_rows_at(ex.back, i, q)
            du_far = fade * dot32(b, dstate16, ((1,), (1,)))
            du = gg_s[:, cols] + du_far
            gb_s[...] += dot32((u * fade).astype(BF16), dstate16)
            overlap = state16.astype(F32) * dstate16.astype(F32)
            edges[LANES[2 * q]] = jnp.sum(overlap[:64], axis=0, keepdims=True)
            edges[LANES[2 * q + 1]] = jnp.sum(overlap[64:], axis=0, keepdims=True)
            x_du = x_du + split_right(x * du, picks[q], 2)
            dy_y = dy_y + split_right(dy * raw_ref[:, cols], picks[q], 2)
            thin = thin + split_right(
                jnp.concatenate(
                    [
                        jnp.broadcast_to(jnp.sum(u * du_far, axis=0, keepdims=True), (8, 128)),
                        jnp.broadcast_to(jnp.sum(dy * x, axis=0, keepdims=True), (8, 128)),
                    ],
                    axis=0,
                ),
                picks[q],
                3,
            )
            conv_back(cols, du * dt_x + pair_row(skip_i, q) * dy)
        nothing = jnp.zeros((1, 128), F32)
        edge_s[pl.ds(pl.multiple_of(16 * i, 16), 16), :] = jnp.concatenate(
            [edges.get(k, nothing) for k in range(16)], axis=0
        )
        xdu_s[...] += pltpu.roll(x_du, 16 * i, 1)
        dyy_s[...] += pltpu.roll(dy_y, 16 * i, 1)
        row_s[...] += pltpu.roll(thin, 16 * i, 1)
        return carry

    lax.fori_loop(0, 8, across, 0)
    dscore16 = dscore_s[...].astype(BF16)
    conv_back(pl.ds(INNER, 128), gb_s[...] + dot32(dscore16, c, ((0,), (0,))))
    conv_back(pl.ds(INNER + 128, 128), gc_s[...] + dot32(dscore16, b))
    ones = jnp.ones((128, 128), BF16)
    edge = split_right(edge_s[...], ones, 3).T[0:1] * jnp.exp(cum[TOK - 1 : TOK]) + row_s[0:1]
    x_du = xdu_s[...]
    drate = split_left(tri_of(False).astype(F32).astype(BF16), dyy_s[...] - dt * x_du, 3) + edge
    speed = jnp.exp(heads[1:2])
    ddt = x_du - drate * speed
    step = side_ref[:, :128].astype(BF16).astype(F32) + heads[0:1]
    dstep = jnp.where(head_lanes(), ddt / (1.0 + jnp.exp(-step)), 0.0) * live
    dstep_ref[...] = dstep
    ghead_ref[...] = jnp.concatenate(
        [
            jnp.sum(dstep, axis=0, keepdims=True),
            jnp.sum(-drate * dt * speed, axis=0, keepdims=True),
            row_s[8:9],
            jnp.zeros((5, 128), F32),
        ],
        axis=0,
    )
    if rider:
        fold.end()
    ex.drain()


def fold_shapes():
    return [(4, 96, CUT), (4, 96, CUT), (4, 4, 48, WALF)]


def block_backward(live, g, side, y, gain, inv, act, dact, dt, cum, raw, pre, halo, heads, dec, w_o, states, grads):
    rider = grads is not None
    tile = pltpu.VMEM((TOK, 128), F32)
    out_shape = [
        jax.ShapeDtypeStruct((TOK, D), BF16),
        jax.ShapeDtypeStruct((TOK, INNER), BF16),
        jax.ShapeDtypeStruct((8, INNER), F32),
        jax.ShapeDtypeStruct((TOK, CONV), F32),
        jax.ShapeDtypeStruct((TOK, 128), F32),
        jax.ShapeDtypeStruct((8, CONV), F32),
        jax.ShapeDtypeStruct((8, 128), F32),
    ]
    scratch = [
        pltpu.VMEM((2, INNER, WALF), BF16), pltpu.VMEM((TOK, INNER), F32), tile, pltpu.VMEM((TOK, INNER), BF16),
        tile, tile, tile, tile, tile, tile, tile, pltpu.VMEM((16, 128), F32),
        pltpu.VMEM((OWNERS, OWN, STATE), BF16), pltpu.SemaphoreType.DMA((2,)),
    ] + exchange_scratch()
    args = [live, g, side, y, gain, inv, act, dact, dt, cum, raw, pre, halo, heads, dec, w_o, states]
    in_specs = [smem()] + [vmem()] * 14 + [any_spec()] * 2
    if rider:
        args += list(grads)
        in_specs += [any_spec()] * 2
        out_shape += [jax.ShapeDtypeStruct(shape, BF16) for shape in fold_shapes()]
        scratch += [pltpu.VMEM((4,) + shape, BF16) for shape in fold_shapes()]
        scratch += [pltpu.SemaphoreType.DMA((9,)), pltpu.SemaphoreType.DMA((9,)), pltpu.SemaphoreType.DMA((3,))]
    return pl.pallas_call(
        functools.partial(backward_body, rider),
        out_shape=tuple(out_shape),
        in_specs=in_specs,
        out_specs=(vmem(),) * len(out_shape),
        scratch_shapes=scratch,
        compiler_params=pltpu.CompilerParams(
            collective_id=5 if rider else 6, has_side_effects=True, vmem_limit_bytes=VMEM_LIMIT
        ),
        name="block_backward",
    )(*args)


class Finish:
    def __init__(self, sums, scratch, sems):
        self.sums = sums
        (self.r2a, self.r2b, self.r2o, self.c3, self.r3, self.o2, self.r3o) = scratch
        self.sems = sems
        self.place = places()
        self.started = []

    def go(self, src, dst, index, peer):
        copy = remote(src, dst, self.sems, index, peer)
        self.started.append(copy)
        return copy

    def second(self):
        _, y, z, x = self.place
        sa, sb, so = self.sums
        self.a = [self.go(sa.at[lax.rem(z + k, 4)], self.r2a.at[k], k - 1, z_peer(k)) for k in range(1, 4)]
        self.b = [self.go(sb.at[lax.rem(y + k, 4)], self.r2b.at[k], 2 + k, y_peer(k)) for k in range(1, 4)]
        self.o = [self.go(so.at[lax.rem(y + k, 4)], self.r2o.at[k], 5 + k, y_peer(k)) for k in range(1, 4)]
        self.r2a[0] = sa[z]
        self.r2b[0] = sb[y]
        self.r2o[0] = so[y]

    def third(self):
        _, y, z, x = self.place
        for copy in self.a + self.b:
            copy.wait_recv()
        for n in range(4):
            at = pl.ds(24 * n, 24)
            for parts, cols in ((self.r2a, pl.ds(0, CUT)), (self.r2b, pl.ds(CUT, CUT))):
                total = parts[0, at, :].astype(F32)
                for k in range(1, 4):
                    total = total + parts[k, at, :].astype(F32)
                self.c3[n, :, cols] = total
        self.x = [self.go(self.c3.at[lax.rem(x + k, 4)], self.r3.at[x], 8 + k, x_peer(k)) for k in range(1, 4)]
        for copy in self.o:
            copy.wait_recv()
        add_blocks(self.r2o, self.o2)
        self.z = [self.go(self.o2.at[lax.rem(z + k, 4)], self.r3o.at[k], 11 + k, z_peer(k)) for k in range(1, 4)]
        self.r3[x] = self.c3[x]
        self.r3o[0] = self.o2[z]

    def last(self, in_ref, out_ref):
        for copy in self.x + self.z:
            copy.wait_recv()
        in_ref[...] = self.r3[0] + self.r3[1] + self.r3[2] + self.r3[3]
        total = self.r3o[0].astype(F32)
        for k in range(1, 4):
            total = total + self.r3o[k].astype(F32)
        out_ref[...] = total
        for copy in self.started:
            copy.wait_send()


def reduce_body(gi_ref, go_ref, sa1, sb1, so1, in0_ref, out0_ref, in1_ref, out1_ref, *scratch):
    sums0 = scratch[:3]
    fold = Fold(gi_ref, go_ref, *sums0, *scratch[3:9])
    near = Finish(sums0, scratch[9:16], scratch[16:18])
    far = Finish((sa1, sb1, so1), scratch[18:25], scratch[25:27])
    greet(False)
    fold.start()
    far.second()
    far.third()
    fold.end()
    near.second()
    far.last(in1_ref, out1_ref)
    near.third()
    near.last(in0_ref, out0_ref)


def reduce_grads(grad_in, grad_out, sums):
    sems = pltpu.SemaphoreType.DMA
    finish = [
        pltpu.VMEM((4, 96, CUT), BF16),
        pltpu.VMEM((4, 96, CUT), BF16),
        pltpu.VMEM((4, 4, 48, WALF), BF16),
        pltpu.VMEM((4, 24, HALF), F32),
        pltpu.VMEM((4, 24, HALF), F32),
        pltpu.VMEM((4, 48, WALF), BF16),
        pltpu.VMEM((4, 48, WALF), BF16),
        sems((15,)),
        sems((15,)),
    ]
    return pl.pallas_call(
        reduce_body,
        out_shape=(
            jax.ShapeDtypeStruct((24, HALF), F32),
            jax.ShapeDtypeStruct((48, WALF), F32),
        )
        * 2,
        in_specs=[any_spec()] * 2 + [vmem()] * 3,
        out_specs=(vmem(),) * 4,
        scratch_shapes=[pltpu.VMEM(shape, BF16) for shape in fold_shapes()]
        + [pltpu.VMEM((4,) + shape, BF16) for shape in fold_shapes()]
        + [sems((9,)), sems((9,)), sems((3,))]
        + finish
        + finish,
        compiler_params=pltpu.CompilerParams(
            collective_id=4, has_side_effects=True, vmem_limit_bytes=VMEM_LIMIT
        ),
        name="reduce_grads",
    )(grad_in, grad_out, *sums)


def settle(section, first_value, second_value):
    own = jnp.where(section == 0, first_value, second_value)
    got = swap_cores(jnp.where(section == 0, second_value, first_value))
    return jnp.where(section == 0, own, got), jnp.where(section == 0, got, own)


def per_device(
    block_input, cotangent, seg_groups, norm_gain, w_gate, w_inner, w_bc, w_step, conv_inner, conv_bc, head_params,
    inner_gain, w_out,
):
    section = lax.axis_index("section")
    seq_pos = lax.axis_index("seq")
    main = jnp.concatenate([w_inner[0], w_bc[0]], axis=1)
    side = jnp.concatenate(
        [
            step_lanes(w_step[0]),
            pack_small(norm_gain[0], inner_gain[0], conv_inner[0], conv_bc[0], head_params[0]),
            w_gate[0],
        ],
        axis=1,
    )
    given_in = jnp.where(section == 0, side, main)
    given_out = jnp.where(section == 0, w_out[0][:, WALF:], w_out[0][:, :WALF])
    taken_in = swap_cores(given_in)
    taken_out = swap_cores(given_out)
    kept_in = jnp.where(section == 0, main, side)
    kept_out = jnp.where(section == 0, w_out[0][:, :WALF], w_out[0][:, WALF:])
    half_in = (jnp.where(section == 0, kept_in, taken_in), jnp.where(section == 0, taken_in, kept_in))
    half_out = (jnp.where(section == 0, kept_out, taken_out), jnp.where(section == 0, taken_out, kept_out))
    near_w, near_o, bands = gather_weights(
        jnp.pad(half_in[0], ((0, 8), (0, 0))), half_out[0], jnp.pad(half_in[1], ((0, 8), (0, 0))), half_out[1]
    )
    weights = [(near_w.reshape(2, D, HALF), near_o.reshape(2, INNER, WALF)), None]
    firsts = (BLOCKS - seg_groups[0]) * (BLOCK_LEN // TOK)
    first = jnp.where(section == 0, firsts[0], firsts[1])
    live = (seq_pos >= first).astype(F32).reshape(1)
    ring = [(s * 16 + i, s * 16 + i + 1) for s in range(2) for i in range(15)] + [(15, 16)]
    jump = [(15, 20)]
    unring = [(b, a) for a, b in ring]
    unjump = [(b, a) for a, b in jump]
    axes = ("section", "seq")

    x = lax.dynamic_index_in_dim(block_input[0], section, 0, keepdims=False)
    kept = []
    outs = []
    for layer in range(2):
        w_in, w_o = weights[layer]
        gain, mid_gain, taps, heads = unpack_small(w_in[1, :, 128:GATE0])
        x32 = x.astype(F32)
        hidden = (x32 * lax.rsqrt(jnp.mean(x32 * x32, axis=-1, keepdims=True) + EPS) * gain[0]).astype(BF16)
        pre = jnp.dot(hidden, w_in[0], preferred_element_type=F32).astype(BF16)
        tail = pre[TOK - 8 :]
        near = lax.ppermute(tail, axes, ring)
        far = lax.ppermute(tail, axes, jump)
        halo = jnp.where(
            seq_pos == first,
            jnp.where(section == 0, jnp.zeros_like(near), jnp.where(first == 0, near, far)),
            near,
        )
        wide = jnp.dot(hidden, w_in[1], preferred_element_type=F32)
        act, dact, dt, cum, dec, states, raw, y, gated, inv, out, *later = block_forward(
            live, pre, wide, halo, taps, heads, mid_gain, x, w_o, bands if layer == 0 else None
        )
        if layer == 0:
            weights[1] = (later[0].reshape(2, D, HALF), later[1].reshape(2, INNER, WALF))
        kept.append((x, hidden, pre, halo, wide, act, dact, dt, cum, dec, states, raw, y, gated, inv, gain, mid_gain, taps, heads))
        outs.append(out)
        x = out

    g = lax.dynamic_index_in_dim(cotangent[0], section, 0, keepdims=False)
    grads_in = [None, None]
    grads = None
    for layer in (1, 0):
        w_in, w_o = weights[layer]
        (x, hidden, pre, halo, wide, act, dact, dt, cum, dec, states, raw, y, gated, inv, gain, mid_gain, taps, heads) = kept[layer]
        gb, dgate, gmid, gsum, dstep, gtaps, ghead, *folded = block_backward(
            live, g, wide, y, mid_gain, inv, act, dact, dt, cum, raw, pre, halo, heads, dec, w_o, states, grads
        )
        head_rows = gsum[:8]
        near = lax.ppermute(head_rows, axes, unring)
        far = lax.ppermute(head_rows, axes, unjump)
        crossing = (section == 0) & (seq_pos == 15) & (firsts[1] != 0)
        after = jnp.where(crossing, far, near) * live
        gpre, gside, g, ggain = input_backward(gsum, after, dstep, taps, dgate, w_in, x, g, gain)
        grads_in[layer] = g
        small = small_grads(ggain[0], gmid[0], gtaps, ghead, seq_pos)
        small = small + swap_cores(small)
        other_gated = swap_cores(gated)
        other_hidden = swap_cores(hidden)
        other_gb = swap_cores(jnp.where(section == 0, gb[:, WALF:], gb[:, :WALF]))
        own_gb = jnp.where(section == 0, gb[:, :WALF], gb[:, WALF:])
        other_g = swap_cores(jnp.where(section == 0, gside, gpre))
        own_g = jnp.where(section == 0, gpre, gside)
        pair = lambda own, other: jnp.concatenate([own, other], axis=0)
        grad_in = dot32(pair(hidden, other_hidden), pair(own_g, other_g), ((0,), (0,))).astype(BF16)
        keep = jnp.where(section == 1, small.astype(BF16), grad_in[:, 128:256])
        grad_in = lax.dynamic_update_slice_in_dim(grad_in, keep, 128, 1)
        grad_out = dot32(pair(gated, other_gated), pair(own_gb, other_gb), ((0,), (0,))).astype(BF16)
        grads = (grad_in.reshape(4, 4, 96, HALF), grad_out.reshape(4, 4, 4, 48, WALF))

    in0, wo0, in1, wo1 = reduce_grads(*grads, folded)
    out_a, out_b = settle(section, outs[0], outs[1])
    in_a, in_b = settle(section, grads_in[0], grads_in[1])
    main, side = settle(section, in0, in1)
    out_left, out_right = settle(section, wo0, wo1)
    grad_out = jnp.concatenate([out_left, out_right], axis=1)
    cells = side[:, 128:GATE0].reshape(-1)
    return (
        jnp.stack([out_a, out_b])[None, None],
        jnp.stack([in_a, in_b])[None, None],
        cells[:24][None],
        side[:, GATE0:][None],
        main[:, :INNER][None],
        main[:, INNER:][None],
        side[:, :128].reshape(24, OWNERS, 8)[:, :, :3].reshape(24, HEADS)[None],
        cells[72:312].reshape(5, 48)[None],
        cells[312:332].reshape(5, 4)[None],
        cells[332:341].reshape(3, 3)[None],
        cells[24:72][None],
        grad_out[None],
    )


def solution(mesh):
    weight = P("section", ROWS_ALL, None)
    vector = P("section", ROWS_ALL)
    taps = P("section", None, ROWS_ALL)
    tokens = P("wsh", None, "seq", None)
    heads = P("section", None, "seq")
    result = P("section", "wsh", None, "seq", None)
    return jax.shard_map(
        per_device,
        mesh=mesh,
        in_specs=(
            tokens, tokens, P("wsh", None), vector, weight, weight, weight, weight, taps, taps, heads, vector, weight,
        ),
        out_specs=(
            result, result, vector, weight, weight, weight, weight, taps, taps, heads, vector, weight,
        ),
        check_vma=False,
    )
```

```python
import functools
import types

import jax
import jax.numpy as jnp
from jax import lax
from jax.experimental import pallas as pl
from jax.experimental.pallas import tpu as pltpu
from jax.sharding import PartitionSpec as P

D = 1536
INNER = 3072
HEADS = 48
STATE = 128
BLOCK_LEN = 256
BLOCKS = 8
TOK = 128
CONV = INNER + 2 * STATE
HALF = CONV
GATE0 = 256
CUT = HALF // 2
WALF = D // 2
OWNERS = 16
OWN = 192
EPS = 1e-05
F32 = jnp.float32
BF16 = jnp.bfloat16
MESH = pl.DeviceIdType.MESH
VMEM_LIMIT = 60 * 1024 * 1024
LANES = (0, 1, 2, 8, 9, 10)
ROWS_ALL = ("seq", "wsh")
ROW_MID, ROW_NORM = 5, 6
ROW_BIAS, ROW_DECAY, ROW_SKIP = 5, 6, 7


def dot32(left, right, dims=((1,), (0,))):
    return lax.dot_general(left, right, (dims, ((), ())), preferred_element_type=F32)


def split_left(exact, value, terms):
    total = None
    for _ in range(terms):
        part = value.astype(BF16)
        value = value - part.astype(F32)
        term = dot32(exact, part)
        total = term if total is None else total + term
    return total


def split_right(value, exact, terms, dims=((1,), (0,))):
    total = None
    for _ in range(terms):
        part = value.astype(BF16)
        value = value - part.astype(F32)
        term = dot32(part, exact, dims)
        total = term if total is None else total + term
    return total


def pair_cols(tile, q):
    lane = lax.broadcasted_iota(jnp.int32, (TOK, 128), 1)
    a = jnp.broadcast_to(tile[:, LANES[2 * q] : LANES[2 * q] + 1], (TOK, 128))
    b = jnp.broadcast_to(tile[:, LANES[2 * q + 1] : LANES[2 * q + 1] + 1], (TOK, 128))
    return a, b, jnp.where(lane < 64, a, b)


def pair_row(row, q):
    lane = lax.broadcasted_iota(jnp.int32, (1, 128), 1)
    a = jnp.broadcast_to(row[:, LANES[2 * q] : LANES[2 * q] + 1], (1, 128))
    b = jnp.broadcast_to(row[:, LANES[2 * q + 1] : LANES[2 * q + 1] + 1], (1, 128))
    return jnp.where(lane < 64, a, b)


def to_front(tile, i):
    return pltpu.roll(tile, lax.rem(128 - 16 * i, 128), 1)


def conv_of(cat, taps):
    total = taps[4:5] + taps[3:4] * cat[8 : 8 + TOK]
    for k in range(3):
        total = total + taps[k : k + 1] * cat[5 + k : 5 + k + TOK]
    return total


def tri_of(lower):
    row = lax.broadcasted_iota(jnp.int32, (TOK, TOK), 0)
    col = lax.broadcasted_iota(jnp.int32, (TOK, TOK), 1)
    return row >= col if lower else row <= col


def head_lanes():
    lane = lax.broadcasted_iota(jnp.int32, (TOK, 128), 1)
    return (lane % 8) < 3


def group_cols(i, q):
    return pl.ds(pl.multiple_of(i * 384 + q * 128, 128), 128)


def gate_cols(i, q):
    return pl.ds(pl.multiple_of(GATE0 + i * 384 + q * 128, 128), 128)


def in_hbm(*shape, dtype=BF16):
    return jax.ShapeDtypeStruct(shape, dtype), pl.BlockSpec(memory_space=pl.ANY)


def in_vmem(*shape, dtype=F32):
    return jax.ShapeDtypeStruct(shape, dtype), pl.BlockSpec(memory_space=pltpu.VMEM)


def call(body, name, ident, inputs, outputs, scratch):
    spaces = {"h": pl.ANY, "v": pltpu.VMEM, "s": pltpu.SMEM}
    names = [key for key in inputs] + [key for key in outputs] + [key for key in scratch]

    def kernel(*refs):
        body(types.SimpleNamespace(**dict(zip(names, refs))))

    out = pl.pallas_call(
        kernel,
        out_shape=tuple(shape for shape, _ in outputs.values()),
        in_specs=[pl.BlockSpec(memory_space=spaces[kind]) for kind, _ in inputs.values()],
        out_specs=tuple(spec for _, spec in outputs.values()),
        scratch_shapes=list(scratch.values()),
        compiler_params=pltpu.CompilerParams(
            collective_id=ident, has_side_effects=True, vmem_limit_bytes=VMEM_LIMIT
        ),
        name=name,
    )(*[value for _, value in inputs.values()])
    return types.SimpleNamespace(**dict(zip(outputs, out)))


def dma_sems(count):
    return pltpu.SemaphoreType.DMA((count,))


def places():
    section = lax.axis_index("section")
    seq = lax.axis_index("seq")
    return section, seq // 4, lax.rem(seq, 4), lax.axis_index("wsh")


def x_peer(k):
    return {"wsh": lax.rem(lax.axis_index("wsh") + k, 4)}


def z_peer(k):
    _, y, z, _ = places()
    return {"seq": y * 4 + lax.rem(z + k, 4)}


def y_peer(k):
    _, y, z, _ = places()
    return {"seq": lax.rem(y + k, 4) * 4 + z}


def sibling():
    return {"section": 1 - lax.axis_index("section")}


def say_hello(peer):
    pl.semaphore_signal(pltpu.get_barrier_semaphore(), inc=1, device_id=peer, device_id_type=MESH)


def greet_axes():
    for k in range(1, 4):
        for peer in (x_peer(k), y_peer(k), z_peer(k)):
            say_hello(peer)
    say_hello(sibling())
    pl.semaphore_wait(pltpu.get_barrier_semaphore(), 10)


def fetch(src, dst, sem):
    copy = pltpu.make_async_copy(src, dst, sem)
    copy.start()
    return copy


class Net:
    def __init__(self, send, recv):
        self.send, self.recv = send, recv
        self.count = 0
        self.started = []

    def go(self, src, dst, peer):
        copy = pltpu.make_async_remote_copy(
            src_ref=src, dst_ref=dst, send_sem=self.send.at[self.count], recv_sem=self.recv.at[self.count],
            device_id=peer, device_id_type=MESH,
        )
        copy.start()
        self.count += 1
        self.started.append(copy)
        return copy

    def drain(self):
        for copy in self.started:
            copy.wait_send()


class Gather:
    def __init__(self, net, p, o, w, wo, stage, rows, own):
        self.net, self.p, self.o, self.w, self.wo = net, p, o, w, wo
        self.stage, self.rows, self.own = stage, rows, own
        self.place = places()
        self.left, self.right = pl.ds(0, CUT), pl.ds(CUT, CUT)
        self.near, self.far, self.passed = {}, {}, []
        self.peers = (y_peer, z_peer, x_peer)

    def band(self, kind, j, moved):
        c, y, z, x = self.place
        if kind == 0:
            return self.w.at[c, lax.rem(y + 4 - moved, 4), lax.rem(z + 4 - j, 4), :, self.left]
        if kind == 1:
            return self.w.at[c, lax.rem(y + 4 - j, 4), lax.rem(z + 4 - moved, 4), :, self.right]
        return self.wo.at[c, lax.rem(y + 4 - j, 4), :, lax.rem(x + 4 - moved, 4)]

    def pass_on(self, part):
        self.passed.append(self.net.go(part, part, sibling()))

    def begin(self):
        c, y, z, x = self.place
        go = self.net.go
        self.first, self.oz = [], []
        for k in range(1, 4):
            self.first.append(go(self.p, self.stage.at[x], x_peer(k)))
            self.oz.append(go(self.o, self.wo.at[c, y, z, x], z_peer(k)))
        self.own_o = fetch(self.o, self.wo.at[c, y, z, x], self.own.at[0])
        self.stage[x] = self.p[...]

    def rows_in(self):
        c, y, z, x = self.place
        go = self.net.go
        for copy in self.first:
            copy.wait_recv()
        self.rows[...] = jnp.concatenate(
            [self.stage[n].astype(F32)[:24] for n in range(4)], axis=0
        ).astype(BF16)
        self.az, self.by, self.oy = [], [], []
        for k in range(1, 4):
            self.az.append(go(self.rows.at[:, self.left], self.w.at[c, y, z, :, self.left], z_peer(k)))
            self.by.append(go(self.rows.at[:, self.right], self.w.at[c, y, z, :, self.right], y_peer(k)))
        own_w = fetch(self.rows, self.w.at[c, y, z], self.own.at[1])
        self.own_o.wait()
        for copy in self.oz:
            copy.wait_recv()
        lane = self.wo.at[c, y, :, x]
        for k in range(1, 4):
            self.oy.append(go(lane, lane, y_peer(k)))
        own_w.wait()
        self.spread(0)

    def spread(self, j):
        if j:
            for copies in (self.az, self.by, self.oy):
                copies[j - 1].wait_recv()
        for k in (1, 3):
            for kind in range(3):
                part = self.band(kind, j, 0)
                self.near[kind, j, k] = self.net.go(part, part, self.peers[kind](k))
        for kind in range(3):
            self.pass_on(self.band(kind, j, 0))

    def relay(self, j):
        for k in (1, 3):
            for kind in range(3):
                self.near[kind, j, k].wait_recv()
                part = self.band(kind, j, k)
                if (k == 1) == (j < 2):
                    self.far[kind, j] = self.net.go(part, part, self.peers[kind](k))
                self.pass_on(part)

    def last(self, j):
        for kind in range(3):
            self.far[kind, j].wait_recv()
            self.pass_on(self.band(kind, j, 2))

    def end(self):
        for copy in self.passed:
            copy.wait_recv()


def gather_scratch():
    return {
        "stage": pltpu.VMEM((4, 32, HALF), BF16),
        "rows": pltpu.VMEM((96, HALF), BF16),
        "own": dma_sems(2),
        "net_send": dma_sems(150),
        "net_recv": dma_sems(150),
    }


def lane_at(shape):
    return lax.broadcasted_iota(jnp.int32, shape, 1)


def place_chunks(cells, width, total):
    tiles = [jnp.zeros((8, 128), F32) for _ in range(total // 128)]
    lane = lane_at((8, 128))
    for d in range(64):
        t, off = (width * d) // 128, (width * d) % 128
        moved = pltpu.roll(cells(d), off, 1) if off else cells(d)
        stop = off + width
        tiles[t] = jnp.where((lane >= off) & (lane < min(stop, 128)), moved, tiles[t])
        if stop > 128:
            tiles[t + 1] = jnp.where(lane < stop - 128, moved, tiles[t + 1])
    return tiles


def take_chunk(ref, base, width, d):
    start = base + width * d
    t, off = start // 128, start % 128
    tile = ref[:, 128 * t : 128 * t + 128]
    tile = pltpu.roll(tile, 128 - off, 1) if off else tile
    if off + width > 128:
        after = pltpu.roll(ref[:, 128 * t + 128 : 128 * t + 256], 128 - off, 1)
        tile = jnp.where(lane_at((8, 128)) < 128 - off, tile, after)
    return tile


def start_body(r):
    c, y, z, x = places()
    greet_axes()
    net = Net(r.net_send, r.net_recv)
    pad = jnp.zeros((8, 1), F32)

    def tall(value):
        return jnp.concatenate(
            [value.astype(F32), jnp.broadcast_to(pad, (8, value.shape[1]))], axis=0
        ).astype(BF16)

    r.mine[0, :, :INNER] = tall(r.inner[...])
    r.mine[0, :, INNER:] = tall(r.bc[...])
    r.mine[1, :, :128] = tall(r.step[...])
    r.mine[1, :, 128:GATE0] = jnp.zeros((32, 128), BF16)
    r.mine[1, :, GATE0:] = tall(r.gate[...])
    given = pl.ds(pl.multiple_of((1 - c) * WALF, 128), WALF)
    swaps = [
        net.go(r.mine.at[1 - c], r.half.at[c], sibling()),
        net.go(r.out.at[:, given], r.halo.at[c], sibling()),
    ]
    small = [net.go(r.blob, r.cells.at[c, y, z, x], x_peer(k)) for k in range(1, 4)]
    r.half[c] = r.mine[c]
    r.halo[c] = jnp.where(c == 0, r.out[:, :WALF], r.out[:, WALF:])
    r.cells[c, y, z, x] = r.blob[...]
    for copy in swaps:
        copy.wait_recv()
    ga = Gather(net, r.half.at[0], r.halo.at[0], r.w, r.wo, r.stage, r.rows, r.own)
    ga.begin()
    for copy in small:
        copy.wait_recv()
    small = [net.go(r.cells.at[c, y, z], r.cells.at[c, y, z], z_peer(k)) for k in range(1, 4)]
    ga.rows_in()
    for copy in small:
        copy.wait_recv()
    small = [net.go(r.cells.at[c, y], r.cells.at[c, y], y_peer(k)) for k in range(1, 4)]
    for j in range(1, 4):
        ga.spread(j)
    for copy in small:
        copy.wait_recv()
    pair = net.go(r.cells.at[c], r.cells.at[c], sibling())
    ga.relay(0)
    r.p1[...] = r.half[1]
    r.o1[...] = r.halo[1]
    ga.relay(1)
    pair.wait_recv()
    for layer in range(2):
        def first_tile(d):
            return r.cells[layer, d // 16, (d // 4) % 4, d % 4, 0:8]

        def second_tile(d):
            return r.cells[layer, d // 16, (d // 4) % 4, d % 4, 8:16]

        for t, tile in enumerate(place_chunks(first_tile, 48, INNER)):
            r.taps[layer, :, 128 * t : 128 * t + 128] = tile
        for t, tile in enumerate(place_chunks(second_tile, 4, 2 * STATE)):
            r.taps[layer, :, INNER + 128 * t : INNER + 128 * t + 128] = tile
        for t, tile in enumerate(place_chunks(first_tile, 24, D)):
            r.gain[layer, :, 128 * t : 128 * t + 128] = tile
        lane = lane_at((8, 128))
        heads = jnp.zeros((8, 128), F32)
        for j in range(OWNERS):
            moved = pltpu.roll(second_tile(4 * j), 8 * j, 1) if j else second_tile(0)
            heads = jnp.where((lane >= 8 * j) & (lane < 8 * j + 3), moved, heads)
        r.heads[layer] = heads
    ga.relay(2)
    ga.relay(3)
    for j in range(4):
        ga.last(j)
    ga.end()
    net.drain()


def start_up(inner, bc, step, gate, out, blob):
    return call(
        start_body, "gather_weights", 1,
        {
            "inner": ("v", inner), "bc": ("v", bc), "step": ("v", step), "gate": ("v", gate), "out": ("v", out),
            "blob": ("v", blob),
        },
        {
            "w": in_hbm(2, 4, 4, 96, HALF),
            "wo": in_hbm(2, 4, 4, 4, 48, WALF),
            "p1": in_vmem(32, HALF, dtype=BF16),
            "o1": in_vmem(48, WALF, dtype=BF16),
            "taps": in_vmem(2, 8, CONV),
            "gain": in_vmem(2, 8, D),
            "heads": in_vmem(2, 8, 128),
        },
        {
            "mine": pltpu.VMEM((2, 32, HALF), BF16),
            "half": pltpu.VMEM((2, 32, HALF), BF16),
            "halo": pltpu.VMEM((2, 48, WALF), BF16),
            "cells": pltpu.VMEM((2, 4, 4, 4, 16, 128), F32),
            **gather_scratch(),
        },
    )


class Exchange:
    def __init__(self, backward, r):
        self.backward, self.r = backward, r
        self.me = lax.axis_index("seq")
        self.section = lax.axis_index("section")

    def first_copy(self, peer, d):
        r = self.r
        return pltpu.make_async_remote_copy(
            src_ref=r.ds.at[peer], dst_ref=r.got.at[self.me], send_sem=r.send_a.at[d], recv_sem=r.recv_a.at[d],
            device_id={"seq": peer}, device_id_type=MESH,
        )

    def send(self, peer):
        d = lax.rem(peer + OWNERS - self.me, OWNERS)

        @pl.when(d != 0)
        def _():
            self.first_copy(peer, d).start()

        @pl.when(d == 0)
        def _():
            self.r.got[self.me] = self.r.ds[self.me]

    def back_copy(self, d):
        r = self.r
        peer = lax.rem(self.me + d, OWNERS)
        return pltpu.make_async_remote_copy(
            src_ref=r.ready.at[peer], dst_ref=r.back.at[self.me], send_sem=r.send_b.at[d], recv_sem=r.recv_b.at[d],
            device_id={"seq": peer}, device_id_type=MESH,
        )

    def scan(self, decays):
        r = self.r

        def rows_of(dec):
            return jnp.concatenate([jnp.broadcast_to(dec[h : h + 1], (64, 128)) for h in range(3)], axis=0)

        for d in range(1, OWNERS):
            self.first_copy(lax.rem(self.me + d, OWNERS), d).wait_recv()
        r.final[...] = jnp.zeros((OWN, STATE), F32)
        r.fade[0] = jnp.ones((8, 128), F32)

        def step(n, carry):
            c = OWNERS - 1 - n if self.backward else n
            state = r.final[...]
            r.kept[c] = state
            dec = decays[c]
            r.final[...] = rows_of(dec) * state + r.got[c].astype(F32)
            r.fade[n + 1] = r.fade[n] * dec
            return carry

        lax.fori_loop(0, OWNERS, step, 0)
        swap = pltpu.make_async_remote_copy(
            src_ref=r.final, dst_ref=r.other, send_sem=r.swap_s.at[0], recv_sem=r.swap_s.at[1],
            device_id=sibling(), device_id_type=MESH,
        )
        swap.start()
        takes = 0 if self.backward else 1
        r.begin[...] = jnp.zeros((OWN, STATE), F32)

        @pl.when(self.section == takes)
        def _():
            swap.wait_recv()
            r.begin[...] = r.other[...]

        begin = r.begin[...]
        for d in range(OWNERS):
            c = lax.rem(self.me + d, OWNERS)
            n = OWNERS - 1 - c if self.backward else c
            value = (r.kept[c] + rows_of(r.fade[n]) * begin).astype(BF16)
            if d == 0:
                r.back[c] = value
            else:
                r.ready[c] = value
                self.back_copy(d).start()

        @pl.when(self.section != takes)
        def _():
            swap.wait_recv()

        swap.wait_send()

    def finish(self):
        for d in range(1, OWNERS):
            self.back_copy(d).wait_recv()

    def drain(self):
        for d in range(1, OWNERS):
            self.first_copy(lax.rem(self.me + d, OWNERS), d).wait_send()
            self.back_copy(d).wait_send()


def exchange_scratch():
    block = pltpu.VMEM((OWNERS, OWN, STATE), BF16)
    part = pltpu.VMEM((OWN, STATE), F32)
    return {
        "ds": block, "got": block, "back": block, "ready": block,
        "kept": pltpu.VMEM((OWNERS, OWN, STATE), F32), "fade": pltpu.VMEM((OWNERS + 1, 8, 128), F32),
        "final": part, "other": part, "begin": part,
        "send_a": dma_sems(OWNERS), "recv_a": dma_sems(OWNERS), "send_b": dma_sems(OWNERS), "recv_b": dma_sems(OWNERS),
        "swap_s": dma_sems(2),
    }


def head_rows_at(ref, i, q):
    parts = []
    for h in (2 * q, 2 * q + 1):
        parts.append(ref[2 * i + h // 3, pl.ds(64 * (h % 3), 64), :])
    return jnp.concatenate(parts, axis=0)


def store_heads(ref, i, q, value):
    for n, h in enumerate((2 * q, 2 * q + 1)):
        ref[2 * i + h // 3, pl.ds(64 * (h % 3), 64), :] = value[64 * n : 64 * n + 64]


def own_group(n):
    return lax.rem(lax.axis_index("seq") // 2 + n, 8)


def greet_layer(rider, forward):
    me = lax.axis_index("seq")
    section = lax.axis_index("section")
    wsh = lax.axis_index("wsh")
    barrier = pltpu.get_barrier_semaphore()
    for d in range(1, OWNERS):
        say_hello({"seq": lax.rem(me + d, OWNERS)})
    say_hello(sibling())
    if rider:
        for k in range(1, 4):
            say_hello(x_peer(k))
    count = OWNERS + (3 if rider else 0)
    late = {"section": 0, "seq": 15, "wsh": wsh}
    if forward:

        @pl.when((section == 1) & ((me == 0) | (me == 4)))
        def _():
            pl.semaphore_signal(barrier, inc=1, device_id=late, device_id_type=MESH)

        more = jnp.where((section == 0) & (me == 15), 2, 0)
    else:

        @pl.when((section == 0) & (me == 15))
        def _():
            for seq in (0, 4):
                pl.semaphore_signal(
                    barrier, inc=1, device_id={"section": 1, "seq": seq, "wsh": wsh}, device_id_type=MESH
                )

        more = jnp.where((section == 1) & ((me == 0) | (me == 4)), 1, 0)
    pl.semaphore_wait(barrier, count + more)


def halo_copy(src, dst, sems, n, section, seq):
    return pltpu.make_async_remote_copy(
        src_ref=src, dst_ref=dst, send_sem=sems.at[n], recv_sem=sems.at[2 + n],
        device_id={"section": section, "seq": seq, "wsh": lax.axis_index("wsh")}, device_id_type=MESH,
    )


class Halo:
    def __init__(self, src, near, far, sems, forward):
        me = lax.axis_index("seq")
        section = lax.axis_index("section")
        edge = 15 if forward else 0
        if forward:
            crossing = (section == 0) & (me == 15)
            jumping = crossing
            self.has_near = (me > 0) | (section == 1)
            self.has_far = (section == 1) & (me == 4)
            target = (1, jnp.where(me == 15, 0, me + 1))
            near_section = jnp.where(crossing, 1, section)
            far_seq, far_section = 4, 1
        else:
            crossing = (section == 1) & (me == 0)
            jumping = (section == 1) & (me == 4)
            self.has_near = (me < 15) | (section == 0)
            self.has_far = (section == 0) & (me == 15)
            target = (0, jnp.where(me == 0, 15, me - 1))
            near_section = jnp.where(crossing, 0, section)
            far_seq, far_section = 15, 0
        self.sends_near = (me != edge) | crossing
        self.sends_far = jumping
        self.near, self.far = near, far
        self.near_copy = halo_copy(src, near, sems, 0, near_section, target[1])
        self.far_copy = halo_copy(src, far, sems, 1, far_section, far_seq)

    def start(self):
        @pl.when(self.sends_near)
        def _():
            self.near_copy.start()

        @pl.when(self.sends_far)
        def _():
            self.far_copy.start()

        @pl.when(jnp.logical_not(self.has_near))
        def _():
            self.near[...] = jnp.zeros_like(self.near)

        @pl.when(jnp.logical_not(self.has_far))
        def _():
            self.far[...] = jnp.zeros_like(self.far)

    def wait(self):
        @pl.when(self.has_near)
        def _():
            self.near_copy.wait_recv()

        @pl.when(self.has_far)
        def _():
            self.far_copy.wait_recv()

    def drain(self):
        @pl.when(self.sends_near)
        def _():
            self.near_copy.wait_send()

        @pl.when(self.sends_far)
        def _():
            self.far_copy.wait_send()


def forward_body(layer, rider, r):
    section = lax.axis_index("section")
    me = lax.axis_index("seq")
    loads = [fetch(r.w.at[n], r.w_s.at[n], r.load.at[n]) for n in range(2)]
    load_o = fetch(r.wo, r.wo_s, r.load.at[2])
    greet_layer(rider, True)
    net = Net(r.pair_send, r.pair_recv)
    if rider:
        ga = Gather(Net(r.net_send, r.net_recv), r.p1, r.o1, r.next_w, r.next_wo, r.stage, r.rows, r.own)
        ga.begin()
    ex = Exchange(False, r)
    live = r.flags[0]
    heads = r.heads[layer]
    x32 = r.x[...].astype(F32)
    hidden_inv = lax.rsqrt(jnp.sum(x32 * x32, axis=1, keepdims=True) / D + EPS)
    r.hidden[...] = (x32 * hidden_inv * r.gain[layer, ROW_NORM : ROW_NORM + 1, :]).astype(BF16)
    loads[0].wait()

    def project_main(n, carry):
        cols = pl.ds(pl.multiple_of(n * 256, 256), 256)
        r.pre[:, cols] = dot32(r.hidden[...], r.w_s[0, :, cols]).astype(BF16)
        return carry

    lax.fori_loop(0, HALF // 256, project_main, 0)
    r.tail[...] = r.pre[TOK - 16 :, :]
    halo = Halo(r.tail, r.halo_near, r.halo_far, r.halo_s, True)
    halo.start()
    if rider:
        ga.rows_in()
    loads[1].wait()

    def project_side(n, carry):
        cols = pl.ds(pl.multiple_of(n * 256, 256), 256)
        r.side[:, cols] = dot32(r.hidden[...], r.w_s[1, :, cols])
        return carry

    lax.fori_loop(0, HALF // 256, project_side, 0)
    pairs = [net.go(r.hidden, r.both_hidden.at[section], sibling())]
    owns = [fetch(r.hidden, r.both_hidden.at[section], r.load.at[3])]
    step = r.side[:, :128].astype(BF16).astype(F32) + heads[ROW_BIAS : ROW_BIAS + 1]
    dt = jnp.maximum(step, 0.0) + jnp.log1p(jnp.exp(-jnp.abs(step)))
    dt = jnp.where(head_lanes(), dt, 0.0) * live
    rate = -dt * jnp.exp(heads[ROW_DECAY : ROW_DECAY + 1])
    cum = split_left(tri_of(True).astype(F32).astype(BF16), rate, 3)
    r.dt[...] = dt
    r.cum[...] = cum
    last = jnp.broadcast_to(cum[TOK - 1 : TOK], (TOK, 128))
    r.dec_s[...] = jnp.exp(last).T.reshape(OWNERS, 8, 128)
    r.dec[me] = r.dec_s[me]

    def dec_copy(d):
        peer = lax.rem(me + d, OWNERS)
        return pltpu.make_async_remote_copy(
            src_ref=r.dec_s.at[peer], dst_ref=r.dec.at[me], send_sem=r.dec_send.at[d], recv_sem=r.dec_recv.at[d],
            device_id={"seq": peer}, device_id_type=MESH,
        )

    for d in range(1, OWNERS):
        dec_copy(d).start()
    weight = dt * jnp.exp(last - cum)
    halo.wait()
    r.halo[...] = jnp.where(
        r.flags[1] > 0.0, r.halo_near[...], jnp.where(r.flags[2] > 0.0, r.halo_far[...], jnp.zeros_like(r.halo_far))
    )

    def conv_tile(cols):
        blk = r.pre[:, cols].astype(F32)
        cat = jnp.concatenate([r.halo[:, cols].astype(F32)[8:], blk], axis=0)
        summed = conv_of(cat, r.taps[layer, :, cols])
        sig = 1.0 / (1.0 + jnp.exp(-summed))
        act = summed * sig
        r.act[:, cols] = act
        r.dact[:, cols] = sig * (1.0 + summed * (1.0 - sig))
        return act

    b = conv_tile(pl.ds(INNER, 128)).astype(BF16)
    c = conv_tile(pl.ds(INNER + 128, 128)).astype(BF16)

    def states(n, carry):
        i = own_group(n)
        wt = to_front(weight, i)
        for q in range(3):
            x = conv_tile(group_cols(i, q))
            scaled = (x * pair_cols(wt, q)[2]).astype(BF16)
            store_heads(r.ds, i, q, dot32(scaled, b, ((0,), (0,))).astype(BF16))
        ex.send(2 * i)
        ex.send(2 * i + 1)
        return carry

    lax.fori_loop(0, 8, states, 0)
    if rider:
        ga.spread(1)
    for d in range(1, OWNERS):
        dec_copy(d).wait_recv()
    ex.scan(r.dec)
    if rider:
        ga.spread(2)
        ga.spread(3)
    r.cumt[...] = cum.T
    causal = tri_of(True)
    scores = dot32(c, b, ((1,), (1,)))
    lane = lax.broadcasted_iota(jnp.int32, (TOK, 128), 1)
    r.square[...] = jnp.zeros((TOK, 128), F32)

    def inside(i, carry):
        cum_i = to_front(cum, i)
        dt_i = to_front(dt, i)
        rows = r.cumt[pl.ds(pl.multiple_of(16 * i, 16), 16), :]
        for q in range(3):
            cols = group_cols(i, q)
            cum_a, cum_b, _ = pair_cols(cum_i, q)
            u = r.act[:, cols] * pair_cols(dt_i, q)[2]
            mixes = []
            for cum_h, off in ((cum_a, LANES[2 * q]), (cum_b, LANES[2 * q + 1])):
                gap = cum_h - rows[off : off + 1]
                mixes.append((scores * jnp.exp(jnp.where(causal, gap, -1e30))).astype(BF16))
            terms = jnp.concatenate(
                [jnp.where(lane < 64, u, 0.0).astype(BF16), jnp.where(lane < 64, 0.0, u).astype(BF16)], axis=0
            )
            r.raw[:, cols] = dot32(jnp.concatenate(mixes, axis=1), terms)
        return carry

    lax.fori_loop(0, 8, inside, 0)
    if rider:
        ga.relay(0)
    ex.finish()
    save = fetch(r.back, r.states, r.load.at[4])

    def across(i, carry):
        cum_i = to_front(cum, i)
        skip_i = pltpu.roll(heads, lax.rem(128 - 16 * i, 128), 1)[ROW_SKIP : ROW_SKIP + 1]
        for q in range(3):
            cols = group_cols(i, q)
            state = head_rows_at(r.back, i, q)
            raw = r.raw[:, cols] + jnp.exp(pair_cols(cum_i, q)[2]) * dot32(c, state, ((1,), (1,)))
            r.raw[:, cols] = raw
            y = (raw + pair_row(skip_i, q) * r.act[:, cols]).astype(BF16)
            r.y[:, cols] = y
            gate = r.side[:, gate_cols(i, q)]
            z = y.astype(F32) * (gate / (1.0 + jnp.exp(-gate)))
            r.z[:, cols] = z
            r.square[...] += z * z
        return carry

    lax.fori_loop(0, 8, across, 0)
    if rider:
        ga.relay(1)
    total = jnp.sum(r.square[...], axis=1, keepdims=True)
    inv = jnp.broadcast_to(lax.rsqrt(total / INNER + EPS), (TOK, 128))
    r.inv[...] = inv

    def scale(i, carry):
        cols = pl.ds(pl.multiple_of(i * 128, 128), 128)
        mid = r.taps[layer, ROW_MID : ROW_MID + 1, cols]
        r.gated[:, cols] = (r.z[:, cols] * inv * mid).astype(BF16)
        return carry

    lax.fori_loop(0, 24, scale, 0)
    pairs.append(net.go(r.gated, r.both_gated.at[section], sibling()))
    owns.append(fetch(r.gated, r.both_gated.at[section], r.load.at[5]))
    load_o.wait()
    for half in range(2):

        def project(n, carry):
            cols = pl.ds(pl.multiple_of(n * 256, 256), 256)
            full = pl.ds(pl.multiple_of(half * WALF + n * 256, 256), 256)
            branch = dot32(r.gated[...], r.wo_s[half, :, cols])
            r.result[:, full] = (r.x[:, full].astype(F32) + live * branch).astype(BF16)
            return carry

        lax.fori_loop(0, WALF // 256, project, 0)
    if rider:
        ga.relay(2)
        ga.relay(3)
        for j in range(4):
            ga.last(j)
        ga.end()
        ga.net.drain()
    save.wait()
    for copy in owns:
        copy.wait()
    for copy in pairs:
        copy.wait_recv()
    net.drain()
    halo.drain()
    for d in range(1, OWNERS):
        dec_copy(d).wait_send()
    ex.drain()


def block_forward(layer, flags, x, w, wo, small, shards):
    rider = shards is not None
    inputs = {
        "flags": ("s", flags), "x": ("v", x), "w": ("h", w), "wo": ("h", wo), "taps": ("v", small.taps),
        "gain": ("v", small.gain), "heads": ("v", small.heads),
    }
    outputs = {
        "act": in_vmem(TOK, CONV), "dact": in_vmem(TOK, CONV), "side": in_vmem(TOK, HALF), "raw": in_vmem(TOK, INNER),
        "dt": in_vmem(TOK, 128), "cum": in_vmem(TOK, 128), "inv": in_vmem(TOK, 128),
        "dec": in_vmem(OWNERS, 8, 128), "pre": in_vmem(TOK, CONV, dtype=BF16), "halo": in_vmem(16, CONV, dtype=BF16),
        "y": in_vmem(TOK, INNER, dtype=BF16), "result": in_vmem(TOK, D, dtype=BF16),
        "states": in_hbm(OWNERS, OWN, STATE), "both_hidden": in_hbm(2, TOK, D), "both_gated": in_hbm(2, TOK, INNER),
    }
    tile = pltpu.VMEM((TOK, 128), F32)
    edge = pltpu.VMEM((16, CONV), BF16)
    scratch = {
        "w_s": pltpu.VMEM((2, D, HALF), BF16), "wo_s": pltpu.VMEM((2, INNER, WALF), BF16),
        "hidden": pltpu.VMEM((TOK, D), BF16), "gated": pltpu.VMEM((TOK, INNER), BF16),
        "z": pltpu.VMEM((TOK, INNER), F32), "cumt": tile, "square": tile,
        "tail": edge, "halo_near": edge, "halo_far": edge, "halo_s": dma_sems(4),
        "dec_s": pltpu.VMEM((OWNERS, 8, 128), F32), "dec_send": dma_sems(OWNERS), "dec_recv": dma_sems(OWNERS),
        "load": dma_sems(6), "pair_send": dma_sems(2), "pair_recv": dma_sems(2),
        **exchange_scratch(),
    }
    if rider:
        inputs.update({"p1": ("v", shards[0]), "o1": ("v", shards[1])})
        outputs.update({"next_w": in_hbm(2, 4, 4, 96, HALF), "next_wo": in_hbm(2, 4, 4, 4, 48, WALF)})
        scratch.update(gather_scratch())
    return call(
        functools.partial(forward_body, layer, rider), "block_forward", 2 + layer, inputs, outputs, scratch
    )


def add_rows(target, first, second, *more):
    rows, lead = target.shape[-2], target.shape[:-2]
    per = rows // 16
    blocks = functools.reduce(lambda a, b: a * b, lead, 1)

    def body(n, carry):
        b = n // per
        spot = (b,) if len(lead) == 1 else (b // lead[1], lax.rem(b, lead[1]))
        at = spot + (pl.ds(pl.multiple_of(lax.rem(n, per) * 16, 16), 16), slice(None))
        total = first[at].astype(F32) + second[at].astype(F32)
        for ref in more:
            total = total + ref[at].astype(F32)
        target[at] = total.astype(target.dtype)
        return carry

    lax.fori_loop(0, blocks * per, body, 0)


def fold_shapes():
    return [(4, 96, CUT), (4, 96, CUT), (4, 4, 48, WALF)]


class Fold:
    def __init__(self, net, gi, go, r):
        self.net, self.gi, self.go_ref = net, gi, go
        self.h, self.m, self.s = (r.ha, r.hb, r.ho), (r.ma, r.mb, r.mo), (r.sa, r.sb, r.so)
        self.own = r.fold_own
        self.place = places()
        self.peers = (y_peer, z_peer, x_peer)

    def part(self, kind, t, half):
        _, y, z, x = self.place
        at = pl.ds(2 * half, 2) if half is not None else slice(None)
        if kind == 0:
            return self.gi.at[lax.rem(y + t, 4), at, :, pl.ds(0, CUT)]
        if kind == 1:
            return self.gi.at[at, lax.rem(z + t, 4), :, pl.ds(CUT, CUT)]
        return self.go_ref.at[at, :, lax.rem(x + t, 4)]

    def begin(self):
        go = self.net.go
        self.hops, self.direct, self.loads = {}, {}, []
        for half, k in ((0, 1), (1, 3)):
            for kind in range(3):
                self.hops[kind, half] = go(
                    self.part(kind, 2, half), self.h[kind].at[pl.ds(2 * half, 2)], self.peers[kind](k)
                )
        for half, k in ((1, 1), (0, 3)):
            for kind in range(3):
                side = 0 if k == 1 else 1
                self.direct[kind, side] = go(
                    self.part(kind, k, half), self.s[kind].at[side, pl.ds(2 * half, 2)], self.peers[kind](k)
                )
        for kind in range(3):
            self.loads.append(
                [
                    fetch(self.part(kind, 1, 0), self.m[kind].at[pl.ds(0, 2)], self.own.at[3 * kind]),
                    fetch(self.part(kind, 3, 1), self.m[kind].at[pl.ds(2, 2)], self.own.at[3 * kind + 1]),
                ]
            )

    def combine(self, kind):
        for copy in self.loads[kind]:
            copy.wait()
        for half in range(2):
            self.hops[kind, half].wait_recv()
        add_rows(self.m[kind], self.m[kind], self.h[kind])
        peer = self.peers[kind]
        for half, k in ((0, 1), (1, 3)):
            at = pl.ds(2 * half, 2)
            self.hops[kind, half] = self.net.go(self.m[kind].at[at], self.s[kind].at[half, at], peer(k))
        self.loads[kind] = [fetch(self.part(kind, 0, None), self.h[kind], self.own.at[3 * kind + 2])]

    def settle(self, kind):
        for copy in self.loads[kind]:
            copy.wait()
        for side in range(2):
            self.direct[kind, side].wait_recv()
            self.hops[kind, side].wait_recv()
        add_rows(self.h[kind], self.h[kind], self.s[kind].at[0], self.s[kind].at[1])


class Finish:
    def __init__(self, net, r):
        self.net, self.r = net, r
        self.place = places()

    def second(self, kind):
        _, y, z, _ = self.place
        r, go = self.r, self.net.go
        if kind == 0:
            self.a = [go(r.ha.at[lax.rem(z + k, 4)], r.r2a.at[k], z_peer(k)) for k in range(1, 4)]
            r.r2a[0] = r.ha[z]
        elif kind == 1:
            self.b = [go(r.hb.at[lax.rem(y + k, 4)], r.r2b.at[k], y_peer(k)) for k in range(1, 4)]
            r.r2b[0] = r.hb[y]
        else:
            self.o = [go(r.ho.at[lax.rem(y + k, 4)], r.r2o.at[k], y_peer(k)) for k in range(1, 4)]
            r.r2o[0] = r.ho[y]

    def third(self):
        _, y, z, x = self.place
        r, go = self.r, self.net.go
        for copy in self.a + self.b:
            copy.wait_recv()
        for n in range(4):
            at = pl.ds(24 * n, 24)
            for parts, cols in ((r.r2a, pl.ds(0, CUT)), (r.r2b, pl.ds(CUT, CUT))):
                total = parts[0, at, :].astype(F32)
                for k in range(1, 4):
                    total = total + parts[k, at, :].astype(F32)
                r.c3[n, :, cols] = total
        self.x = [go(r.c3.at[lax.rem(x + k, 4)], r.r3.at[x], x_peer(k)) for k in range(1, 4)]
        for copy in self.o:
            copy.wait_recv()
        add_rows(r.o2, r.r2o.at[0], r.r2o.at[1], r.r2o.at[2], r.r2o.at[3])
        self.z = [go(r.o2.at[lax.rem(z + k, 4)], r.r3o.at[k], z_peer(k)) for k in range(1, 4)]
        r.r3[x] = r.c3[x]
        r.r3o[0] = r.o2[z]

    def last(self, in_ref, out_ref):
        r = self.r
        for copy in self.x + self.z:
            copy.wait_recv()
        in_ref[...] = r.r3[0] + r.r3[1] + r.r3[2] + r.r3[3]
        total = r.r3o[0].astype(F32)
        for k in range(1, 4):
            total = total + r.r3o[k].astype(F32)
        out_ref[...] = total


def fold_scratch():
    a, b, o = fold_shapes()
    return {
        "ha": pltpu.VMEM(a, BF16), "hb": pltpu.VMEM(b, BF16), "ho": pltpu.VMEM(o, BF16),
        "ma": pltpu.VMEM(a, BF16), "mb": pltpu.VMEM(b, BF16), "mo": pltpu.VMEM(o, BF16),
        "sa": pltpu.VMEM((2,) + a, BF16), "sb": pltpu.VMEM((2,) + b, BF16), "so": pltpu.VMEM((2,) + o, BF16),
        "fold_own": dma_sems(9),
        "r2a": pltpu.VMEM(a, BF16), "r2b": pltpu.VMEM(b, BF16), "r2o": pltpu.VMEM(o, BF16),
        "c3": pltpu.VMEM((4, 24, HALF), F32), "r3": pltpu.VMEM((4, 24, HALF), F32),
        "o2": pltpu.VMEM((4, 48, WALF), BF16), "r3o": pltpu.VMEM((4, 48, WALF), BF16),
        "net_send": dma_sems(48), "net_recv": dma_sems(48),
    }


SLOTS = 3


def backward_body(layer, rider, r):
    section = lax.axis_index("section")
    load_state = fetch(r.states, r.state_s, r.load.at[0])

    def wo_tile(i):
        rows = pl.ds(pl.multiple_of(i * 384, 384), 384)
        slot = lax.rem(i, SLOTS)
        return pltpu.make_async_copy(r.wo.at[:, rows], r.wo_s.at[slot], r.wo_load.at[slot])

    def w_tile(n):
        slot = lax.rem(n, SLOTS)
        rows = pl.ds(pl.multiple_of((n // 2) * 256, 256), 256)
        return pltpu.make_async_copy(r.w.at[lax.rem(n, 2), rows], r.w_s.at[slot], r.w_load.at[slot])

    for n in range(SLOTS):
        wo_tile(n).start()
        w_tile(n).start()
    greet_layer(rider, False)
    net = Net(r.pair_send, r.pair_recv)
    if rider:
        fold = Fold(Net(r.net_send, r.net_recv), r.gi, r.go, r)
        fold.begin()
        rest = Finish(fold.net, r)
    ex = Exchange(True, r)
    live = r.flags[0]
    heads = r.heads[layer]
    r.gb[...] = (r.g[...].astype(F32) * live).astype(BF16)
    inv = r.inv[...]
    b = r.act[:, INNER : INNER + 128].astype(BF16)
    c = r.act[:, INNER + 128 : CONV].astype(BF16)
    dt = r.dt[...]
    cum = r.cum[...]
    r.dots[...] = jnp.zeros((TOK, 128), F32)
    own_half = pl.ds(pl.multiple_of(section * WALF, 128), WALF)
    other_half = pl.ds(pl.multiple_of((1 - section) * WALF, 128), WALF)
    pairs = [net.go(r.gb.at[:, other_half], r.both_gb.at[section], sibling())]
    owns = [fetch(r.gb.at[:, own_half], r.both_gb.at[section], r.load.at[1])]

    def first(i, carry):
        slot = lax.rem(i, SLOTS)
        wo_tile(i).wait()
        gg = dot32(r.gb[:, :WALF], r.wo_s[slot, 0], ((1,), (1,)))
        gg = gg + dot32(r.gb[:, WALF:], r.wo_s[slot, 1], ((1,), (1,)))

        @pl.when(i + SLOTS < 8)
        def _():
            wo_tile(i + SLOTS).start()

        r.gg[:, pl.ds(pl.multiple_of(i * 384, 384), 384)] = gg
        for q in range(3):
            cols = group_cols(i, q)
            gate = r.side[:, gate_cols(i, q)]
            z = r.y[:, cols].astype(F32) * (gate / (1.0 + jnp.exp(-gate)))
            mid = r.taps[layer, ROW_MID : ROW_MID + 1, cols]
            r.dots[...] += gg[:, 128 * q : 128 * q + 128] * mid * z
        return carry

    lax.fori_loop(0, 8, first, 0)
    total = jnp.broadcast_to(jnp.sum(r.dots[...], axis=1, keepdims=True), (TOK, 128))
    shift = total * inv * inv * inv / INNER
    r.gtaps[...] = jnp.zeros_like(r.gtaps)

    def second(n, carry):
        i = own_group(n)
        cum_i = to_front(cum, i)
        for q in range(3):
            cols = group_cols(i, q)
            gate = r.side[:, gate_cols(i, q)]
            y = r.y[:, cols].astype(F32)
            gg = r.gg[:, cols]
            sig = 1.0 / (1.0 + jnp.exp(-gate))
            act = gate * sig
            z = y * act
            dz = gg * r.taps[layer, ROW_MID : ROW_MID + 1, cols] * inv - z * shift
            dy = (dz * act).astype(BF16)
            r.dy[:, cols] = dy
            r.gside[:, gate_cols(i, q)] = (dz * y * (sig * (1.0 + gate * (1.0 - sig)))).astype(BF16)
            r.gtaps[ROW_MID : ROW_MID + 1, cols] = jnp.sum(gg * z * inv, axis=0, keepdims=True)
            far = (dy.astype(F32) * jnp.exp(pair_cols(cum_i, q)[2])).astype(BF16)
            store_heads(r.ds, i, q, dot32(far, c, ((0,), (0,))).astype(BF16))
        ex.send(2 * i)
        ex.send(2 * i + 1)
        return carry

    lax.fori_loop(0, 8, second, 0)
    if rider:
        for kind in (2, 0, 1):
            fold.combine(kind)
    ex.scan(r.dec)
    load_state.wait()
    r.cumt[...] = cum.T
    causal = tri_of(True)
    scores = dot32(c, b, ((1,), (1,)))
    lane = lax.broadcasted_iota(jnp.int32, (TOK, 128), 1)
    pick_row = lax.broadcasted_iota(jnp.int32, (128, 128), 0)
    pick_col = lax.broadcasted_iota(jnp.int32, (128, 128), 1)
    picks = []
    for q in range(3):
        target = jnp.where(pick_row < 64, LANES[2 * q], LANES[2 * q + 1])
        picks.append((pick_col == target).astype(F32).astype(BF16))
    for ref in (r.dscore, r.grad_b, r.grad_c, r.xdu, r.dyy, r.thin):
        ref[...] = jnp.zeros_like(ref)

    def inside(i, carry):
        cum_i = to_front(cum, i)
        dt_i = to_front(dt, i)
        rows = r.cumt[pl.ds(pl.multiple_of(16 * i, 16), 16), :]
        for q in range(3):
            cols = group_cols(i, q)
            cum_a, cum_b, cum_x = pair_cols(cum_i, q)
            u16 = (r.act[:, cols] * pair_cols(dt_i, q)[2]).astype(BF16)
            dy16 = r.dy[:, cols]
            nil = jnp.zeros_like(dy16)
            dys = jnp.concatenate([jnp.where(lane < 64, dy16, nil), jnp.where(lane < 64, nil, dy16)], axis=0)
            both = dot32(dys, u16, ((1,), (1,)))
            mixes = []
            for n, (cum_h, off) in enumerate(((cum_a, LANES[2 * q]), (cum_b, LANES[2 * q + 1]))):
                gap = cum_h - rows[off : off + 1]
                decay = jnp.exp(jnp.where(causal, gap, -1e30))
                mixes.append((scores * decay).astype(BF16))
                r.dscore[...] += both[n * TOK : n * TOK + TOK] * decay
            r.gg[:, cols] = dot32(jnp.concatenate(mixes, axis=0), dys, ((0,), (0,)))
            far = (dy16.astype(F32) * jnp.exp(cum_x)).astype(BF16)
            r.grad_c[...] += dot32(far, head_rows_at(r.state_s, i, q))
        return carry

    lax.fori_loop(0, 8, inside, 0)
    if rider:
        for kind in (2, 0, 1):
            fold.settle(kind)
            rest.second(kind)

    def conv_back(cols, gact):
        gsum = gact * r.dact[:, cols]
        r.gsum[:, cols] = gsum
        blk = r.pre[:, cols].astype(F32)
        cat = jnp.concatenate([r.halo[:, cols].astype(F32)[8:], blk], axis=0)
        sums = [jnp.sum(gsum * cat[5 + k : 5 + k + TOK], axis=0, keepdims=True) for k in range(4)]
        sums.append(jnp.sum(gsum, axis=0, keepdims=True))
        r.gtaps[0:5, cols] = jnp.concatenate(sums, axis=0)

    ex.finish()

    def across(i, carry):
        cum_i = to_front(cum, i)
        dt_i = to_front(dt, i)
        skip_i = pltpu.roll(heads, lax.rem(128 - 16 * i, 128), 1)[ROW_SKIP : ROW_SKIP + 1]
        x_du = jnp.zeros((TOK, 128), F32)
        dy_y = jnp.zeros((TOK, 128), F32)
        thin = jnp.zeros((16, 128), F32)
        edges = {}
        for q in range(3):
            cols = group_cols(i, q)
            x = r.act[:, cols]
            cum_x = pair_cols(cum_i, q)[2]
            dt_x = pair_cols(dt_i, q)[2]
            fade = jnp.exp(cum_x[TOK - 1 : TOK] - cum_x)
            u = x * dt_x
            dy = r.dy[:, cols].astype(F32)
            state16 = head_rows_at(r.state_s, i, q)
            dstate16 = head_rows_at(r.back, i, q)
            du_far = fade * dot32(b, dstate16, ((1,), (1,)))
            du = r.gg[:, cols] + du_far
            r.grad_b[...] += dot32((u * fade).astype(BF16), dstate16)
            overlap = state16.astype(F32) * dstate16.astype(F32)
            edges[LANES[2 * q]] = jnp.sum(overlap[:64], axis=0, keepdims=True)
            edges[LANES[2 * q + 1]] = jnp.sum(overlap[64:], axis=0, keepdims=True)
            x_du = x_du + split_right(x * du, picks[q], 2)
            dy_y = dy_y + split_right(dy * r.raw[:, cols], picks[q], 2)
            thin = thin + split_right(
                jnp.concatenate(
                    [
                        jnp.broadcast_to(jnp.sum(u * du_far, axis=0, keepdims=True), (8, 128)),
                        jnp.broadcast_to(jnp.sum(dy * x, axis=0, keepdims=True), (8, 128)),
                    ],
                    axis=0,
                ),
                picks[q],
                3,
            )
            conv_back(cols, du * dt_x + pair_row(skip_i, q) * dy)
        nothing = jnp.zeros((1, 128), F32)
        r.edge[pl.ds(pl.multiple_of(16 * i, 16), 16), :] = jnp.concatenate(
            [edges.get(k, nothing) for k in range(16)], axis=0
        )
        r.xdu[...] += pltpu.roll(x_du, 16 * i, 1)
        r.dyy[...] += pltpu.roll(dy_y, 16 * i, 1)
        r.thin[...] += pltpu.roll(thin, 16 * i, 1)
        return carry

    lax.fori_loop(0, 8, across, 0)
    dscore16 = r.dscore[...].astype(BF16)
    conv_back(pl.ds(INNER, 128), r.grad_b[...] + dot32(dscore16, c, ((0,), (0,))))
    conv_back(pl.ds(INNER + 128, 128), r.grad_c[...] + dot32(dscore16, b))
    r.tail[...] = r.gsum[:8, :]
    halo = Halo(r.tail, r.halo_near, r.halo_far, r.halo_s, False)
    halo.start()
    ones = jnp.ones((128, 128), BF16)
    edge = split_right(r.edge[...], ones, 3).T[0:1] * jnp.exp(cum[TOK - 1 : TOK]) + r.thin[0:1]
    x_du = r.xdu[...]
    drate = split_left(tri_of(False).astype(F32).astype(BF16), r.dyy[...] - dt * x_du, 3) + edge
    speed = jnp.exp(heads[ROW_DECAY : ROW_DECAY + 1])
    ddt = x_du - drate * speed
    step = r.side[:, :128].astype(BF16).astype(F32) + heads[ROW_BIAS : ROW_BIAS + 1]
    dstep = jnp.where(head_lanes(), ddt / (1.0 + jnp.exp(-step)), 0.0) * live
    r.gside[:, :128] = dstep.astype(BF16)
    r.gside[:, 128:GATE0] = jnp.zeros((TOK, 128), BF16)
    r.ghead[...] = jnp.concatenate(
        [
            jnp.zeros((5, 128), F32),
            jnp.sum(dstep, axis=0, keepdims=True),
            jnp.sum(-drate * dt * speed, axis=0, keepdims=True),
            r.thin[8:9],
        ],
        axis=0,
    )
    halo.wait()
    after = jnp.where(r.flags[3] > 0.0, r.halo_far[...], r.halo_near[...])
    r.halo_near[...] = jnp.where(live > 0.0, after, jnp.zeros_like(after))

    def conv_tile(i, carry):
        cols = pl.ds(pl.multiple_of(i * 128, 128), 128)
        cat = jnp.concatenate([r.gsum[:, cols], r.halo_near[:, cols]], axis=0)
        taps = r.taps[layer, :, cols]
        total = taps[3:4] * cat[:TOK]
        for k in range(3):
            total = total + taps[k : k + 1] * cat[3 - k : 3 - k + TOK]
        r.gpre[:, cols] = total.astype(BF16)
        return carry

    lax.fori_loop(0, CONV // 128, conv_tile, 0)

    @pl.when(section == 0)
    def _():
        net_copy(net, r.gside, r.both_g.at[0], 1).start()
        pltpu.make_async_copy(r.gpre, r.both_g.at[0], r.load.at[2]).start()

    @pl.when(section == 1)
    def _():
        net_copy(net, r.gpre, r.both_g.at[1], 1).start()
        pltpu.make_async_copy(r.gside, r.both_g.at[1], r.load.at[2]).start()

    def project(n, carry):
        rows = pl.ds(pl.multiple_of(n * 256, 256), 256)
        w_tile(2 * n).wait()
        value = dot32(r.gpre[...], r.w_s[lax.rem(2 * n, SLOTS)], ((1,), (1,)))

        @pl.when(2 * n + SLOTS < 12)
        def _():
            w_tile(2 * n + SLOTS).start()

        w_tile(2 * n + 1).wait()
        value = value + dot32(r.gside[...], r.w_s[lax.rem(2 * n + 1, SLOTS)], ((1,), (1,)))

        @pl.when(2 * n + 1 + SLOTS < 12)
        def _():
            w_tile(2 * n + 1 + SLOTS).start()

        r.hid[:, rows] = value
        return carry

    lax.fori_loop(0, D // 256, project, 0)
    x = r.x[...].astype(F32)
    grad = r.hid[...]
    inv_x = lax.rsqrt(jnp.sum(x * x, axis=1, keepdims=True) / D + EPS)
    scaled = grad * r.gain[layer, ROW_NORM : ROW_NORM + 1, :]
    dots = jnp.sum(scaled * x, axis=1, keepdims=True)
    dx = scaled * inv_x - x * (dots * inv_x * inv_x * inv_x / D)
    r.result[...] = (r.g[...].astype(F32) + dx).astype(BF16)
    r.ggain[...] = jnp.broadcast_to(jnp.sum(grad * x * inv_x, axis=0, keepdims=True), (8, D))
    if rider:
        rest.third()
        rest.last(r.fin_in, r.fin_out)
        fold.net.drain()
    for copy in owns:
        copy.wait()
    pltpu.make_async_copy(r.gpre, r.both_g.at[section], r.load.at[2]).wait()
    for copy in pairs:
        copy.wait_recv()
    swap = net_copy(net, r.gpre, r.both_g.at[section], 1)
    swap.wait_recv()
    swap.wait_send()
    net.drain()
    halo.drain()
    ex.drain()


def net_copy(net, src, dst, n):
    return pltpu.make_async_remote_copy(
        src_ref=src, dst_ref=dst, send_sem=net.send.at[n], recv_sem=net.recv.at[n],
        device_id=sibling(), device_id_type=MESH,
    )


def block_backward(layer, flags, g, x, w, wo, small, kept, grads):
    rider = grads is not None
    inputs = {
        "flags": ("s", flags), "g": ("v", g), "x": ("v", x), "w": ("h", w), "wo": ("h", wo), "taps": ("v", small.taps),
        "gain": ("v", small.gain), "heads": ("v", small.heads), "states": ("h", kept.states),
    }
    for key in ("act", "dact", "side", "raw", "dt", "cum", "inv", "dec", "pre", "halo", "y"):
        inputs[key] = ("v", getattr(kept, key))
    outputs = {
        "result": in_vmem(TOK, D, dtype=BF16), "both_gb": in_hbm(2, TOK, WALF), "both_g": in_hbm(2, TOK, HALF),
        "gtaps": in_vmem(8, CONV), "ggain": in_vmem(8, D), "ghead": in_vmem(8, 128),
    }
    tile = pltpu.VMEM((TOK, 128), F32)
    edge = pltpu.VMEM((8, CONV), F32)
    scratch = {
        "wo_s": pltpu.VMEM((SLOTS, 2, 384, WALF), BF16), "w_s": pltpu.VMEM((SLOTS, 256, HALF), BF16),
        "wo_load": dma_sems(SLOTS), "w_load": dma_sems(SLOTS), "load": dma_sems(3),
        "state_s": pltpu.VMEM((OWNERS, OWN, STATE), BF16),
        "gb": pltpu.VMEM((TOK, D), BF16), "gg": pltpu.VMEM((TOK, INNER), F32), "dy": pltpu.VMEM((TOK, INNER), BF16),
        "gsum": pltpu.VMEM((TOK, CONV), F32), "gpre": pltpu.VMEM((TOK, HALF), BF16), "gside": pltpu.VMEM((TOK, HALF), BF16),
        "hid": pltpu.VMEM((TOK, D), F32),
        "dots": tile, "cumt": tile, "edge": tile, "dscore": tile, "grad_b": tile, "grad_c": tile, "xdu": tile, "dyy": tile,
        "thin": pltpu.VMEM((16, 128), F32),
        "tail": edge, "halo_near": edge, "halo_far": edge, "halo_s": dma_sems(4),
        "pair_send": dma_sems(2), "pair_recv": dma_sems(2),
        **exchange_scratch(),
    }
    if rider:
        inputs.update({"gi": ("h", grads[0]), "go": ("h", grads[1])})
        outputs.update({"fin_in": in_vmem(24, HALF), "fin_out": in_vmem(48, WALF)})
        scratch.update(fold_scratch())
    return call(
        functools.partial(backward_body, layer, rider), "block_backward", 4 + layer, inputs, outputs, scratch
    )


def reduce_body(r):
    c, y, z, x = places()
    greet_axes()
    net = Net(r.net_send, r.net_recv)
    fold = Fold(net, r.gi, r.go, r)
    rest = Finish(net, r)
    fold.begin()
    row = lax.broadcasted_iota(jnp.int32, (8, 128), 0)
    lane = lane_at((8, 128))
    for layer in range(2):
        taps, gain, heads = r.gtaps.at[layer], r.ggain.at[layer], r.ghead.at[layer]
        for d in range(64):
            cell = (layer, d // 16, (d // 4) % 4, d % 4)
            first = jnp.where(lane < 48, take_chunk(taps, 0, 48, d), 0.0)
            norm = jnp.where(lane < 24, take_chunk(gain, 0, 24, d), 0.0)
            r.cells[cell + (slice(0, 8),)] = jnp.where(row == ROW_NORM, norm, first)
            second = jnp.where(lane < 4, take_chunk(taps, INNER, 4, d), 0.0)
            head = jnp.where(lane < 3, take_chunk(heads, 0, 8, d // 4), 0.0)
            r.cells[cell + (slice(8, 16),)] = jnp.where(row >= 5, head, second)
    pair = net.go(r.cells.at[1 - c], r.other, sibling())
    other_in = net.go(r.far_in, r.got_in, sibling())
    other_out = net.go(r.far_out, r.got_out, sibling())
    pair.wait_recv()
    r.sum0[...] = r.cells[c] + r.other[...]
    hops = [net.go(r.sum0.at[lax.rem(y + k, 4)], r.in_y.at[k], y_peer(k)) for k in range(1, 4)]
    for kind in (2, 0, 1):
        fold.combine(kind)
    for copy in hops:
        copy.wait_recv()
    r.sum1[...] = r.sum0[y] + r.in_y[1] + r.in_y[2] + r.in_y[3]
    hops = [net.go(r.sum1.at[lax.rem(z + k, 4)], r.in_z.at[k], z_peer(k)) for k in range(1, 4)]
    for kind in (2, 0, 1):
        fold.settle(kind)
        rest.second(kind)
    for copy in hops:
        copy.wait_recv()
    r.sum2[...] = r.sum1[z] + r.in_z[1] + r.in_z[2] + r.in_z[3]
    r.in_x[x] = r.sum2[x]
    hops = [net.go(r.sum2.at[lax.rem(x + k, 4)], r.in_x.at[x], x_peer(k)) for k in range(1, 4)]
    rest.third()
    for copy in hops:
        copy.wait_recv()
    r.blob[...] = r.in_x[0] + r.in_x[1] + r.in_x[2] + r.in_x[3]
    rest.last(r.near_in, r.near_out)
    near_in = net.go(r.near_in, r.got_near_in, sibling())
    near_out = net.go(r.near_out, r.got_near_out, sibling())
    for copy in (other_in, other_out, near_in, near_out):
        copy.wait_recv()

    @pl.when(c == 0)
    def _():
        r.inner[...] = r.near_in[:, :INNER]
        r.bc[...] = r.near_in[:, INNER:]
        r.step[...] = r.got_near_in[:, :128]
        r.gate[...] = r.got_near_in[:, GATE0:]
        r.out[:, :WALF] = r.near_out[...]
        r.out[:, WALF:] = r.got_near_out[...]

    @pl.when(c == 1)
    def _():
        r.inner[...] = r.got_in[:, :INNER]
        r.bc[...] = r.got_in[:, INNER:]
        r.step[...] = r.far_in[:, :128]
        r.gate[...] = r.far_in[:, GATE0:]
        r.out[:, :WALF] = r.got_out[...]
        r.out[:, WALF:] = r.far_out[...]

    net.drain()


def reduce_all(grads, far, gtaps, ggain, ghead):
    cell = (4, 4, 16, 128)
    return call(
        reduce_body, "reduce_grads", 6,
        {
            "gi": ("h", grads[0]), "go": ("h", grads[1]), "far_in": ("v", far[0]), "far_out": ("v", far[1]),
            "gtaps": ("v", gtaps), "ggain": ("v", ggain), "ghead": ("v", ghead),
        },
        {
            "inner": in_vmem(24, INNER), "bc": in_vmem(24, 2 * STATE), "step": in_vmem(24, 128),
            "gate": in_vmem(24, INNER), "out": in_vmem(48, D), "blob": in_vmem(16, 128),
        },
        {
            "near_in": pltpu.VMEM((24, HALF), F32), "near_out": pltpu.VMEM((48, WALF), F32),
            "got_near_in": pltpu.VMEM((24, HALF), F32), "got_near_out": pltpu.VMEM((48, WALF), F32),
            "got_in": pltpu.VMEM((24, HALF), F32), "got_out": pltpu.VMEM((48, WALF), F32),
            "cells": pltpu.VMEM((2, 4) + cell, F32), "other": pltpu.VMEM((4,) + cell, F32),
            "sum0": pltpu.VMEM((4,) + cell, F32), "in_y": pltpu.VMEM((4,) + cell, F32),
            "sum1": pltpu.VMEM(cell, F32), "in_z": pltpu.VMEM((4,) + cell[1:], F32),
            "sum2": pltpu.VMEM(cell[1:], F32), "in_x": pltpu.VMEM((4, 16, 128), F32),
            **fold_scratch(),
        },
    )


def step_lanes(step):
    lead = step.shape[0]
    return jnp.pad(step.reshape(lead, OWNERS, 3), ((0, 0), (0, 0), (0, 5))).reshape(lead, 128)


def small_blob(norm_gain, inner_gain, conv_inner, conv_bc, heads):
    def row(value):
        return jnp.pad(value.astype(F32), ((0, 0), (0, 128 - value.shape[1])))

    return jnp.concatenate(
        [
            row(conv_inner), row(inner_gain[None]), row(norm_gain[None]), jnp.zeros((1, 128), F32),
            row(conv_bc), row(heads),
        ],
        axis=0,
    )


def settle(section, first_value, second_value):
    own = jnp.where(section == 0, first_value, second_value)
    got = lax.ppermute(jnp.where(section == 0, second_value, first_value), "section", [(0, 1), (1, 0)])
    return jnp.stack([jnp.where(section == 0, own, got), jnp.where(section == 0, got, own)])


def per_device(
    block_input, cotangent, seg_groups, norm_gain, w_gate, w_inner, w_bc, w_step, conv_inner, conv_bc, head_params,
    inner_gain, w_out,
):
    section = lax.axis_index("section")
    seq_pos = lax.axis_index("seq")
    small = start_up(
        w_inner[0], w_bc[0], step_lanes(w_step[0]), w_gate[0], w_out[0],
        small_blob(norm_gain[0], inner_gain[0], conv_inner[0], conv_bc[0], head_params[0]),
    )
    weights = [(small.w.reshape(2, D, HALF), small.wo.reshape(2, INNER, WALF)), None]
    firsts = (BLOCKS - seg_groups[0]) * (BLOCK_LEN // TOK)
    first = jnp.where(section == 0, firsts[0], firsts[1])
    at_start = seq_pos == first
    flags = jnp.stack(
        [
            seq_pos >= first,
            jnp.logical_not(at_start) | ((section == 1) & (first == 0)),
            at_start & (section == 1) & (first != 0),
            (section == 0) & (seq_pos == 15) & (firsts[1] != 0),
        ]
    ).astype(F32)

    x = lax.dynamic_index_in_dim(block_input[0], section, 0, keepdims=False)
    kept, inputs = [], []
    for layer in range(2):
        w, wo = weights[layer]
        made = block_forward(
            layer, flags, x, w, wo, small, (small.p1, small.o1) if layer == 0 else None
        )
        if layer == 0:
            weights[1] = (made.next_w.reshape(2, D, HALF), made.next_wo.reshape(2, INNER, WALF))
        kept.append(made)
        inputs.append(x)
        x = made.result

    g = lax.dynamic_index_in_dim(cotangent[0], section, 0, keepdims=False)
    grads = None
    backs = [None, None]
    for layer in (1, 0):
        w, wo = weights[layer]
        back = block_backward(layer, flags, g, inputs[layer], w, wo, small, kept[layer], grads)
        backs[layer] = back
        g = back.result
        hidden = kept[layer].both_hidden.reshape(2 * TOK, D)
        gated = kept[layer].both_gated.reshape(2 * TOK, INNER)
        grad_in = dot32(hidden, back.both_g.reshape(2 * TOK, HALF), ((0,), (0,))).astype(BF16)
        grad_out = dot32(gated, back.both_gb.reshape(2 * TOK, WALF), ((0,), (0,))).astype(BF16)
        grads = (grad_in.reshape(4, 4, 96, HALF), grad_out.reshape(4, 4, 4, 48, WALF))

    final = reduce_all(
        grads, (backs[0].fin_in, backs[0].fin_out),
        jnp.stack([backs[0].gtaps, backs[1].gtaps]), jnp.stack([backs[0].ggain, backs[1].ggain]),
        jnp.stack([backs[0].ghead, backs[1].ghead]),
    )
    blob = final.blob
    return (
        settle(section, kept[0].result, kept[1].result)[None, None],
        settle(section, backs[0].result, backs[1].result)[None, None],
        blob[ROW_NORM : ROW_NORM + 1, :24],
        final.gate[None],
        final.inner[None],
        final.bc[None],
        final.step.reshape(24, OWNERS, 8)[:, :, :3].reshape(24, HEADS)[None],
        blob[None, 0:5, :48],
        blob[None, 8:13, :4],
        blob[None, 13:16, :3],
        blob[ROW_MID : ROW_MID + 1, :48],
        final.out[None],
    )


def solution(mesh):
    weight = P("section", ROWS_ALL, None)
    vector = P("section", ROWS_ALL)
    taps = P("section", None, ROWS_ALL)
    tokens = P("wsh", None, "seq", None)
    heads = P("section", None, "seq")
    result = P("section", "wsh", None, "seq", None)
    return jax.shard_map(
        per_device,
        mesh=mesh,
        in_specs=(
            tokens, tokens, P("wsh", None), vector, weight, weight, weight, weight, taps, taps, heads, vector, weight,
        ),
        out_specs=(
            result, result, vector, weight, weight, weight, weight, taps, taps, heads, vector, weight,
        ),
        check_vma=False,
    )
```

```python
import functools
import types

import jax
import jax.numpy as jnp
from jax import lax
from jax.experimental import pallas as pl
from jax.experimental.pallas import tpu as pltpu
from jax.sharding import PartitionSpec as P

D = 1536
INNER = 3072
HEADS = 48
STATE = 128
BLOCK_LEN = 256
BLOCKS = 8
TOK = 128
CONV = INNER + 2 * STATE
HALF = CONV
GATE0 = 256
CUT = HALF // 2
WALF = D // 2
WCUT = WALF // 2
ECOLS = INNER // 2
LCOLS = HALF // 2 + 128
LSPLIT = LCOLS
OWNERS = 16
OWN = 192
EPS = 1e-05
F32 = jnp.float32
BF16 = jnp.bfloat16
MESH = pl.DeviceIdType.MESH
VMEM_LIMIT = 61 * 1024 * 1024
LANES = (0, 1, 2, 8, 9, 10)
ROWS_ALL = ("seq", "wsh")
ROW_MID, ROW_NORM = 5, 6
ROW_BIAS, ROW_DECAY, ROW_SKIP = 5, 6, 7


def dot32(left, right, dims=((1,), (0,))):
    return lax.dot_general(left, right, (dims, ((), ())), preferred_element_type=F32)


def split_left(exact, value, terms):
    total = None
    for _ in range(terms):
        part = value.astype(BF16)
        value = value - part.astype(F32)
        term = dot32(exact, part)
        total = term if total is None else total + term
    return total


def split_right(value, exact, terms, dims=((1,), (0,))):
    total = None
    for _ in range(terms):
        part = value.astype(BF16)
        value = value - part.astype(F32)
        term = dot32(part, exact, dims)
        total = term if total is None else total + term
    return total


def pair_cols(tile, q):
    lane = lax.broadcasted_iota(jnp.int32, (TOK, 128), 1)
    a = jnp.broadcast_to(tile[:, LANES[2 * q] : LANES[2 * q] + 1], (TOK, 128))
    b = jnp.broadcast_to(tile[:, LANES[2 * q + 1] : LANES[2 * q + 1] + 1], (TOK, 128))
    return a, b, jnp.where(lane < 64, a, b)


def pair_row(row, q):
    lane = lax.broadcasted_iota(jnp.int32, (1, 128), 1)
    a = jnp.broadcast_to(row[:, LANES[2 * q] : LANES[2 * q] + 1], (1, 128))
    b = jnp.broadcast_to(row[:, LANES[2 * q + 1] : LANES[2 * q + 1] + 1], (1, 128))
    return jnp.where(lane < 64, a, b)


def to_front(tile, i):
    return pltpu.roll(tile, lax.rem(128 - 16 * i, 128), 1)


def conv_of(cat, taps):
    total = taps[4:5] + taps[3:4] * cat[8 : 8 + TOK]
    for k in range(3):
        total = total + taps[k : k + 1] * cat[5 + k : 5 + k + TOK]
    return total


def tri_of(lower):
    row = lax.broadcasted_iota(jnp.int32, (TOK, TOK), 0)
    col = lax.broadcasted_iota(jnp.int32, (TOK, TOK), 1)
    return row >= col if lower else row <= col


def head_lanes():
    lane = lax.broadcasted_iota(jnp.int32, (TOK, 128), 1)
    return (lane % 8) < 3


def group_cols(i, q):
    return pl.ds(pl.multiple_of(i * 384 + q * 128, 128), 128)


def gate_cols(i, q):
    return pl.ds(pl.multiple_of(GATE0 + i * 384 + q * 128, 128), 128)


def in_hbm(*shape, dtype=BF16):
    return jax.ShapeDtypeStruct(shape, dtype), pl.BlockSpec(memory_space=pl.ANY)


def in_vmem(*shape, dtype=F32):
    return jax.ShapeDtypeStruct(shape, dtype), pl.BlockSpec(memory_space=pltpu.VMEM)


def call(body, name, ident, inputs, outputs, scratch):
    spaces = {"h": pl.ANY, "v": pltpu.VMEM, "s": pltpu.SMEM}
    names = [key for key in inputs] + [key for key in outputs] + [key for key in scratch]

    def kernel(*refs):
        body(types.SimpleNamespace(**dict(zip(names, refs))))

    out = pl.pallas_call(
        kernel,
        out_shape=tuple(shape for shape, _ in outputs.values()),
        in_specs=[pl.BlockSpec(memory_space=spaces[kind]) for kind, _ in inputs.values()],
        out_specs=tuple(spec for _, spec in outputs.values()),
        scratch_shapes=list(scratch.values()),
        compiler_params=pltpu.CompilerParams(
            collective_id=ident, has_side_effects=True, vmem_limit_bytes=VMEM_LIMIT
        ),
        name=name,
    )(*[value for _, value in inputs.values()])
    return types.SimpleNamespace(**dict(zip(outputs, out)))


def dma_sems(count):
    return pltpu.SemaphoreType.DMA((count,))


def places():
    section = lax.axis_index("section")
    seq = lax.axis_index("seq")
    return section, seq // 4, lax.rem(seq, 4), lax.axis_index("wsh")


def x_peer(k):
    return {"wsh": lax.rem(lax.axis_index("wsh") + k, 4)}


def z_peer(k):
    _, y, z, _ = places()
    return {"seq": y * 4 + lax.rem(z + k, 4)}


def y_peer(k):
    _, y, z, _ = places()
    return {"seq": lax.rem(y + k, 4) * 4 + z}


def sibling():
    return {"section": 1 - lax.axis_index("section")}


def say_hello(peer):
    pl.semaphore_signal(pltpu.get_barrier_semaphore(), inc=1, device_id=peer, device_id_type=MESH)


def greet_axes():
    for k in range(1, 4):
        for peer in (x_peer(k), y_peer(k), z_peer(k)):
            say_hello(peer)
    say_hello(sibling())
    pl.semaphore_wait(pltpu.get_barrier_semaphore(), 10)


def fetch(src, dst, sem):
    copy = pltpu.make_async_copy(src, dst, sem)
    copy.start()
    return copy


class Net:
    def __init__(self, send, recv):
        self.send, self.recv = send, recv
        self.count = 0
        self.started = []

    def go(self, src, dst, peer):
        copy = pltpu.make_async_remote_copy(
            src_ref=src, dst_ref=dst, send_sem=self.send.at[self.count], recv_sem=self.recv.at[self.count],
            device_id=peer, device_id_type=MESH,
        )
        copy.start()
        self.count += 1
        self.started.append(copy)
        return copy

    def drain(self):
        for copy in self.started:
            copy.wait_send()


class Gather:
    def __init__(self, net, p, o, w, wo, stage, rows, own):
        self.net, self.p, self.o, self.w, self.wo = net, p, o, w, wo
        self.stage, self.rows, self.own = stage, rows, own
        self.place = places()
        self.near, self.far, self.inner, self.passed = {}, {}, {}, []
        self.peers = (y_peer, z_peer, x_peer, x_peer)
        self.inner_peers = (z_peer, y_peer, y_peer, z_peer)

    def band(self, kind, j, moved, half=None):
        c, y, z, x = self.place
        rows = slice(None) if half is None else pl.ds(48 * half, 48)
        many = slice(None) if half is None else pl.ds(2 * half, 2)
        if kind == 0:
            return self.w.at[c, lax.rem(y + 4 - moved, 4), lax.rem(z + 4 - j, 4), rows, pl.ds(0, CUT)]
        if kind == 1:
            return self.w.at[c, lax.rem(y + 4 - j, 4), lax.rem(z + 4 - moved, 4), rows, pl.ds(CUT, CUT)]
        if kind == 2:
            return self.wo.at[c, lax.rem(y + 4 - j, 4), many, lax.rem(x + 4 - moved, 4), :, pl.ds(0, WCUT)]
        return self.wo.at[c, many, lax.rem(z + 4 - j, 4), lax.rem(x + 4 - moved, 4), :, pl.ds(WCUT, WCUT)]

    def pass_on(self, part):
        self.passed.append(self.net.go(part, part, sibling()))

    def begin(self):
        c, y, z, x = self.place
        go = self.net.go
        self.first, self.spots = [], []
        spot = self.wo.at[c, y, z, x]
        for k in range(1, 4):
            self.first.append(go(self.p, self.stage.at[x], x_peer(k)))
            for cols, peer in ((pl.ds(0, WCUT), z_peer), (pl.ds(WCUT, WCUT), y_peer)):
                self.spots.append(go(self.o.at[:, cols], spot.at[:, cols], peer(k)))
        self.own_o = fetch(self.o, spot, self.own.at[0])
        self.stage[x] = self.p[...]

    def rows_in(self):
        c, y, z, x = self.place
        go = self.net.go
        for copy in self.first:
            copy.wait_recv()
        self.rows[...] = jnp.concatenate(
            [self.stage[n].astype(F32)[:24] for n in range(4)], axis=0
        ).astype(BF16)
        for k in (1, 3):
            for kind, cols in ((0, pl.ds(0, CUT)), (1, pl.ds(CUT, CUT))):
                self.inner[kind, k] = go(
                    self.rows.at[:, cols], self.band(kind, 0, 0), self.inner_peers[kind](k)
                )
        own_w = fetch(self.rows, self.w.at[c, y, z], self.own.at[1])
        self.own_o.wait()
        for copy in self.spots:
            copy.wait_recv()
        for k in (1, 3):
            for kind in (2, 3):
                part = self.band(kind, 0, 0)
                self.inner[kind, k] = go(part, part, self.inner_peers[kind](k))
        own_w.wait()
        self.spread(0)

    def spread(self, j):
        if j in (1, 3):
            for kind in range(4):
                self.inner[kind, j].wait_recv()
                part = self.band(kind, j, 0, 0 if j == 1 else 1)
                self.inner[kind, 2, j] = self.net.go(part, part, self.inner_peers[kind](j))
        if j == 2:
            for kind in range(4):
                self.inner[kind, 2, 1].wait_recv()
                self.inner[kind, 2, 3].wait_recv()
        for k in (1, 3):
            for kind in range(4):
                part = self.band(kind, j, 0)
                self.near[kind, j, k] = self.net.go(part, part, self.peers[kind](k))
        for kind in range(4):
            self.pass_on(self.band(kind, j, 0))

    def relay(self, j):
        for k in (1, 3):
            for kind in range(4):
                self.near[kind, j, k].wait_recv()
                part = self.band(kind, j, k)
                if (k == 1) == (j < 2):
                    self.far[kind, j] = self.net.go(part, part, self.peers[kind](k))
                self.pass_on(part)

    def last(self, j):
        for kind in range(4):
            self.far[kind, j].wait_recv()
            self.pass_on(self.band(kind, j, 2))

    def end(self):
        for copy in self.passed:
            copy.wait_recv()


def gather_scratch():
    return {
        "stage": pltpu.VMEM((4, 32, HALF), BF16),
        "rows": pltpu.VMEM((96, HALF), BF16),
        "own": dma_sems(2),
    }


def lane_at(shape):
    return lax.broadcasted_iota(jnp.int32, shape, 1)


def place_chunks(cells, width, total):
    tiles = [jnp.zeros((8, 128), F32) for _ in range(total // 128)]
    lane = lane_at((8, 128))
    for d in range(64):
        t, off = (width * d) // 128, (width * d) % 128
        moved = pltpu.roll(cells(d), off, 1) if off else cells(d)
        stop = off + width
        tiles[t] = jnp.where((lane >= off) & (lane < min(stop, 128)), moved, tiles[t])
        if stop > 128:
            tiles[t + 1] = jnp.where(lane < stop - 128, moved, tiles[t + 1])
    return tiles


def take_chunk(ref, base, width, d):
    start = base + width * d
    t, off = start // 128, start % 128
    tile = ref[:, 128 * t : 128 * t + 128]
    tile = pltpu.roll(tile, 128 - off, 1) if off else tile
    if off + width > 128:
        after = pltpu.roll(ref[:, 128 * t + 128 : 128 * t + 256], 128 - off, 1)
        tile = jnp.where(lane_at((8, 128)) < 128 - off, tile, after)
    return tile


def start_body(r, net, after):
    c, y, z, x = places()
    pad = jnp.zeros((8, 1), F32)

    def tall(value):
        return jnp.concatenate(
            [value.astype(F32), jnp.broadcast_to(pad, (8, value.shape[1]))], axis=0
        ).astype(BF16)

    r.mine[0, :, :INNER] = tall(r.inner[...])
    r.mine[0, :, INNER:] = tall(r.bc[...])
    r.mine[1, :, :128] = tall(r.step[...])
    r.mine[1, :, 128:GATE0] = jnp.zeros((32, 128), BF16)
    r.mine[1, :, GATE0:] = tall(r.gate[...])
    given = pl.ds(pl.multiple_of((1 - c) * WALF, 128), WALF)
    swaps = [
        net.go(r.mine.at[1 - c], r.half.at[c], sibling()),
        net.go(r.out.at[:, given], r.half_o.at[c], sibling()),
    ]
    small = [net.go(r.blob, r.cells.at[c, y, z, x], x_peer(k)) for k in range(1, 4)]
    r.half[c] = r.mine[c]
    r.half_o[c] = jnp.where(c == 0, r.out[:, :WALF], r.out[:, WALF:])
    r.cells[c, y, z, x] = r.blob[...]
    for copy in swaps:
        copy.wait_recv()
    ga = Gather(net, r.half.at[0], r.half_o.at[0], r.w0, r.wo0, r.stage0, r.rows0, r.own0)
    ga.begin()
    for copy in small:
        copy.wait_recv()
    small = [net.go(r.cells.at[c, y, z], r.cells.at[c, y, z], z_peer(k)) for k in range(1, 4)]
    ga.rows_in()
    after.begin()
    for copy in small:
        copy.wait_recv()
    small = [net.go(r.cells.at[c, y], r.cells.at[c, y], y_peer(k)) for k in range(1, 4)]
    for j in (1, 3, 2):
        ga.spread(j)
    for copy in small:
        copy.wait_recv()
    pair = net.go(r.cells.at[c], r.cells.at[c], sibling())
    ga.relay(0)
    ga.relay(1)
    pair.wait_recv()
    for layer in range(2):
        def first_tile(d):
            return r.cells[layer, d // 16, (d // 4) % 4, d % 4, 0:8]

        def second_tile(d):
            return r.cells[layer, d // 16, (d // 4) % 4, d % 4, 8:16]

        for t, tile in enumerate(place_chunks(first_tile, 48, INNER)):
            r.taps[layer, :, 128 * t : 128 * t + 128] = tile
        for t, tile in enumerate(place_chunks(second_tile, 4, 2 * STATE)):
            r.taps[layer, :, INNER + 128 * t : INNER + 128 * t + 128] = tile
        for t, tile in enumerate(place_chunks(first_tile, 24, D)):
            r.gain[layer, :, 128 * t : 128 * t + 128] = tile
        lane = lane_at((8, 128))
        heads = jnp.zeros((8, 128), F32)
        for j in range(OWNERS):
            moved = pltpu.roll(second_tile(4 * j), 8 * j, 1) if j else second_tile(0)
            heads = jnp.where((lane >= 8 * j) & (lane < 8 * j + 3), moved, heads)
        r.heads[layer] = heads
    after.rows_in()
    ga.relay(3)
    ga.relay(2)
    after.spread(1)
    after.spread(3)
    for j in (0, 1, 3, 2):
        ga.last(j)
    after.spread(2)
    ga.end()


TURNS = (1, 4, 3, 12, 5, 15, 7, 13, 2, 8, 6, 9, 14, 11, 10)


def seq_peer(d):
    _, y, z, _ = places()
    return lax.rem(y + d // 4, 4) * 4 + lax.rem(z + d % 4, 4)


class Exchange:
    def __init__(self, backward, r):
        self.backward, self.r = backward, r
        self.me = lax.axis_index("seq")
        self.section = lax.axis_index("section")

    def first_copy(self, peer, d):
        r = self.r
        return pltpu.make_async_remote_copy(
            src_ref=r.ds.at[peer], dst_ref=r.got.at[self.me], send_sem=r.send_a.at[d], recv_sem=r.recv_a.at[d],
            device_id={"seq": peer}, device_id_type=MESH,
        )

    def send(self, peer):
        _, y, z, _ = places()
        d = lax.rem(peer // 4 + 4 - y, 4) * 4 + lax.rem(lax.rem(peer, 4) + 4 - z, 4)

        @pl.when(d != 0)
        def _():
            self.first_copy(peer, d).start()

        @pl.when(d == 0)
        def _():
            self.r.got[self.me] = self.r.ds[self.me]

    def back_copy(self, d):
        r = self.r
        peer = seq_peer(d)
        return pltpu.make_async_remote_copy(
            src_ref=r.ready.at[peer], dst_ref=r.back.at[self.me], send_sem=r.send_b.at[d], recv_sem=r.recv_b.at[d],
            device_id={"seq": peer}, device_id_type=MESH,
        )

    def scan(self, decays):
        r = self.r

        def rows_of(dec):
            return jnp.concatenate([jnp.broadcast_to(dec[h : h + 1], (64, 128)) for h in range(3)], axis=0)

        for d in TURNS:
            self.first_copy(seq_peer(d), d).wait_recv()
        r.final[...] = jnp.zeros((OWN, STATE), F32)
        r.fade[0] = jnp.ones((8, 128), F32)

        def step(n, carry):
            c = OWNERS - 1 - n if self.backward else n
            state = r.final[...]
            r.kept[c] = state
            dec = decays[c]
            r.final[...] = rows_of(dec) * state + r.got[c].astype(F32)
            r.fade[n + 1] = r.fade[n] * dec
            return carry

        lax.fori_loop(0, OWNERS, step, 0)
        swap = pltpu.make_async_remote_copy(
            src_ref=r.final, dst_ref=r.other, send_sem=r.swap_s.at[0], recv_sem=r.swap_s.at[1],
            device_id=sibling(), device_id_type=MESH,
        )
        swap.start()
        takes = 0 if self.backward else 1
        r.begin[...] = jnp.zeros((OWN, STATE), F32)

        @pl.when(self.section == takes)
        def _():
            swap.wait_recv()
            r.begin[...] = r.other[...]

        begin = r.begin[...]
        for d in TURNS + (0,):
            c = seq_peer(d)
            n = OWNERS - 1 - c if self.backward else c
            value = (r.kept[c] + rows_of(r.fade[n]) * begin).astype(BF16)
            if d == 0:
                r.back[c] = value
            else:
                r.ready[c] = value
                self.back_copy(d).start()

        @pl.when(self.section != takes)
        def _():
            swap.wait_recv()

        swap.wait_send()

    def finish(self):
        for d in TURNS:
            self.back_copy(d).wait_recv()

    def drain(self):
        for d in range(1, OWNERS):
            self.first_copy(seq_peer(d), d).wait_send()
            self.back_copy(d).wait_send()


def exchange_scratch():
    block = pltpu.VMEM((OWNERS, OWN, STATE), BF16)
    part = pltpu.VMEM((OWN, STATE), F32)
    return {
        "ds": block, "got": block, "back": block, "ready": block,
        "kept": pltpu.VMEM((OWNERS, OWN, STATE), F32), "fade": pltpu.VMEM((OWNERS + 1, 8, 128), F32),
        "final": part, "other": part, "begin": part,
        "send_a": dma_sems(OWNERS), "recv_a": dma_sems(OWNERS), "send_b": dma_sems(OWNERS), "recv_b": dma_sems(OWNERS),
        "swap_s": dma_sems(2),
    }


def head_rows_at(ref, i, q):
    parts = []
    for h in (2 * q, 2 * q + 1):
        parts.append(ref[2 * i + h // 3, pl.ds(64 * (h % 3), 64), :])
    return jnp.concatenate(parts, axis=0)


def store_heads(ref, i, q, value):
    for n, h in enumerate((2 * q, 2 * q + 1)):
        ref[2 * i + h // 3, pl.ds(64 * (h % 3), 64), :] = value[64 * n : 64 * n + 64]


def own_group(n):
    return lax.rem(lax.axis_index("seq") // 2 + n, 8)


def greet_layer(rider, forward):
    me = lax.axis_index("seq")
    section = lax.axis_index("section")
    wsh = lax.axis_index("wsh")
    barrier = pltpu.get_barrier_semaphore()
    for d in range(1, OWNERS):
        say_hello({"seq": lax.rem(me + d, OWNERS)})
    say_hello(sibling())
    if rider:
        for k in range(1, 4):
            say_hello(x_peer(k))
    count = OWNERS + (3 if rider else 0)
    late = {"section": 0, "seq": 15, "wsh": wsh}
    if forward:

        @pl.when((section == 1) & ((me == 0) | (me == 4)))
        def _():
            pl.semaphore_signal(barrier, inc=1, device_id=late, device_id_type=MESH)

        more = jnp.where((section == 0) & (me == 15), 2, 0)
    else:

        @pl.when((section == 0) & (me == 15))
        def _():
            for seq in (0, 4):
                pl.semaphore_signal(
                    barrier, inc=1, device_id={"section": 1, "seq": seq, "wsh": wsh}, device_id_type=MESH
                )

        more = jnp.where((section == 1) & ((me == 0) | (me == 4)), 1, 0)
    pl.semaphore_wait(barrier, count + more)


def halo_copy(src, dst, sems, n, section, seq):
    return pltpu.make_async_remote_copy(
        src_ref=src, dst_ref=dst, send_sem=sems.at[n], recv_sem=sems.at[2 + n],
        device_id={"section": section, "seq": seq, "wsh": lax.axis_index("wsh")}, device_id_type=MESH,
    )


class Halo:
    def __init__(self, src, near, far, sems, forward):
        me = lax.axis_index("seq")
        section = lax.axis_index("section")
        edge = 15 if forward else 0
        if forward:
            crossing = (section == 0) & (me == 15)
            jumping = crossing
            self.has_near = (me > 0) | (section == 1)
            self.has_far = (section == 1) & (me == 4)
            target = (1, jnp.where(me == 15, 0, me + 1))
            near_section = jnp.where(crossing, 1, section)
            far_seq, far_section = 4, 1
        else:
            crossing = (section == 1) & (me == 0)
            jumping = (section == 1) & (me == 4)
            self.has_near = (me < 15) | (section == 0)
            self.has_far = (section == 0) & (me == 15)
            target = (0, jnp.where(me == 0, 15, me - 1))
            near_section = jnp.where(crossing, 0, section)
            far_seq, far_section = 15, 0
        self.sends_near = (me != edge) | crossing
        self.sends_far = jumping
        self.near, self.far = near, far
        self.near_copy = halo_copy(src, near, sems, 0, near_section, target[1])
        self.far_copy = halo_copy(src, far, sems, 1, far_section, far_seq)

    def start(self):
        @pl.when(self.sends_near)
        def _():
            self.near_copy.start()

        @pl.when(self.sends_far)
        def _():
            self.far_copy.start()

        @pl.when(jnp.logical_not(self.has_near))
        def _():
            self.near[...] = jnp.zeros_like(self.near)

        @pl.when(jnp.logical_not(self.has_far))
        def _():
            self.far[...] = jnp.zeros_like(self.far)

    def wait(self):
        @pl.when(self.has_near)
        def _():
            self.near_copy.wait_recv()

        @pl.when(self.has_far)
        def _():
            self.far_copy.wait_recv()

    def drain(self):
        @pl.when(self.sends_near)
        def _():
            self.near_copy.wait_send()

        @pl.when(self.sends_far)
        def _():
            self.far_copy.wait_send()


def forward_body(layer, rider, r):
    section = lax.axis_index("section")
    me = lax.axis_index("seq")
    net = Net(r.pair_send, r.pair_recv)
    if rider:
        greet_layer(rider, True)
        bulk = Net(r.net_send, r.net_recv)
        ga = Gather(bulk, r.half.at[1], r.half_o.at[1], r.next_w, r.next_wo, r.stage, r.rows, r.own)
        start_body(r, bulk, ga)
        w, wo = r.w0.reshape(2, D, HALF), r.wo0.reshape(2, INNER, WALF)
    else:
        w, wo = r.w, r.wo
    loads = [fetch(w.at[n], r.w_s.at[n], r.load.at[n]) for n in range(2)]
    load_o = fetch(wo, r.wo_s, r.load.at[2])
    if not rider:
        greet_layer(rider, True)
    ex = Exchange(False, r)
    live = r.flags[0]
    heads = r.heads[layer]
    x32 = r.x[...].astype(F32)
    hidden_inv = lax.rsqrt(jnp.sum(x32 * x32, axis=1, keepdims=True) / D + EPS)
    r.hidden[...] = (x32 * hidden_inv * r.gain[layer, ROW_NORM : ROW_NORM + 1, :]).astype(BF16)
    loads[0].wait()

    def project_main(n, carry):
        cols = pl.ds(pl.multiple_of(n * 256, 256), 256)
        r.pre[:, cols] = dot32(r.hidden[...], r.w_s[0, :, cols]).astype(BF16)
        return carry

    lax.fori_loop(0, HALF // 256, project_main, 0)
    r.tail[...] = r.pre[TOK - 16 :, :]
    halo = Halo(r.tail, r.halo_near, r.halo_far, r.halo_s, True)
    halo.start()
    loads[1].wait()

    def project_side(n, carry):
        cols = pl.ds(pl.multiple_of(n * 256, 256), 256)
        r.side[:, cols] = dot32(r.hidden[...], r.w_s[1, :, cols])
        return carry

    lax.fori_loop(0, HALF // 256, project_side, 0)
    if rider:
        ga.relay(0)
    pairs = [net.go(r.hidden, r.both_hidden.at[section], sibling())]
    owns = [fetch(r.hidden, r.both_hidden.at[section], r.load.at[3])]
    step = r.side[:, :128].astype(BF16).astype(F32) + heads[ROW_BIAS : ROW_BIAS + 1]
    dt = jnp.maximum(step, 0.0) + jnp.log1p(jnp.exp(-jnp.abs(step)))
    dt = jnp.where(head_lanes(), dt, 0.0) * live
    rate = -dt * jnp.exp(heads[ROW_DECAY : ROW_DECAY + 1])
    cum = split_left(tri_of(True).astype(F32).astype(BF16), rate, 3)
    r.dt[...] = dt
    r.cum[...] = cum
    last = jnp.broadcast_to(cum[TOK - 1 : TOK], (TOK, 128))
    r.dec_s[...] = jnp.exp(last).T.reshape(OWNERS, 8, 128)
    r.dec[me] = r.dec_s[me]

    def dec_copy(d):
        peer = lax.rem(me + d, OWNERS)
        return pltpu.make_async_remote_copy(
            src_ref=r.dec_s.at[peer], dst_ref=r.dec.at[me], send_sem=r.dec_send.at[d], recv_sem=r.dec_recv.at[d],
            device_id={"seq": peer}, device_id_type=MESH,
        )

    for d in range(1, OWNERS):
        dec_copy(d).start()
    weight = dt * jnp.exp(last - cum)
    halo.wait()
    r.halo[...] = jnp.where(
        r.flags[1] > 0.0, r.halo_near[...], jnp.where(r.flags[2] > 0.0, r.halo_far[...], jnp.zeros_like(r.halo_far))
    )

    def conv_tile(cols):
        blk = r.pre[:, cols].astype(F32)
        cat = jnp.concatenate([r.halo[:, cols].astype(F32)[8:], blk], axis=0)
        summed = conv_of(cat, r.taps[layer, :, cols])
        sig = 1.0 / (1.0 + jnp.exp(-summed))
        act = summed * sig
        r.act[:, cols] = act
        r.dact[:, cols] = sig * (1.0 + summed * (1.0 - sig))
        return act

    b = conv_tile(pl.ds(INNER, 128)).astype(BF16)
    c = conv_tile(pl.ds(INNER + 128, 128)).astype(BF16)

    def states(n, carry):
        i = own_group(n)
        wt = to_front(weight, i)
        for q in range(3):
            x = conv_tile(group_cols(i, q))
            scaled = (x * pair_cols(wt, q)[2]).astype(BF16)
            store_heads(r.ds, i, q, dot32(scaled, b, ((0,), (0,))).astype(BF16))
        ex.send(2 * i)
        ex.send(2 * i + 1)
        return carry

    lax.fori_loop(0, 8, states, 0)
    if rider:
        ga.relay(1)
    for d in range(1, OWNERS):
        dec_copy(d).wait_recv()
    ex.scan(r.dec)
    if rider:
        ga.relay(3)
    r.cumt[...] = cum.T
    causal = tri_of(True)
    scores = dot32(c, b, ((1,), (1,)))
    lane = lax.broadcasted_iota(jnp.int32, (TOK, 128), 1)
    r.square[...] = jnp.zeros((TOK, 128), F32)

    def inside(i, carry):
        cum_i = to_front(cum, i)
        dt_i = to_front(dt, i)
        rows = r.cumt[pl.ds(pl.multiple_of(16 * i, 16), 16), :]
        for q in range(3):
            cols = group_cols(i, q)
            cum_a, cum_b, _ = pair_cols(cum_i, q)
            u = r.act[:, cols] * pair_cols(dt_i, q)[2]
            mixes = []
            for cum_h, off in ((cum_a, LANES[2 * q]), (cum_b, LANES[2 * q + 1])):
                gap = cum_h - rows[off : off + 1]
                mixes.append((scores * jnp.exp(jnp.where(causal, gap, -1e30))).astype(BF16))
            terms = jnp.concatenate(
                [jnp.where(lane < 64, u, 0.0).astype(BF16), jnp.where(lane < 64, 0.0, u).astype(BF16)], axis=0
            )
            r.raw[:, cols] = dot32(jnp.concatenate(mixes, axis=1), terms)
        return carry

    lax.fori_loop(0, 8, inside, 0)
    if rider:
        ga.relay(2)
    ex.finish()
    save = fetch(r.back, r.states, r.load.at[4])

    def across(i, carry):
        cum_i = to_front(cum, i)
        skip_i = pltpu.roll(heads, lax.rem(128 - 16 * i, 128), 1)[ROW_SKIP : ROW_SKIP + 1]
        for q in range(3):
            cols = group_cols(i, q)
            state = head_rows_at(r.back, i, q)
            raw = r.raw[:, cols] + jnp.exp(pair_cols(cum_i, q)[2]) * dot32(c, state, ((1,), (1,)))
            r.raw[:, cols] = raw
            y = (raw + pair_row(skip_i, q) * r.act[:, cols]).astype(BF16)
            r.y[:, cols] = y
            gate = r.side[:, gate_cols(i, q)]
            z = y.astype(F32) * (gate / (1.0 + jnp.exp(-gate)))
            r.z[:, cols] = z
            r.square[...] += z * z
        return carry

    lax.fori_loop(0, 8, across, 0)
    if rider:
        ga.last(0)
        ga.last(1)
    total = jnp.sum(r.square[...], axis=1, keepdims=True)
    inv = jnp.broadcast_to(lax.rsqrt(total / INNER + EPS), (TOK, 128))
    r.inv[...] = inv

    def scale(i, carry):
        cols = pl.ds(pl.multiple_of(i * 128, 128), 128)
        mid = r.taps[layer, ROW_MID : ROW_MID + 1, cols]
        r.gated[:, cols] = (r.z[:, cols] * inv * mid).astype(BF16)
        return carry

    lax.fori_loop(0, 24, scale, 0)
    pairs.append(net.go(r.gated, r.both_gated.at[section], sibling()))
    owns.append(fetch(r.gated, r.both_gated.at[section], r.load.at[5]))
    load_o.wait()
    for half in range(2):

        def project(n, carry):
            cols = pl.ds(pl.multiple_of(n * 256, 256), 256)
            full = pl.ds(pl.multiple_of(half * WALF + n * 256, 256), 256)
            branch = dot32(r.gated[...], r.wo_s[half, :, cols])
            r.result[:, full] = (r.x[:, full].astype(F32) + live * branch).astype(BF16)
            return carry

        lax.fori_loop(0, WALF // 256, project, 0)
    if rider:
        for j in (3, 2):
            ga.last(j)
        ga.end()
        bulk.drain()
    save.wait()
    for copy in owns:
        copy.wait()
    for copy in pairs:
        copy.wait_recv()
    net.drain()
    halo.drain()
    for d in range(1, OWNERS):
        dec_copy(d).wait_send()
    ex.drain()


def block_forward(layer, flags, x, given):
    rider = layer == 0
    inputs = {"flags": ("s", flags), "x": ("v", x)}
    if rider:
        for key in ("inner", "bc", "step", "gate", "out", "blob"):
            inputs[key] = ("v", given[key])
    else:
        w, wo, small = given
        inputs.update({
            "w": ("h", w), "wo": ("h", wo), "taps": ("v", small.taps), "gain": ("v", small.gain),
            "heads": ("v", small.heads),
        })
    outputs = {
        "act": in_vmem(TOK, CONV), "dact": in_vmem(TOK, CONV), "side": in_vmem(TOK, HALF), "raw": in_vmem(TOK, INNER),
        "dt": in_vmem(TOK, 128), "cum": in_vmem(TOK, 128), "inv": in_vmem(TOK, 128),
        "dec": in_vmem(OWNERS, 8, 128), "pre": in_vmem(TOK, CONV, dtype=BF16), "halo": in_vmem(16, CONV, dtype=BF16),
        "y": in_vmem(TOK, INNER, dtype=BF16), "result": in_vmem(TOK, D, dtype=BF16),
        "states": in_hbm(OWNERS, OWN, STATE), "both_hidden": in_hbm(2, TOK, D), "both_gated": in_hbm(2, TOK, INNER),
    }
    tile = pltpu.VMEM((TOK, 128), F32)
    edge = pltpu.VMEM((16, CONV), BF16)
    scratch = {
        "w_s": pltpu.VMEM((2, D, HALF), BF16), "wo_s": pltpu.VMEM((2, INNER, WALF), BF16),
        "hidden": pltpu.VMEM((TOK, D), BF16), "gated": pltpu.VMEM((TOK, INNER), BF16),
        "z": pltpu.VMEM((TOK, INNER), F32), "cumt": tile, "square": tile,
        "tail": edge, "halo_near": edge, "halo_far": edge, "halo_s": dma_sems(4),
        "dec_s": pltpu.VMEM((OWNERS, 8, 128), F32), "dec_send": dma_sems(OWNERS), "dec_recv": dma_sems(OWNERS),
        "load": dma_sems(6), "pair_send": dma_sems(2), "pair_recv": dma_sems(2),
        **exchange_scratch(),
    }
    if rider:
        outputs.update({
            "w0": in_hbm(2, 4, 4, 96, HALF), "wo0": in_hbm(2, 4, 4, 4, 48, WALF),
            "next_w": in_hbm(2, 4, 4, 96, HALF), "next_wo": in_hbm(2, 4, 4, 4, 48, WALF),
            "taps": in_vmem(2, 8, CONV), "gain": in_vmem(2, 8, D), "heads": in_vmem(2, 8, 128),
        })
        scratch.update({
            "mine": pltpu.VMEM((2, 32, HALF), BF16), "half": pltpu.VMEM((2, 32, HALF), BF16),
            "half_o": pltpu.VMEM((2, 48, WALF), BF16), "cells": pltpu.VMEM((2, 4, 4, 4, 16, 128), F32),
            "net_send": dma_sems(400), "net_recv": dma_sems(400),
        })
        scratch.update({key + "0": value for key, value in gather_scratch().items()})
        scratch.update(gather_scratch())
    return call(
        functools.partial(forward_body, layer, rider), "block_forward", 2 + layer, inputs, outputs, scratch
    )


def add_rows(target, *parts):
    lead = target.shape[:-2]
    blocks = functools.reduce(lambda a, b: a * b, lead, 1)

    def body(b, carry):
        spot = (b,) if len(lead) == 1 else (b // lead[1], lax.rem(b, lead[1]))
        total = parts[0][spot].astype(F32)
        for ref in parts[1:]:
            total = total + ref[spot].astype(F32)
        target[spot] = total.astype(target.dtype)
        return carry

    lax.fori_loop(0, blocks, body, 0)


def fold_scratch(tag, cols, with_out):
    shapes = {"a": (4, 96, cols // 2), "b": (4, 96, cols // 2)}
    if with_out:
        shapes["o"] = (4, 4, 48, WALF)
    scratch = {}
    for key, shape in shapes.items():
        scratch[tag + "m" + key] = pltpu.VMEM(shape, BF16)
        scratch[tag + "s" + key] = pltpu.VMEM((2,) + shape, BF16)
    scratch[tag + "own"] = dma_sems(9)
    return scratch


def fold_targets(tag, cols, with_out, make):
    targets = {tag + "ha": make(4, 96, cols // 2), tag + "hb": make(4, 96, cols // 2)}
    if with_out:
        targets[tag + "ho"] = make(4, 4, 48, WALF)
    return targets


class Fold:
    def __init__(self, net, r, tag, cols, gi, go):
        self.net, self.gi, self.go_ref, self.cut = net, gi, go, cols // 2
        self.kinds = (0, 1, 2) if go is not None else (0, 1)
        keys = "abo"
        self.h = [getattr(r, tag + "h" + keys[n]) for n in self.kinds]
        self.m = [getattr(r, tag + "m" + keys[n]) for n in self.kinds]
        self.s = [getattr(r, tag + "s" + keys[n]) for n in self.kinds]
        self.own = getattr(r, tag + "own")
        self.place = places()
        self.peers = (y_peer, z_peer, x_peer)
        self.hops, self.direct, self.loads = {}, {}, {}

    def part(self, kind, t, half):
        _, y, z, x = self.place
        at = pl.ds(2 * half, 2) if half is not None else slice(None)
        if kind == 0:
            return self.gi.at[lax.rem(y + t, 4), at, :, pl.ds(0, self.cut)]
        if kind == 1:
            return self.gi.at[at, lax.rem(z + t, 4), :, pl.ds(self.cut, self.cut)]
        return self.go_ref.at[at, :, lax.rem(x + t, 4)]

    def begin(self, kinds):
        go = self.net.go
        for half, k in ((0, 1), (1, 3)):
            for kind in kinds:
                self.hops[kind, half] = go(
                    self.part(kind, 2, half), self.h[kind].at[pl.ds(2 * half, 2)], self.peers[kind](k)
                )
        for half, k in ((1, 1), (0, 3)):
            for kind in kinds:
                side = 0 if k == 1 else 1
                self.direct[kind, side] = go(
                    self.part(kind, k, half), self.s[kind].at[side, pl.ds(2 * half, 2)], self.peers[kind](k)
                )
        for kind in kinds:
            self.loads[kind] = [
                fetch(self.part(kind, 1, 0), self.m[kind].at[pl.ds(0, 2)], self.own.at[3 * kind]),
                fetch(self.part(kind, 3, 1), self.m[kind].at[pl.ds(2, 2)], self.own.at[3 * kind + 1]),
            ]

    def combine(self, kind):
        for copy in self.loads[kind]:
            copy.wait()
        for half in range(2):
            self.hops[kind, half].wait_recv()
        add_rows(self.m[kind], self.m[kind], self.h[kind])
        peer = self.peers[kind]
        for half, k in ((0, 1), (1, 3)):
            at = pl.ds(2 * half, 2)
            self.hops[kind, half] = self.net.go(self.m[kind].at[at], self.s[kind].at[half, at], peer(k))
        self.loads[kind] = [fetch(self.part(kind, 0, None), self.h[kind], self.own.at[3 * kind + 2])]

    def settle(self, kind):
        for copy in self.loads[kind]:
            copy.wait()
        for side in range(2):
            self.direct[kind, side].wait_recv()
            self.hops[kind, side].wait_recv()
        add_rows(self.h[kind], self.h[kind], self.s[kind].at[0], self.s[kind].at[1])


class Finish:
    def __init__(self, net, r, tag, cols, sums):
        self.net, self.sums, self.cut, self.cols = net, sums, cols // 2, cols
        for key in ("r2a", "r2b", "c3", "r3") + (("r2o", "o2", "r3o") if len(sums) > 2 else ()):
            setattr(self, key, getattr(r, tag + key))
        self.place = places()

    def second(self):
        _, y, z, _ = self.place
        go = self.net.go
        ha, hb = self.sums[:2]
        self.a, self.b, self.o = [], [], []
        for k in range(1, 4):
            self.a.append(go(ha.at[lax.rem(z + k, 4)], self.r2a.at[k], z_peer(k)))
            self.b.append(go(hb.at[lax.rem(y + k, 4)], self.r2b.at[k], y_peer(k)))
        self.r2a[0] = ha[z]
        self.r2b[0] = hb[y]
        if len(self.sums) > 2:
            ho = self.sums[2]
            one, two = pl.ds(0, WCUT), pl.ds(WCUT, WCUT)
            for k in range(1, 4):
                self.o.append(go(ho.at[lax.rem(y + k, 4), :, :, one], self.r2o.at[0, k], y_peer(k)))
                self.o.append(go(ho.at[:, lax.rem(z + k, 4), :, two], self.r2o.at[1, k], z_peer(k)))
            self.r2o[0, 0] = ho[y, :, :, :WCUT]
            for n in range(4):
                self.r2o[1, 0, n] = ho[n, z, :, WCUT:]

    def third(self):
        _, y, z, x = self.place
        go = self.net.go
        for copy in self.a + self.b:
            copy.wait_recv()
        for n in range(4):
            at = pl.ds(24 * n, 24)
            for parts, cols in ((self.r2a, pl.ds(0, self.cut)), (self.r2b, pl.ds(self.cut, self.cut))):
                total = parts[0, at, :].astype(F32)
                for k in range(1, 4):
                    total = total + parts[k, at, :].astype(F32)
                self.c3[n, :, cols] = total
        self.x = [go(self.c3.at[lax.rem(x + k, 4)], self.r3.at[x], x_peer(k)) for k in range(1, 4)]
        self.r3[x] = self.c3[x]
        if self.o:
            for copy in self.o:
                copy.wait_recv()
            for n in range(2):
                add_rows(self.o2.at[n], *[self.r2o.at[n, k] for k in range(4)])
            for k in range(1, 4):
                self.x.append(go(self.o2.at[0, lax.rem(z + k, 4)], self.r3o.at[0, k], z_peer(k)))
                self.x.append(go(self.o2.at[1, lax.rem(y + k, 4)], self.r3o.at[1, k], y_peer(k)))
            self.r3o[0, 0] = self.o2[0, z]
            self.r3o[1, 0] = self.o2[1, y]

    def last(self, in_ref, out_ref=None):
        for copy in self.x:
            copy.wait_recv()
        in_ref[...] = self.r3[0] + self.r3[1] + self.r3[2] + self.r3[3]
        if self.o:
            for n in range(2):
                total = self.r3o[n, 0].astype(F32)
                for k in range(1, 4):
                    total = total + self.r3o[n, k].astype(F32)
                out_ref[:, WCUT * n : WCUT * n + WCUT] = total


def finish_scratch(tag, cols, with_out):
    cut = cols // 2
    scratch = {
        tag + "r2a": pltpu.VMEM((4, 96, cut), BF16), tag + "r2b": pltpu.VMEM((4, 96, cut), BF16),
        tag + "c3": pltpu.VMEM((4, 24, cols), F32), tag + "r3": pltpu.VMEM((4, 24, cols), F32),
    }
    if with_out:
        scratch[tag + "r2o"] = pltpu.VMEM((2, 4, 4, 48, WCUT), BF16)
        scratch[tag + "o2"] = pltpu.VMEM((2, 4, 48, WCUT), BF16)
        scratch[tag + "r3o"] = pltpu.VMEM((2, 4, 48, WCUT), BF16)
    return scratch


def net_scratch(count):
    return {"net_send": dma_sems(count), "net_recv": dma_sems(count)}


def early_products(r, which):
    left, right, stage, target = (
        (r.gated2, r.gb2, r.stage_o, r.go) if which == 0 else (r.hid2, r.dg2, r.stage_e, r.ge)
    )
    tile = stage.shape[1]

    def body(i, carry):
        slot = lax.rem(i, 2)
        rows = pl.ds(pl.multiple_of(i * tile, tile), tile)
        copy = pltpu.make_async_copy(stage.at[slot], target.at[rows], r.stage_s.at[2 * which + slot])

        @pl.when(i >= 2)
        def _():
            copy.wait()

        stage[slot] = dot32(left[:, rows], right[...], ((0,), (0,))).astype(BF16)
        copy.start()
        return carry

    lax.fori_loop(0, target.shape[0] // tile, body, 0)
    for slot in range(2):
        pltpu.make_async_copy(stage.at[slot], target.at[pl.ds(0, tile)], r.stage_s.at[2 * which + slot]).wait()


def backward_body(layer, rider, r):
    section = lax.axis_index("section")
    slots_o, slots_w = r.wo_s.shape[0], r.w_s.shape[0]
    load_state = fetch(r.states, r.state_s, r.load.at[0])
    load_two = [fetch(r.both_hidden, r.hid2, r.load.at[3]), fetch(r.both_gated, r.gated2, r.load.at[4])]

    def wo_tile(i):
        rows = pl.ds(pl.multiple_of(i * 384, 384), 384)
        slot = lax.rem(i, slots_o)
        return pltpu.make_async_copy(r.wo.at[:, rows], r.wo_s.at[slot], r.wo_load.at[slot])

    def w_tile(n):
        slot = lax.rem(n, slots_w)
        rows = pl.ds(pl.multiple_of((n // 2) * 256, 256), 256)
        return pltpu.make_async_copy(r.w.at[lax.rem(n, 2), rows], r.w_s.at[slot], r.w_load.at[slot])

    for n in range(slots_o):
        wo_tile(n).start()
    for n in range(slots_w):
        w_tile(n).start()
    greet_layer(True, False)
    net = Net(r.pair_send, r.pair_recv)
    bulk = Net(r.net_send, r.net_recv)
    if rider:
        late = Fold(bulk, r, "l", LCOLS, r.gl, None)
        late.begin((0, 1))
        early_end = Finish(bulk, r, "e", ECOLS, (r.e1a, r.e1b, r.e1o))
        early_end.second()
        late_end = Finish(bulk, r, "l", LCOLS, late.h)
    early = Fold(
        bulk, r, "e", ECOLS, r.ge.reshape(4, 4, 96, ECOLS), r.go.reshape(4, 4, 4, 48, WALF)
    )
    ex = Exchange(True, r)
    live = r.flags[0]
    heads = r.heads[layer]
    r.gb[...] = (r.g[...].astype(F32) * live).astype(BF16)
    inv = r.inv[...]
    b = r.act[:, INNER : INNER + 128].astype(BF16)
    c = r.act[:, INNER + 128 : CONV].astype(BF16)
    dt = r.dt[...]
    cum = r.cum[...]
    r.dots[...] = jnp.zeros((TOK, 128), F32)
    other_half = pl.ds(pl.multiple_of((1 - section) * WALF, 128), WALF)
    own_rows = pl.ds(pl.multiple_of(section * TOK, 128), TOK)
    pairs = [net.go(r.gb.at[:, other_half], r.gb2.at[own_rows], sibling())]
    r.gb2[own_rows, :] = jnp.where(section == 0, r.gb[:, :WALF], r.gb[:, WALF:])
    load_two[1].wait()
    pairs[0].wait_recv()
    early_products(r, 0)
    early.begin((2,))

    def first(i, carry):
        slot = lax.rem(i, slots_o)
        wo_tile(i).wait()
        gg = dot32(r.gb[:, :WALF], r.wo_s[slot, 0], ((1,), (1,)))
        gg = gg + dot32(r.gb[:, WALF:], r.wo_s[slot, 1], ((1,), (1,)))

        @pl.when(i + slots_o < 8)
        def _():
            wo_tile(i + slots_o).start()

        r.gg[:, pl.ds(pl.multiple_of(i * 384, 384), 384)] = gg
        for q in range(3):
            cols = group_cols(i, q)
            gate = r.side[:, gate_cols(i, q)]
            z = r.y[:, cols].astype(F32) * (gate / (1.0 + jnp.exp(-gate)))
            mid = r.taps[layer, ROW_MID : ROW_MID + 1, cols]
            r.dots[...] += gg[:, 128 * q : 128 * q + 128] * mid * z
        return carry

    lax.fori_loop(0, 8, first, 0)
    total = jnp.broadcast_to(jnp.sum(r.dots[...], axis=1, keepdims=True), (TOK, 128))
    shift = total * inv * inv * inv / INNER
    r.gtaps[...] = jnp.zeros_like(r.gtaps)

    def second(n, carry):
        i = own_group(n)
        cum_i = to_front(cum, i)
        for q in range(3):
            cols = group_cols(i, q)
            gate = r.side[:, gate_cols(i, q)]
            y = r.y[:, cols].astype(F32)
            gg = r.gg[:, cols]
            sig = 1.0 / (1.0 + jnp.exp(-gate))
            act = gate * sig
            z = y * act
            dz = gg * r.taps[layer, ROW_MID : ROW_MID + 1, cols] * inv - z * shift
            dy = (dz * act).astype(BF16)
            r.dy[:, cols] = dy
            r.gside[:, gate_cols(i, q)] = (dz * y * (sig * (1.0 + gate * (1.0 - sig)))).astype(BF16)
            r.gtaps[ROW_MID : ROW_MID + 1, cols] = jnp.sum(gg * z * inv, axis=0, keepdims=True)
            far = (dy.astype(F32) * jnp.exp(pair_cols(cum_i, q)[2])).astype(BF16)
            store_heads(r.ds, i, q, dot32(far, c, ((0,), (0,))).astype(BF16))
        ex.send(2 * i)
        ex.send(2 * i + 1)
        return carry

    lax.fori_loop(0, 8, second, 0)
    other_cols = pl.ds(pl.multiple_of(GATE0 + (1 - section) * ECOLS, 128), ECOLS)
    pairs.append(net.go(r.gside.at[:, other_cols], r.dg2.at[own_rows], sibling()))
    r.dg2[own_rows, :] = jnp.where(
        section == 0, r.gside[:, GATE0 : GATE0 + ECOLS], r.gside[:, GATE0 + ECOLS :]
    )
    if rider:
        late.combine(0)
        late.combine(1)
    load_two[0].wait()
    pairs[1].wait_recv()
    early_products(r, 1)
    ex.scan(r.dec)
    early.begin((0, 1))
    load_state.wait()
    r.cumt[...] = cum.T
    causal = tri_of(True)
    scores = dot32(c, b, ((1,), (1,)))
    lane = lax.broadcasted_iota(jnp.int32, (TOK, 128), 1)
    pick_row = lax.broadcasted_iota(jnp.int32, (128, 128), 0)
    pick_col = lax.broadcasted_iota(jnp.int32, (128, 128), 1)
    picks = []
    for q in range(3):
        target = jnp.where(pick_row < 64, LANES[2 * q], LANES[2 * q + 1])
        picks.append((pick_col == target).astype(F32).astype(BF16))
    for ref in (r.dscore, r.grad_b, r.grad_c, r.xdu, r.dyy, r.thin):
        ref[...] = jnp.zeros_like(ref)

    def inside(i, carry):
        cum_i = to_front(cum, i)
        dt_i = to_front(dt, i)
        rows = r.cumt[pl.ds(pl.multiple_of(16 * i, 16), 16), :]
        for q in range(3):
            cols = group_cols(i, q)
            cum_a, cum_b, cum_x = pair_cols(cum_i, q)
            u16 = (r.act[:, cols] * pair_cols(dt_i, q)[2]).astype(BF16)
            dy16 = r.dy[:, cols]
            nil = jnp.zeros_like(dy16)
            dys = jnp.concatenate([jnp.where(lane < 64, dy16, nil), jnp.where(lane < 64, nil, dy16)], axis=0)
            both = dot32(dys, u16, ((1,), (1,)))
            mixes = []
            for n, (cum_h, off) in enumerate(((cum_a, LANES[2 * q]), (cum_b, LANES[2 * q + 1]))):
                gap = cum_h - rows[off : off + 1]
                decay = jnp.exp(jnp.where(causal, gap, -1e30))
                mixes.append((scores * decay).astype(BF16))
                r.dscore[...] += both[n * TOK : n * TOK + TOK] * decay
            r.gg[:, cols] = dot32(jnp.concatenate(mixes, axis=0), dys, ((0,), (0,)))
            far = (dy16.astype(F32) * jnp.exp(cum_x)).astype(BF16)
            r.grad_c[...] += dot32(far, head_rows_at(r.state_s, i, q))
        return carry

    lax.fori_loop(0, 8, inside, 0)
    if rider:
        late.settle(0)
        late.settle(1)
        late_end.second()

    def conv_back(cols, gact):
        gsum = gact * r.dact[:, cols]
        r.gsum[:, cols] = gsum
        blk = r.pre[:, cols].astype(F32)
        cat = jnp.concatenate([r.halo[:, cols].astype(F32)[8:], blk], axis=0)
        sums = [jnp.sum(gsum * cat[5 + k : 5 + k + TOK], axis=0, keepdims=True) for k in range(4)]
        sums.append(jnp.sum(gsum, axis=0, keepdims=True))
        r.gtaps[0:5, cols] = jnp.concatenate(sums, axis=0)

    ex.finish()

    def across(i, carry):
        cum_i = to_front(cum, i)
        dt_i = to_front(dt, i)
        skip_i = pltpu.roll(heads, lax.rem(128 - 16 * i, 128), 1)[ROW_SKIP : ROW_SKIP + 1]
        x_du = jnp.zeros((TOK, 128), F32)
        dy_y = jnp.zeros((TOK, 128), F32)
        thin = jnp.zeros((16, 128), F32)
        edges = {}
        for q in range(3):
            cols = group_cols(i, q)
            x = r.act[:, cols]
            cum_x = pair_cols(cum_i, q)[2]
            dt_x = pair_cols(dt_i, q)[2]
            fade = jnp.exp(cum_x[TOK - 1 : TOK] - cum_x)
            u = x * dt_x
            dy = r.dy[:, cols].astype(F32)
            state16 = head_rows_at(r.state_s, i, q)
            dstate16 = head_rows_at(r.back, i, q)
            du_far = fade * dot32(b, dstate16, ((1,), (1,)))
            du = r.gg[:, cols] + du_far
            r.grad_b[...] += dot32((u * fade).astype(BF16), dstate16)
            overlap = state16.astype(F32) * dstate16.astype(F32)
            edges[LANES[2 * q]] = jnp.sum(overlap[:64], axis=0, keepdims=True)
            edges[LANES[2 * q + 1]] = jnp.sum(overlap[64:], axis=0, keepdims=True)
            x_du = x_du + split_right(x * du, picks[q], 2)
            dy_y = dy_y + split_right(dy * r.raw[:, cols], picks[q], 2)
            thin = thin + split_right(
                jnp.concatenate(
                    [
                        jnp.broadcast_to(jnp.sum(u * du_far, axis=0, keepdims=True), (8, 128)),
                        jnp.broadcast_to(jnp.sum(dy * x, axis=0, keepdims=True), (8, 128)),
                    ],
                    axis=0,
                ),
                picks[q],
                3,
            )
            conv_back(cols, du * dt_x + pair_row(skip_i, q) * dy)
        nothing = jnp.zeros((1, 128), F32)
        r.edge[pl.ds(pl.multiple_of(16 * i, 16), 16), :] = jnp.concatenate(
            [edges.get(k, nothing) for k in range(16)], axis=0
        )
        r.xdu[...] += pltpu.roll(x_du, 16 * i, 1)
        r.dyy[...] += pltpu.roll(dy_y, 16 * i, 1)
        r.thin[...] += pltpu.roll(thin, 16 * i, 1)
        return carry

    lax.fori_loop(0, 8, across, 0)
    early.combine(2)
    early.combine(0)
    early.combine(1)
    dscore16 = r.dscore[...].astype(BF16)
    conv_back(pl.ds(INNER, 128), r.grad_b[...] + dot32(dscore16, c, ((0,), (0,))))
    conv_back(pl.ds(INNER + 128, 128), r.grad_c[...] + dot32(dscore16, b))
    r.tail[...] = r.gsum[:8, :]
    halo = Halo(r.tail, r.halo_near, r.halo_far, r.halo_s, False)
    halo.start()
    ones = jnp.ones((128, 128), BF16)
    edge = split_right(r.edge[...], ones, 3).T[0:1] * jnp.exp(cum[TOK - 1 : TOK]) + r.thin[0:1]
    x_du = r.xdu[...]
    drate = split_left(tri_of(False).astype(F32).astype(BF16), r.dyy[...] - dt * x_du, 3) + edge
    speed = jnp.exp(heads[ROW_DECAY : ROW_DECAY + 1])
    ddt = x_du - drate * speed
    step = r.side[:, :128].astype(BF16).astype(F32) + heads[ROW_BIAS : ROW_BIAS + 1]
    dstep = jnp.where(head_lanes(), ddt / (1.0 + jnp.exp(-step)), 0.0) * live
    r.gside[:, :128] = dstep.astype(BF16)
    r.gside[:, 128:GATE0] = jnp.zeros((TOK, 128), BF16)
    r.ghead[...] = jnp.concatenate(
        [
            jnp.zeros((5, 128), F32),
            jnp.sum(dstep, axis=0, keepdims=True),
            jnp.sum(-drate * dt * speed, axis=0, keepdims=True),
            r.thin[8:9],
        ],
        axis=0,
    )
    halo.wait()
    after = jnp.where(r.flags[3] > 0.0, r.halo_far[...], r.halo_near[...])
    r.halo_near[...] = jnp.where(live > 0.0, after, jnp.zeros_like(after))

    def conv_tile(i, carry):
        cols = pl.ds(pl.multiple_of(i * 128, 128), 128)
        cat = jnp.concatenate([r.gsum[:, cols], r.halo_near[:, cols]], axis=0)
        taps = r.taps[layer, :, cols]
        total = taps[3:4] * cat[:TOK]
        for k in range(3):
            total = total + taps[k : k + 1] * cat[3 - k : 3 - k + TOK]
        r.gpre[:, cols] = total.astype(BF16)
        return carry

    lax.fori_loop(0, CONV // 128, conv_tile, 0)
    if rider:
        early_end.third()
        late_end.third()

    tail_cols = HALF - LCOLS
    side_cols = pl.ds(0, GATE0)
    moves = (
        net_copy(net, r.gpre.at[:, pl.ds(LCOLS, tail_cols)], r.both_gl.at[0, :, pl.ds(0, tail_cols)], 2),
        net_copy(net, r.gside.at[:, side_cols], r.both_gl.at[0, :, pl.ds(tail_cols, GATE0)], 3),
        net_copy(net, r.gpre.at[:, pl.ds(0, LCOLS)], r.both_gl.at[1], 2),
    )
    keeps = (
        pltpu.make_async_copy(r.gpre.at[:, pl.ds(LCOLS, tail_cols)], r.both_gl.at[1, :, pl.ds(0, tail_cols)], r.load.at[1]),
        pltpu.make_async_copy(r.gside.at[:, side_cols], r.both_gl.at[1, :, pl.ds(tail_cols, GATE0)], r.load.at[2]),
        pltpu.make_async_copy(r.gpre.at[:, pl.ds(0, LCOLS)], r.both_gl.at[0], r.load.at[1]),
    )

    @pl.when(section == 0)
    def _():
        moves[0].start()
        moves[1].start()
        keeps[2].start()

    @pl.when(section == 1)
    def _():
        moves[2].start()
        keeps[0].start()
        keeps[1].start()

    def project(n, carry):
        rows = pl.ds(pl.multiple_of(n * 256, 256), 256)
        w_tile(2 * n).wait()
        value = dot32(r.gpre[...], r.w_s[lax.rem(2 * n, slots_w)], ((1,), (1,)))

        @pl.when(2 * n + slots_w < 12)
        def _():
            w_tile(2 * n + slots_w).start()

        w_tile(2 * n + 1).wait()
        value = value + dot32(r.gside[...], r.w_s[lax.rem(2 * n + 1, slots_w)], ((1,), (1,)))

        @pl.when(2 * n + 1 + slots_w < 12)
        def _():
            w_tile(2 * n + 1 + slots_w).start()

        r.gg[:, rows] = value
        return carry

    lax.fori_loop(0, D // 256, project, 0)
    x = r.x[...].astype(F32)
    grad = r.gg[:, :D]
    inv_x = lax.rsqrt(jnp.sum(x * x, axis=1, keepdims=True) / D + EPS)
    scaled = grad * r.gain[layer, ROW_NORM : ROW_NORM + 1, :]
    dots = jnp.sum(scaled * x, axis=1, keepdims=True)
    dx = scaled * inv_x - x * (dots * inv_x * inv_x * inv_x / D)
    r.result[...] = (r.g[...].astype(F32) + dx).astype(BF16)
    r.ggain[...] = jnp.broadcast_to(jnp.sum(grad * x * inv_x, axis=0, keepdims=True), (8, D))
    for kind in range(3):
        early.settle(kind)
    if rider:
        early_end.last(r.fin_e, r.fin_o)
        late_end.last(r.fin_l)
    bulk.drain()

    @pl.when(section == 0)
    def _():
        moves[0].wait_send()
        moves[1].wait_send()
        keeps[2].wait()
        moves[2].wait_recv()

    @pl.when(section == 1)
    def _():
        moves[2].wait_send()
        keeps[0].wait()
        keeps[1].wait()
        moves[0].wait_recv()
        moves[1].wait_recv()

    net.drain()
    halo.drain()
    ex.drain()


def net_copy(net, src, dst, n):
    return pltpu.make_async_remote_copy(
        src_ref=src, dst_ref=dst, send_sem=net.send.at[n], recv_sem=net.recv.at[n],
        device_id=sibling(), device_id_type=MESH,
    )


def block_backward(layer, flags, g, x, w, wo, small, kept, grads):
    rider = grads is not None
    inputs = {
        "flags": ("s", flags), "g": ("v", g), "x": ("v", x), "w": ("h", w), "wo": ("h", wo), "taps": ("v", small.taps),
        "gain": ("v", small.gain), "heads": ("v", small.heads), "states": ("h", kept.states),
        "both_hidden": ("h", kept.both_hidden.reshape(2 * TOK, D)),
        "both_gated": ("h", kept.both_gated.reshape(2 * TOK, INNER)),
    }
    for key in ("act", "dact", "side", "raw", "dt", "cum", "inv", "dec", "pre", "halo", "y"):
        inputs[key] = ("v", getattr(kept, key))
    outputs = {
        "result": in_vmem(TOK, D, dtype=BF16), "both_gl": in_hbm(2, TOK, LCOLS),
        "gtaps": in_vmem(8, CONV), "ggain": in_vmem(8, D), "ghead": in_vmem(8, 128),
        "ge": in_hbm(D, ECOLS), "go": in_hbm(INNER, WALF),
        **fold_targets("e", ECOLS, True, lambda *shape: in_vmem(*shape, dtype=BF16)),
    }
    tile = pltpu.VMEM((TOK, 128), F32)
    edge = pltpu.VMEM((8, CONV), F32)
    slots, tile_rows = (2, 128) if rider else (4, 512)
    scratch = {
        "wo_s": pltpu.VMEM((slots, 2, 384, WALF), BF16), "w_s": pltpu.VMEM((slots, 256, HALF), BF16),
        "wo_load": dma_sems(slots), "w_load": dma_sems(slots), "load": dma_sems(5),
        "hid2": pltpu.VMEM((2 * TOK, D), BF16), "gated2": pltpu.VMEM((2 * TOK, INNER), BF16),
        "gb2": pltpu.VMEM((2 * TOK, WALF), BF16), "dg2": pltpu.VMEM((2 * TOK, ECOLS), BF16),
        "stage_o": pltpu.VMEM((2, tile_rows, WALF), BF16), "stage_e": pltpu.VMEM((2, tile_rows, ECOLS), BF16), "stage_s": dma_sems(4),
        "state_s": pltpu.VMEM((OWNERS, OWN, STATE), BF16),
        "gb": pltpu.VMEM((TOK, D), BF16), "gg": pltpu.VMEM((TOK, INNER), F32), "dy": pltpu.VMEM((TOK, INNER), BF16),
        "gsum": pltpu.VMEM((TOK, CONV), F32), "gpre": pltpu.VMEM((TOK, HALF), BF16), "gside": pltpu.VMEM((TOK, HALF), BF16),
        "dots": tile, "cumt": tile, "edge": tile, "dscore": tile, "grad_b": tile, "grad_c": tile, "xdu": tile, "dyy": tile,
        "thin": pltpu.VMEM((16, 128), F32),
        "tail": edge, "halo_near": edge, "halo_far": edge, "halo_s": dma_sems(4),
        "pair_send": dma_sems(4), "pair_recv": dma_sems(4),
        **exchange_scratch(), **fold_scratch("e", ECOLS, True), **net_scratch(64),
    }
    if rider:
        inputs.update({"gl": ("h", grads[0]), "e1a": ("v", grads[1]), "e1b": ("v", grads[2]), "e1o": ("v", grads[3])})
        outputs.update({"fin_e": in_vmem(24, ECOLS), "fin_l": in_vmem(24, LCOLS), "fin_o": in_vmem(48, WALF)})
        scratch.update(fold_scratch("l", LCOLS, False))
        scratch.update(fold_targets("l", LCOLS, False, lambda *shape: pltpu.VMEM(shape, BF16)))
        scratch.update(finish_scratch("e", ECOLS, True))
        scratch.update(finish_scratch("l", LCOLS, False))
    return call(
        functools.partial(backward_body, layer, rider), "block_backward", 4 + layer, inputs, outputs, scratch
    )


def reduce_body(r):
    c, y, z, x = places()
    greet_axes()
    net = Net(r.net_send, r.net_recv)
    late = Fold(net, r, "l", LCOLS, r.gl, None)
    late.begin((0, 1))
    early_end = Finish(net, r, "e", ECOLS, (r.e0a, r.e0b, r.e0o))
    early_end.second()
    late_end = Finish(net, r, "l", LCOLS, late.h)
    row = lax.broadcasted_iota(jnp.int32, (8, 128), 0)
    lane = lane_at((8, 128))
    for layer in range(2):
        taps, gain, heads = r.gtaps.at[layer], r.ggain.at[layer], r.ghead.at[layer]
        for d in range(64):
            cell = (layer, d // 16, (d // 4) % 4, d % 4)
            first = jnp.where(lane < 48, take_chunk(taps, 0, 48, d), 0.0)
            norm = jnp.where(lane < 24, take_chunk(gain, 0, 24, d), 0.0)
            r.cells[cell + (slice(0, 8),)] = jnp.where(row == ROW_NORM, norm, first)
            second = jnp.where(lane < 4, take_chunk(taps, INNER, 4, d), 0.0)
            head = jnp.where(lane < 3, take_chunk(heads, 0, 8, d // 4), 0.0)
            r.cells[cell + (slice(8, 16),)] = jnp.where(row >= 5, head, second)
    pair = net.go(r.cells.at[1 - c], r.other, sibling())
    others = [
        net.go(r.far_e, r.got_far_e, sibling()),
        net.go(r.far_l, r.got_far_l, sibling()),
        net.go(r.far_o, r.got_far_o, sibling()),
    ]
    pair.wait_recv()
    r.sum0[...] = r.cells[c] + r.other[...]
    hops = [net.go(r.sum0.at[lax.rem(y + k, 4)], r.in_y.at[k], y_peer(k)) for k in range(1, 4)]
    late.combine(0)
    late.combine(1)
    early_end.third()
    for copy in hops:
        copy.wait_recv()
    r.sum1[...] = r.sum0[y] + r.in_y[1] + r.in_y[2] + r.in_y[3]
    hops = [net.go(r.sum1.at[lax.rem(z + k, 4)], r.in_z.at[k], z_peer(k)) for k in range(1, 4)]
    late.settle(0)
    late.settle(1)
    late_end.second()
    for copy in hops:
        copy.wait_recv()
    r.sum2[...] = r.sum1[z] + r.in_z[1] + r.in_z[2] + r.in_z[3]
    r.in_x[x] = r.sum2[x]
    hops = [net.go(r.sum2.at[lax.rem(x + k, 4)], r.in_x.at[x], x_peer(k)) for k in range(1, 4)]
    early_end.last(r.near_e, r.near_o)
    others.append(net.go(r.near_e, r.got_near_e, sibling()))
    others.append(net.go(r.near_o, r.got_near_o, sibling()))
    late_end.third()
    for copy in hops:
        copy.wait_recv()
    r.blob[...] = r.in_x[0] + r.in_x[1] + r.in_x[2] + r.in_x[3]
    late_end.last(r.near_l)
    others.append(net.go(r.near_l, r.got_near_l, sibling()))
    for copy in others:
        copy.wait_recv()

    def put(first_l, second_l, first_e, second_e, first_o, second_o):
        r.inner[:, :LCOLS] = first_l[...]
        r.inner[:, LCOLS:] = second_l[:, : INNER - LCOLS]
        r.bc[...] = second_l[:, INNER - LCOLS : CONV - LCOLS]
        r.step[...] = second_l[:, CONV - LCOLS : CONV - LCOLS + 128]
        r.gate[:, :ECOLS] = first_e[...]
        r.gate[:, ECOLS:] = second_e[...]
        r.out[:, :WALF] = first_o[...]
        r.out[:, WALF:] = second_o[...]

    @pl.when(c == 0)
    def _():
        put(r.near_l, r.got_near_l, r.near_e, r.got_near_e, r.near_o, r.got_near_o)

    @pl.when(c == 1)
    def _():
        put(r.got_far_l, r.far_l, r.got_far_e, r.far_e, r.got_far_o, r.far_o)

    net.drain()


def reduce_all(grads, far, gtaps, ggain, ghead):
    cell = (4, 4, 16, 128)
    return call(
        reduce_body, "reduce_grads", 6,
        {
            "gl": ("h", grads[0]), "e0a": ("v", grads[1]), "e0b": ("v", grads[2]), "e0o": ("v", grads[3]),
            "far_e": ("v", far[0]), "far_l": ("v", far[1]), "far_o": ("v", far[2]),
            "gtaps": ("v", gtaps), "ggain": ("v", ggain), "ghead": ("v", ghead),
        },
        {
            "inner": in_vmem(24, INNER), "bc": in_vmem(24, 2 * STATE), "step": in_vmem(24, 128),
            "gate": in_vmem(24, INNER), "out": in_vmem(48, D), "blob": in_vmem(16, 128),
        },
        {
            **{
                name + part: pltpu.VMEM(shape, F32)
                for name in ("near_", "got_near_", "got_far_")
                for part, shape in (("e", (24, ECOLS)), ("l", (24, LCOLS)), ("o", (48, WALF)))
            },
            "cells": pltpu.VMEM((2, 4) + cell, F32), "other": pltpu.VMEM((4,) + cell, F32),
            "sum0": pltpu.VMEM((4,) + cell, F32), "in_y": pltpu.VMEM((4,) + cell, F32),
            "sum1": pltpu.VMEM(cell, F32), "in_z": pltpu.VMEM((4,) + cell[1:], F32),
            "sum2": pltpu.VMEM(cell[1:], F32), "in_x": pltpu.VMEM((4, 16, 128), F32),
            **fold_scratch("l", LCOLS, False),
            **fold_targets("l", LCOLS, False, lambda *shape: pltpu.VMEM(shape, BF16)),
            **finish_scratch("e", ECOLS, True), **finish_scratch("l", LCOLS, False), **net_scratch(64),
        },
    )


def step_lanes(step):
    lead = step.shape[0]
    return jnp.pad(step.reshape(lead, OWNERS, 3), ((0, 0), (0, 0), (0, 5))).reshape(lead, 128)


def small_blob(norm_gain, inner_gain, conv_inner, conv_bc, heads):
    def row(value):
        return jnp.pad(value.astype(F32), ((0, 0), (0, 128 - value.shape[1])))

    return jnp.concatenate(
        [
            row(conv_inner), row(inner_gain[None]), row(norm_gain[None]), jnp.zeros((1, 128), F32),
            row(conv_bc), row(heads),
        ],
        axis=0,
    )


def settle(section, first_value, second_value):
    own = jnp.where(section == 0, first_value, second_value)
    got = lax.ppermute(jnp.where(section == 0, second_value, first_value), "section", [(0, 1), (1, 0)])
    return jnp.stack([jnp.where(section == 0, own, got), jnp.where(section == 0, got, own)])


def per_device(
    block_input, cotangent, seg_groups, norm_gain, w_gate, w_inner, w_bc, w_step, conv_inner, conv_bc, head_params,
    inner_gain, w_out,
):
    section = lax.axis_index("section")
    seq_pos = lax.axis_index("seq")
    shards = {
        "inner": w_inner[0], "bc": w_bc[0], "step": step_lanes(w_step[0]), "gate": w_gate[0], "out": w_out[0],
        "blob": small_blob(norm_gain[0], inner_gain[0], conv_inner[0], conv_bc[0], head_params[0]),
    }
    firsts = (BLOCKS - seg_groups[0]) * (BLOCK_LEN // TOK)
    first = jnp.where(section == 0, firsts[0], firsts[1])
    at_start = seq_pos == first
    flags = jnp.stack(
        [
            seq_pos >= first,
            jnp.logical_not(at_start) | ((section == 1) & (first == 0)),
            at_start & (section == 1) & (first != 0),
            (section == 0) & (seq_pos == 15) & (firsts[1] != 0),
        ]
    ).astype(F32)

    x = lax.dynamic_index_in_dim(block_input[0], section, 0, keepdims=False)
    start = block_forward(0, flags, x, shards)
    weights = (
        (start.w0.reshape(2, D, HALF), start.wo0.reshape(2, INNER, WALF)),
        (start.next_w.reshape(2, D, HALF), start.next_wo.reshape(2, INNER, WALF)),
    )
    kept = [start, block_forward(1, flags, start.result, weights[1] + (start,))]
    inputs = [x, start.result]

    g = lax.dynamic_index_in_dim(cotangent[0], section, 0, keepdims=False)
    grads = None
    backs = [None, None]
    for layer in (1, 0):
        w, wo = weights[layer]
        back = block_backward(layer, flags, g, inputs[layer], w, wo, start, kept[layer], grads)
        backs[layer] = back
        g = back.result
        hidden = kept[layer].both_hidden.reshape(2 * TOK, D)
        grad_late = dot32(hidden, back.both_gl.reshape(2 * TOK, LCOLS), ((0,), (0,))).astype(BF16)
        grads = (grad_late.reshape(4, 4, 96, LCOLS), back.eha, back.ehb, back.eho)

    final = reduce_all(
        grads, (backs[0].fin_e, backs[0].fin_l, backs[0].fin_o),
        jnp.stack([backs[0].gtaps, backs[1].gtaps]), jnp.stack([backs[0].ggain, backs[1].ggain]),
        jnp.stack([backs[0].ghead, backs[1].ghead]),
    )
    blob = final.blob
    return (
        settle(section, kept[0].result, kept[1].result)[None, None],
        settle(section, backs[0].result, backs[1].result)[None, None],
        blob[ROW_NORM : ROW_NORM + 1, :24],
        final.gate[None],
        final.inner[None],
        final.bc[None],
        final.step.reshape(24, OWNERS, 8)[:, :, :3].reshape(24, HEADS)[None],
        blob[None, 0:5, :48],
        blob[None, 8:13, :4],
        blob[None, 13:16, :3],
        blob[ROW_MID : ROW_MID + 1, :48],
        final.out[None],
    )


def solution(mesh):
    weight = P("section", ROWS_ALL, None)
    vector = P("section", ROWS_ALL)
    taps = P("section", None, ROWS_ALL)
    tokens = P("wsh", None, "seq", None)
    heads = P("section", None, "seq")
    result = P("section", "wsh", None, "seq", None)
    return jax.shard_map(
        per_device,
        mesh=mesh,
        in_specs=(
            tokens, tokens, P("wsh", None), vector, weight, weight, weight, weight, taps, taps, heads, vector, weight,
        ),
        out_specs=(
            result, result, vector, weight, weight, weight, weight, taps, taps, heads, vector, weight,
        ),
        check_vma=False,
    )
```

```python
import functools
import types

import jax
import jax.numpy as jnp
from jax import lax
from jax.experimental import pallas as pl
from jax.experimental.pallas import tpu as pltpu
from jax.sharding import PartitionSpec as P

D = 1536
INNER = 3072
HEADS = 48
STATE = 128
BLOCK_LEN = 256
BLOCKS = 8
TOK = 128
CONV = INNER + 2 * STATE
HALF = CONV
GATE0 = 256
CUT = HALF // 2
WALF = D // 2
WCUT = WALF // 2
ECOLS = INNER // 2
LCOLS = HALF // 2 + 128
LSPLIT = LCOLS
OWNERS = 16
OWN = 192
EPS = 1e-05
F32 = jnp.float32
BF16 = jnp.bfloat16
MESH = pl.DeviceIdType.MESH
VMEM_LIMIT = 61 * 1024 * 1024
LANES = (0, 1, 2, 8, 9, 10)
ROWS_ALL = ("seq", "wsh")
ROW_MID, ROW_NORM = 5, 6
ROW_BIAS, ROW_DECAY, ROW_SKIP = 5, 6, 7


def dot32(left, right, dims=((1,), (0,))):
    return lax.dot_general(left, right, (dims, ((), ())), preferred_element_type=F32)


def split_left(exact, value, terms):
    total = None
    for _ in range(terms):
        part = value.astype(BF16)
        value = value - part.astype(F32)
        term = dot32(exact, part)
        total = term if total is None else total + term
    return total


def split_right(value, exact, terms, dims=((1,), (0,))):
    total = None
    for _ in range(terms):
        part = value.astype(BF16)
        value = value - part.astype(F32)
        term = dot32(part, exact, dims)
        total = term if total is None else total + term
    return total


def pair_cols(tile, q):
    lane = lax.broadcasted_iota(jnp.int32, (TOK, 128), 1)
    a = jnp.broadcast_to(tile[:, LANES[2 * q] : LANES[2 * q] + 1], (TOK, 128))
    b = jnp.broadcast_to(tile[:, LANES[2 * q + 1] : LANES[2 * q + 1] + 1], (TOK, 128))
    return a, b, jnp.where(lane < 64, a, b)


def pair_row(row, q):
    lane = lax.broadcasted_iota(jnp.int32, (1, 128), 1)
    a = jnp.broadcast_to(row[:, LANES[2 * q] : LANES[2 * q] + 1], (1, 128))
    b = jnp.broadcast_to(row[:, LANES[2 * q + 1] : LANES[2 * q + 1] + 1], (1, 128))
    return jnp.where(lane < 64, a, b)


def to_front(tile, i):
    return pltpu.roll(tile, lax.rem(128 - 16 * i, 128), 1)


def conv_of(cat, taps):
    total = taps[4:5] + taps[3:4] * cat[8 : 8 + TOK]
    for k in range(3):
        total = total + taps[k : k + 1] * cat[5 + k : 5 + k + TOK]
    return total


def tri_of(lower):
    row = lax.broadcasted_iota(jnp.int32, (TOK, TOK), 0)
    col = lax.broadcasted_iota(jnp.int32, (TOK, TOK), 1)
    return row >= col if lower else row <= col


def head_lanes():
    lane = lax.broadcasted_iota(jnp.int32, (TOK, 128), 1)
    return (lane % 8) < 3


def group_cols(i, q):
    return pl.ds(pl.multiple_of(i * 384 + q * 128, 128), 128)


def gate_cols(i, q):
    return pl.ds(pl.multiple_of(GATE0 + i * 384 + q * 128, 128), 128)


def in_hbm(*shape, dtype=BF16):
    return jax.ShapeDtypeStruct(shape, dtype), pl.BlockSpec(memory_space=pl.ANY)


def in_vmem(*shape, dtype=F32):
    return jax.ShapeDtypeStruct(shape, dtype), pl.BlockSpec(memory_space=pltpu.VMEM)


def saved(*shape, dtype=F32):
    return jax.ShapeDtypeStruct(shape, dtype), None


def call(body, name, ident, inputs, outputs, scratch):
    spaces = {"h": pl.ANY, "v": pltpu.VMEM, "s": pltpu.SMEM, "p": pl.ANY}
    early = [key for key, (kind, _) in inputs.items() if kind == "p"]
    late = [key for key, (_, spec) in outputs.items() if spec is None]
    scratch = dict(scratch)
    for key in early:
        scratch[key] = pltpu.VMEM(inputs[key][1].shape, inputs[key][1].dtype)
    for key in late:
        scratch[key] = pltpu.VMEM(outputs[key][0].shape, outputs[key][0].dtype)
    if early or late:
        scratch["move_sems"] = dma_sems(len(early) + len(late))
    names = [key + "_far" if key in early else key for key in inputs]
    names += [key + "_far" if key in late else key for key in outputs] + list(scratch)

    def kernel(*refs):
        r = types.SimpleNamespace(**dict(zip(names, refs)))

        def mover(key):
            near, far = getattr(r, key), getattr(r, key + "_far")
            src, dst = (far, near) if key in early else (near, far)
            return pltpu.make_async_copy(src, dst, r.move_sems.at[(early + late).index(key)])

        def start(*keys):
            for key in keys:
                mover(key).start()

        def wait(*keys):
            for key in keys:
                mover(key).wait()

        r.move, r.moved = start, wait
        body(r)

    out = pl.pallas_call(
        kernel,
        out_shape=tuple(shape for shape, _ in outputs.values()),
        in_specs=[pl.BlockSpec(memory_space=spaces[kind]) for kind, _ in inputs.values()],
        out_specs=tuple(
            pl.BlockSpec(memory_space=pl.ANY) if spec is None else spec for _, spec in outputs.values()
        ),
        scratch_shapes=list(scratch.values()),
        compiler_params=pltpu.CompilerParams(
            collective_id=ident, has_side_effects=True, vmem_limit_bytes=VMEM_LIMIT
        ),
        name=name,
    )(*[value for _, value in inputs.values()])
    return types.SimpleNamespace(**dict(zip(outputs, out)))


def dma_sems(count):
    return pltpu.SemaphoreType.DMA((count,))


def places():
    section = lax.axis_index("section")
    seq = lax.axis_index("seq")
    return section, seq // 4, lax.rem(seq, 4), lax.axis_index("wsh")


def x_peer(k):
    return {"wsh": lax.rem(lax.axis_index("wsh") + k, 4)}


def z_peer(k):
    _, y, z, _ = places()
    return {"seq": y * 4 + lax.rem(z + k, 4)}


def y_peer(k):
    _, y, z, _ = places()
    return {"seq": lax.rem(y + k, 4) * 4 + z}


def sibling():
    return {"section": 1 - lax.axis_index("section")}


def say_hello(peer):
    pl.semaphore_signal(pltpu.get_barrier_semaphore(), inc=1, device_id=peer, device_id_type=MESH)


def greet_axes():
    for k in range(1, 4):
        for peer in (x_peer(k), y_peer(k), z_peer(k)):
            say_hello(peer)
    say_hello(sibling())
    pl.semaphore_wait(pltpu.get_barrier_semaphore(), 10)


def fetch(src, dst, sem):
    copy = pltpu.make_async_copy(src, dst, sem)
    copy.start()
    return copy


class Net:
    def __init__(self, send, recv):
        self.send, self.recv = send, recv
        self.count = 0
        self.started = []

    def go(self, src, dst, peer):
        copy = pltpu.make_async_remote_copy(
            src_ref=src, dst_ref=dst, send_sem=self.send.at[self.count], recv_sem=self.recv.at[self.count],
            device_id=peer, device_id_type=MESH,
        )
        copy.start()
        self.count += 1
        self.started.append(copy)
        return copy

    def drain(self):
        for copy in self.started:
            copy.wait_send()


class Gather:
    def __init__(self, net, p, o, w, wo, stage, rows, own):
        self.net, self.p, self.o, self.w, self.wo = net, p, o, w, wo
        self.stage, self.rows, self.own = stage, rows, own
        self.place = places()
        self.near, self.far, self.inner, self.passed = {}, {}, {}, []
        self.peers = (y_peer, z_peer, x_peer, x_peer)
        self.inner_peers = (z_peer, y_peer, y_peer, z_peer)

    def band(self, kind, j, moved, half=None):
        c, y, z, x = self.place
        rows = slice(None) if half is None else pl.ds(48 * half, 48)
        many = slice(None) if half is None else pl.ds(2 * half, 2)
        if kind == 0:
            return self.w.at[c, lax.rem(y + 4 - moved, 4), lax.rem(z + 4 - j, 4), rows, pl.ds(0, CUT)]
        if kind == 1:
            return self.w.at[c, lax.rem(y + 4 - j, 4), lax.rem(z + 4 - moved, 4), rows, pl.ds(CUT, CUT)]
        if kind == 2:
            return self.wo.at[c, lax.rem(y + 4 - j, 4), many, lax.rem(x + 4 - moved, 4), :, pl.ds(0, WCUT)]
        return self.wo.at[c, many, lax.rem(z + 4 - j, 4), lax.rem(x + 4 - moved, 4), :, pl.ds(WCUT, WCUT)]

    def pass_on(self, part):
        self.passed.append(self.net.go(part, part, sibling()))

    def begin(self):
        c, y, z, x = self.place
        go = self.net.go
        self.first, self.spots = [], []
        spot = self.wo.at[c, y, z, x]
        for k in range(1, 4):
            self.first.append(go(self.p, self.stage.at[x], x_peer(k)))
            for cols, peer in ((pl.ds(0, WCUT), z_peer), (pl.ds(WCUT, WCUT), y_peer)):
                self.spots.append(go(self.o.at[:, cols], spot.at[:, cols], peer(k)))
        self.own_o = fetch(self.o, spot, self.own.at[0])
        self.stage[x] = self.p[...]

    def rows_in(self):
        c, y, z, x = self.place
        go = self.net.go
        for copy in self.first:
            copy.wait_recv()
        for side in range(2):
            self.rows[:, CUT * side : CUT * side + CUT] = jnp.concatenate(
                [self.stage[n].astype(F32)[24 * side : 24 * side + 24] for n in range(4)], axis=0
            ).astype(BF16)
        for k in (1, 3):
            for kind, cols in ((0, pl.ds(0, CUT)), (1, pl.ds(CUT, CUT))):
                self.inner[kind, k] = go(
                    self.rows.at[:, cols], self.band(kind, 0, 0), self.inner_peers[kind](k)
                )
        own_w = fetch(self.rows, self.w.at[c, y, z], self.own.at[1])
        self.own_o.wait()
        for copy in self.spots:
            copy.wait_recv()
        for k in (1, 3):
            for kind in (2, 3):
                part = self.band(kind, 0, 0)
                self.inner[kind, k] = go(part, part, self.inner_peers[kind](k))
        own_w.wait()
        self.spread(0)

    def spread(self, j):
        if j in (1, 3):
            for kind in range(4):
                self.inner[kind, j].wait_recv()
                part = self.band(kind, j, 0, 0 if j == 1 else 1)
                self.inner[kind, 2, j] = self.net.go(part, part, self.inner_peers[kind](j))
        if j == 2:
            for kind in range(4):
                self.inner[kind, 2, 1].wait_recv()
                self.inner[kind, 2, 3].wait_recv()
        for k in (1, 3):
            for kind in range(4):
                part = self.band(kind, j, 0)
                self.near[kind, j, k] = self.net.go(part, part, self.peers[kind](k))
        for kind in range(4):
            self.pass_on(self.band(kind, j, 0))

    def relay(self, j):
        for k in (1, 3):
            for kind in range(4):
                self.near[kind, j, k].wait_recv()
                part = self.band(kind, j, k)
                if (k == 1) == (j < 2):
                    self.far[kind, j] = self.net.go(part, part, self.peers[kind](k))
                self.pass_on(part)

    def last(self, j):
        for kind in range(4):
            self.far[kind, j].wait_recv()
            self.pass_on(self.band(kind, j, 2))

    def end(self):
        for copy in self.passed:
            copy.wait_recv()


def gather_scratch():
    return {
        "stage": pltpu.VMEM((4, 48, CUT), BF16),
        "rows": pltpu.VMEM((96, HALF), BF16),
        "own": dma_sems(2),
    }


def lane_at(shape):
    return lax.broadcasted_iota(jnp.int32, shape, 1)


def place_chunks(cells, width, total):
    tiles = [jnp.zeros((8, 128), F32) for _ in range(total // 128)]
    lane = lane_at((8, 128))
    for d in range(64):
        t, off = (width * d) // 128, (width * d) % 128
        moved = pltpu.roll(cells(d), off, 1) if off else cells(d)
        stop = off + width
        tiles[t] = jnp.where((lane >= off) & (lane < min(stop, 128)), moved, tiles[t])
        if stop > 128:
            tiles[t + 1] = jnp.where(lane < stop - 128, moved, tiles[t + 1])
    return tiles


def take_chunk(ref, base, width, d):
    start = base + width * d
    t, off = start // 128, start % 128
    tile = ref[:, 128 * t : 128 * t + 128]
    tile = pltpu.roll(tile, 128 - off, 1) if off else tile
    if off + width > 128:
        after = pltpu.roll(ref[:, 128 * t + 128 : 128 * t + 256], 128 - off, 1)
        tile = jnp.where(lane_at((8, 128)) < 128 - off, tile, after)
    return tile


def start_body(r, net, after):
    c, y, z, x = places()

    def stacked(first, second):
        return jnp.concatenate([first.astype(F32), second.astype(F32)], axis=0).astype(BF16)

    r.wide[...] = jnp.zeros_like(r.wide)
    r.wide[0:24, 0:48] = r.step[...].astype(F32)
    lane24 = lane_at((24, 128))
    spread_step = jnp.zeros((24, 128), F32)
    for n in range(OWNERS):
        moved = pltpu.roll(r.wide[0:24, :], 5 * n, 1) if n else r.wide[0:24, :]
        spread_step = jnp.where((lane24 >= 8 * n) & (lane24 < 8 * n + 3), moved, spread_step)
    gate_cut = CUT - GATE0
    r.mine[0, :, : INNER - CUT] = stacked(r.inner[:, : INNER - CUT], r.inner[:, CUT:])
    r.mine[0, :, INNER - CUT :] = stacked(r.inner[:, INNER - CUT : CUT], r.bc[...])
    r.mine[1, :, :128] = stacked(spread_step, r.gate[:, gate_cut : gate_cut + 128])
    r.mine[1, :, 128:GATE0] = stacked(jnp.zeros((24, 128), F32), r.gate[:, gate_cut + 128 : gate_cut + GATE0])
    r.mine[1, :, GATE0:] = stacked(r.gate[:, :gate_cut], r.gate[:, gate_cut + GATE0 :])
    r.blob[...] = jnp.zeros_like(r.blob)
    r.blob[0:5, 0:48] = r.conv_inner[...].astype(F32)
    r.blob[ROW_MID : ROW_MID + 1, 0:48] = r.mid[...].astype(F32)
    r.blob[ROW_NORM : ROW_NORM + 1, 0:24] = r.norm[...].astype(F32)
    r.blob[8:13, 0:4] = r.conv_bc[...].astype(F32)
    r.blob[13:16, 0:3] = r.head[...]
    given = pl.ds(pl.multiple_of((1 - c) * WALF, 128), WALF)
    swaps = [
        net.go(r.mine.at[1 - c], r.half.at[c], sibling()),
        net.go(r.out.at[:, given], r.half_o.at[c], sibling()),
    ]
    small = [net.go(r.blob, r.cells.at[c, y, z, x], x_peer(k)) for k in range(1, 4)]
    r.half[c] = r.mine[c]
    r.half_o[c] = jnp.where(c == 0, r.out[:, :WALF], r.out[:, WALF:])
    r.cells[c, y, z, x] = r.blob[...]
    for copy in swaps:
        copy.wait_recv()
    ga = Gather(net, r.half.at[0], r.half_o.at[0], r.w0, r.wo0, r.stage0, r.rows0, r.own0)
    ga.begin()
    for copy in small:
        copy.wait_recv()
    small = [net.go(r.cells.at[c, y, z], r.cells.at[c, y, z], z_peer(k)) for k in range(1, 4)]
    ga.rows_in()
    after.begin()
    for copy in small:
        copy.wait_recv()
    small = [net.go(r.cells.at[c, y], r.cells.at[c, y], y_peer(k)) for k in range(1, 4)]
    for j in (1, 3, 2):
        ga.spread(j)
    for copy in small:
        copy.wait_recv()
    pair = net.go(r.cells.at[c], r.cells.at[c], sibling())
    ga.relay(0)
    ga.relay(1)
    pair.wait_recv()
    for layer in range(2):
        def first_tile(d):
            return r.cells[layer, d // 16, (d // 4) % 4, d % 4, 0:8]

        def second_tile(d):
            return r.cells[layer, d // 16, (d // 4) % 4, d % 4, 8:16]

        for t, tile in enumerate(place_chunks(first_tile, 48, INNER)):
            r.taps[layer, :, 128 * t : 128 * t + 128] = tile
        for t, tile in enumerate(place_chunks(second_tile, 4, 2 * STATE)):
            r.taps[layer, :, INNER + 128 * t : INNER + 128 * t + 128] = tile
        for t, tile in enumerate(place_chunks(first_tile, 24, D)):
            r.gain[layer, :, 128 * t : 128 * t + 128] = tile
        lane = lane_at((8, 128))
        heads = jnp.zeros((8, 128), F32)
        for j in range(OWNERS):
            moved = pltpu.roll(second_tile(4 * j), 8 * j, 1) if j else second_tile(0)
            heads = jnp.where((lane >= 8 * j) & (lane < 8 * j + 3), moved, heads)
        r.heads[layer] = heads
    after.rows_in()
    ga.relay(3)
    ga.relay(2)
    after.spread(1)
    after.spread(3)
    for j in (0, 1, 3, 2):
        ga.last(j)
    after.spread(2)
    ga.end()


TURNS = (1, 4, 3, 12, 5, 15, 7, 13, 2, 8, 6, 9, 14, 11, 10)


def seq_peer(d):
    _, y, z, _ = places()
    return lax.rem(y + d // 4, 4) * 4 + lax.rem(z + d % 4, 4)


class Exchange:
    def __init__(self, backward, r):
        self.backward, self.r = backward, r
        self.me = lax.axis_index("seq")
        self.section = lax.axis_index("section")

    def first_copy(self, peer, d):
        r = self.r
        return pltpu.make_async_remote_copy(
            src_ref=r.ds.at[peer], dst_ref=r.got.at[self.me], send_sem=r.send_a.at[d], recv_sem=r.recv_a.at[d],
            device_id={"seq": peer}, device_id_type=MESH,
        )

    def send(self, peer):
        _, y, z, _ = places()
        d = lax.rem(peer // 4 + 4 - y, 4) * 4 + lax.rem(lax.rem(peer, 4) + 4 - z, 4)

        @pl.when(d != 0)
        def _():
            self.first_copy(peer, d).start()

        @pl.when(d == 0)
        def _():
            self.r.got[self.me] = self.r.ds[self.me]

    def back_copy(self, d):
        r = self.r
        peer = seq_peer(d)
        return pltpu.make_async_remote_copy(
            src_ref=r.ready.at[peer], dst_ref=r.back.at[self.me], send_sem=r.send_b.at[d], recv_sem=r.recv_b.at[d],
            device_id={"seq": peer}, device_id_type=MESH,
        )

    def scan(self, decays):
        r = self.r

        def rows_of(dec):
            return jnp.concatenate([jnp.broadcast_to(dec[h : h + 1], (64, 128)) for h in range(3)], axis=0)

        for d in TURNS:
            self.first_copy(seq_peer(d), d).wait_recv()
        r.final[...] = jnp.zeros((OWN, STATE), F32)
        r.fade[0] = jnp.ones((8, 128), F32)

        def step(n, carry):
            c = OWNERS - 1 - n if self.backward else n
            state = r.final[...]
            r.kept[c] = state
            dec = decays[c]
            r.final[...] = rows_of(dec) * state + r.got[c].astype(F32)
            r.fade[n + 1] = r.fade[n] * dec
            return carry

        lax.fori_loop(0, OWNERS, step, 0)
        swap = pltpu.make_async_remote_copy(
            src_ref=r.final, dst_ref=r.other, send_sem=r.swap_s.at[0], recv_sem=r.swap_s.at[1],
            device_id=sibling(), device_id_type=MESH,
        )
        swap.start()
        takes = 0 if self.backward else 1
        r.begin[...] = jnp.zeros((OWN, STATE), F32)

        @pl.when(self.section == takes)
        def _():
            swap.wait_recv()
            r.begin[...] = r.other[...]

        begin = r.begin[...]
        for d in TURNS + (0,):
            c = seq_peer(d)
            n = OWNERS - 1 - c if self.backward else c
            value = (r.kept[c] + rows_of(r.fade[n]) * begin).astype(BF16)
            if d == 0:
                r.back[c] = value
            else:
                r.ready[c] = value
                self.back_copy(d).start()

        @pl.when(self.section != takes)
        def _():
            swap.wait_recv()

        swap.wait_send()

    def finish(self):
        for d in TURNS:
            self.back_copy(d).wait_recv()

    def drain(self):
        for d in range(1, OWNERS):
            self.first_copy(seq_peer(d), d).wait_send()
            self.back_copy(d).wait_send()


def exchange_scratch():
    block = pltpu.VMEM((OWNERS, OWN, STATE), BF16)
    part = pltpu.VMEM((OWN, STATE), F32)
    return {
        "ds": block, "got": block, "back": block, "ready": block,
        "kept": pltpu.VMEM((OWNERS, OWN, STATE), F32), "fade": pltpu.VMEM((OWNERS + 1, 8, 128), F32),
        "final": part, "other": part, "begin": part,
        "send_a": dma_sems(OWNERS), "recv_a": dma_sems(OWNERS), "send_b": dma_sems(OWNERS), "recv_b": dma_sems(OWNERS),
        "swap_s": dma_sems(2),
    }


def head_rows_at(ref, i, q):
    parts = []
    for h in (2 * q, 2 * q + 1):
        parts.append(ref[2 * i + h // 3, pl.ds(64 * (h % 3), 64), :])
    return jnp.concatenate(parts, axis=0)


def store_heads(ref, i, q, value):
    for n, h in enumerate((2 * q, 2 * q + 1)):
        ref[2 * i + h // 3, pl.ds(64 * (h % 3), 64), :] = value[64 * n : 64 * n + 64]


def own_group(n):
    return lax.rem(lax.axis_index("seq") // 2 + n, 8)


def greet_layer(rider, forward):
    me = lax.axis_index("seq")
    section = lax.axis_index("section")
    wsh = lax.axis_index("wsh")
    barrier = pltpu.get_barrier_semaphore()
    for d in range(1, OWNERS):
        say_hello({"seq": lax.rem(me + d, OWNERS)})
    say_hello(sibling())
    if rider:
        for k in range(1, 4):
            say_hello(x_peer(k))
    count = OWNERS + (3 if rider else 0)
    late = {"section": 0, "seq": 15, "wsh": wsh}
    if forward:

        @pl.when((section == 1) & ((me == 0) | (me == 4)))
        def _():
            pl.semaphore_signal(barrier, inc=1, device_id=late, device_id_type=MESH)

        more = jnp.where((section == 0) & (me == 15), 2, 0)
    else:

        @pl.when((section == 0) & (me == 15))
        def _():
            for seq in (0, 4):
                pl.semaphore_signal(
                    barrier, inc=1, device_id={"section": 1, "seq": seq, "wsh": wsh}, device_id_type=MESH
                )

        more = jnp.where((section == 1) & ((me == 0) | (me == 4)), 1, 0)
    pl.semaphore_wait(barrier, count + more)


def flags_of(seg):
    section = lax.axis_index("section")
    seq = lax.axis_index("seq")
    starts = [(BLOCKS - seg[0, n]) * (BLOCK_LEN // TOK) for n in range(2)]
    first = jnp.where(section == 0, starts[0], starts[1])
    at_start = seq == first
    second = section == 1

    def number(cond):
        return jnp.where(cond, 1.0, 0.0)

    live = number(seq >= first)
    near = number(jnp.logical_not(at_start) | (second & (first == 0)))
    far = number(at_start & second & (first != 0))
    cross = number((section == 0) & (seq == 15) & (starts[1] != 0))
    return live, near, far, cross


def halo_copy(src, dst, sems, n, section, seq):
    return pltpu.make_async_remote_copy(
        src_ref=src, dst_ref=dst, send_sem=sems.at[n], recv_sem=sems.at[2 + n],
        device_id={"section": section, "seq": seq, "wsh": lax.axis_index("wsh")}, device_id_type=MESH,
    )


class Halo:
    def __init__(self, src, near, far, sems, forward):
        me = lax.axis_index("seq")
        section = lax.axis_index("section")
        edge = 15 if forward else 0
        if forward:
            crossing = (section == 0) & (me == 15)
            jumping = crossing
            self.has_near = (me > 0) | (section == 1)
            self.has_far = (section == 1) & (me == 4)
            target = (1, jnp.where(me == 15, 0, me + 1))
            near_section = jnp.where(crossing, 1, section)
            far_seq, far_section = 4, 1
        else:
            crossing = (section == 1) & (me == 0)
            jumping = (section == 1) & (me == 4)
            self.has_near = (me < 15) | (section == 0)
            self.has_far = (section == 0) & (me == 15)
            target = (0, jnp.where(me == 0, 15, me - 1))
            near_section = jnp.where(crossing, 0, section)
            far_seq, far_section = 15, 0
        self.sends_near = (me != edge) | crossing
        self.sends_far = jumping
        self.near, self.far = near, far
        self.near_copy = halo_copy(src, near, sems, 0, near_section, target[1])
        self.far_copy = halo_copy(src, far, sems, 1, far_section, far_seq)

    def start(self):
        @pl.when(self.sends_near)
        def _():
            self.near_copy.start()

        @pl.when(self.sends_far)
        def _():
            self.far_copy.start()

        @pl.when(jnp.logical_not(self.has_near))
        def _():
            self.near[...] = jnp.zeros_like(self.near)

        @pl.when(jnp.logical_not(self.has_far))
        def _():
            self.far[...] = jnp.zeros_like(self.far)

    def wait(self):
        @pl.when(self.has_near)
        def _():
            self.near_copy.wait_recv()

        @pl.when(self.has_far)
        def _():
            self.far_copy.wait_recv()

    def drain(self):
        @pl.when(self.sends_near)
        def _():
            self.near_copy.wait_send()

        @pl.when(self.sends_far)
        def _():
            self.far_copy.wait_send()


def forward_body(layer, rider, r):
    section = lax.axis_index("section")
    me = lax.axis_index("seq")
    net = Net(r.pair_send, r.pair_recv)
    if rider:
        greet_layer(rider, True)
        bulk = Net(r.net_send, r.net_recv)
        ga = Gather(bulk, r.half.at[1], r.half_o.at[1], r.next_w, r.next_wo, r.stage, r.rows, r.own)
        start_body(r, bulk, ga)
        w, wo = r.w0.reshape(2, D, HALF), r.wo0.reshape(2, INNER, WALF)
    else:
        w, wo = r.w, r.wo
    loads = [fetch(w.at[n], r.w_s.at[n], r.load.at[n]) for n in range(2)]
    load_o = fetch(wo, r.wo_s, r.load.at[2])
    if not rider:
        greet_layer(rider, True)
    ex = Exchange(False, r)
    flags = flags_of(r.flags)
    live = flags[0]
    heads = r.heads[layer]
    x_ref = r.x.at[section] if rider else r.x
    x32 = x_ref[...].astype(F32)
    hidden_inv = lax.rsqrt(jnp.sum(x32 * x32, axis=1, keepdims=True) / D + EPS)
    r.hidden[...] = (x32 * hidden_inv * r.gain[layer, ROW_NORM : ROW_NORM + 1, :]).astype(BF16)
    loads[0].wait()

    def project_main(n, carry):
        cols = pl.ds(pl.multiple_of(n * 256, 256), 256)
        r.pre[:, cols] = dot32(r.hidden[...], r.w_s[0, :, cols]).astype(BF16)
        return carry

    lax.fori_loop(0, HALF // 256, project_main, 0)
    r.tail[...] = r.pre[TOK - 16 :, :]
    halo = Halo(r.tail, r.halo_near, r.halo_far, r.halo_s, True)
    halo.start()
    loads[1].wait()

    def project_side(n, carry):
        cols = pl.ds(pl.multiple_of(n * 256, 256), 256)
        r.side[:, cols] = dot32(r.hidden[...], r.w_s[1, :, cols])
        return carry

    lax.fori_loop(0, HALF // 256, project_side, 0)
    if rider:
        ga.relay(0)
    r.move("pre", "side")
    pairs = [net.go(r.hidden, r.both_hidden.at[section], sibling())]
    owns = [fetch(r.hidden, r.both_hidden.at[section], r.load.at[3])]
    step = r.side[:, :128].astype(BF16).astype(F32) + heads[ROW_BIAS : ROW_BIAS + 1]
    dt = jnp.maximum(step, 0.0) + jnp.log1p(jnp.exp(-jnp.abs(step)))
    dt = jnp.where(head_lanes(), dt, 0.0) * live
    rate = -dt * jnp.exp(heads[ROW_DECAY : ROW_DECAY + 1])
    cum = split_left(tri_of(True).astype(F32).astype(BF16), rate, 3)
    r.dt[...] = dt
    r.cum[...] = cum
    last = jnp.broadcast_to(cum[TOK - 1 : TOK], (TOK, 128))
    r.dec_s[...] = jnp.exp(last).T.reshape(OWNERS, 8, 128)
    r.dec[me] = r.dec_s[me]

    def dec_copy(d):
        peer = lax.rem(me + d, OWNERS)
        return pltpu.make_async_remote_copy(
            src_ref=r.dec_s.at[peer], dst_ref=r.dec.at[me], send_sem=r.dec_send.at[d], recv_sem=r.dec_recv.at[d],
            device_id={"seq": peer}, device_id_type=MESH,
        )

    for d in range(1, OWNERS):
        dec_copy(d).start()
    weight = dt * jnp.exp(last - cum)
    halo.wait()
    r.halo[...] = jnp.where(
        flags[1] > 0.0, r.halo_near[...], jnp.where(flags[2] > 0.0, r.halo_far[...], jnp.zeros_like(r.halo_far))
    )

    def conv_tile(cols):
        blk = r.pre[:, cols].astype(F32)
        cat = jnp.concatenate([r.halo[:, cols].astype(F32)[8:], blk], axis=0)
        summed = conv_of(cat, r.taps[layer, :, cols])
        sig = 1.0 / (1.0 + jnp.exp(-summed))
        act = summed * sig
        r.act[:, cols] = act
        r.dact[:, cols] = sig * (1.0 + summed * (1.0 - sig))
        return act

    b = conv_tile(pl.ds(INNER, 128)).astype(BF16)
    c = conv_tile(pl.ds(INNER + 128, 128)).astype(BF16)

    def states(n, carry):
        i = own_group(n)
        wt = to_front(weight, i)
        for q in range(3):
            x = conv_tile(group_cols(i, q))
            scaled = (x * pair_cols(wt, q)[2]).astype(BF16)
            store_heads(r.ds, i, q, dot32(scaled, b, ((0,), (0,))).astype(BF16))
        ex.send(2 * i)
        ex.send(2 * i + 1)
        return carry

    lax.fori_loop(0, 8, states, 0)
    r.move("act", "dact")
    if rider:
        ga.relay(1)
    for d in range(1, OWNERS):
        dec_copy(d).wait_recv()
    ex.scan(r.dec)
    if rider:
        ga.relay(3)
    r.cumt[...] = cum.T
    causal = tri_of(True)
    scores = dot32(c, b, ((1,), (1,)))
    lane = lax.broadcasted_iota(jnp.int32, (TOK, 128), 1)
    r.square[...] = jnp.zeros((TOK, 128), F32)

    def inside(i, carry):
        cum_i = to_front(cum, i)
        dt_i = to_front(dt, i)
        rows = r.cumt[pl.ds(pl.multiple_of(16 * i, 16), 16), :]
        for q in range(3):
            cols = group_cols(i, q)
            cum_a, cum_b, _ = pair_cols(cum_i, q)
            u = r.act[:, cols] * pair_cols(dt_i, q)[2]
            mixes = []
            for cum_h, off in ((cum_a, LANES[2 * q]), (cum_b, LANES[2 * q + 1])):
                gap = cum_h - rows[off : off + 1]
                mixes.append((scores * jnp.exp(jnp.where(causal, gap, -1e30))).astype(BF16))
            terms = jnp.concatenate(
                [jnp.where(lane < 64, u, 0.0).astype(BF16), jnp.where(lane < 64, 0.0, u).astype(BF16)], axis=0
            )
            r.raw[:, cols] = dot32(jnp.concatenate(mixes, axis=1), terms)
        return carry

    lax.fori_loop(0, 8, inside, 0)
    if rider:
        ga.relay(2)
    ex.finish()
    save = fetch(r.back, r.states, r.load.at[4])

    def across(i, carry):
        cum_i = to_front(cum, i)
        skip_i = pltpu.roll(heads, lax.rem(128 - 16 * i, 128), 1)[ROW_SKIP : ROW_SKIP + 1]
        for q in range(3):
            cols = group_cols(i, q)
            state = head_rows_at(r.back, i, q)
            raw = r.raw[:, cols] + jnp.exp(pair_cols(cum_i, q)[2]) * dot32(c, state, ((1,), (1,)))
            r.raw[:, cols] = raw
            y = (raw + pair_row(skip_i, q) * r.act[:, cols]).astype(BF16)
            r.y[:, cols] = y
            gate = r.side[:, gate_cols(i, q)]
            z = y.astype(F32) * (gate / (1.0 + jnp.exp(-gate)))
            r.z[:, cols] = z
            r.square[...] += z * z
        return carry

    lax.fori_loop(0, 8, across, 0)
    r.move("raw", "y")
    if rider:
        ga.last(0)
        ga.last(1)
    total = jnp.sum(r.square[...], axis=1, keepdims=True)
    inv = jnp.broadcast_to(lax.rsqrt(total / INNER + EPS), (TOK, 128))
    r.inv[...] = inv

    def scale(i, carry):
        cols = pl.ds(pl.multiple_of(i * 128, 128), 128)
        mid = r.taps[layer, ROW_MID : ROW_MID + 1, cols]
        r.gated[:, cols] = (r.z[:, cols] * inv * mid).astype(BF16)
        return carry

    lax.fori_loop(0, 24, scale, 0)
    pairs.append(net.go(r.gated, r.both_gated.at[section], sibling()))
    owns.append(fetch(r.gated, r.both_gated.at[section], r.load.at[5]))
    load_o.wait()
    for half in range(2):

        def project(n, carry):
            cols = pl.ds(pl.multiple_of(n * 256, 256), 256)
            full = pl.ds(pl.multiple_of(half * WALF + n * 256, 256), 256)
            branch = dot32(r.gated[...], r.wo_s[half, :, cols])
            r.result[:, full] = (x_ref[:, full].astype(F32) + live * branch).astype(BF16)
            return carry

        lax.fori_loop(0, WALF // 256, project, 0)
    if rider:
        for j in (3, 2):
            ga.last(j)
        ga.end()
        bulk.drain()
    if not rider:
        cross = [
            pltpu.make_async_remote_copy(
                src_ref=src, dst_ref=r.finals.at[section], send_sem=r.final_s.at[0], recv_sem=r.final_s.at[1],
                device_id=sibling(), device_id_type=MESH,
            )
            for src in (r.result, r.x)
        ]
        stay = [pltpu.make_async_copy(src, r.finals.at[section], r.final_s.at[2]) for src in (r.x, r.result)]
        for n in range(2):

            @pl.when(section == n)
            def _():
                cross[n].start()
                stay[n].start()

        cross[0].wait_recv()
        cross[0].wait_send()
        stay[0].wait()
    r.moved("pre", "side", "act", "dact", "raw", "y")
    save.wait()
    for copy in owns:
        copy.wait()
    for copy in pairs:
        copy.wait_recv()
    net.drain()
    halo.drain()
    for d in range(1, OWNERS):
        dec_copy(d).wait_send()
    ex.drain()


def block_forward(layer, flags, x, given):
    rider = layer == 0
    inputs = {"flags": ("s", flags), "x": ("v", x)}
    if rider:
        for key, value in given.items():
            inputs[key] = ("v", value)
    else:
        w, wo, small = given
        inputs.update({
            "w": ("h", w), "wo": ("h", wo), "taps": ("v", small.taps), "gain": ("v", small.gain),
            "heads": ("v", small.heads),
        })
    outputs = {
        "act": saved(TOK, CONV), "dact": saved(TOK, CONV), "side": saved(TOK, HALF), "raw": saved(TOK, INNER),
        "dt": in_vmem(TOK, 128), "cum": in_vmem(TOK, 128), "inv": in_vmem(TOK, 128),
        "dec": in_vmem(OWNERS, 8, 128), "pre": saved(TOK, CONV, dtype=BF16), "halo": in_vmem(16, CONV, dtype=BF16),
        "y": saved(TOK, INNER, dtype=BF16), "result": in_vmem(TOK, D, dtype=BF16),
        "states": in_hbm(OWNERS, OWN, STATE), "both_hidden": in_hbm(2, TOK, D), "both_gated": in_hbm(2, TOK, INNER),
    }
    tile = pltpu.VMEM((TOK, 128), F32)
    edge = pltpu.VMEM((16, CONV), BF16)
    scratch = {
        "w_s": pltpu.VMEM((2, D, HALF), BF16), "wo_s": pltpu.VMEM((2, INNER, WALF), BF16),
        "hidden": pltpu.VMEM((TOK, D), BF16), "gated": pltpu.VMEM((TOK, INNER), BF16),
        "z": pltpu.VMEM((TOK, INNER), F32), "cumt": tile, "square": tile,
        "tail": edge, "halo_near": edge, "halo_far": edge, "halo_s": dma_sems(4),
        "dec_s": pltpu.VMEM((OWNERS, 8, 128), F32), "dec_send": dma_sems(OWNERS), "dec_recv": dma_sems(OWNERS),
        "load": dma_sems(6), "pair_send": dma_sems(2), "pair_recv": dma_sems(2),
        **exchange_scratch(),
    }
    if not rider:
        outputs["finals"] = in_hbm(2, TOK, D)
        scratch["final_s"] = dma_sems(3)
    if rider:
        outputs.update({
            "w0": in_hbm(2, 4, 4, 96, HALF), "wo0": in_hbm(2, 4, 4, 4, 48, WALF),
            "next_w": in_hbm(2, 4, 4, 96, HALF), "next_wo": in_hbm(2, 4, 4, 4, 48, WALF),
            "taps": in_vmem(2, 8, CONV), "gain": in_vmem(2, 8, D), "heads": in_vmem(2, 8, 128),
        })
        scratch.update({
            "mine": pltpu.VMEM((2, 48, CUT), BF16), "half": pltpu.VMEM((2, 48, CUT), BF16),
            "wide": pltpu.VMEM((24, 128), F32), "blob": pltpu.VMEM((16, 128), F32),
            "half_o": pltpu.VMEM((2, 48, WALF), BF16), "cells": pltpu.VMEM((2, 4, 4, 4, 16, 128), F32),
            "net_send": dma_sems(400), "net_recv": dma_sems(400),
        })
        scratch.update({key + "0": value for key, value in gather_scratch().items()})
        scratch.update(gather_scratch())
    return call(
        functools.partial(forward_body, layer, rider), "block_forward", 2 + layer, inputs, outputs, scratch
    )


def add_rows(target, *parts):
    lead = target.shape[:-2]
    blocks = functools.reduce(lambda a, b: a * b, lead, 1)

    def body(b, carry):
        spot = (b,) if len(lead) == 1 else (b // lead[1], lax.rem(b, lead[1]))
        total = parts[0][spot].astype(F32)
        for ref in parts[1:]:
            total = total + ref[spot].astype(F32)
        target[spot] = total.astype(target.dtype)
        return carry

    lax.fori_loop(0, blocks, body, 0)


def fold_scratch(tag, cols, with_out):
    shapes = {"a": (4, 96, cols // 2), "b": (4, 96, cols // 2)}
    if with_out:
        shapes["o"] = (4, 4, 48, WALF)
    scratch = {}
    for key, shape in shapes.items():
        scratch[tag + "m" + key] = pltpu.VMEM(shape, BF16)
        scratch[tag + "s" + key] = pltpu.VMEM((2,) + shape, BF16)
    scratch[tag + "own"] = dma_sems(9)
    return scratch


def fold_targets(tag, cols, with_out, make):
    targets = {tag + "ha": make(4, 96, cols // 2), tag + "hb": make(4, 96, cols // 2)}
    if with_out:
        targets[tag + "ho"] = make(4, 4, 48, WALF)
    return targets


class Fold:
    def __init__(self, net, r, tag, cols, gi, go):
        self.net, self.gi, self.go_ref, self.cut = net, gi, go, cols // 2
        self.kinds = (0, 1, 2) if go is not None else (0, 1)
        keys = "abo"
        self.h = [getattr(r, tag + "h" + keys[n]) for n in self.kinds]
        self.m = [getattr(r, tag + "m" + keys[n]) for n in self.kinds]
        self.s = [getattr(r, tag + "s" + keys[n]) for n in self.kinds]
        self.own = getattr(r, tag + "own")
        self.place = places()
        self.peers = (y_peer, z_peer, x_peer)
        self.hops, self.direct, self.loads = {}, {}, {}

    def part(self, kind, t, half):
        _, y, z, x = self.place
        at = pl.ds(2 * half, 2) if half is not None else slice(None)
        if kind == 0:
            return self.gi.at[lax.rem(y + t, 4), at, :, pl.ds(0, self.cut)]
        if kind == 1:
            return self.gi.at[at, lax.rem(z + t, 4), :, pl.ds(self.cut, self.cut)]
        return self.go_ref.at[at, :, lax.rem(x + t, 4)]

    def begin(self, kinds):
        go = self.net.go
        for half, k in ((0, 1), (1, 3)):
            for kind in kinds:
                self.hops[kind, half] = go(
                    self.part(kind, 2, half), self.h[kind].at[pl.ds(2 * half, 2)], self.peers[kind](k)
                )
        for half, k in ((1, 1), (0, 3)):
            for kind in kinds:
                side = 0 if k == 1 else 1
                self.direct[kind, side] = go(
                    self.part(kind, k, half), self.s[kind].at[side, pl.ds(2 * half, 2)], self.peers[kind](k)
                )
        for kind in kinds:
            self.loads[kind] = [
                fetch(self.part(kind, 1, 0), self.m[kind].at[pl.ds(0, 2)], self.own.at[3 * kind]),
                fetch(self.part(kind, 3, 1), self.m[kind].at[pl.ds(2, 2)], self.own.at[3 * kind + 1]),
            ]

    def combine(self, kind):
        for copy in self.loads[kind]:
            copy.wait()
        for half in range(2):
            self.hops[kind, half].wait_recv()
        add_rows(self.m[kind], self.m[kind], self.h[kind])
        peer = self.peers[kind]
        for half, k in ((0, 1), (1, 3)):
            at = pl.ds(2 * half, 2)
            self.hops[kind, half] = self.net.go(self.m[kind].at[at], self.s[kind].at[half, at], peer(k))
        self.loads[kind] = [fetch(self.part(kind, 0, None), self.h[kind], self.own.at[3 * kind + 2])]

    def settle(self, kind):
        for copy in self.loads[kind]:
            copy.wait()
        for side in range(2):
            self.direct[kind, side].wait_recv()
            self.hops[kind, side].wait_recv()
        add_rows(self.h[kind], self.h[kind], self.s[kind].at[0], self.s[kind].at[1])


class Finish:
    def __init__(self, net, r, tag, cols, sums):
        self.net, self.sums, self.cut, self.cols = net, sums, cols // 2, cols
        for key in ("r2a", "r2b", "c3", "r3") + (("r2o", "o2", "r3o") if len(sums) > 2 else ()):
            setattr(self, key, getattr(r, tag + key))
        self.place = places()

    def second(self):
        _, y, z, _ = self.place
        go = self.net.go
        ha, hb = self.sums[:2]
        self.a, self.b, self.o = [], [], []
        for k in range(1, 4):
            self.a.append(go(ha.at[lax.rem(z + k, 4)], self.r2a.at[k], z_peer(k)))
            self.b.append(go(hb.at[lax.rem(y + k, 4)], self.r2b.at[k], y_peer(k)))
        self.r2a[0] = ha[z]
        self.r2b[0] = hb[y]
        if len(self.sums) > 2:
            ho = self.sums[2]
            one, two = pl.ds(0, WCUT), pl.ds(WCUT, WCUT)
            for k in range(1, 4):
                self.o.append(go(ho.at[lax.rem(y + k, 4), :, :, one], self.r2o.at[0, k], y_peer(k)))
                self.o.append(go(ho.at[:, lax.rem(z + k, 4), :, two], self.r2o.at[1, k], z_peer(k)))
            self.r2o[0, 0] = ho[y, :, :, :WCUT]
            for n in range(4):
                self.r2o[1, 0, n] = ho[n, z, :, WCUT:]

    def third(self):
        _, y, z, x = self.place
        go = self.net.go
        for copy in self.a + self.b:
            copy.wait_recv()
        for n in range(4):
            at = pl.ds(24 * n, 24)
            for parts, cols in ((self.r2a, pl.ds(0, self.cut)), (self.r2b, pl.ds(self.cut, self.cut))):
                total = parts[0, at, :].astype(F32)
                for k in range(1, 4):
                    total = total + parts[k, at, :].astype(F32)
                self.c3[n, :, cols] = total
        self.x = [go(self.c3.at[lax.rem(x + k, 4)], self.r3.at[x], x_peer(k)) for k in range(1, 4)]
        self.r3[x] = self.c3[x]
        if self.o:
            for copy in self.o:
                copy.wait_recv()
            for n in range(2):
                add_rows(self.o2.at[n], *[self.r2o.at[n, k] for k in range(4)])
            for k in range(1, 4):
                self.x.append(go(self.o2.at[0, lax.rem(z + k, 4)], self.r3o.at[0, k], z_peer(k)))
                self.x.append(go(self.o2.at[1, lax.rem(y + k, 4)], self.r3o.at[1, k], y_peer(k)))
            self.r3o[0, 0] = self.o2[0, z]
            self.r3o[1, 0] = self.o2[1, y]

    def last(self, in_ref, out_ref=None):
        for copy in self.x:
            copy.wait_recv()
        in_ref[...] = self.r3[0] + self.r3[1] + self.r3[2] + self.r3[3]
        if self.o:
            for n in range(2):
                total = self.r3o[n, 0].astype(F32)
                for k in range(1, 4):
                    total = total + self.r3o[n, k].astype(F32)
                out_ref[:, WCUT * n : WCUT * n + WCUT] = total


def finish_scratch(tag, cols, with_out):
    cut = cols // 2
    scratch = {
        tag + "r2a": pltpu.VMEM((4, 96, cut), BF16), tag + "r2b": pltpu.VMEM((4, 96, cut), BF16),
        tag + "c3": pltpu.VMEM((4, 24, cols), F32), tag + "r3": pltpu.VMEM((4, 24, cols), F32),
    }
    if with_out:
        scratch[tag + "r2o"] = pltpu.VMEM((2, 4, 4, 48, WCUT), BF16)
        scratch[tag + "o2"] = pltpu.VMEM((2, 4, 48, WCUT), BF16)
        scratch[tag + "r3o"] = pltpu.VMEM((2, 4, 48, WCUT), BF16)
    return scratch


def net_scratch(count):
    return {"net_send": dma_sems(count), "net_recv": dma_sems(count)}


def early_products(r, which):
    left, right, stage, target = (
        (r.gated2, r.gb2, r.stage_o, r.go) if which == 0 else (r.hid2, r.dg2, r.stage_e, r.ge)
    )
    tile = stage.shape[1]

    def body(i, carry):
        slot = lax.rem(i, 2)
        rows = pl.ds(pl.multiple_of(i * tile, tile), tile)
        copy = pltpu.make_async_copy(stage.at[slot], target.at[rows], r.stage_s.at[2 * which + slot])

        @pl.when(i >= 2)
        def _():
            copy.wait()

        stage[slot] = dot32(left[:, rows], right[...], ((0,), (0,))).astype(BF16)
        copy.start()
        return carry

    lax.fori_loop(0, target.shape[0] // tile, body, 0)
    for slot in range(2):
        pltpu.make_async_copy(stage.at[slot], target.at[pl.ds(0, tile)], r.stage_s.at[2 * which + slot]).wait()


def backward_body(layer, rider, r):
    section = lax.axis_index("section")
    slots_o, slots_w = r.wo_s.shape[0], r.w_s.shape[0]
    load_state = fetch(r.states, r.state_s, r.load.at[0])
    load_two = [fetch(r.both_hidden, r.hid2, r.load.at[3]), fetch(r.both_gated, r.gated2, r.load.at[4])]

    def wo_tile(i):
        rows = pl.ds(pl.multiple_of(i * 384, 384), 384)
        slot = lax.rem(i, slots_o)
        return pltpu.make_async_copy(r.wo.at[:, rows], r.wo_s.at[slot], r.wo_load.at[slot])

    def w_tile(n):
        slot = lax.rem(n, slots_w)
        rows = pl.ds(pl.multiple_of((n // 2) * 256, 256), 256)
        return pltpu.make_async_copy(r.w.at[lax.rem(n, 2), rows], r.w_s.at[slot], r.w_load.at[slot])

    for n in range(slots_o):
        wo_tile(n).start()
    r.move("side", "y", "act", "raw", "dact", "pre")
    for n in range(slots_w):
        w_tile(n).start()
    greet_layer(True, False)
    net = Net(r.pair_send, r.pair_recv)
    bulk = Net(r.net_send, r.net_recv)
    if rider:
        late = Fold(bulk, r, "l", LCOLS, r.gl, None)
        late.begin((0, 1))
        early_end = Finish(bulk, r, "e", ECOLS, (r.e1a, r.e1b, r.e1o))
        early_end.second()
        late_end = Finish(bulk, r, "l", LCOLS, late.h)
    early = Fold(
        bulk, r, "e", ECOLS, r.ge.reshape(4, 4, 96, ECOLS), r.go.reshape(4, 4, 4, 48, WALF)
    )
    ex = Exchange(True, r)
    flags = flags_of(r.flags)
    live = flags[0]
    heads = r.heads[layer]
    g_ref = r.g if rider else r.g.at[section]
    r.gb[...] = (g_ref[...].astype(F32) * live).astype(BF16)
    inv = r.inv[...]
    dt = r.dt[...]
    cum = r.cum[...]
    r.dots[...] = jnp.zeros((TOK, 128), F32)
    other_half = pl.ds(pl.multiple_of((1 - section) * WALF, 128), WALF)
    own_rows = pl.ds(pl.multiple_of(section * TOK, 128), TOK)
    pairs = [net.go(r.gb.at[:, other_half], r.gb2.at[own_rows], sibling())]
    r.gb2[own_rows, :] = jnp.where(section == 0, r.gb[:, :WALF], r.gb[:, WALF:])
    load_two[1].wait()
    pairs[0].wait_recv()
    early_products(r, 0)
    early.begin((2,))

    def first(i, carry):
        slot = lax.rem(i, slots_o)
        wo_tile(i).wait()
        gg = dot32(r.gb[:, :WALF], r.wo_s[slot, 0], ((1,), (1,)))
        gg = gg + dot32(r.gb[:, WALF:], r.wo_s[slot, 1], ((1,), (1,)))

        @pl.when(i + slots_o < 8)
        def _():
            wo_tile(i + slots_o).start()

        r.gg[:, pl.ds(pl.multiple_of(i * 384, 384), 384)] = gg
        for q in range(3):
            cols = group_cols(i, q)
            gate = r.side[:, gate_cols(i, q)]
            z = r.y[:, cols].astype(F32) * (gate / (1.0 + jnp.exp(-gate)))
            mid = r.taps[layer, ROW_MID : ROW_MID + 1, cols]
            r.dots[...] += gg[:, 128 * q : 128 * q + 128] * mid * z
        return carry

    r.moved("side", "y")
    lax.fori_loop(0, 8, first, 0)
    r.moved("act")
    b = r.act[:, INNER : INNER + 128].astype(BF16)
    c = r.act[:, INNER + 128 : CONV].astype(BF16)
    total = jnp.broadcast_to(jnp.sum(r.dots[...], axis=1, keepdims=True), (TOK, 128))
    shift = total * inv * inv * inv / INNER
    r.gtaps[...] = jnp.zeros_like(r.gtaps)

    def second(n, carry):
        i = own_group(n)
        cum_i = to_front(cum, i)
        for q in range(3):
            cols = group_cols(i, q)
            gate = r.side[:, gate_cols(i, q)]
            y = r.y[:, cols].astype(F32)
            gg = r.gg[:, cols]
            sig = 1.0 / (1.0 + jnp.exp(-gate))
            act = gate * sig
            z = y * act
            dz = gg * r.taps[layer, ROW_MID : ROW_MID + 1, cols] * inv - z * shift
            dy = (dz * act).astype(BF16)
            r.dy[:, cols] = dy
            r.gside[:, gate_cols(i, q)] = (dz * y * (sig * (1.0 + gate * (1.0 - sig)))).astype(BF16)
            r.gtaps[ROW_MID : ROW_MID + 1, cols] = jnp.sum(gg * z * inv, axis=0, keepdims=True)
            far = (dy.astype(F32) * jnp.exp(pair_cols(cum_i, q)[2])).astype(BF16)
            store_heads(r.ds, i, q, dot32(far, c, ((0,), (0,))).astype(BF16))
        ex.send(2 * i)
        ex.send(2 * i + 1)
        return carry

    lax.fori_loop(0, 8, second, 0)
    other_cols = pl.ds(pl.multiple_of(GATE0 + (1 - section) * ECOLS, 128), ECOLS)
    pairs.append(net.go(r.gside.at[:, other_cols], r.dg2.at[own_rows], sibling()))
    r.dg2[own_rows, :] = jnp.where(
        section == 0, r.gside[:, GATE0 : GATE0 + ECOLS], r.gside[:, GATE0 + ECOLS :]
    )
    if rider:
        late.combine(0)
        late.combine(1)
    load_two[0].wait()
    pairs[1].wait_recv()
    early_products(r, 1)
    ex.scan(r.dec)
    early.begin((0, 1))
    load_state.wait()
    r.cumt[...] = cum.T
    causal = tri_of(True)
    scores = dot32(c, b, ((1,), (1,)))
    lane = lax.broadcasted_iota(jnp.int32, (TOK, 128), 1)
    pick_row = lax.broadcasted_iota(jnp.int32, (128, 128), 0)
    pick_col = lax.broadcasted_iota(jnp.int32, (128, 128), 1)
    picks = []
    for q in range(3):
        target = jnp.where(pick_row < 64, LANES[2 * q], LANES[2 * q + 1])
        picks.append((pick_col == target).astype(F32).astype(BF16))
    for ref in (r.dscore, r.grad_b, r.grad_c, r.xdu, r.dyy, r.thin):
        ref[...] = jnp.zeros_like(ref)

    def inside(i, carry):
        cum_i = to_front(cum, i)
        dt_i = to_front(dt, i)
        rows = r.cumt[pl.ds(pl.multiple_of(16 * i, 16), 16), :]
        for q in range(3):
            cols = group_cols(i, q)
            cum_a, cum_b, cum_x = pair_cols(cum_i, q)
            u16 = (r.act[:, cols] * pair_cols(dt_i, q)[2]).astype(BF16)
            dy16 = r.dy[:, cols]
            nil = jnp.zeros_like(dy16)
            dys = jnp.concatenate([jnp.where(lane < 64, dy16, nil), jnp.where(lane < 64, nil, dy16)], axis=0)
            both = dot32(dys, u16, ((1,), (1,)))
            mixes = []
            for n, (cum_h, off) in enumerate(((cum_a, LANES[2 * q]), (cum_b, LANES[2 * q + 1]))):
                gap = cum_h - rows[off : off + 1]
                decay = jnp.exp(jnp.where(causal, gap, -1e30))
                mixes.append((scores * decay).astype(BF16))
                r.dscore[...] += both[n * TOK : n * TOK + TOK] * decay
            r.gg[:, cols] = dot32(jnp.concatenate(mixes, axis=0), dys, ((0,), (0,)))
            far = (dy16.astype(F32) * jnp.exp(cum_x)).astype(BF16)
            r.grad_c[...] += dot32(far, head_rows_at(r.state_s, i, q))
        return carry

    lax.fori_loop(0, 8, inside, 0)
    if rider:
        late.settle(0)
        late.settle(1)
        late_end.second()

    def conv_back(cols, gact):
        gsum = gact * r.dact[:, cols]
        r.gsum[:, cols] = gsum
        blk = r.pre[:, cols].astype(F32)
        cat = jnp.concatenate([r.halo[:, cols].astype(F32)[8:], blk], axis=0)
        sums = [jnp.sum(gsum * cat[5 + k : 5 + k + TOK], axis=0, keepdims=True) for k in range(4)]
        sums.append(jnp.sum(gsum, axis=0, keepdims=True))
        r.gtaps[0:5, cols] = jnp.concatenate(sums, axis=0)

    r.moved("raw", "dact", "pre")
    ex.finish()

    def across(i, carry):
        cum_i = to_front(cum, i)
        dt_i = to_front(dt, i)
        skip_i = pltpu.roll(heads, lax.rem(128 - 16 * i, 128), 1)[ROW_SKIP : ROW_SKIP + 1]
        x_du = jnp.zeros((TOK, 128), F32)
        dy_y = jnp.zeros((TOK, 128), F32)
        thin = jnp.zeros((16, 128), F32)
        edges = {}
        for q in range(3):
            cols = group_cols(i, q)
            x = r.act[:, cols]
            cum_x = pair_cols(cum_i, q)[2]
            dt_x = pair_cols(dt_i, q)[2]
            fade = jnp.exp(cum_x[TOK - 1 : TOK] - cum_x)
            u = x * dt_x
            dy = r.dy[:, cols].astype(F32)
            state16 = head_rows_at(r.state_s, i, q)
            dstate16 = head_rows_at(r.back, i, q)
            du_far = fade * dot32(b, dstate16, ((1,), (1,)))
            du = r.gg[:, cols] + du_far
            r.grad_b[...] += dot32((u * fade).astype(BF16), dstate16)
            overlap = state16.astype(F32) * dstate16.astype(F32)
            edges[LANES[2 * q]] = jnp.sum(overlap[:64], axis=0, keepdims=True)
            edges[LANES[2 * q + 1]] = jnp.sum(overlap[64:], axis=0, keepdims=True)
            x_du = x_du + split_right(x * du, picks[q], 2)
            dy_y = dy_y + split_right(dy * r.raw[:, cols], picks[q], 2)
            thin = thin + split_right(
                jnp.concatenate(
                    [
                        jnp.broadcast_to(jnp.sum(u * du_far, axis=0, keepdims=True), (8, 128)),
                        jnp.broadcast_to(jnp.sum(dy * x, axis=0, keepdims=True), (8, 128)),
                    ],
                    axis=0,
                ),
                picks[q],
                3,
            )
            conv_back(cols, du * dt_x + pair_row(skip_i, q) * dy)
        nothing = jnp.zeros((1, 128), F32)
        r.edge[pl.ds(pl.multiple_of(16 * i, 16), 16), :] = jnp.concatenate(
            [edges.get(k, nothing) for k in range(16)], axis=0
        )
        r.xdu[...] += pltpu.roll(x_du, 16 * i, 1)
        r.dyy[...] += pltpu.roll(dy_y, 16 * i, 1)
        r.thin[...] += pltpu.roll(thin, 16 * i, 1)
        return carry

    lax.fori_loop(0, 8, across, 0)
    early.combine(2)
    early.combine(0)
    early.combine(1)
    dscore16 = r.dscore[...].astype(BF16)
    conv_back(pl.ds(INNER, 128), r.grad_b[...] + dot32(dscore16, c, ((0,), (0,))))
    conv_back(pl.ds(INNER + 128, 128), r.grad_c[...] + dot32(dscore16, b))
    r.tail[...] = r.gsum[:8, :]
    halo = Halo(r.tail, r.halo_near, r.halo_far, r.halo_s, False)
    halo.start()
    ones = jnp.ones((128, 128), BF16)
    edge = split_right(r.edge[...], ones, 3).T[0:1] * jnp.exp(cum[TOK - 1 : TOK]) + r.thin[0:1]
    x_du = r.xdu[...]
    drate = split_left(tri_of(False).astype(F32).astype(BF16), r.dyy[...] - dt * x_du, 3) + edge
    speed = jnp.exp(heads[ROW_DECAY : ROW_DECAY + 1])
    ddt = x_du - drate * speed
    step = r.side[:, :128].astype(BF16).astype(F32) + heads[ROW_BIAS : ROW_BIAS + 1]
    dstep = jnp.where(head_lanes(), ddt / (1.0 + jnp.exp(-step)), 0.0) * live
    r.gside[:, :128] = dstep.astype(BF16)
    r.gside[:, 128:GATE0] = jnp.zeros((TOK, 128), BF16)
    r.ghead[...] = jnp.concatenate(
        [
            jnp.zeros((5, 128), F32),
            jnp.sum(dstep, axis=0, keepdims=True),
            jnp.sum(-drate * dt * speed, axis=0, keepdims=True),
            r.thin[8:9],
        ],
        axis=0,
    )
    halo.wait()
    after = jnp.where(flags[3] > 0.0, r.halo_far[...], r.halo_near[...])
    r.halo_near[...] = jnp.where(live > 0.0, after, jnp.zeros_like(after))

    def conv_tile(i, carry):
        cols = pl.ds(pl.multiple_of(i * 128, 128), 128)
        cat = jnp.concatenate([r.gsum[:, cols], r.halo_near[:, cols]], axis=0)
        taps = r.taps[layer, :, cols]
        total = taps[3:4] * cat[:TOK]
        for k in range(3):
            total = total + taps[k : k + 1] * cat[3 - k : 3 - k + TOK]
        r.gpre[:, cols] = total.astype(BF16)
        return carry

    lax.fori_loop(0, CONV // 128, conv_tile, 0)
    if rider:
        early_end.third()
        late_end.third()

    tail_cols = HALF - LCOLS
    side_cols = pl.ds(0, GATE0)
    moves = (
        net_copy(net, r.gpre.at[:, pl.ds(LCOLS, tail_cols)], r.both_gl.at[0, :, pl.ds(0, tail_cols)], 2),
        net_copy(net, r.gside.at[:, side_cols], r.both_gl.at[0, :, pl.ds(tail_cols, GATE0)], 3),
        net_copy(net, r.gpre.at[:, pl.ds(0, LCOLS)], r.both_gl.at[1], 2),
    )
    keeps = (
        pltpu.make_async_copy(r.gpre.at[:, pl.ds(LCOLS, tail_cols)], r.both_gl.at[1, :, pl.ds(0, tail_cols)], r.load.at[1]),
        pltpu.make_async_copy(r.gside.at[:, side_cols], r.both_gl.at[1, :, pl.ds(tail_cols, GATE0)], r.load.at[2]),
        pltpu.make_async_copy(r.gpre.at[:, pl.ds(0, LCOLS)], r.both_gl.at[0], r.load.at[1]),
    )

    @pl.when(section == 0)
    def _():
        moves[0].start()
        moves[1].start()
        keeps[2].start()

    @pl.when(section == 1)
    def _():
        moves[2].start()
        keeps[0].start()
        keeps[1].start()

    def project(n, carry):
        rows = pl.ds(pl.multiple_of(n * 256, 256), 256)
        w_tile(2 * n).wait()
        value = dot32(r.gpre[...], r.w_s[lax.rem(2 * n, slots_w)], ((1,), (1,)))

        @pl.when(2 * n + slots_w < 12)
        def _():
            w_tile(2 * n + slots_w).start()

        w_tile(2 * n + 1).wait()
        value = value + dot32(r.gside[...], r.w_s[lax.rem(2 * n + 1, slots_w)], ((1,), (1,)))

        @pl.when(2 * n + 1 + slots_w < 12)
        def _():
            w_tile(2 * n + 1 + slots_w).start()

        r.gg[:, rows] = value
        return carry

    lax.fori_loop(0, D // 256, project, 0)
    x = (r.x[section] if rider else r.x[...]).astype(F32)
    grad = r.gg[:, :D]
    inv_x = lax.rsqrt(jnp.sum(x * x, axis=1, keepdims=True) / D + EPS)
    scaled = grad * r.gain[layer, ROW_NORM : ROW_NORM + 1, :]
    dots = jnp.sum(scaled * x, axis=1, keepdims=True)
    dx = scaled * inv_x - x * (dots * inv_x * inv_x * inv_x / D)
    r.result[...] = (g_ref[...].astype(F32) + dx).astype(BF16)
    r.ggain[...] = jnp.broadcast_to(jnp.sum(grad * x * inv_x, axis=0, keepdims=True), (8, D))
    for kind in range(3):
        early.settle(kind)
    if rider:
        early_end.last(r.fin_e, r.fin_o)
        late_end.last(r.fin_l)
    if rider:
        cross = [
            pltpu.make_async_remote_copy(
                src_ref=src, dst_ref=r.finals.at[section], send_sem=r.final_s.at[0], recv_sem=r.final_s.at[1],
                device_id=sibling(), device_id_type=MESH,
            )
            for src in (r.g, r.result)
        ]
        stay = [pltpu.make_async_copy(src, r.finals.at[section], r.final_s.at[2]) for src in (r.result, r.g)]
        for n in range(2):

            @pl.when(section == n)
            def _():
                cross[n].start()
                stay[n].start()

        cross[0].wait_recv()
        cross[0].wait_send()
        stay[0].wait()
    bulk.drain()

    @pl.when(section == 0)
    def _():
        moves[0].wait_send()
        moves[1].wait_send()
        keeps[2].wait()
        moves[2].wait_recv()

    @pl.when(section == 1)
    def _():
        moves[2].wait_send()
        keeps[0].wait()
        keeps[1].wait()
        moves[0].wait_recv()
        moves[1].wait_recv()

    net.drain()
    halo.drain()
    ex.drain()


def net_copy(net, src, dst, n):
    return pltpu.make_async_remote_copy(
        src_ref=src, dst_ref=dst, send_sem=net.send.at[n], recv_sem=net.recv.at[n],
        device_id=sibling(), device_id_type=MESH,
    )


def block_backward(layer, flags, g, x, w, wo, small, kept, grads):
    rider = grads is not None
    inputs = {
        "flags": ("s", flags), "g": ("v", g), "x": ("v", x), "w": ("h", w), "wo": ("h", wo), "taps": ("v", small.taps),
        "gain": ("v", small.gain), "heads": ("v", small.heads), "states": ("h", kept.states),
        "both_hidden": ("h", kept.both_hidden.reshape(2 * TOK, D)),
        "both_gated": ("h", kept.both_gated.reshape(2 * TOK, INNER)),
    }
    for key in ("dt", "cum", "inv", "dec", "halo"):
        inputs[key] = ("v", getattr(kept, key))
    for key in ("side", "y", "act", "raw", "dact", "pre"):
        inputs[key] = ("p", getattr(kept, key))
    outputs = {
        "result": in_vmem(TOK, D, dtype=BF16), "both_gl": in_hbm(2, TOK, LCOLS),
        "gtaps": in_vmem(8, CONV), "ggain": in_vmem(8, D), "ghead": in_vmem(8, 128),
        "ge": in_hbm(D, ECOLS), "go": in_hbm(INNER, WALF),
        **fold_targets("e", ECOLS, True, lambda *shape: in_vmem(*shape, dtype=BF16)),
    }
    tile = pltpu.VMEM((TOK, 128), F32)
    edge = pltpu.VMEM((8, CONV), F32)
    slots, tile_rows = (2, 128) if rider else (4, 512)
    scratch = {
        "wo_s": pltpu.VMEM((slots, 2, 384, WALF), BF16), "w_s": pltpu.VMEM((slots, 256, HALF), BF16),
        "wo_load": dma_sems(slots), "w_load": dma_sems(slots), "load": dma_sems(5),
        "hid2": pltpu.VMEM((2 * TOK, D), BF16), "gated2": pltpu.VMEM((2 * TOK, INNER), BF16),
        "gb2": pltpu.VMEM((2 * TOK, WALF), BF16), "dg2": pltpu.VMEM((2 * TOK, ECOLS), BF16),
        "stage_o": pltpu.VMEM((2, tile_rows, WALF), BF16), "stage_e": pltpu.VMEM((2, tile_rows, ECOLS), BF16), "stage_s": dma_sems(4),
        "state_s": pltpu.VMEM((OWNERS, OWN, STATE), BF16),
        "gb": pltpu.VMEM((TOK, D), BF16), "gg": pltpu.VMEM((TOK, INNER), F32), "dy": pltpu.VMEM((TOK, INNER), BF16),
        "gsum": pltpu.VMEM((TOK, CONV), F32), "gpre": pltpu.VMEM((TOK, HALF), BF16), "gside": pltpu.VMEM((TOK, HALF), BF16),
        "dots": tile, "cumt": tile, "edge": tile, "dscore": tile, "grad_b": tile, "grad_c": tile, "xdu": tile, "dyy": tile,
        "thin": pltpu.VMEM((16, 128), F32),
        "tail": edge, "halo_near": edge, "halo_far": edge, "halo_s": dma_sems(4),
        "pair_send": dma_sems(4), "pair_recv": dma_sems(4),
        **exchange_scratch(), **fold_scratch("e", ECOLS, True), **net_scratch(64),
    }
    if rider:
        inputs.update({"gl": ("h", grads[0]), "e1a": ("v", grads[1]), "e1b": ("v", grads[2]), "e1o": ("v", grads[3])})
        outputs["finals"] = in_hbm(2, TOK, D)
        scratch["final_s"] = dma_sems(3)
        outputs.update({"fin_e": in_vmem(24, ECOLS), "fin_l": in_vmem(24, LCOLS), "fin_o": in_vmem(48, WALF)})
        scratch.update(fold_scratch("l", LCOLS, False))
        scratch.update(fold_targets("l", LCOLS, False, lambda *shape: pltpu.VMEM(shape, BF16)))
        scratch.update(finish_scratch("e", ECOLS, True))
        scratch.update(finish_scratch("l", LCOLS, False))
    return call(
        functools.partial(backward_body, layer, rider), "block_backward", 4 + layer, inputs, outputs, scratch
    )


def reduce_body(r):
    c, y, z, x = places()
    greet_axes()
    net = Net(r.net_send, r.net_recv)
    late = Fold(net, r, "l", LCOLS, r.gl, None)
    late.begin((0, 1))
    early_end = Finish(net, r, "e", ECOLS, (r.e0a, r.e0b, r.e0o))
    early_end.second()
    late_end = Finish(net, r, "l", LCOLS, late.h)
    row = lax.broadcasted_iota(jnp.int32, (8, 128), 0)
    lane = lane_at((8, 128))
    for layer in range(2):
        taps, gain, heads = (getattr(r, key + str(layer)) for key in ("gtaps", "ggain", "ghead"))
        for d in range(64):
            cell = (layer, d // 16, (d // 4) % 4, d % 4)
            first = jnp.where(lane < 48, take_chunk(taps, 0, 48, d), 0.0)
            norm = jnp.where(lane < 24, take_chunk(gain, 0, 24, d), 0.0)
            r.cells[cell + (slice(0, 8),)] = jnp.where(row == ROW_NORM, norm, first)
            second = jnp.where(lane < 4, take_chunk(taps, INNER, 4, d), 0.0)
            head = jnp.where(lane < 3, take_chunk(heads, 0, 8, d // 4), 0.0)
            r.cells[cell + (slice(8, 16),)] = jnp.where(row >= 5, head, second)
    pair = net.go(r.cells.at[1 - c], r.other, sibling())
    others = [
        net.go(r.far_e, r.got_far_e, sibling()),
        net.go(r.far_l, r.got_far_l, sibling()),
        net.go(r.far_o, r.got_far_o, sibling()),
    ]
    pair.wait_recv()
    r.sum0[...] = r.cells[c] + r.other[...]
    hops = [net.go(r.sum0.at[lax.rem(y + k, 4)], r.in_y.at[k], y_peer(k)) for k in range(1, 4)]
    late.combine(0)
    late.combine(1)
    early_end.third()
    for copy in hops:
        copy.wait_recv()
    r.sum1[...] = r.sum0[y] + r.in_y[1] + r.in_y[2] + r.in_y[3]
    hops = [net.go(r.sum1.at[lax.rem(z + k, 4)], r.in_z.at[k], z_peer(k)) for k in range(1, 4)]
    late.settle(0)
    late.settle(1)
    late_end.second()
    for copy in hops:
        copy.wait_recv()
    r.sum2[...] = r.sum1[z] + r.in_z[1] + r.in_z[2] + r.in_z[3]
    r.in_x[x] = r.sum2[x]
    hops = [net.go(r.sum2.at[lax.rem(x + k, 4)], r.in_x.at[x], x_peer(k)) for k in range(1, 4)]
    early_end.last(r.near_e, r.near_o)
    others.append(net.go(r.near_e, r.got_near_e, sibling()))
    others.append(net.go(r.near_o, r.got_near_o, sibling()))
    late_end.third()
    for copy in hops:
        copy.wait_recv()
    blob = r.in_x[0] + r.in_x[1] + r.in_x[2] + r.in_x[3]
    r.conv_inner[...] = blob[0:5, :48]
    r.mid[...] = blob[ROW_MID : ROW_MID + 1, :48]
    r.norm[...] = blob[ROW_NORM : ROW_NORM + 1, :24]
    r.conv_bc[...] = blob[8:13, :4]
    r.head[...] = blob[13:16, :3]
    late_end.last(r.near_l)
    others.append(net.go(r.near_l, r.got_near_l, sibling()))
    for copy in others:
        copy.wait_recv()

    def put(first_l, second_l, first_e, second_e, first_o, second_o):
        r.inner[:, :LCOLS] = first_l[...]
        r.inner[:, LCOLS:] = second_l[:, : INNER - LCOLS]
        r.bc[...] = second_l[:, INNER - LCOLS : CONV - LCOLS]
        wide = second_l[:, CONV - LCOLS : CONV - LCOLS + 128]
        lane24 = lane_at((24, 128))
        steps = jnp.zeros((24, 128), F32)
        for n in range(OWNERS):
            moved = pltpu.roll(wide, 128 - 5 * n, 1) if n else wide
            steps = jnp.where((lane24 >= 3 * n) & (lane24 < 3 * n + 3), moved, steps)
        r.step[...] = steps[:, :HEADS]
        r.gate[:, :ECOLS] = first_e[...]
        r.gate[:, ECOLS:] = second_e[...]
        r.out[:, :WALF] = first_o[...]
        r.out[:, WALF:] = second_o[...]

    @pl.when(c == 0)
    def _():
        put(r.near_l, r.got_near_l, r.near_e, r.got_near_e, r.near_o, r.got_near_o)

    @pl.when(c == 1)
    def _():
        put(r.got_far_l, r.far_l, r.got_far_e, r.far_e, r.got_far_o, r.far_o)

    net.drain()


def reduce_all(grads, far, backs):
    cell = (4, 4, 16, 128)
    return call(
        reduce_body, "reduce_grads", 6,
        {
            "gl": ("h", grads[0]), "e0a": ("v", grads[1]), "e0b": ("v", grads[2]), "e0o": ("v", grads[3]),
            "far_e": ("v", far[0]), "far_l": ("v", far[1]), "far_o": ("v", far[2]),
            **{
                key + str(n): ("v", getattr(backs[n], key)) for n in range(2) for key in ("gtaps", "ggain", "ghead")
            },
        },
        {
            "inner": in_vmem(24, INNER), "bc": in_vmem(24, 2 * STATE), "step": in_vmem(24, HEADS),
            "gate": in_vmem(24, INNER), "out": in_vmem(48, D), "conv_inner": in_vmem(5, 48), "mid": in_vmem(1, 48),
            "norm": in_vmem(1, 24), "conv_bc": in_vmem(5, 4), "head": in_vmem(3, 3),
        },
        {
            **{
                name + part: pltpu.VMEM(shape, F32)
                for name in ("near_", "got_near_", "got_far_")
                for part, shape in (("e", (24, ECOLS)), ("l", (24, LCOLS)), ("o", (48, WALF)))
            },
            "cells": pltpu.VMEM((2, 4) + cell, F32), "other": pltpu.VMEM((4,) + cell, F32),
            "sum0": pltpu.VMEM((4,) + cell, F32), "in_y": pltpu.VMEM((4,) + cell, F32),
            "sum1": pltpu.VMEM(cell, F32), "in_z": pltpu.VMEM((4,) + cell[1:], F32),
            "sum2": pltpu.VMEM(cell[1:], F32), "in_x": pltpu.VMEM((4, 16, 128), F32),
            **fold_scratch("l", LCOLS, False),
            **fold_targets("l", LCOLS, False, lambda *shape: pltpu.VMEM(shape, BF16)),
            **finish_scratch("e", ECOLS, True), **finish_scratch("l", LCOLS, False), **net_scratch(64),
        },
    )


def deliver_body(*refs):
    count = len(refs) // 2
    for given, made in zip(refs[:count], refs[count:]):
        made[...] = given[...]


def deliver(*arrays):
    return pl.pallas_call(
        deliver_body,
        out_shape=tuple(jax.ShapeDtypeStruct(value.shape, value.dtype) for value in arrays),
        in_specs=[pl.BlockSpec(memory_space=pltpu.VMEM)] * len(arrays),
        out_specs=(pl.BlockSpec(memory_space=pltpu.VMEM),) * len(arrays),
        compiler_params=pltpu.CompilerParams(vmem_limit_bytes=VMEM_LIMIT),
        name="deliver",
    )(*arrays)


def per_device(
    block_input, cotangent, seg_groups, norm_gain, w_gate, w_inner, w_bc, w_step, conv_inner, conv_bc, head_params,
    inner_gain, w_out,
):
    shards = {
        "inner": w_inner[0], "bc": w_bc[0], "step": w_step[0], "gate": w_gate[0], "out": w_out[0],
        "norm": norm_gain, "mid": inner_gain, "conv_inner": conv_inner[0], "conv_bc": conv_bc[0], "head": head_params[0],
    }
    flags = seg_groups
    x = block_input[0]
    start = block_forward(0, flags, x, shards)
    weights = (
        (start.w0.reshape(2, D, HALF), start.wo0.reshape(2, INNER, WALF)),
        (start.next_w.reshape(2, D, HALF), start.next_wo.reshape(2, INNER, WALF)),
    )
    kept = [start, block_forward(1, flags, start.result, weights[1] + (start,))]
    inputs = [x, start.result]

    g = cotangent[0]
    grads = None
    backs = [None, None]
    for layer in (1, 0):
        w, wo = weights[layer]
        back = block_backward(layer, flags, g, inputs[layer], w, wo, start, kept[layer], grads)
        backs[layer] = back
        g = back.result
        hidden = kept[layer].both_hidden.reshape(2 * TOK, D)
        grad_late = dot32(hidden, back.both_gl.reshape(2 * TOK, LCOLS), ((0,), (0,))).astype(BF16)
        grads = (grad_late.reshape(4, 4, 96, LCOLS), back.eha, back.ehb, back.eho)

    final = reduce_all(grads, (backs[0].fin_e, backs[0].fin_l, backs[0].fin_o), backs)
    return deliver(
        kept[1].finals[None, None],
        backs[0].finals[None, None],
        final.norm,
        final.gate[None],
        final.inner[None],
        final.bc[None],
        final.step[None],
        final.conv_inner[None],
        final.conv_bc[None],
        final.head[None],
        final.mid,
        final.out[None],
    )


def solution(mesh):
    weight = P("section", ROWS_ALL, None)
    vector = P("section", ROWS_ALL)
    taps = P("section", None, ROWS_ALL)
    tokens = P("wsh", None, "seq", None)
    heads = P("section", None, "seq")
    result = P("section", "wsh", None, "seq", None)
    return jax.shard_map(
        per_device,
        mesh=mesh,
        in_specs=(
            tokens, tokens, P("wsh", None), vector, weight, weight, weight, weight, taps, taps, heads, vector, weight,
        ),
        out_specs=(
            result, result, vector, weight, weight, weight, weight, taps, taps, heads, vector, weight,
        ),
        check_vma=False,
    )
```

```python
import functools
import types

import jax
import jax.numpy as jnp
from jax import lax
from jax.experimental import pallas as pl
from jax.experimental.pallas import tpu as pltpu
from jax.sharding import PartitionSpec as P

D = 1536
INNER = 3072
HEADS = 48
STATE = 128
BLOCK_LEN = 256
BLOCKS = 8
TOK = 128
CONV = INNER + 2 * STATE
HALF = CONV
GATE0 = 256
CUT = HALF // 2
WALF = D // 2
WCUT = WALF // 2
ECOLS = INNER // 2
LCOLS = HALF // 2 + 128
LSPLIT = LCOLS
OWNERS = 16
OWN = 192
EPS = 1e-05
F32 = jnp.float32
BF16 = jnp.bfloat16
MESH = pl.DeviceIdType.MESH
VMEM_LIMIT = 61 * 1024 * 1024
LANES = (0, 1, 2, 8, 9, 10)
ROWS_ALL = ("seq", "wsh")
ROW_MID, ROW_NORM = 5, 6
ROW_BIAS, ROW_DECAY, ROW_SKIP = 5, 6, 7


def dot32(left, right, dims=((1,), (0,))):
    return lax.dot_general(left, right, (dims, ((), ())), preferred_element_type=F32)


def split_left(exact, value, terms):
    total = None
    for _ in range(terms):
        part = value.astype(BF16)
        value = value - part.astype(F32)
        term = dot32(exact, part)
        total = term if total is None else total + term
    return total


def split_right(value, exact, terms, dims=((1,), (0,))):
    total = None
    for _ in range(terms):
        part = value.astype(BF16)
        value = value - part.astype(F32)
        term = dot32(part, exact, dims)
        total = term if total is None else total + term
    return total


def pair_cols(tile, q):
    lane = lax.broadcasted_iota(jnp.int32, (TOK, 128), 1)
    a = jnp.broadcast_to(tile[:, LANES[2 * q] : LANES[2 * q] + 1], (TOK, 128))
    b = jnp.broadcast_to(tile[:, LANES[2 * q + 1] : LANES[2 * q + 1] + 1], (TOK, 128))
    return a, b, jnp.where(lane < 64, a, b)


def pair_row(row, q):
    lane = lax.broadcasted_iota(jnp.int32, (1, 128), 1)
    a = jnp.broadcast_to(row[:, LANES[2 * q] : LANES[2 * q] + 1], (1, 128))
    b = jnp.broadcast_to(row[:, LANES[2 * q + 1] : LANES[2 * q + 1] + 1], (1, 128))
    return jnp.where(lane < 64, a, b)


def to_front(tile, i):
    return pltpu.roll(tile, lax.rem(128 - 16 * i, 128), 1)


def conv_of(cat, taps):
    total = taps[4:5] + taps[3:4] * cat[8 : 8 + TOK]
    for k in range(3):
        total = total + taps[k : k + 1] * cat[5 + k : 5 + k + TOK]
    return total


def tri_of(lower):
    row = lax.broadcasted_iota(jnp.int32, (TOK, TOK), 0)
    col = lax.broadcasted_iota(jnp.int32, (TOK, TOK), 1)
    return row >= col if lower else row <= col


def head_lanes():
    lane = lax.broadcasted_iota(jnp.int32, (TOK, 128), 1)
    return (lane % 8) < 3


def group_cols(i, q):
    return pl.ds(pl.multiple_of(i * 384 + q * 128, 128), 128)


def gate_cols(i, q):
    return pl.ds(pl.multiple_of(GATE0 + i * 384 + q * 128, 128), 128)


def in_hbm(*shape, dtype=BF16):
    return jax.ShapeDtypeStruct(shape, dtype), pl.BlockSpec(memory_space=pl.ANY)


def in_vmem(*shape, dtype=F32):
    return jax.ShapeDtypeStruct(shape, dtype), pl.BlockSpec(memory_space=pltpu.VMEM)


def saved(*shape, dtype=F32):
    return jax.ShapeDtypeStruct(shape, dtype), None


def call(body, name, ident, inputs, outputs, scratch):
    spaces = {"h": pl.ANY, "v": pltpu.VMEM, "s": pltpu.SMEM, "p": pl.ANY}
    early = [key for key, (kind, _) in inputs.items() if kind == "p"]
    late = [key for key, (_, spec) in outputs.items() if spec is None]
    scratch = dict(scratch)
    for key in early:
        scratch[key] = pltpu.VMEM(inputs[key][1].shape, inputs[key][1].dtype)
    for key in late:
        scratch[key] = pltpu.VMEM(outputs[key][0].shape, outputs[key][0].dtype)
    if early or late:
        scratch["move_sems"] = dma_sems(len(early) + len(late))
    names = [key + "_far" if key in early else key for key in inputs]
    names += [key + "_far" if key in late else key for key in outputs] + list(scratch)

    def kernel(*refs):
        r = types.SimpleNamespace(**dict(zip(names, refs)))

        def mover(key):
            near, far = getattr(r, key), getattr(r, key + "_far")
            src, dst = (far, near) if key in early else (near, far)
            return pltpu.make_async_copy(src, dst, r.move_sems.at[(early + late).index(key)])

        def start(*keys):
            for key in keys:
                mover(key).start()

        def wait(*keys):
            for key in keys:
                mover(key).wait()

        r.move, r.moved = start, wait
        body(r)

    out = pl.pallas_call(
        kernel,
        out_shape=tuple(shape for shape, _ in outputs.values()),
        in_specs=[pl.BlockSpec(memory_space=spaces[kind]) for kind, _ in inputs.values()],
        out_specs=tuple(
            pl.BlockSpec(memory_space=pl.ANY) if spec is None else spec for _, spec in outputs.values()
        ),
        scratch_shapes=list(scratch.values()),
        compiler_params=pltpu.CompilerParams(
            collective_id=ident, has_side_effects=True, vmem_limit_bytes=VMEM_LIMIT
        ),
        name=name,
    )(*[value for _, value in inputs.values()])
    return types.SimpleNamespace(**dict(zip(outputs, out)))


def dma_sems(count):
    return pltpu.SemaphoreType.DMA((count,))


def places():
    section = lax.axis_index("section")
    seq = lax.axis_index("seq")
    return section, seq // 4, lax.rem(seq, 4), lax.axis_index("wsh")


def x_peer(k):
    return {"wsh": lax.rem(lax.axis_index("wsh") + k, 4)}


def z_peer(k):
    _, y, z, _ = places()
    return {"seq": y * 4 + lax.rem(z + k, 4)}


def y_peer(k):
    _, y, z, _ = places()
    return {"seq": lax.rem(y + k, 4) * 4 + z}


def sibling():
    return {"section": 1 - lax.axis_index("section")}


def say_hello(peer):
    pl.semaphore_signal(pltpu.get_barrier_semaphore(), inc=1, device_id=peer, device_id_type=MESH)


def greet_axes():
    for k in range(1, 4):
        for peer in (x_peer(k), y_peer(k), z_peer(k)):
            say_hello(peer)
    say_hello(sibling())
    pl.semaphore_wait(pltpu.get_barrier_semaphore(), 10)


def fetch(src, dst, sem):
    copy = pltpu.make_async_copy(src, dst, sem)
    copy.start()
    return copy


class Net:
    def __init__(self, send, recv):
        self.send, self.recv = send, recv
        self.count = 0
        self.started = []

    def go(self, src, dst, peer):
        copy = pltpu.make_async_remote_copy(
            src_ref=src, dst_ref=dst, send_sem=self.send.at[self.count], recv_sem=self.recv.at[self.count],
            device_id=peer, device_id_type=MESH,
        )
        copy.start()
        self.count += 1
        self.started.append(copy)
        return copy

    def drain(self):
        for copy in self.started:
            copy.wait_send()


class Gather:
    def __init__(self, net, p, o, w, wo, stage, rows, own):
        self.net, self.p, self.o, self.w, self.wo = net, p, o, w, wo
        self.stage, self.rows, self.own = stage, rows, own
        self.place = places()
        self.near, self.far, self.inner, self.passed = {}, {}, {}, []
        self.peers = (y_peer, z_peer, x_peer, x_peer)
        self.inner_peers = (z_peer, y_peer, y_peer, z_peer)

    def band(self, kind, j, moved, half=None):
        c, y, z, x = self.place
        rows = slice(None) if half is None else pl.ds(48 * half, 48)
        many = slice(None) if half is None else pl.ds(2 * half, 2)
        if kind == 0:
            return self.w.at[c, lax.rem(y + 4 - moved, 4), lax.rem(z + 4 - j, 4), rows, pl.ds(0, CUT)]
        if kind == 1:
            return self.w.at[c, lax.rem(y + 4 - j, 4), lax.rem(z + 4 - moved, 4), rows, pl.ds(CUT, CUT)]
        if kind == 2:
            return self.wo.at[c, lax.rem(y + 4 - j, 4), many, lax.rem(x + 4 - moved, 4), :, pl.ds(0, WCUT)]
        return self.wo.at[c, many, lax.rem(z + 4 - j, 4), lax.rem(x + 4 - moved, 4), :, pl.ds(WCUT, WCUT)]

    def pass_on(self, part):
        self.passed.append(self.net.go(part, part, sibling()))

    def begin(self):
        c, y, z, x = self.place
        go = self.net.go
        self.first, self.spots = [], []
        spot = self.wo.at[c, y, z, x]
        for k in range(1, 4):
            self.first.append(go(self.p, self.stage.at[x], x_peer(k)))
            for cols, peer in ((pl.ds(0, WCUT), z_peer), (pl.ds(WCUT, WCUT), y_peer)):
                self.spots.append(go(self.o.at[:, cols], spot.at[:, cols], peer(k)))
        self.own_o = fetch(self.o, spot, self.own.at[0])
        self.stage[x] = self.p[...]

    def rows_in(self):
        c, y, z, x = self.place
        go = self.net.go
        for copy in self.first:
            copy.wait_recv()
        for side in range(2):
            self.rows[:, CUT * side : CUT * side + CUT] = jnp.concatenate(
                [self.stage[n].astype(F32)[24 * side : 24 * side + 24] for n in range(4)], axis=0
            ).astype(BF16)
        for k in (1, 3):
            for kind, cols in ((0, pl.ds(0, CUT)), (1, pl.ds(CUT, CUT))):
                self.inner[kind, k] = go(
                    self.rows.at[:, cols], self.band(kind, 0, 0), self.inner_peers[kind](k)
                )
        own_w = fetch(self.rows, self.w.at[c, y, z], self.own.at[1])
        self.own_o.wait()
        for copy in self.spots:
            copy.wait_recv()
        for k in (1, 3):
            for kind in (2, 3):
                part = self.band(kind, 0, 0)
                self.inner[kind, k] = go(part, part, self.inner_peers[kind](k))
        own_w.wait()
        self.spread(0)

    def spread(self, j):
        if j in (1, 3):
            for kind in range(4):
                self.inner[kind, j].wait_recv()
                part = self.band(kind, j, 0, 0 if j == 1 else 1)
                self.inner[kind, 2, j] = self.net.go(part, part, self.inner_peers[kind](j))
        if j == 2:
            for kind in range(4):
                self.inner[kind, 2, 1].wait_recv()
                self.inner[kind, 2, 3].wait_recv()
        for k in (1, 3):
            for kind in range(4):
                part = self.band(kind, j, 0)
                self.near[kind, j, k] = self.net.go(part, part, self.peers[kind](k))
        for kind in range(4):
            self.pass_on(self.band(kind, j, 0))

    def relay(self, j):
        for k in (1, 3):
            for kind in range(4):
                self.near[kind, j, k].wait_recv()
                part = self.band(kind, j, k)
                if (k == 1) == (j < 2):
                    self.far[kind, j] = self.net.go(part, part, self.peers[kind](k))
                self.pass_on(part)

    def last(self, j):
        for kind in range(4):
            self.far[kind, j].wait_recv()
            self.pass_on(self.band(kind, j, 2))

    def end(self):
        for copy in self.passed:
            copy.wait_recv()


def gather_scratch():
    return {
        "stage": pltpu.VMEM((4, 48, CUT), BF16),
        "rows": pltpu.VMEM((96, HALF), BF16),
        "own": dma_sems(2),
    }


def lane_at(shape):
    return lax.broadcasted_iota(jnp.int32, shape, 1)


def place_chunks(cells, width, total):
    tiles = [jnp.zeros((8, 128), F32) for _ in range(total // 128)]
    lane = lane_at((8, 128))
    for d in range(64):
        t, off = (width * d) // 128, (width * d) % 128
        moved = pltpu.roll(cells(d), off, 1) if off else cells(d)
        stop = off + width
        tiles[t] = jnp.where((lane >= off) & (lane < min(stop, 128)), moved, tiles[t])
        if stop > 128:
            tiles[t + 1] = jnp.where(lane < stop - 128, moved, tiles[t + 1])
    return tiles


def take_chunk(ref, base, width, d):
    start = base + width * d
    t, off = start // 128, start % 128
    tile = ref[:, 128 * t : 128 * t + 128]
    tile = pltpu.roll(tile, 128 - off, 1) if off else tile
    if off + width > 128:
        after = pltpu.roll(ref[:, 128 * t + 128 : 128 * t + 256], 128 - off, 1)
        tile = jnp.where(lane_at((8, 128)) < 128 - off, tile, after)
    return tile


def start_body(r, net, after):
    c, y, z, x = places()

    def stacked(first, second):
        return jnp.concatenate([first.astype(F32), second.astype(F32)], axis=0).astype(BF16)

    r.wide[...] = jnp.zeros_like(r.wide)
    r.wide[0:24, 0:48] = r.step[...].astype(F32)
    lane24 = lane_at((24, 128))
    spread_step = jnp.zeros((24, 128), F32)
    for n in range(OWNERS):
        moved = pltpu.roll(r.wide[0:24, :], 5 * n, 1) if n else r.wide[0:24, :]
        spread_step = jnp.where((lane24 >= 8 * n) & (lane24 < 8 * n + 3), moved, spread_step)
    gate_cut = CUT - GATE0
    r.mine[0, :, : INNER - CUT] = stacked(r.inner[:, : INNER - CUT], r.inner[:, CUT:])
    r.mine[0, :, INNER - CUT :] = stacked(r.inner[:, INNER - CUT : CUT], r.bc[...])
    r.mine[1, :, :128] = stacked(spread_step, r.gate[:, gate_cut : gate_cut + 128])
    r.mine[1, :, 128:GATE0] = stacked(jnp.zeros((24, 128), F32), r.gate[:, gate_cut + 128 : gate_cut + GATE0])
    r.mine[1, :, GATE0:] = stacked(r.gate[:, :gate_cut], r.gate[:, gate_cut + GATE0 :])
    r.blob[...] = jnp.zeros_like(r.blob)
    r.blob[0:5, 0:48] = r.conv_inner[...].astype(F32)
    r.blob[ROW_MID : ROW_MID + 1, 0:48] = r.mid[...].astype(F32)
    r.blob[ROW_NORM : ROW_NORM + 1, 0:24] = r.norm[...].astype(F32)
    r.square_s[...] = jnp.zeros_like(r.square_s)
    r.square_s[0:4, 0:5] = r.conv_bc[0].astype(F32)
    r.blob[8:13, 0:4] = r.square_s[...].T[0:5, 0:4]
    r.blob[13:16, 0:3] = r.head[:, 0, :]
    given = pl.ds(pl.multiple_of((1 - c) * WALF, 128), WALF)
    swaps = [
        net.go(r.mine.at[1 - c], r.half.at[c], sibling()),
        net.go(r.out.at[:, given], r.half_o.at[c], sibling()),
    ]
    small = [net.go(r.blob, r.cells.at[c, y, z, x], x_peer(k)) for k in range(1, 4)]
    r.half[c] = r.mine[c]
    r.half_o[c] = jnp.where(c == 0, r.out[:, :WALF], r.out[:, WALF:])
    r.cells[c, y, z, x] = r.blob[...]
    for copy in swaps:
        copy.wait_recv()
    ga = Gather(net, r.half.at[0], r.half_o.at[0], r.w0, r.wo0, r.stage0, r.rows0, r.own0)
    ga.begin()
    for copy in small:
        copy.wait_recv()
    small = [net.go(r.cells.at[c, y, z], r.cells.at[c, y, z], z_peer(k)) for k in range(1, 4)]
    ga.rows_in()
    after.begin()
    for copy in small:
        copy.wait_recv()
    small = [net.go(r.cells.at[c, y], r.cells.at[c, y], y_peer(k)) for k in range(1, 4)]
    for j in (1, 3, 2):
        ga.spread(j)
    for copy in small:
        copy.wait_recv()
    pair = net.go(r.cells.at[c], r.cells.at[c], sibling())
    ga.relay(0)
    ga.relay(1)
    pair.wait_recv()
    for layer in range(2):
        def first_tile(d):
            return r.cells[layer, d // 16, (d // 4) % 4, d % 4, 0:8]

        def second_tile(d):
            return r.cells[layer, d // 16, (d // 4) % 4, d % 4, 8:16]

        for t, tile in enumerate(place_chunks(first_tile, 48, INNER)):
            r.taps[layer, :, 128 * t : 128 * t + 128] = tile
        for t, tile in enumerate(place_chunks(second_tile, 4, 2 * STATE)):
            r.taps[layer, :, INNER + 128 * t : INNER + 128 * t + 128] = tile
        for t, tile in enumerate(place_chunks(first_tile, 24, D)):
            r.gain[layer, :, 128 * t : 128 * t + 128] = tile
        lane = lane_at((8, 128))
        heads = jnp.zeros((8, 128), F32)
        for j in range(OWNERS):
            moved = pltpu.roll(second_tile(4 * j), 8 * j, 1) if j else second_tile(0)
            heads = jnp.where((lane >= 8 * j) & (lane < 8 * j + 3), moved, heads)
        r.heads[layer] = heads
    ga.relay(3)
    after.rows_in()
    ga.relay(2)
    for j in (0, 1, 3):
        ga.last(j)
    after.spread(1)
    after.spread(3)
    ga.last(2)
    ga.end()
    after.spread(2)


TURNS = (1, 4, 3, 12, 5, 15, 7, 13, 2, 8, 6, 9, 14, 11, 10)


def seq_peer(d):
    _, y, z, _ = places()
    return lax.rem(y + d // 4, 4) * 4 + lax.rem(z + d % 4, 4)


class Exchange:
    def __init__(self, backward, r):
        self.backward, self.r = backward, r
        self.me = lax.axis_index("seq")
        self.section = lax.axis_index("section")

    def first_copy(self, peer, d):
        r = self.r
        return pltpu.make_async_remote_copy(
            src_ref=r.ds.at[peer], dst_ref=r.got.at[self.me], send_sem=r.send_a.at[d], recv_sem=r.recv_a.at[d],
            device_id={"seq": peer}, device_id_type=MESH,
        )

    def send(self, peer):
        _, y, z, _ = places()
        d = lax.rem(peer // 4 + 4 - y, 4) * 4 + lax.rem(lax.rem(peer, 4) + 4 - z, 4)

        @pl.when(d != 0)
        def _():
            self.first_copy(peer, d).start()

        @pl.when(d == 0)
        def _():
            self.r.got[self.me] = self.r.ds[self.me]

    def back_copy(self, d):
        r = self.r
        peer = seq_peer(d)
        return pltpu.make_async_remote_copy(
            src_ref=r.ready.at[peer], dst_ref=r.back.at[self.me], send_sem=r.send_b.at[d], recv_sem=r.recv_b.at[d],
            device_id={"seq": peer}, device_id_type=MESH,
        )

    def scan(self, decays):
        r = self.r

        def rows_of(dec):
            return jnp.concatenate([jnp.broadcast_to(dec[h : h + 1], (64, 128)) for h in range(3)], axis=0)

        for d in TURNS:
            self.first_copy(seq_peer(d), d).wait_recv()
        r.final[...] = jnp.zeros((OWN, STATE), F32)
        r.fade[0] = jnp.ones((8, 128), F32)

        def step(n, carry):
            c = OWNERS - 1 - n if self.backward else n
            state = r.final[...]
            r.kept[c] = state
            dec = decays[c]
            r.final[...] = rows_of(dec) * state + r.got[c].astype(F32)
            r.fade[n + 1] = r.fade[n] * dec
            return carry

        lax.fori_loop(0, OWNERS, step, 0)
        swap = pltpu.make_async_remote_copy(
            src_ref=r.final, dst_ref=r.other, send_sem=r.swap_s.at[0], recv_sem=r.swap_s.at[1],
            device_id=sibling(), device_id_type=MESH,
        )
        swap.start()
        takes = 0 if self.backward else 1
        r.begin[...] = jnp.zeros((OWN, STATE), F32)

        @pl.when(self.section == takes)
        def _():
            swap.wait_recv()
            r.begin[...] = r.other[...]

        begin = r.begin[...]
        for d in TURNS + (0,):
            c = seq_peer(d)
            n = OWNERS - 1 - c if self.backward else c
            value = (r.kept[c] + rows_of(r.fade[n]) * begin).astype(BF16)
            if d == 0:
                r.back[c] = value
            else:
                r.ready[c] = value
                self.back_copy(d).start()

        @pl.when(self.section != takes)
        def _():
            swap.wait_recv()

        swap.wait_send()

    def finish(self):
        for d in TURNS:
            self.back_copy(d).wait_recv()

    def drain(self):
        for d in range(1, OWNERS):
            self.first_copy(seq_peer(d), d).wait_send()
            self.back_copy(d).wait_send()


def exchange_scratch():
    block = pltpu.VMEM((OWNERS, OWN, STATE), BF16)
    part = pltpu.VMEM((OWN, STATE), F32)
    return {
        "ds": block, "got": block, "back": block, "ready": block,
        "kept": pltpu.VMEM((OWNERS, OWN, STATE), F32), "fade": pltpu.VMEM((OWNERS + 1, 8, 128), F32),
        "final": part, "other": part, "begin": part,
        "send_a": dma_sems(OWNERS), "recv_a": dma_sems(OWNERS), "send_b": dma_sems(OWNERS), "recv_b": dma_sems(OWNERS),
        "swap_s": dma_sems(2),
    }


def head_rows_at(ref, i, q):
    parts = []
    for h in (2 * q, 2 * q + 1):
        parts.append(ref[2 * i + h // 3, pl.ds(64 * (h % 3), 64), :])
    return jnp.concatenate(parts, axis=0)


def store_heads(ref, i, q, value):
    for n, h in enumerate((2 * q, 2 * q + 1)):
        ref[2 * i + h // 3, pl.ds(64 * (h % 3), 64), :] = value[64 * n : 64 * n + 64]


def own_group(n):
    return lax.rem(lax.axis_index("seq") // 2 + n, 8)


def greet_layer(rider, forward):
    me = lax.axis_index("seq")
    section = lax.axis_index("section")
    wsh = lax.axis_index("wsh")
    barrier = pltpu.get_barrier_semaphore()
    for d in range(1, OWNERS):
        say_hello({"seq": lax.rem(me + d, OWNERS)})
    say_hello(sibling())
    if rider:
        for k in range(1, 4):
            say_hello(x_peer(k))
    count = OWNERS + (3 if rider else 0)
    late = {"section": 0, "seq": 15, "wsh": wsh}
    if forward:

        @pl.when((section == 1) & ((me == 0) | (me == 4)))
        def _():
            pl.semaphore_signal(barrier, inc=1, device_id=late, device_id_type=MESH)

        more = jnp.where((section == 0) & (me == 15), 2, 0)
    else:

        @pl.when((section == 0) & (me == 15))
        def _():
            for seq in (0, 4):
                pl.semaphore_signal(
                    barrier, inc=1, device_id={"section": 1, "seq": seq, "wsh": wsh}, device_id_type=MESH
                )

        more = jnp.where((section == 1) & ((me == 0) | (me == 4)), 1, 0)
    pl.semaphore_wait(barrier, count + more)


def flags_of(seg):
    section = lax.axis_index("section")
    seq = lax.axis_index("seq")
    starts = [(BLOCKS - seg[0, n]) * (BLOCK_LEN // TOK) for n in range(2)]
    first = jnp.where(section == 0, starts[0], starts[1])
    at_start = seq == first
    second = section == 1

    def number(cond):
        return jnp.where(cond, 1.0, 0.0)

    live = number(seq >= first)
    near = number(jnp.logical_not(at_start) | (second & (first == 0)))
    far = number(at_start & second & (first != 0))
    cross = number((section == 0) & (seq == 15) & (starts[1] != 0))
    return live, near, far, cross


def halo_copy(src, dst, sems, n, section, seq):
    return pltpu.make_async_remote_copy(
        src_ref=src, dst_ref=dst, send_sem=sems.at[n], recv_sem=sems.at[2 + n],
        device_id={"section": section, "seq": seq, "wsh": lax.axis_index("wsh")}, device_id_type=MESH,
    )


class Halo:
    def __init__(self, src, near, far, sems, forward):
        me = lax.axis_index("seq")
        section = lax.axis_index("section")
        edge = 15 if forward else 0
        if forward:
            crossing = (section == 0) & (me == 15)
            jumping = crossing
            self.has_near = (me > 0) | (section == 1)
            self.has_far = (section == 1) & (me == 4)
            target = (1, jnp.where(me == 15, 0, me + 1))
            near_section = jnp.where(crossing, 1, section)
            far_seq, far_section = 4, 1
        else:
            crossing = (section == 1) & (me == 0)
            jumping = (section == 1) & (me == 4)
            self.has_near = (me < 15) | (section == 0)
            self.has_far = (section == 0) & (me == 15)
            target = (0, jnp.where(me == 0, 15, me - 1))
            near_section = jnp.where(crossing, 0, section)
            far_seq, far_section = 15, 0
        self.sends_near = (me != edge) | crossing
        self.sends_far = jumping
        self.near, self.far = near, far
        self.near_copy = halo_copy(src, near, sems, 0, near_section, target[1])
        self.far_copy = halo_copy(src, far, sems, 1, far_section, far_seq)

    def start(self):
        @pl.when(self.sends_near)
        def _():
            self.near_copy.start()

        @pl.when(self.sends_far)
        def _():
            self.far_copy.start()

        @pl.when(jnp.logical_not(self.has_near))
        def _():
            self.near[...] = jnp.zeros_like(self.near)

        @pl.when(jnp.logical_not(self.has_far))
        def _():
            self.far[...] = jnp.zeros_like(self.far)

    def wait(self):
        @pl.when(self.has_near)
        def _():
            self.near_copy.wait_recv()

        @pl.when(self.has_far)
        def _():
            self.far_copy.wait_recv()

    def drain(self):
        @pl.when(self.sends_near)
        def _():
            self.near_copy.wait_send()

        @pl.when(self.sends_far)
        def _():
            self.far_copy.wait_send()


def forward_body(layer, rider, r):
    section = lax.axis_index("section")
    me = lax.axis_index("seq")
    net = Net(r.pair_send, r.pair_recv)
    if rider:
        greet_layer(rider, True)
        bulk = Net(r.net_send, r.net_recv)
        ga = Gather(bulk, r.half.at[1], r.half_o.at[1], r.next_w, r.next_wo, r.stage, r.rows, r.own)
        start_body(r, bulk, ga)
        w, wo = r.w0.reshape(2, D, HALF), r.wo0.reshape(2, INNER, WALF)
    else:
        w, wo = r.w, r.wo
    loads = [fetch(w.at[n], r.w_s.at[n], r.load.at[n]) for n in range(2)]
    load_o = fetch(wo, r.wo_s, r.load.at[2])
    if not rider:
        greet_layer(rider, True)
    ex = Exchange(False, r)
    flags = flags_of(r.flags)
    live = flags[0]
    heads = r.heads[layer]
    x_ref = r.x.at[section] if rider else r.x
    x32 = x_ref[...].astype(F32)
    hidden_inv = lax.rsqrt(jnp.sum(x32 * x32, axis=1, keepdims=True) / D + EPS)
    r.hidden[...] = (x32 * hidden_inv * r.gain[layer, ROW_NORM : ROW_NORM + 1, :]).astype(BF16)
    loads[0].wait()

    def project_main(n, carry):
        cols = pl.ds(pl.multiple_of(n * 256, 256), 256)
        r.pre[:, cols] = dot32(r.hidden[...], r.w_s[0, :, cols]).astype(BF16)
        return carry

    lax.fori_loop(0, HALF // 256, project_main, 0)
    r.tail[...] = r.pre[TOK - 16 :, :]
    halo = Halo(r.tail, r.halo_near, r.halo_far, r.halo_s, True)
    halo.start()
    loads[1].wait()

    def project_side(n, carry):
        cols = pl.ds(pl.multiple_of(n * 256, 256), 256)
        r.side[:, cols] = dot32(r.hidden[...], r.w_s[1, :, cols])
        return carry

    early_tiles = 1 if rider else HALF // 256
    lax.fori_loop(0, early_tiles, project_side, 0)
    r.move("pre")
    pairs = [net.go(r.hidden, r.both_hidden.at[section], sibling())]
    owns = [fetch(r.hidden, r.both_hidden.at[section], r.load.at[3])]
    step = r.side[:, :128].astype(BF16).astype(F32) + heads[ROW_BIAS : ROW_BIAS + 1]
    dt = jnp.maximum(step, 0.0) + jnp.log1p(jnp.exp(-jnp.abs(step)))
    dt = jnp.where(head_lanes(), dt, 0.0) * live
    rate = -dt * jnp.exp(heads[ROW_DECAY : ROW_DECAY + 1])
    cum = split_left(tri_of(True).astype(F32).astype(BF16), rate, 3)
    r.dt[...] = dt
    r.cum[...] = cum
    last = jnp.broadcast_to(cum[TOK - 1 : TOK], (TOK, 128))
    r.dec_s[...] = jnp.exp(last).T.reshape(OWNERS, 8, 128)
    r.dec[me] = r.dec_s[me]

    def dec_copy(d):
        peer = lax.rem(me + d, OWNERS)
        return pltpu.make_async_remote_copy(
            src_ref=r.dec_s.at[peer], dst_ref=r.dec.at[me], send_sem=r.dec_send.at[d], recv_sem=r.dec_recv.at[d],
            device_id={"seq": peer}, device_id_type=MESH,
        )

    for d in range(1, OWNERS):
        dec_copy(d).start()
    weight = dt * jnp.exp(last - cum)
    halo.wait()
    r.halo[...] = jnp.where(
        flags[1] > 0.0, r.halo_near[...], jnp.where(flags[2] > 0.0, r.halo_far[...], jnp.zeros_like(r.halo_far))
    )

    def conv_tile(cols):
        blk = r.pre[:, cols].astype(F32)
        cat = jnp.concatenate([r.halo[:, cols].astype(F32)[8:], blk], axis=0)
        summed = conv_of(cat, r.taps[layer, :, cols])
        sig = 1.0 / (1.0 + jnp.exp(-summed))
        act = summed * sig
        r.act[:, cols] = act
        r.dact[:, cols] = sig * (1.0 + summed * (1.0 - sig))
        return act

    b = conv_tile(pl.ds(INNER, 128)).astype(BF16)
    c = conv_tile(pl.ds(INNER + 128, 128)).astype(BF16)

    def states(n, carry):
        i = own_group(n)
        wt = to_front(weight, i)
        for q in range(3):
            x = conv_tile(group_cols(i, q))
            scaled = (x * pair_cols(wt, q)[2]).astype(BF16)
            store_heads(r.ds, i, q, dot32(scaled, b, ((0,), (0,))).astype(BF16))
        ex.send(2 * i)
        ex.send(2 * i + 1)
        return carry

    lax.fori_loop(0, 8, states, 0)
    r.move("act", "dact")
    lax.fori_loop(early_tiles, HALF // 256, project_side, 0)
    r.move("side")
    if rider:
        ga.relay(0)
    if rider:
        ga.relay(1)
    for d in range(1, OWNERS):
        dec_copy(d).wait_recv()
    ex.scan(r.dec)
    if rider:
        ga.relay(3)
    r.cumt[...] = cum.T
    causal = tri_of(True)
    scores = dot32(c, b, ((1,), (1,)))
    lane = lax.broadcasted_iota(jnp.int32, (TOK, 128), 1)
    r.square[...] = jnp.zeros((TOK, 128), F32)

    def inside(i, carry):
        cum_i = to_front(cum, i)
        dt_i = to_front(dt, i)
        rows = r.cumt[pl.ds(pl.multiple_of(16 * i, 16), 16), :]
        for q in range(3):
            cols = group_cols(i, q)
            cum_a, cum_b, _ = pair_cols(cum_i, q)
            u = r.act[:, cols] * pair_cols(dt_i, q)[2]
            mixes = []
            for cum_h, off in ((cum_a, LANES[2 * q]), (cum_b, LANES[2 * q + 1])):
                gap = cum_h - rows[off : off + 1]
                mixes.append((scores * jnp.exp(jnp.where(causal, gap, -1e30))).astype(BF16))
            terms = jnp.concatenate(
                [jnp.where(lane < 64, u, 0.0).astype(BF16), jnp.where(lane < 64, 0.0, u).astype(BF16)], axis=0
            )
            r.raw[:, cols] = dot32(jnp.concatenate(mixes, axis=1), terms)
        return carry

    lax.fori_loop(0, 8, inside, 0)
    if rider:
        ga.relay(2)
    ex.finish()
    save = fetch(r.back, r.states, r.load.at[4])

    def across(i, carry):
        cum_i = to_front(cum, i)
        skip_i = pltpu.roll(heads, lax.rem(128 - 16 * i, 128), 1)[ROW_SKIP : ROW_SKIP + 1]
        for q in range(3):
            cols = group_cols(i, q)
            state = head_rows_at(r.back, i, q)
            raw = r.raw[:, cols] + jnp.exp(pair_cols(cum_i, q)[2]) * dot32(c, state, ((1,), (1,)))
            r.raw[:, cols] = raw
            y = (raw + pair_row(skip_i, q) * r.act[:, cols]).astype(BF16)
            r.y[:, cols] = y
            gate = r.side[:, gate_cols(i, q)]
            z = y.astype(F32) * (gate / (1.0 + jnp.exp(-gate)))
            r.z[:, cols] = z
            r.square[...] += z * z
        return carry

    lax.fori_loop(0, 8, across, 0)
    r.move("raw", "y")
    if rider:
        ga.last(0)
        ga.last(1)
    total = jnp.sum(r.square[...], axis=1, keepdims=True)
    inv = jnp.broadcast_to(lax.rsqrt(total / INNER + EPS), (TOK, 128))
    r.inv[...] = inv

    def scale(i, carry):
        cols = pl.ds(pl.multiple_of(i * 128, 128), 128)
        mid = r.taps[layer, ROW_MID : ROW_MID + 1, cols]
        r.gated[:, cols] = (r.z[:, cols] * inv * mid).astype(BF16)
        return carry

    lax.fori_loop(0, 24, scale, 0)
    pairs.append(net.go(r.gated, r.both_gated.at[section], sibling()))
    owns.append(fetch(r.gated, r.both_gated.at[section], r.load.at[5]))
    load_o.wait()
    for half in range(2):

        def project(n, carry):
            cols = pl.ds(pl.multiple_of(n * 256, 256), 256)
            full = pl.ds(pl.multiple_of(half * WALF + n * 256, 256), 256)
            branch = dot32(r.gated[...], r.wo_s[half, :, cols])
            r.result[:, full] = (x_ref[:, full].astype(F32) + live * branch).astype(BF16)
            return carry

        lax.fori_loop(0, WALF // 256, project, 0)
    if rider:
        for j in (3, 2):
            ga.last(j)
        ga.end()
        bulk.drain()
    r.moved("pre", "side", "act", "dact", "raw", "y")
    save.wait()
    for copy in owns:
        copy.wait()
    for copy in pairs:
        copy.wait_recv()
    net.drain()
    halo.drain()
    for d in range(1, OWNERS):
        dec_copy(d).wait_send()
    ex.drain()


def block_forward(layer, flags, x, given):
    rider = layer == 0
    inputs = {"flags": ("s", flags), "x": ("v", x)}
    if rider:
        for key, value in given.items():
            inputs[key] = ("v", value)
    else:
        w, wo, small = given
        inputs.update({
            "w": ("h", w), "wo": ("h", wo), "taps": ("v", small.taps), "gain": ("v", small.gain),
            "heads": ("v", small.heads),
        })
    outputs = {
        "act": saved(TOK, CONV), "dact": saved(TOK, CONV), "side": saved(TOK, HALF), "raw": saved(TOK, INNER),
        "dt": in_vmem(TOK, 128), "cum": in_vmem(TOK, 128), "inv": in_vmem(TOK, 128),
        "dec": in_vmem(OWNERS, 8, 128), "pre": saved(TOK, CONV, dtype=BF16), "halo": in_vmem(16, CONV, dtype=BF16),
        "y": saved(TOK, INNER, dtype=BF16), "result": in_vmem(TOK, D, dtype=BF16),
        "states": in_hbm(OWNERS, OWN, STATE), "both_hidden": in_hbm(2, TOK, D), "both_gated": in_hbm(2, TOK, INNER),
    }
    tile = pltpu.VMEM((TOK, 128), F32)
    edge = pltpu.VMEM((16, CONV), BF16)
    scratch = {
        "w_s": pltpu.VMEM((2, D, HALF), BF16), "wo_s": pltpu.VMEM((2, INNER, WALF), BF16),
        "hidden": pltpu.VMEM((TOK, D), BF16), "gated": pltpu.VMEM((TOK, INNER), BF16),
        "z": pltpu.VMEM((TOK, INNER), F32), "cumt": tile, "square": tile,
        "tail": edge, "halo_near": edge, "halo_far": edge, "halo_s": dma_sems(4),
        "dec_s": pltpu.VMEM((OWNERS, 8, 128), F32), "dec_send": dma_sems(OWNERS), "dec_recv": dma_sems(OWNERS),
        "load": dma_sems(6), "pair_send": dma_sems(2), "pair_recv": dma_sems(2),
        **exchange_scratch(),
    }
    if rider:
        outputs.update({
            "w0": in_hbm(2, 4, 4, 96, HALF), "wo0": in_hbm(2, 4, 4, 4, 48, WALF),
            "next_w": in_hbm(2, 4, 4, 96, HALF), "next_wo": in_hbm(2, 4, 4, 4, 48, WALF),
            "taps": in_vmem(2, 8, CONV), "gain": in_vmem(2, 8, D), "heads": in_vmem(2, 8, 128),
        })
        scratch.update({
            "mine": pltpu.VMEM((2, 48, CUT), BF16), "half": pltpu.VMEM((2, 48, CUT), BF16),
            "wide": pltpu.VMEM((24, 128), F32), "blob": pltpu.VMEM((16, 128), F32),
            "square_s": pltpu.VMEM((128, 128), F32),
            "half_o": pltpu.VMEM((2, 48, WALF), BF16), "cells": pltpu.VMEM((2, 4, 4, 4, 16, 128), F32),
            "net_send": dma_sems(400), "net_recv": dma_sems(400),
        })
        scratch.update({key + "0": value for key, value in gather_scratch().items()})
        scratch.update(gather_scratch())
    return call(
        functools.partial(forward_body, layer, rider), "block_forward", 2 + layer, inputs, outputs, scratch
    )


def add_rows(target, *parts):
    lead = target.shape[:-2]
    blocks = functools.reduce(lambda a, b: a * b, lead, 1)

    def body(b, carry):
        spot = (b,) if len(lead) == 1 else (b // lead[1], lax.rem(b, lead[1]))
        total = parts[0][spot].astype(F32)
        for ref in parts[1:]:
            total = total + ref[spot].astype(F32)
        target[spot] = total.astype(target.dtype)
        return carry

    lax.fori_loop(0, blocks, body, 0)


def fold_scratch(tag, cols, with_out):
    shapes = {"a": (4, 96, cols // 2), "b": (4, 96, cols // 2)}
    if with_out:
        shapes["o"] = (4, 4, 48, WALF)
    scratch = {}
    for key, shape in shapes.items():
        scratch[tag + "m" + key] = pltpu.VMEM(shape, BF16)
        scratch[tag + "s" + key] = pltpu.VMEM((2,) + shape, BF16)
    scratch[tag + "own"] = dma_sems(9)
    return scratch


def fold_targets(tag, cols, with_out, make):
    targets = {tag + "ha": make(4, 96, cols // 2), tag + "hb": make(4, 96, cols // 2)}
    if with_out:
        targets[tag + "ho"] = make(4, 4, 48, WALF)
    return targets


class Fold:
    def __init__(self, net, r, tag, cols, gi, go):
        self.net, self.gi, self.go_ref, self.cut = net, gi, go, cols // 2
        self.kinds = (0, 1, 2) if go is not None else (0, 1)
        keys = "abo"
        self.h = [getattr(r, tag + "h" + keys[n]) for n in self.kinds]
        self.m = [getattr(r, tag + "m" + keys[n]) for n in self.kinds]
        self.s = [getattr(r, tag + "s" + keys[n]) for n in self.kinds]
        self.own = getattr(r, tag + "own")
        self.place = places()
        self.peers = (y_peer, z_peer, x_peer)
        self.hops, self.direct, self.loads = {}, {}, {}

    def part(self, kind, t, half):
        _, y, z, x = self.place
        at = pl.ds(2 * half, 2) if half is not None else slice(None)
        if kind == 0:
            return self.gi.at[lax.rem(y + t, 4), at, :, pl.ds(0, self.cut)]
        if kind == 1:
            return self.gi.at[at, lax.rem(z + t, 4), :, pl.ds(self.cut, self.cut)]
        return self.go_ref.at[at, :, lax.rem(x + t, 4)]

    def begin(self, kinds):
        go = self.net.go
        for half, k in ((0, 1), (1, 3)):
            for kind in kinds:
                self.hops[kind, half] = go(
                    self.part(kind, 2, half), self.h[kind].at[pl.ds(2 * half, 2)], self.peers[kind](k)
                )
        for half, k in ((1, 1), (0, 3)):
            for kind in kinds:
                side = 0 if k == 1 else 1
                self.direct[kind, side] = go(
                    self.part(kind, k, half), self.s[kind].at[side, pl.ds(2 * half, 2)], self.peers[kind](k)
                )
        for kind in kinds:
            self.loads[kind] = [
                fetch(self.part(kind, 1, 0), self.m[kind].at[pl.ds(0, 2)], self.own.at[3 * kind]),
                fetch(self.part(kind, 3, 1), self.m[kind].at[pl.ds(2, 2)], self.own.at[3 * kind + 1]),
            ]

    def combine(self, kind):
        for copy in self.loads[kind]:
            copy.wait()
        for half in range(2):
            self.hops[kind, half].wait_recv()
        add_rows(self.m[kind], self.m[kind], self.h[kind])
        peer = self.peers[kind]
        for half, k in ((0, 1), (1, 3)):
            at = pl.ds(2 * half, 2)
            self.hops[kind, half] = self.net.go(self.m[kind].at[at], self.s[kind].at[half, at], peer(k))
        self.loads[kind] = [fetch(self.part(kind, 0, None), self.h[kind], self.own.at[3 * kind + 2])]

    def settle(self, kind):
        for copy in self.loads[kind]:
            copy.wait()
        for side in range(2):
            self.direct[kind, side].wait_recv()
            self.hops[kind, side].wait_recv()
        add_rows(self.h[kind], self.h[kind], self.s[kind].at[0], self.s[kind].at[1])


class Finish:
    def __init__(self, net, r, tag, cols, sums):
        self.net, self.sums, self.cut, self.cols = net, sums, cols // 2, cols
        for key in ("r2a", "r2b", "c3", "r3") + (("r2o", "o2", "r3o") if len(sums) > 2 else ()):
            setattr(self, key, getattr(r, tag + key))
        self.place = places()

    def second(self):
        _, y, z, _ = self.place
        go = self.net.go
        ha, hb = self.sums[:2]
        self.a, self.b, self.o = [], [], []
        for k in range(1, 4):
            self.a.append(go(ha.at[lax.rem(z + k, 4)], self.r2a.at[k], z_peer(k)))
            self.b.append(go(hb.at[lax.rem(y + k, 4)], self.r2b.at[k], y_peer(k)))
        self.r2a[0] = ha[z]
        self.r2b[0] = hb[y]
        if len(self.sums) > 2:
            ho = self.sums[2]
            one, two = pl.ds(0, WCUT), pl.ds(WCUT, WCUT)
            for k in range(1, 4):
                self.o.append(go(ho.at[lax.rem(y + k, 4), :, :, one], self.r2o.at[0, k], y_peer(k)))
                self.o.append(go(ho.at[:, lax.rem(z + k, 4), :, two], self.r2o.at[1, k], z_peer(k)))
            self.r2o[0, 0] = ho[y, :, :, :WCUT]
            for n in range(4):
                self.r2o[1, 0, n] = ho[n, z, :, WCUT:]

    def third(self):
        _, y, z, x = self.place
        go = self.net.go
        for copy in self.a + self.b:
            copy.wait_recv()
        for n in range(4):
            at = pl.ds(24 * n, 24)
            for parts, cols in ((self.r2a, pl.ds(0, self.cut)), (self.r2b, pl.ds(self.cut, self.cut))):
                total = parts[0, at, :].astype(F32)
                for k in range(1, 4):
                    total = total + parts[k, at, :].astype(F32)
                self.c3[n, :, cols] = total
        self.x = [go(self.c3.at[lax.rem(x + k, 4)], self.r3.at[x], x_peer(k)) for k in range(1, 4)]
        self.r3[x] = self.c3[x]
        if self.o:
            for copy in self.o:
                copy.wait_recv()
            for n in range(2):
                add_rows(self.o2.at[n], *[self.r2o.at[n, k] for k in range(4)])
            for k in range(1, 4):
                self.x.append(go(self.o2.at[0, lax.rem(z + k, 4)], self.r3o.at[0, k], z_peer(k)))
                self.x.append(go(self.o2.at[1, lax.rem(y + k, 4)], self.r3o.at[1, k], y_peer(k)))
            self.r3o[0, 0] = self.o2[0, z]
            self.r3o[1, 0] = self.o2[1, y]

    def last(self, in_ref, out_ref=None):
        for copy in self.x:
            copy.wait_recv()
        in_ref[...] = self.r3[0] + self.r3[1] + self.r3[2] + self.r3[3]
        if self.o:
            for n in range(2):
                total = self.r3o[n, 0].astype(F32)
                for k in range(1, 4):
                    total = total + self.r3o[n, k].astype(F32)
                out_ref[:, WCUT * n : WCUT * n + WCUT] = total


def finish_scratch(tag, cols, with_out):
    cut = cols // 2
    scratch = {
        tag + "r2a": pltpu.VMEM((4, 96, cut), BF16), tag + "r2b": pltpu.VMEM((4, 96, cut), BF16),
        tag + "c3": pltpu.VMEM((4, 24, cols), F32), tag + "r3": pltpu.VMEM((4, 24, cols), F32),
    }
    if with_out:
        scratch[tag + "r2o"] = pltpu.VMEM((2, 4, 4, 48, WCUT), BF16)
        scratch[tag + "o2"] = pltpu.VMEM((2, 4, 48, WCUT), BF16)
        scratch[tag + "r3o"] = pltpu.VMEM((2, 4, 48, WCUT), BF16)
    return scratch


def net_scratch(count):
    return {"net_send": dma_sems(count), "net_recv": dma_sems(count)}


def early_products(r, which):
    left, right, stage, target = (
        (r.gated2, r.gb2, r.stage_o, r.go) if which == 0 else (r.hid2, r.dg2, r.stage_e, r.ge)
    )
    tile = stage.shape[1]

    def body(i, carry):
        slot = lax.rem(i, 2)
        rows = pl.ds(pl.multiple_of(i * tile, tile), tile)
        copy = pltpu.make_async_copy(stage.at[slot], target.at[rows], r.stage_s.at[2 * which + slot])

        @pl.when(i >= 2)
        def _():
            copy.wait()

        stage[slot] = dot32(left[:, rows], right[...], ((0,), (0,))).astype(BF16)
        copy.start()
        return carry

    lax.fori_loop(0, target.shape[0] // tile, body, 0)
    for slot in range(2):
        pltpu.make_async_copy(stage.at[slot], target.at[pl.ds(0, tile)], r.stage_s.at[2 * which + slot]).wait()


def backward_body(layer, rider, r):
    section = lax.axis_index("section")
    slots_o, slots_w = r.wo_s.shape[0], r.w_s.shape[0]
    load_state = fetch(r.states, r.state_s, r.load.at[0])
    load_two = [fetch(r.both_hidden, r.hid2, r.load.at[3]), fetch(r.both_gated, r.gated2, r.load.at[4])]

    def wo_tile(i):
        rows = pl.ds(pl.multiple_of(i * 384, 384), 384)
        slot = lax.rem(i, slots_o)
        return pltpu.make_async_copy(r.wo.at[:, rows], r.wo_s.at[slot], r.wo_load.at[slot])

    def w_tile(n):
        slot = lax.rem(n, slots_w)
        rows = pl.ds(pl.multiple_of((n // 2) * 256, 256), 256)
        return pltpu.make_async_copy(r.w.at[lax.rem(n, 2), rows], r.w_s.at[slot], r.w_load.at[slot])

    for n in range(slots_o):
        wo_tile(n).start()
    r.move("side", "y", "act", "raw", "dact", "pre")
    for n in range(slots_w):
        w_tile(n).start()
    greet_layer(True, False)
    net = Net(r.pair_send, r.pair_recv)
    bulk = Net(r.net_send, r.net_recv)
    if rider:
        late = Fold(bulk, r, "l", LCOLS, r.gl, None)
        late.begin((0, 1))
        early_end = Finish(bulk, r, "e", ECOLS, (r.e1a, r.e1b, r.e1o))
        early_end.second()
        late_end = Finish(bulk, r, "l", LCOLS, late.h)
    early = Fold(
        bulk, r, "e", ECOLS, r.ge.reshape(4, 4, 96, ECOLS), r.go.reshape(4, 4, 4, 48, WALF)
    )
    ex = Exchange(True, r)
    flags = flags_of(r.flags)
    live = flags[0]
    heads = r.heads[layer]
    g_ref = r.g if rider else r.g.at[section]
    r.gb[...] = (g_ref[...].astype(F32) * live).astype(BF16)
    inv = r.inv[...]
    dt = r.dt[...]
    cum = r.cum[...]
    r.dots[...] = jnp.zeros((TOK, 128), F32)
    other_half = pl.ds(pl.multiple_of((1 - section) * WALF, 128), WALF)
    own_rows = pl.ds(pl.multiple_of(section * TOK, 128), TOK)
    pairs = [net.go(r.gb.at[:, other_half], r.gb2.at[own_rows], sibling())]
    r.gb2[own_rows, :] = jnp.where(section == 0, r.gb[:, :WALF], r.gb[:, WALF:])
    load_two[1].wait()
    pairs[0].wait_recv()
    early_products(r, 0)
    early.begin((2,))

    def first(i, carry):
        slot = lax.rem(i, slots_o)
        wo_tile(i).wait()
        gg = dot32(r.gb[:, :WALF], r.wo_s[slot, 0], ((1,), (1,)))
        gg = gg + dot32(r.gb[:, WALF:], r.wo_s[slot, 1], ((1,), (1,)))

        @pl.when(i + slots_o < 8)
        def _():
            wo_tile(i + slots_o).start()

        r.gg[:, pl.ds(pl.multiple_of(i * 384, 384), 384)] = gg
        for q in range(3):
            cols = group_cols(i, q)
            gate = r.side[:, gate_cols(i, q)]
            z = r.y[:, cols].astype(F32) * (gate / (1.0 + jnp.exp(-gate)))
            mid = r.taps[layer, ROW_MID : ROW_MID + 1, cols]
            r.dots[...] += gg[:, 128 * q : 128 * q + 128] * mid * z
        return carry

    r.moved("side", "y")
    lax.fori_loop(0, 8, first, 0)
    r.moved("act")
    b = r.act[:, INNER : INNER + 128].astype(BF16)
    c = r.act[:, INNER + 128 : CONV].astype(BF16)
    total = jnp.broadcast_to(jnp.sum(r.dots[...], axis=1, keepdims=True), (TOK, 128))
    shift = total * inv * inv * inv / INNER
    r.gtaps[...] = jnp.zeros_like(r.gtaps)

    def second(n, carry):
        i = own_group(n)
        cum_i = to_front(cum, i)
        for q in range(3):
            cols = group_cols(i, q)
            gate = r.side[:, gate_cols(i, q)]
            y = r.y[:, cols].astype(F32)
            gg = r.gg[:, cols]
            sig = 1.0 / (1.0 + jnp.exp(-gate))
            act = gate * sig
            z = y * act
            dz = gg * r.taps[layer, ROW_MID : ROW_MID + 1, cols] * inv - z * shift
            dy = (dz * act).astype(BF16)
            r.dy[:, cols] = dy
            r.gside[:, gate_cols(i, q)] = (dz * y * (sig * (1.0 + gate * (1.0 - sig)))).astype(BF16)
            r.gtaps[ROW_MID : ROW_MID + 1, cols] = jnp.sum(gg * z * inv, axis=0, keepdims=True)
            far = (dy.astype(F32) * jnp.exp(pair_cols(cum_i, q)[2])).astype(BF16)
            store_heads(r.ds, i, q, dot32(far, c, ((0,), (0,))).astype(BF16))
        ex.send(2 * i)
        ex.send(2 * i + 1)
        return carry

    lax.fori_loop(0, 8, second, 0)
    other_cols = pl.ds(pl.multiple_of(GATE0 + (1 - section) * ECOLS, 128), ECOLS)
    pairs.append(net.go(r.gside.at[:, other_cols], r.dg2.at[own_rows], sibling()))
    r.dg2[own_rows, :] = jnp.where(
        section == 0, r.gside[:, GATE0 : GATE0 + ECOLS], r.gside[:, GATE0 + ECOLS :]
    )
    if rider:
        late.combine(0)
        late.combine(1)
    load_two[0].wait()
    pairs[1].wait_recv()
    early_products(r, 1)
    ex.scan(r.dec)
    early.begin((0, 1))
    load_state.wait()
    r.cumt[...] = cum.T
    causal = tri_of(True)
    scores = dot32(c, b, ((1,), (1,)))
    lane = lax.broadcasted_iota(jnp.int32, (TOK, 128), 1)
    pick_row = lax.broadcasted_iota(jnp.int32, (128, 128), 0)
    pick_col = lax.broadcasted_iota(jnp.int32, (128, 128), 1)
    picks = []
    for q in range(3):
        target = jnp.where(pick_row < 64, LANES[2 * q], LANES[2 * q + 1])
        picks.append((pick_col == target).astype(F32).astype(BF16))
    for ref in (r.dscore, r.grad_b, r.grad_c, r.xdu, r.dyy, r.thin):
        ref[...] = jnp.zeros_like(ref)

    def inside(i, carry):
        cum_i = to_front(cum, i)
        dt_i = to_front(dt, i)
        rows = r.cumt[pl.ds(pl.multiple_of(16 * i, 16), 16), :]
        for q in range(3):
            cols = group_cols(i, q)
            cum_a, cum_b, cum_x = pair_cols(cum_i, q)
            u16 = (r.act[:, cols] * pair_cols(dt_i, q)[2]).astype(BF16)
            dy16 = r.dy[:, cols]
            nil = jnp.zeros_like(dy16)
            dys = jnp.concatenate([jnp.where(lane < 64, dy16, nil), jnp.where(lane < 64, nil, dy16)], axis=0)
            both = dot32(dys, u16, ((1,), (1,)))
            mixes = []
            for n, (cum_h, off) in enumerate(((cum_a, LANES[2 * q]), (cum_b, LANES[2 * q + 1]))):
                gap = cum_h - rows[off : off + 1]
                decay = jnp.exp(jnp.where(causal, gap, -1e30))
                mixes.append((scores * decay).astype(BF16))
                r.dscore[...] += both[n * TOK : n * TOK + TOK] * decay
            r.gg[:, cols] = dot32(jnp.concatenate(mixes, axis=0), dys, ((0,), (0,)))
            far = (dy16.astype(F32) * jnp.exp(cum_x)).astype(BF16)
            r.grad_c[...] += dot32(far, head_rows_at(r.state_s, i, q))
        return carry

    lax.fori_loop(0, 8, inside, 0)
    if rider:
        late.settle(0)
        late.settle(1)
        late_end.second()

    def conv_back(cols, gact):
        gsum = gact * r.dact[:, cols]
        r.gsum[:, cols] = gsum
        blk = r.pre[:, cols].astype(F32)
        cat = jnp.concatenate([r.halo[:, cols].astype(F32)[8:], blk], axis=0)
        sums = [jnp.sum(gsum * cat[5 + k : 5 + k + TOK], axis=0, keepdims=True) for k in range(4)]
        sums.append(jnp.sum(gsum, axis=0, keepdims=True))
        r.gtaps[0:5, cols] = jnp.concatenate(sums, axis=0)

    r.moved("raw", "dact", "pre")
    ex.finish()

    def across(i, carry):
        cum_i = to_front(cum, i)
        dt_i = to_front(dt, i)
        skip_i = pltpu.roll(heads, lax.rem(128 - 16 * i, 128), 1)[ROW_SKIP : ROW_SKIP + 1]
        x_du = jnp.zeros((TOK, 128), F32)
        dy_y = jnp.zeros((TOK, 128), F32)
        thin = jnp.zeros((16, 128), F32)
        edges = {}
        for q in range(3):
            cols = group_cols(i, q)
            x = r.act[:, cols]
            cum_x = pair_cols(cum_i, q)[2]
            dt_x = pair_cols(dt_i, q)[2]
            fade = jnp.exp(cum_x[TOK - 1 : TOK] - cum_x)
            u = x * dt_x
            dy = r.dy[:, cols].astype(F32)
            state16 = head_rows_at(r.state_s, i, q)
            dstate16 = head_rows_at(r.back, i, q)
            du_far = fade * dot32(b, dstate16, ((1,), (1,)))
            du = r.gg[:, cols] + du_far
            r.grad_b[...] += dot32((u * fade).astype(BF16), dstate16)
            overlap = state16.astype(F32) * dstate16.astype(F32)
            edges[LANES[2 * q]] = jnp.sum(overlap[:64], axis=0, keepdims=True)
            edges[LANES[2 * q + 1]] = jnp.sum(overlap[64:], axis=0, keepdims=True)
            x_du = x_du + split_right(x * du, picks[q], 2)
            dy_y = dy_y + split_right(dy * r.raw[:, cols], picks[q], 2)
            thin = thin + split_right(
                jnp.concatenate(
                    [
                        jnp.broadcast_to(jnp.sum(u * du_far, axis=0, keepdims=True), (8, 128)),
                        jnp.broadcast_to(jnp.sum(dy * x, axis=0, keepdims=True), (8, 128)),
                    ],
                    axis=0,
                ),
                picks[q],
                3,
            )
            conv_back(cols, du * dt_x + pair_row(skip_i, q) * dy)
        nothing = jnp.zeros((1, 128), F32)
        r.edge[pl.ds(pl.multiple_of(16 * i, 16), 16), :] = jnp.concatenate(
            [edges.get(k, nothing) for k in range(16)], axis=0
        )
        r.xdu[...] += pltpu.roll(x_du, 16 * i, 1)
        r.dyy[...] += pltpu.roll(dy_y, 16 * i, 1)
        r.thin[...] += pltpu.roll(thin, 16 * i, 1)
        return carry

    lax.fori_loop(0, 8, across, 0)
    early.combine(2)
    early.combine(0)
    early.combine(1)
    dscore16 = r.dscore[...].astype(BF16)
    conv_back(pl.ds(INNER, 128), r.grad_b[...] + dot32(dscore16, c, ((0,), (0,))))
    conv_back(pl.ds(INNER + 128, 128), r.grad_c[...] + dot32(dscore16, b))
    r.tail[...] = r.gsum[:8, :]
    halo = Halo(r.tail, r.halo_near, r.halo_far, r.halo_s, False)
    halo.start()
    ones = jnp.ones((128, 128), BF16)
    edge = split_right(r.edge[...], ones, 3).T[0:1] * jnp.exp(cum[TOK - 1 : TOK]) + r.thin[0:1]
    x_du = r.xdu[...]
    drate = split_left(tri_of(False).astype(F32).astype(BF16), r.dyy[...] - dt * x_du, 3) + edge
    speed = jnp.exp(heads[ROW_DECAY : ROW_DECAY + 1])
    ddt = x_du - drate * speed
    step = r.side[:, :128].astype(BF16).astype(F32) + heads[ROW_BIAS : ROW_BIAS + 1]
    dstep = jnp.where(head_lanes(), ddt / (1.0 + jnp.exp(-step)), 0.0) * live
    r.gside[:, :128] = dstep.astype(BF16)
    r.gside[:, 128:GATE0] = jnp.zeros((TOK, 128), BF16)
    r.ghead[...] = jnp.concatenate(
        [
            jnp.zeros((5, 128), F32),
            jnp.sum(dstep, axis=0, keepdims=True),
            jnp.sum(-drate * dt * speed, axis=0, keepdims=True),
            r.thin[8:9],
        ],
        axis=0,
    )
    halo.wait()
    after = jnp.where(flags[3] > 0.0, r.halo_far[...], r.halo_near[...])
    r.halo_near[...] = jnp.where(live > 0.0, after, jnp.zeros_like(after))

    def conv_tile(i, carry):
        cols = pl.ds(pl.multiple_of(i * 128, 128), 128)
        cat = jnp.concatenate([r.gsum[:, cols], r.halo_near[:, cols]], axis=0)
        taps = r.taps[layer, :, cols]
        total = taps[3:4] * cat[:TOK]
        for k in range(3):
            total = total + taps[k : k + 1] * cat[3 - k : 3 - k + TOK]
        r.gpre[:, cols] = total.astype(BF16)
        return carry

    lax.fori_loop(0, CONV // 128, conv_tile, 0)
    if rider:
        early_end.third()
        late_end.third()

    tail_cols = HALF - LCOLS
    side_cols = pl.ds(0, GATE0)
    both_gl = r.both_gl if rider else r.gl2
    moves = (
        net_copy(net, r.gpre.at[:, pl.ds(LCOLS, tail_cols)], both_gl.at[0, :, pl.ds(0, tail_cols)], 2),
        net_copy(net, r.gside.at[:, side_cols], both_gl.at[0, :, pl.ds(tail_cols, GATE0)], 3),
        net_copy(net, r.gpre.at[:, pl.ds(0, LCOLS)], both_gl.at[1], 2),
    )
    keeps = (
        pltpu.make_async_copy(r.gpre.at[:, pl.ds(LCOLS, tail_cols)], both_gl.at[1, :, pl.ds(0, tail_cols)], r.load.at[1]),
        pltpu.make_async_copy(r.gside.at[:, side_cols], both_gl.at[1, :, pl.ds(tail_cols, GATE0)], r.load.at[2]),
        pltpu.make_async_copy(r.gpre.at[:, pl.ds(0, LCOLS)], both_gl.at[0], r.load.at[1]),
    )

    @pl.when(section == 0)
    def _():
        moves[0].start()
        moves[1].start()
        keeps[2].start()

    @pl.when(section == 1)
    def _():
        moves[2].start()
        keeps[0].start()
        keeps[1].start()

    def project(n, carry):
        rows = pl.ds(pl.multiple_of(n * 256, 256), 256)
        w_tile(2 * n).wait()
        value = dot32(r.gpre[...], r.w_s[lax.rem(2 * n, slots_w)], ((1,), (1,)))

        @pl.when(2 * n + slots_w < 12)
        def _():
            w_tile(2 * n + slots_w).start()

        w_tile(2 * n + 1).wait()
        value = value + dot32(r.gside[...], r.w_s[lax.rem(2 * n + 1, slots_w)], ((1,), (1,)))

        @pl.when(2 * n + 1 + slots_w < 12)
        def _():
            w_tile(2 * n + 1 + slots_w).start()

        r.gg[:, rows] = value
        return carry

    lax.fori_loop(0, D // 256, project, 0)
    x = (r.x[section] if rider else r.x[...]).astype(F32)
    grad = r.gg[:, :D]
    inv_x = lax.rsqrt(jnp.sum(x * x, axis=1, keepdims=True) / D + EPS)
    scaled = grad * r.gain[layer, ROW_NORM : ROW_NORM + 1, :]
    dots = jnp.sum(scaled * x, axis=1, keepdims=True)
    dx = scaled * inv_x - x * (dots * inv_x * inv_x * inv_x / D)
    r.result[...] = (g_ref[...].astype(F32) + dx).astype(BF16)
    r.ggain[...] = jnp.broadcast_to(jnp.sum(grad * x * inv_x, axis=0, keepdims=True), (8, D))
    if rider:
        early_end.last(r.fin_e, r.fin_o)
        late_end.last(r.fin_l)

    @pl.when(section == 0)
    def _():
        moves[0].wait_send()
        moves[1].wait_send()
        keeps[2].wait()
        moves[2].wait_recv()

    @pl.when(section == 1)
    def _():
        moves[2].wait_send()
        keeps[0].wait()
        keeps[1].wait()
        moves[0].wait_recv()
        moves[1].wait_recv()

    if not rider:
        tile = r.stage_l.shape[1]
        late_grads = jnp.concatenate([r.gl2[0], r.gl2[1]], axis=0)
        writes = []
        for n in range(D // tile):
            rows = pl.ds(n * tile, tile)
            if n >= 2:
                writes[n - 2].wait()
            r.stage_l[n % 2] = dot32(r.hid2[:, rows], late_grads, ((0,), (0,))).astype(BF16)
            writes.append(fetch(r.stage_l.at[n % 2], r.glate.at[rows], r.late_s.at[n % 2]))
    for kind in range(3):
        early.settle(kind)
    if not rider:
        for copy in writes[-2:]:
            copy.wait()
    bulk.drain()
    net.drain()
    halo.drain()
    ex.drain()


def net_copy(net, src, dst, n):
    return pltpu.make_async_remote_copy(
        src_ref=src, dst_ref=dst, send_sem=net.send.at[n], recv_sem=net.recv.at[n],
        device_id=sibling(), device_id_type=MESH,
    )


def block_backward(layer, flags, g, x, w, wo, small, kept, grads):
    rider = grads is not None
    inputs = {
        "flags": ("s", flags), "g": ("v", g), "x": ("v", x), "w": ("h", w), "wo": ("h", wo), "taps": ("v", small.taps),
        "gain": ("v", small.gain), "heads": ("v", small.heads), "states": ("h", kept.states),
        "both_hidden": ("h", kept.both_hidden.reshape(2 * TOK, D)),
        "both_gated": ("h", kept.both_gated.reshape(2 * TOK, INNER)),
    }
    for key in ("dt", "cum", "inv", "dec", "halo"):
        inputs[key] = ("v", getattr(kept, key))
    for key in ("side", "y", "act", "raw", "dact", "pre"):
        inputs[key] = ("p", getattr(kept, key))
    outputs = {
        "result": in_vmem(TOK, D, dtype=BF16),
        "gtaps": in_vmem(8, CONV), "ggain": in_vmem(8, D), "ghead": in_vmem(8, 128),
        "ge": in_hbm(D, ECOLS), "go": in_hbm(INNER, WALF),
        **fold_targets("e", ECOLS, True, lambda *shape: in_vmem(*shape, dtype=BF16)),
    }
    tile = pltpu.VMEM((TOK, 128), F32)
    edge = pltpu.VMEM((8, CONV), F32)
    slots, tile_rows = (2, 128) if rider else (3, 512)
    scratch = {
        "wo_s": pltpu.VMEM((slots, 2, 384, WALF), BF16), "w_s": pltpu.VMEM((slots, 256, HALF), BF16),
        "wo_load": dma_sems(slots), "w_load": dma_sems(slots), "load": dma_sems(5),
        "hid2": pltpu.VMEM((2 * TOK, D), BF16), "gated2": pltpu.VMEM((2 * TOK, INNER), BF16),
        "gb2": pltpu.VMEM((2 * TOK, WALF), BF16), "dg2": pltpu.VMEM((2 * TOK, ECOLS), BF16),
        "stage_o": pltpu.VMEM((2, tile_rows, WALF), BF16), "stage_e": pltpu.VMEM((2, tile_rows, ECOLS), BF16), "stage_s": dma_sems(4),
        "state_s": pltpu.VMEM((OWNERS, OWN, STATE), BF16),
        "gb": pltpu.VMEM((TOK, D), BF16), "gg": pltpu.VMEM((TOK, INNER), F32), "dy": pltpu.VMEM((TOK, INNER), BF16),
        "gsum": pltpu.VMEM((TOK, CONV), F32), "gpre": pltpu.VMEM((TOK, HALF), BF16), "gside": pltpu.VMEM((TOK, HALF), BF16),
        "dots": tile, "cumt": tile, "edge": tile, "dscore": tile, "grad_b": tile, "grad_c": tile, "xdu": tile, "dyy": tile,
        "thin": pltpu.VMEM((16, 128), F32),
        "tail": edge, "halo_near": edge, "halo_far": edge, "halo_s": dma_sems(4),
        "pair_send": dma_sems(4), "pair_recv": dma_sems(4),
        **exchange_scratch(), **fold_scratch("e", ECOLS, True), **net_scratch(64),
    }
    if not rider:
        outputs["glate"] = in_hbm(D, LCOLS)
        scratch.update({
            "gl2": pltpu.VMEM((2, TOK, LCOLS), BF16), "stage_l": pltpu.VMEM((2, 256, LCOLS), BF16), "late_s": dma_sems(2),
        })
    if rider:
        outputs["both_gl"] = in_hbm(2, TOK, LCOLS)
        inputs.update({"gl": ("h", grads[0]), "e1a": ("v", grads[1]), "e1b": ("v", grads[2]), "e1o": ("v", grads[3])})
        outputs.update({"fin_e": in_vmem(24, ECOLS), "fin_l": in_vmem(24, LCOLS), "fin_o": in_vmem(48, WALF)})
        scratch.update(fold_scratch("l", LCOLS, False))
        scratch.update(fold_targets("l", LCOLS, False, lambda *shape: pltpu.VMEM(shape, BF16)))
        scratch.update(finish_scratch("e", ECOLS, True))
        scratch.update(finish_scratch("l", LCOLS, False))
    return call(
        functools.partial(backward_body, layer, rider), "block_backward", 4 + layer, inputs, outputs, scratch
    )


def reduce_body(r):
    c, y, z, x = places()
    greet_axes()
    net = Net(r.net_send, r.net_recv)
    late = Fold(net, r, "l", LCOLS, r.gl, None)
    late.begin((0, 1))
    early_end = Finish(net, r, "e", ECOLS, (r.e0a, r.e0b, r.e0o))
    early_end.second()
    late_end = Finish(net, r, "l", LCOLS, late.h)
    results = []
    for n, (first, second, target) in enumerate(((r.y0, r.y1, r.ys), (r.x0, r.x1, r.xs))):
        cross = [
            pltpu.make_async_remote_copy(
                src_ref=src, dst_ref=target.at[c], send_sem=r.final_s.at[3 * n], recv_sem=r.final_s.at[3 * n + 1],
                device_id=sibling(), device_id_type=MESH,
            )
            for src in (second, first)
        ]
        stay = [pltpu.make_async_copy(src, target.at[c], r.final_s.at[3 * n + 2]) for src in (first, second)]
        for core in range(2):

            @pl.when(c == core)
            def _():
                cross[core].start()
                stay[core].start()

        results.append((cross[0], stay[0]))
    row = lax.broadcasted_iota(jnp.int32, (8, 128), 0)
    lane = lane_at((8, 128))
    for layer in range(2):
        taps, gain, heads = (getattr(r, key + str(layer)) for key in ("gtaps", "ggain", "ghead"))
        for d in range(64):
            cell = (layer, d // 16, (d // 4) % 4, d % 4)
            first = jnp.where(lane < 48, take_chunk(taps, 0, 48, d), 0.0)
            norm = jnp.where(lane < 24, take_chunk(gain, 0, 24, d), 0.0)
            r.cells[cell + (slice(0, 8),)] = jnp.where(row == ROW_NORM, norm, first)
            second = jnp.where(lane < 4, take_chunk(taps, INNER, 4, d), 0.0)
            head = jnp.where(lane < 3, take_chunk(heads, 0, 8, d // 4), 0.0)
            r.cells[cell + (slice(8, 16),)] = jnp.where(row >= 5, head, second)
    pair = net.go(r.cells.at[1 - c], r.other, sibling())
    others = [
        net.go(r.far_e, r.got_far_e, sibling()),
        net.go(r.far_l, r.got_far_l, sibling()),
        net.go(r.far_o, r.got_far_o, sibling()),
    ]
    pair.wait_recv()
    r.sum0[...] = r.cells[c] + r.other[...]
    hops = [net.go(r.sum0.at[lax.rem(y + k, 4)], r.in_y.at[k], y_peer(k)) for k in range(1, 4)]
    late.combine(0)
    late.combine(1)
    early_end.third()
    for copy in hops:
        copy.wait_recv()
    r.sum1[...] = r.sum0[y] + r.in_y[1] + r.in_y[2] + r.in_y[3]
    hops = [net.go(r.sum1.at[lax.rem(z + k, 4)], r.in_z.at[k], z_peer(k)) for k in range(1, 4)]
    late.settle(0)
    late.settle(1)
    late_end.second()
    for copy in hops:
        copy.wait_recv()
    r.sum2[...] = r.sum1[z] + r.in_z[1] + r.in_z[2] + r.in_z[3]
    r.in_x[x] = r.sum2[x]
    hops = [net.go(r.sum2.at[lax.rem(x + k, 4)], r.in_x.at[x], x_peer(k)) for k in range(1, 4)]
    early_end.last(r.near_e, r.near_o)
    others.append(net.go(r.near_e, r.got_near_e, sibling()))
    others.append(net.go(r.near_o, r.got_near_o, sibling()))
    late_end.third()
    for copy in hops:
        copy.wait_recv()
    blob = r.in_x[0] + r.in_x[1] + r.in_x[2] + r.in_x[3]
    for n in range(5):
        r.conv_inner[n] = blob[n : n + 1, :48]
    r.mid[...] = blob[ROW_MID : ROW_MID + 1, :48]
    r.norm[...] = blob[ROW_NORM : ROW_NORM + 1, :24]
    r.square_s[...] = jnp.zeros_like(r.square_s)
    r.square_s[0:16, :] = blob
    r.conv_bc[0] = r.square_s[...].T[0:4, 8:13]
    for n in range(3):
        r.head[n] = blob[13 + n : 14 + n, :3]
    late_end.last(r.near_l)
    others.append(net.go(r.near_l, r.got_near_l, sibling()))
    for copy in others:
        copy.wait_recv()
    for cross, stay in results:
        cross.wait_recv()
        cross.wait_send()
        stay.wait()

    def put(first_l, second_l, first_e, second_e, first_o, second_o):
        r.inner[:, :LCOLS] = first_l[...]
        r.inner[:, LCOLS:] = second_l[:, : INNER - LCOLS]
        r.bc[...] = second_l[:, INNER - LCOLS : CONV - LCOLS]
        wide = second_l[:, CONV - LCOLS : CONV - LCOLS + 128]
        lane24 = lane_at((24, 128))
        steps = jnp.zeros((24, 128), F32)
        for n in range(OWNERS):
            moved = pltpu.roll(wide, 128 - 5 * n, 1) if n else wide
            steps = jnp.where((lane24 >= 3 * n) & (lane24 < 3 * n + 3), moved, steps)
        r.step[...] = steps[:, :HEADS]
        r.gate[:, :ECOLS] = first_e[...]
        r.gate[:, ECOLS:] = second_e[...]
        r.out[:, :WALF] = first_o[...]
        r.out[:, WALF:] = second_o[...]

    @pl.when(c == 0)
    def _():
        put(r.near_l, r.got_near_l, r.near_e, r.got_near_e, r.near_o, r.got_near_o)

    @pl.when(c == 1)
    def _():
        put(r.got_far_l, r.far_l, r.got_far_e, r.far_e, r.got_far_o, r.far_o)

    net.drain()


def reduce_all(grads, far, backs, outs):
    cell = (4, 4, 16, 128)
    return call(
        reduce_body, "reduce_grads", 6,
        {
            "gl": ("h", grads[0]), "e0a": ("v", grads[1]), "e0b": ("v", grads[2]), "e0o": ("v", grads[3]),
            "y0": ("v", outs[0]), "y1": ("v", outs[1]), "x0": ("v", backs[0].result), "x1": ("v", backs[1].result),
            "far_e": ("v", far[0]), "far_l": ("v", far[1]), "far_o": ("v", far[2]),
            **{
                key + str(n): ("v", getattr(backs[n], key)) for n in range(2) for key in ("gtaps", "ggain", "ghead")
            },
        },
        {
            "ys": in_hbm(2, TOK, D), "xs": in_hbm(2, TOK, D),
            "inner": in_vmem(24, INNER), "bc": in_vmem(24, 2 * STATE), "step": in_vmem(24, HEADS),
            "gate": in_vmem(24, INNER), "out": in_vmem(48, D), "conv_inner": in_vmem(5, 1, 48), "mid": in_vmem(1, 48),
            "norm": in_vmem(1, 24), "conv_bc": in_vmem(1, 4, 5), "head": in_vmem(3, 1, 3),
        },
        {
            **{
                name + part: pltpu.VMEM(shape, F32)
                for name in ("near_", "got_near_", "got_far_")
                for part, shape in (("e", (24, ECOLS)), ("l", (24, LCOLS)), ("o", (48, WALF)))
            },
            "final_s": dma_sems(6), "square_s": pltpu.VMEM((128, 128), F32),
            "cells": pltpu.VMEM((2, 4) + cell, F32), "other": pltpu.VMEM((4,) + cell, F32),
            "sum0": pltpu.VMEM((4,) + cell, F32), "in_y": pltpu.VMEM((4,) + cell, F32),
            "sum1": pltpu.VMEM(cell, F32), "in_z": pltpu.VMEM((4,) + cell[1:], F32),
            "sum2": pltpu.VMEM(cell[1:], F32), "in_x": pltpu.VMEM((4, 16, 128), F32),
            **fold_scratch("l", LCOLS, False),
            **fold_targets("l", LCOLS, False, lambda *shape: pltpu.VMEM(shape, BF16)),
            **finish_scratch("e", ECOLS, True), **finish_scratch("l", LCOLS, False), **net_scratch(64),
        },
    )


def deliver_body(*refs):
    count = len(refs) // 2
    for given, made in zip(refs[:count], refs[count:]):
        made[...] = given[...]


def deliver(*arrays):
    return pl.pallas_call(
        deliver_body,
        out_shape=tuple(jax.ShapeDtypeStruct(value.shape, value.dtype) for value in arrays),
        in_specs=[pl.BlockSpec(memory_space=pltpu.VMEM)] * len(arrays),
        out_specs=(pl.BlockSpec(memory_space=pltpu.VMEM),) * len(arrays),
        compiler_params=pltpu.CompilerParams(vmem_limit_bytes=VMEM_LIMIT),
        name="deliver",
    )(*arrays)


def per_device(
    block_input, cotangent, seg_groups, norm_gain, w_gate, w_inner, w_bc, w_step, conv_inner, conv_bc, head_params,
    inner_gain, w_out,
):
    shards = {
        "inner": w_inner[0], "bc": w_bc[0], "step": w_step[0], "gate": w_gate[0], "out": w_out[0],
        "norm": norm_gain, "mid": inner_gain, "conv_inner": conv_inner[0], "conv_bc": conv_bc.transpose(0, 2, 1),
        "head": head_params.transpose(1, 0, 2),
    }
    flags = seg_groups
    x = block_input[0]
    start = block_forward(0, flags, x, shards)
    weights = (
        (start.w0.reshape(2, D, HALF), start.wo0.reshape(2, INNER, WALF)),
        (start.next_w.reshape(2, D, HALF), start.next_wo.reshape(2, INNER, WALF)),
    )
    kept = [start, block_forward(1, flags, start.result, weights[1] + (start,))]
    inputs = [x, start.result]

    g = cotangent[0]
    grads = None
    backs = [None, None]
    for layer in (1, 0):
        w, wo = weights[layer]
        back = block_backward(layer, flags, g, inputs[layer], w, wo, start, kept[layer], grads)
        backs[layer] = back
        g = back.result
        if layer == 1:
            grad_late = back.glate
        else:
            hidden = kept[layer].both_hidden.reshape(2 * TOK, D)
            grad_late = dot32(hidden, back.both_gl.reshape(2 * TOK, LCOLS), ((0,), (0,))).astype(BF16)
        grads = (grad_late.reshape(4, 4, 96, LCOLS), back.eha, back.ehb, back.eho)

    final = reduce_all(
        grads, (backs[0].fin_e, backs[0].fin_l, backs[0].fin_o), backs, (kept[0].result, kept[1].result)
    )
    ys, xs, norm, gate, inner, bc, step, conv_inner_grad, conv_bc_grad, head, mid, out = deliver(
        final.ys[None, None], final.xs[None, None], final.norm, final.gate[None], final.inner[None], final.bc[None],
        final.step[None], final.conv_inner, final.conv_bc, final.head, final.mid, final.out[None],
    )
    return (
        ys, xs, norm, gate, inner, bc, step, conv_inner_grad.transpose(1, 0, 2), conv_bc_grad.transpose(0, 2, 1),
        head.transpose(1, 0, 2), mid, out,
    )


def solution(mesh):
    weight = P("section", ROWS_ALL, None)
    vector = P("section", ROWS_ALL)
    taps = P("section", None, ROWS_ALL)
    tokens = P("wsh", None, "seq", None)
    heads = P("section", None, "seq")
    result = P("section", "wsh", None, "seq", None)
    return jax.shard_map(
        per_device,
        mesh=mesh,
        in_specs=(
            tokens, tokens, P("wsh", None), vector, weight, weight, weight, weight, taps, taps, heads, vector, weight,
        ),
        out_specs=(
            result, result, vector, weight, weight, weight, weight, taps, taps, heads, vector, weight,
        ),
        check_vma=False,
    )
```

```python
import functools
import types

import jax
import jax.numpy as jnp
from jax import lax
from jax.experimental import pallas as pl
from jax.experimental.pallas import tpu as pltpu
from jax.sharding import PartitionSpec as P

D = 1536
INNER = 3072
HEADS = 48
STATE = 128
BLOCK_LEN = 256
BLOCKS = 8
TOK = 128
CONV = INNER + 2 * STATE
HALF = CONV
GATE0 = 256
CUT = HALF // 2
WALF = D // 2
WCUT = WALF // 2
ECOLS = INNER // 2
LCOLS = HALF // 2 + 128
LSPLIT = LCOLS
OWNERS = 16
OWN = 192
EPS = 1e-05
F32 = jnp.float32
BF16 = jnp.bfloat16
MESH = pl.DeviceIdType.MESH
VMEM_LIMIT = 61 * 1024 * 1024
LANES = (0, 1, 2, 8, 9, 10)
ROWS_ALL = ("seq", "wsh")
ROW_MID, ROW_NORM = 5, 6
ROW_BIAS, ROW_DECAY, ROW_SKIP = 5, 6, 7


def dot32(left, right, dims=((1,), (0,))):
    return lax.dot_general(left, right, (dims, ((), ())), preferred_element_type=F32)


def split_left(exact, value, terms):
    total = None
    for _ in range(terms):
        part = value.astype(BF16)
        value = value - part.astype(F32)
        term = dot32(exact, part)
        total = term if total is None else total + term
    return total


def split_right(value, exact, terms, dims=((1,), (0,))):
    total = None
    for _ in range(terms):
        part = value.astype(BF16)
        value = value - part.astype(F32)
        term = dot32(part, exact, dims)
        total = term if total is None else total + term
    return total


def pair_cols(tile, q):
    lane = lax.broadcasted_iota(jnp.int32, (TOK, 128), 1)
    a = jnp.broadcast_to(tile[:, LANES[2 * q] : LANES[2 * q] + 1], (TOK, 128))
    b = jnp.broadcast_to(tile[:, LANES[2 * q + 1] : LANES[2 * q + 1] + 1], (TOK, 128))
    return a, b, jnp.where(lane < 64, a, b)


def pair_row(row, q):
    lane = lax.broadcasted_iota(jnp.int32, (1, 128), 1)
    a = jnp.broadcast_to(row[:, LANES[2 * q] : LANES[2 * q] + 1], (1, 128))
    b = jnp.broadcast_to(row[:, LANES[2 * q + 1] : LANES[2 * q + 1] + 1], (1, 128))
    return jnp.where(lane < 64, a, b)


def to_front(tile, i):
    return pltpu.roll(tile, lax.rem(128 - 16 * i, 128), 1)


def conv_of(cat, taps):
    total = taps[4:5] + taps[3:4] * cat[8 : 8 + TOK]
    for k in range(3):
        total = total + taps[k : k + 1] * cat[5 + k : 5 + k + TOK]
    return total


def tri_of(lower):
    row = lax.broadcasted_iota(jnp.int32, (TOK, TOK), 0)
    col = lax.broadcasted_iota(jnp.int32, (TOK, TOK), 1)
    return row >= col if lower else row <= col


def head_lanes():
    lane = lax.broadcasted_iota(jnp.int32, (TOK, 128), 1)
    return (lane % 8) < 3


def group_cols(i, q):
    return pl.ds(pl.multiple_of(i * 384 + q * 128, 128), 128)


def gate_cols(i, q):
    return pl.ds(pl.multiple_of(GATE0 + i * 384 + q * 128, 128), 128)


def in_hbm(*shape, dtype=BF16):
    return jax.ShapeDtypeStruct(shape, dtype), pl.BlockSpec(memory_space=pl.ANY)


def in_vmem(*shape, dtype=F32):
    return jax.ShapeDtypeStruct(shape, dtype), pl.BlockSpec(memory_space=pltpu.VMEM)


def saved(*shape, dtype=F32):
    return jax.ShapeDtypeStruct(shape, dtype), None


def call(body, name, ident, inputs, outputs, scratch):
    spaces = {"h": pl.ANY, "v": pltpu.VMEM, "s": pltpu.SMEM, "p": pl.ANY}
    early = [key for key, (kind, _) in inputs.items() if kind == "p"]
    late = [key for key, (_, spec) in outputs.items() if spec is None]
    scratch = dict(scratch)
    for key in early:
        scratch[key] = pltpu.VMEM(inputs[key][1].shape, inputs[key][1].dtype)
    for key in late:
        scratch[key] = pltpu.VMEM(outputs[key][0].shape, outputs[key][0].dtype)
    if early or late:
        scratch["move_sems"] = dma_sems(len(early) + len(late))
    names = [key + "_far" if key in early else key for key in inputs]
    names += [key + "_far" if key in late else key for key in outputs] + list(scratch)

    def kernel(*refs):
        r = types.SimpleNamespace(**dict(zip(names, refs)))

        def mover(key):
            near, far = getattr(r, key), getattr(r, key + "_far")
            src, dst = (far, near) if key in early else (near, far)
            return pltpu.make_async_copy(src, dst, r.move_sems.at[(early + late).index(key)])

        def start(*keys):
            for key in keys:
                mover(key).start()

        def wait(*keys):
            for key in keys:
                mover(key).wait()

        r.move, r.moved = start, wait
        body(r)

    out = pl.pallas_call(
        kernel,
        out_shape=tuple(shape for shape, _ in outputs.values()),
        in_specs=[pl.BlockSpec(memory_space=spaces[kind]) for kind, _ in inputs.values()],
        out_specs=tuple(
            pl.BlockSpec(memory_space=pl.ANY) if spec is None else spec for _, spec in outputs.values()
        ),
        scratch_shapes=list(scratch.values()),
        compiler_params=pltpu.CompilerParams(
            collective_id=ident, has_side_effects=True, vmem_limit_bytes=VMEM_LIMIT
        ),
        name=name,
    )(*[value for _, value in inputs.values()])
    return types.SimpleNamespace(**dict(zip(outputs, out)))


def dma_sems(count):
    return pltpu.SemaphoreType.DMA((count,))


def places():
    section = lax.axis_index("section")
    seq = lax.axis_index("seq")
    return section, seq // 4, lax.rem(seq, 4), lax.axis_index("wsh")


def x_peer(k):
    return {"wsh": lax.rem(lax.axis_index("wsh") + k, 4)}


def z_peer(k):
    _, y, z, _ = places()
    return {"seq": y * 4 + lax.rem(z + k, 4)}


def y_peer(k):
    _, y, z, _ = places()
    return {"seq": lax.rem(y + k, 4) * 4 + z}


def sibling():
    return {"section": 1 - lax.axis_index("section")}


def say_hello(peer):
    pl.semaphore_signal(pltpu.get_barrier_semaphore(), inc=1, device_id=peer, device_id_type=MESH)


def greet_axes():
    for k in range(1, 4):
        for peer in (x_peer(k), y_peer(k), z_peer(k)):
            say_hello(peer)
    say_hello(sibling())
    pl.semaphore_wait(pltpu.get_barrier_semaphore(), 10)


def fetch(src, dst, sem):
    copy = pltpu.make_async_copy(src, dst, sem)
    copy.start()
    return copy


class Net:
    def __init__(self, send, recv):
        self.send, self.recv = send, recv
        self.count = 0
        self.started = []

    def go(self, src, dst, peer):
        copy = pltpu.make_async_remote_copy(
            src_ref=src, dst_ref=dst, send_sem=self.send.at[self.count], recv_sem=self.recv.at[self.count],
            device_id=peer, device_id_type=MESH,
        )
        copy.start()
        self.count += 1
        self.started.append(copy)
        return copy

    def drain(self):
        for copy in self.started:
            copy.wait_send()


class Gather:
    def __init__(self, net, p, o, w, wo, stage, rows, own):
        self.net, self.p, self.o, self.w, self.wo = net, p, o, w, wo
        self.stage, self.rows, self.own = stage, rows, own
        self.place = places()
        self.near, self.far, self.inner, self.passed = {}, {}, {}, []
        self.peers = (y_peer, z_peer, x_peer, x_peer)
        self.inner_peers = (z_peer, y_peer, y_peer, z_peer)

    def band(self, kind, j, moved, half=None):
        c, y, z, x = self.place
        rows = slice(None) if half is None else pl.ds(48 * half, 48)
        many = slice(None) if half is None else pl.ds(2 * half, 2)
        if kind == 0:
            return self.w.at[c, lax.rem(y + 4 - moved, 4), lax.rem(z + 4 - j, 4), rows, pl.ds(0, CUT)]
        if kind == 1:
            return self.w.at[c, lax.rem(y + 4 - j, 4), lax.rem(z + 4 - moved, 4), rows, pl.ds(CUT, CUT)]
        if kind == 2:
            return self.wo.at[c, lax.rem(y + 4 - j, 4), many, lax.rem(x + 4 - moved, 4), :, pl.ds(0, WCUT)]
        return self.wo.at[c, many, lax.rem(z + 4 - j, 4), lax.rem(x + 4 - moved, 4), :, pl.ds(WCUT, WCUT)]

    def pass_on(self, part):
        self.passed.append(self.net.go(part, part, sibling()))

    def begin(self):
        c, y, z, x = self.place
        go = self.net.go
        self.first, self.spots = [], []
        spot = self.wo.at[c, y, z, x]
        for k in range(1, 4):
            self.first.append(go(self.p, self.stage.at[x], x_peer(k)))
            for cols, peer in ((pl.ds(0, WCUT), z_peer), (pl.ds(WCUT, WCUT), y_peer)):
                self.spots.append(go(self.o.at[:, cols], spot.at[:, cols], peer(k)))
        self.own_o = fetch(self.o, spot, self.own.at[0])
        self.stage[x] = self.p[...]

    def rows_in(self):
        c, y, z, x = self.place
        go = self.net.go
        for copy in self.first:
            copy.wait_recv()
        for side in range(2):
            self.rows[:, CUT * side : CUT * side + CUT] = jnp.concatenate(
                [self.stage[n].astype(F32)[24 * side : 24 * side + 24] for n in range(4)], axis=0
            ).astype(BF16)
        for k in (1, 3):
            for kind, cols in ((0, pl.ds(0, CUT)), (1, pl.ds(CUT, CUT))):
                self.inner[kind, k] = go(
                    self.rows.at[:, cols], self.band(kind, 0, 0), self.inner_peers[kind](k)
                )
        own_w = fetch(self.rows, self.w.at[c, y, z], self.own.at[1])
        self.own_o.wait()
        for copy in self.spots:
            copy.wait_recv()
        for k in (1, 3):
            for kind in (2, 3):
                part = self.band(kind, 0, 0)
                self.inner[kind, k] = go(part, part, self.inner_peers[kind](k))
        own_w.wait()
        self.spread(0)

    def spread(self, j):
        if j in (1, 3):
            for kind in range(4):
                self.inner[kind, j].wait_recv()
                part = self.band(kind, j, 0, 0 if j == 1 else 1)
                self.inner[kind, 2, j] = self.net.go(part, part, self.inner_peers[kind](j))
        if j == 2:
            for kind in range(4):
                self.inner[kind, 2, 1].wait_recv()
                self.inner[kind, 2, 3].wait_recv()
        for k in (1, 3):
            for kind in range(4):
                part = self.band(kind, j, 0)
                self.near[kind, j, k] = self.net.go(part, part, self.peers[kind](k))
        for kind in range(4):
            self.pass_on(self.band(kind, j, 0))

    def relay(self, j):
        for k in (1, 3):
            for kind in range(4):
                self.near[kind, j, k].wait_recv()
                part = self.band(kind, j, k)
                if (k == 1) == (j < 2):
                    self.far[kind, j] = self.net.go(part, part, self.peers[kind](k))
                self.pass_on(part)

    def last(self, j):
        for kind in range(4):
            self.far[kind, j].wait_recv()
            self.pass_on(self.band(kind, j, 2))

    def end(self):
        for copy in self.passed:
            copy.wait_recv()


def gather_scratch():
    return {
        "stage": pltpu.VMEM((4, 48, CUT), BF16),
        "rows": pltpu.VMEM((96, HALF), BF16),
        "own": dma_sems(2),
    }


def lane_at(shape):
    return lax.broadcasted_iota(jnp.int32, shape, 1)


def place_chunks(cells, width, total):
    tiles = [jnp.zeros((8, 128), F32) for _ in range(total // 128)]
    lane = lane_at((8, 128))
    for d in range(64):
        t, off = (width * d) // 128, (width * d) % 128
        moved = pltpu.roll(cells(d), off, 1) if off else cells(d)
        stop = off + width
        tiles[t] = jnp.where((lane >= off) & (lane < min(stop, 128)), moved, tiles[t])
        if stop > 128:
            tiles[t + 1] = jnp.where(lane < stop - 128, moved, tiles[t + 1])
    return tiles


def take_chunk(ref, base, width, d):
    start = base + width * d
    t, off = start // 128, start % 128
    tile = ref[:, 128 * t : 128 * t + 128]
    tile = pltpu.roll(tile, 128 - off, 1) if off else tile
    if off + width > 128:
        after = pltpu.roll(ref[:, 128 * t + 128 : 128 * t + 256], 128 - off, 1)
        tile = jnp.where(lane_at((8, 128)) < 128 - off, tile, after)
    return tile


def start_body(r, net, after):
    c, y, z, x = places()

    def stacked(first, second):
        return jnp.concatenate([first.astype(F32), second.astype(F32)], axis=0).astype(BF16)

    r.wide[...] = jnp.zeros_like(r.wide)
    r.wide[0:24, 0:48] = r.step[...].astype(F32)
    lane24 = lane_at((24, 128))
    spread_step = jnp.zeros((24, 128), F32)
    for n in range(OWNERS):
        moved = pltpu.roll(r.wide[0:24, :], 5 * n, 1) if n else r.wide[0:24, :]
        spread_step = jnp.where((lane24 >= 8 * n) & (lane24 < 8 * n + 3), moved, spread_step)
    gate_cut = CUT - GATE0
    r.mine[0, :, : INNER - CUT] = stacked(r.inner[:, : INNER - CUT], r.inner[:, CUT:])
    r.mine[0, :, INNER - CUT :] = stacked(r.inner[:, INNER - CUT : CUT], r.bc[...])
    r.mine[1, :, :128] = stacked(spread_step, r.gate[:, gate_cut : gate_cut + 128])
    r.mine[1, :, 128:GATE0] = stacked(jnp.zeros((24, 128), F32), r.gate[:, gate_cut + 128 : gate_cut + GATE0])
    r.mine[1, :, GATE0:] = stacked(r.gate[:, :gate_cut], r.gate[:, gate_cut + GATE0 :])
    r.blob[...] = jnp.zeros_like(r.blob)
    r.blob[0:5, 0:48] = r.conv_inner[...].astype(F32)
    r.blob[ROW_MID : ROW_MID + 1, 0:48] = r.mid[...].astype(F32)
    r.blob[ROW_NORM : ROW_NORM + 1, 0:24] = r.norm[...].astype(F32)
    r.square_s[...] = jnp.zeros_like(r.square_s)
    r.square_s[0:4, 0:5] = r.conv_bc[0].astype(F32)
    r.blob[8:13, 0:4] = r.square_s[...].T[0:5, 0:4]
    r.blob[13:16, 0:3] = r.head[:, 0, :]
    given = pl.ds(pl.multiple_of((1 - c) * WALF, 128), WALF)
    swaps = [
        net.go(r.mine.at[1 - c], r.half.at[c], sibling()),
        net.go(r.out.at[:, given], r.half_o.at[c], sibling()),
    ]
    small = [net.go(r.blob, r.cells.at[c, y, z, x], x_peer(k)) for k in range(1, 4)]
    r.half[c] = r.mine[c]
    r.half_o[c] = jnp.where(c == 0, r.out[:, :WALF], r.out[:, WALF:])
    r.cells[c, y, z, x] = r.blob[...]
    for copy in swaps:
        copy.wait_recv()
    ga = Gather(net, r.half.at[0], r.half_o.at[0], r.w0, r.wo0, r.stage0, r.rows0, r.own0)
    ga.begin()
    for copy in small:
        copy.wait_recv()
    small = [net.go(r.cells.at[c, y, z], r.cells.at[c, y, z], z_peer(k)) for k in range(1, 4)]
    ga.rows_in()
    after.begin()
    for copy in small:
        copy.wait_recv()
    small = [net.go(r.cells.at[c, y], r.cells.at[c, y], y_peer(k)) for k in range(1, 4)]
    for j in (1, 3, 2):
        ga.spread(j)
    for copy in small:
        copy.wait_recv()
    pair = net.go(r.cells.at[c], r.cells.at[c], sibling())
    ga.relay(0)
    ga.relay(1)
    pair.wait_recv()
    for layer in range(2):
        def first_tile(d):
            return r.cells[layer, d // 16, (d // 4) % 4, d % 4, 0:8]

        def second_tile(d):
            return r.cells[layer, d // 16, (d // 4) % 4, d % 4, 8:16]

        for t, tile in enumerate(place_chunks(first_tile, 48, INNER)):
            r.taps[layer, :, 128 * t : 128 * t + 128] = tile
        for t, tile in enumerate(place_chunks(second_tile, 4, 2 * STATE)):
            r.taps[layer, :, INNER + 128 * t : INNER + 128 * t + 128] = tile
        for t, tile in enumerate(place_chunks(first_tile, 24, D)):
            r.gain[layer, :, 128 * t : 128 * t + 128] = tile
        lane = lane_at((8, 128))
        heads = jnp.zeros((8, 128), F32)
        for j in range(OWNERS):
            moved = pltpu.roll(second_tile(4 * j), 8 * j, 1) if j else second_tile(0)
            heads = jnp.where((lane >= 8 * j) & (lane < 8 * j + 3), moved, heads)
        r.heads[layer] = heads
    ga.relay(3)
    after.rows_in()
    ga.relay(2)
    for j in (0, 1, 3):
        ga.last(j)
    after.spread(1)
    after.spread(3)
    ga.last(2)
    ga.end()
    after.spread(2)


TURNS = (1, 4, 3, 12, 5, 15, 7, 13, 2, 8, 6, 9, 14, 11, 10)


def seq_peer(d):
    _, y, z, _ = places()
    return lax.rem(y + d // 4, 4) * 4 + lax.rem(z + d % 4, 4)


class Exchange:
    def __init__(self, backward, r):
        self.backward, self.r = backward, r
        self.me = lax.axis_index("seq")
        self.section = lax.axis_index("section")

    def first_copy(self, peer, d):
        r = self.r
        return pltpu.make_async_remote_copy(
            src_ref=r.ds.at[peer], dst_ref=r.got.at[self.me], send_sem=r.send_a.at[d], recv_sem=r.recv_a.at[d],
            device_id={"seq": peer}, device_id_type=MESH,
        )

    def send(self, peer):
        _, y, z, _ = places()
        d = lax.rem(peer // 4 + 4 - y, 4) * 4 + lax.rem(lax.rem(peer, 4) + 4 - z, 4)

        @pl.when(d != 0)
        def _():
            self.first_copy(peer, d).start()

        @pl.when(d == 0)
        def _():
            self.r.got[self.me] = self.r.ds[self.me]

    def back_copy(self, d):
        r = self.r
        peer = seq_peer(d)
        return pltpu.make_async_remote_copy(
            src_ref=r.ready.at[peer], dst_ref=r.back.at[self.me], send_sem=r.send_b.at[d], recv_sem=r.recv_b.at[d],
            device_id={"seq": peer}, device_id_type=MESH,
        )

    def scan(self, decays):
        r = self.r

        def rows_of(dec):
            return jnp.concatenate([jnp.broadcast_to(dec[h : h + 1], (64, 128)) for h in range(3)], axis=0)

        for d in TURNS:
            self.first_copy(seq_peer(d), d).wait_recv()
        r.final[...] = jnp.zeros((OWN, STATE), F32)
        r.fade[0] = jnp.ones((8, 128), F32)

        def step(n, carry):
            c = OWNERS - 1 - n if self.backward else n
            state = r.final[...]
            r.kept[c] = state
            dec = decays[c]
            r.final[...] = rows_of(dec) * state + r.got[c].astype(F32)
            r.fade[n + 1] = r.fade[n] * dec
            return carry

        lax.fori_loop(0, OWNERS, step, 0)
        swap = pltpu.make_async_remote_copy(
            src_ref=r.final, dst_ref=r.other, send_sem=r.swap_s.at[0], recv_sem=r.swap_s.at[1],
            device_id=sibling(), device_id_type=MESH,
        )
        swap.start()
        takes = 0 if self.backward else 1
        r.begin[...] = jnp.zeros((OWN, STATE), F32)

        @pl.when(self.section == takes)
        def _():
            swap.wait_recv()
            r.begin[...] = r.other[...]

        begin = r.begin[...]
        for d in TURNS + (0,):
            c = seq_peer(d)
            n = OWNERS - 1 - c if self.backward else c
            value = (r.kept[c] + rows_of(r.fade[n]) * begin).astype(BF16)
            if d == 0:
                r.back[c] = value
            else:
                r.ready[c] = value
                self.back_copy(d).start()

        @pl.when(self.section != takes)
        def _():
            swap.wait_recv()

        swap.wait_send()

    def finish(self):
        for d in TURNS:
            self.back_copy(d).wait_recv()

    def drain(self):
        for d in range(1, OWNERS):
            self.first_copy(seq_peer(d), d).wait_send()
            self.back_copy(d).wait_send()


def exchange_scratch():
    block = pltpu.VMEM((OWNERS, OWN, STATE), BF16)
    part = pltpu.VMEM((OWN, STATE), F32)
    return {
        "ds": block, "got": block, "back": block, "ready": block,
        "kept": pltpu.VMEM((OWNERS, OWN, STATE), F32), "fade": pltpu.VMEM((OWNERS + 1, 8, 128), F32),
        "final": part, "other": part, "begin": part,
        "send_a": dma_sems(OWNERS), "recv_a": dma_sems(OWNERS), "send_b": dma_sems(OWNERS), "recv_b": dma_sems(OWNERS),
        "swap_s": dma_sems(2),
    }


def head_rows_at(ref, i, q):
    parts = []
    for h in (2 * q, 2 * q + 1):
        parts.append(ref[2 * i + h // 3, pl.ds(64 * (h % 3), 64), :])
    return jnp.concatenate(parts, axis=0)


def store_heads(ref, i, q, value):
    for n, h in enumerate((2 * q, 2 * q + 1)):
        ref[2 * i + h // 3, pl.ds(64 * (h % 3), 64), :] = value[64 * n : 64 * n + 64]


def own_group(n):
    return lax.rem(lax.axis_index("seq") // 2 + n, 8)


def greet_layer(rider, forward):
    me = lax.axis_index("seq")
    section = lax.axis_index("section")
    wsh = lax.axis_index("wsh")
    barrier = pltpu.get_barrier_semaphore()
    for d in range(1, OWNERS):
        say_hello({"seq": lax.rem(me + d, OWNERS)})
    say_hello(sibling())
    if rider:
        for k in range(1, 4):
            say_hello(x_peer(k))
    count = OWNERS + (3 if rider else 0)
    late = {"section": 0, "seq": 15, "wsh": wsh}
    if forward:

        @pl.when((section == 1) & ((me == 0) | (me == 4)))
        def _():
            pl.semaphore_signal(barrier, inc=1, device_id=late, device_id_type=MESH)

        more = jnp.where((section == 0) & (me == 15), 2, 0)
    else:

        @pl.when((section == 0) & (me == 15))
        def _():
            for seq in (0, 4):
                pl.semaphore_signal(
                    barrier, inc=1, device_id={"section": 1, "seq": seq, "wsh": wsh}, device_id_type=MESH
                )

        more = jnp.where((section == 1) & ((me == 0) | (me == 4)), 1, 0)
    pl.semaphore_wait(barrier, count + more)


def flags_of(seg):
    section = lax.axis_index("section")
    seq = lax.axis_index("seq")
    starts = [(BLOCKS - seg[0, n]) * (BLOCK_LEN // TOK) for n in range(2)]
    first = jnp.where(section == 0, starts[0], starts[1])
    at_start = seq == first
    second = section == 1

    def number(cond):
        return jnp.where(cond, 1.0, 0.0)

    live = number(seq >= first)
    near = number(jnp.logical_not(at_start) | (second & (first == 0)))
    far = number(at_start & second & (first != 0))
    cross = number((section == 0) & (seq == 15) & (starts[1] != 0))
    return live, near, far, cross


def halo_copy(src, dst, sems, n, section, seq):
    return pltpu.make_async_remote_copy(
        src_ref=src, dst_ref=dst, send_sem=sems.at[n], recv_sem=sems.at[2 + n],
        device_id={"section": section, "seq": seq, "wsh": lax.axis_index("wsh")}, device_id_type=MESH,
    )


class Halo:
    def __init__(self, src, near, far, sems, forward):
        me = lax.axis_index("seq")
        section = lax.axis_index("section")
        edge = 15 if forward else 0
        if forward:
            crossing = (section == 0) & (me == 15)
            jumping = crossing
            self.has_near = (me > 0) | (section == 1)
            self.has_far = (section == 1) & (me == 4)
            target = (1, jnp.where(me == 15, 0, me + 1))
            near_section = jnp.where(crossing, 1, section)
            far_seq, far_section = 4, 1
        else:
            crossing = (section == 1) & (me == 0)
            jumping = (section == 1) & (me == 4)
            self.has_near = (me < 15) | (section == 0)
            self.has_far = (section == 0) & (me == 15)
            target = (0, jnp.where(me == 0, 15, me - 1))
            near_section = jnp.where(crossing, 0, section)
            far_seq, far_section = 15, 0
        self.sends_near = (me != edge) | crossing
        self.sends_far = jumping
        self.near, self.far = near, far
        self.near_copy = halo_copy(src, near, sems, 0, near_section, target[1])
        self.far_copy = halo_copy(src, far, sems, 1, far_section, far_seq)

    def start(self):
        @pl.when(self.sends_near)
        def _():
            self.near_copy.start()

        @pl.when(self.sends_far)
        def _():
            self.far_copy.start()

        @pl.when(jnp.logical_not(self.has_near))
        def _():
            self.near[...] = jnp.zeros_like(self.near)

        @pl.when(jnp.logical_not(self.has_far))
        def _():
            self.far[...] = jnp.zeros_like(self.far)

    def wait(self):
        @pl.when(self.has_near)
        def _():
            self.near_copy.wait_recv()

        @pl.when(self.has_far)
        def _():
            self.far_copy.wait_recv()

    def drain(self):
        @pl.when(self.sends_near)
        def _():
            self.near_copy.wait_send()

        @pl.when(self.sends_far)
        def _():
            self.far_copy.wait_send()


def forward_body(layer, rider, r):
    section = lax.axis_index("section")
    me = lax.axis_index("seq")
    net = Net(r.pair_send, r.pair_recv)
    if rider:
        greet_layer(rider, True)
        bulk = Net(r.net_send, r.net_recv)
        ga = Gather(bulk, r.half.at[1], r.half_o.at[1], r.next_w, r.next_wo, r.stage, r.rows, r.own)
        start_body(r, bulk, ga)
        w, wo = r.w0.reshape(2, D, HALF), r.wo0.reshape(2, INNER, WALF)
    else:
        w, wo = r.w, r.wo
    loads = [fetch(w.at[n], r.w_s.at[n], r.load.at[n]) for n in range(2)]
    load_o = fetch(wo, r.wo_s, r.load.at[2])
    if not rider:
        greet_layer(rider, True)
    ex = Exchange(False, r)
    flags = flags_of(r.flags)
    live = flags[0]
    heads = r.heads[layer]
    x_ref = r.x.at[section] if rider else r.x
    x32 = x_ref[...].astype(F32)
    hidden_inv = lax.rsqrt(jnp.sum(x32 * x32, axis=1, keepdims=True) / D + EPS)
    r.hidden[...] = (x32 * hidden_inv * r.gain[layer, ROW_NORM : ROW_NORM + 1, :]).astype(BF16)
    loads[0].wait()

    def project_main(n, carry):
        cols = pl.ds(pl.multiple_of(n * 256, 256), 256)
        r.pre[:, cols] = dot32(r.hidden[...], r.w_s[0, :, cols]).astype(BF16)
        return carry

    lax.fori_loop(0, HALF // 256, project_main, 0)
    r.tail[...] = r.pre[TOK - 16 :, :]
    halo = Halo(r.tail, r.halo_near, r.halo_far, r.halo_s, True)
    halo.start()
    loads[1].wait()

    def project_side(n, carry):
        cols = pl.ds(pl.multiple_of(n * 256, 256), 256)
        r.side[:, cols] = dot32(r.hidden[...], r.w_s[1, :, cols])
        return carry

    early_tiles = 1 if rider else HALF // 256
    lax.fori_loop(0, early_tiles, project_side, 0)
    r.move("pre")
    if not rider:
        r.move("side")
    pairs = [net.go(r.hidden, r.both_hidden.at[section], sibling())]
    owns = [fetch(r.hidden, r.both_hidden.at[section], r.load.at[3])]
    step = r.side[:, :128].astype(BF16).astype(F32) + heads[ROW_BIAS : ROW_BIAS + 1]
    dt = jnp.maximum(step, 0.0) + jnp.log1p(jnp.exp(-jnp.abs(step)))
    dt = jnp.where(head_lanes(), dt, 0.0) * live
    rate = -dt * jnp.exp(heads[ROW_DECAY : ROW_DECAY + 1])
    cum = split_left(tri_of(True).astype(F32).astype(BF16), rate, 3)
    r.dt[...] = dt
    r.cum[...] = cum
    last = jnp.broadcast_to(cum[TOK - 1 : TOK], (TOK, 128))
    r.dec_s[...] = jnp.exp(last).T.reshape(OWNERS, 8, 128)
    r.dec[me] = r.dec_s[me]

    def dec_copy(d):
        peer = lax.rem(me + d, OWNERS)
        return pltpu.make_async_remote_copy(
            src_ref=r.dec_s.at[peer], dst_ref=r.dec.at[me], send_sem=r.dec_send.at[d], recv_sem=r.dec_recv.at[d],
            device_id={"seq": peer}, device_id_type=MESH,
        )

    for d in range(1, OWNERS):
        dec_copy(d).start()
    weight = dt * jnp.exp(last - cum)
    halo.wait()
    r.halo[...] = jnp.where(
        flags[1] > 0.0, r.halo_near[...], jnp.where(flags[2] > 0.0, r.halo_far[...], jnp.zeros_like(r.halo_far))
    )

    def conv_tile(cols):
        blk = r.pre[:, cols].astype(F32)
        cat = jnp.concatenate([r.halo[:, cols].astype(F32)[8:], blk], axis=0)
        summed = conv_of(cat, r.taps[layer, :, cols])
        sig = 1.0 / (1.0 + jnp.exp(-summed))
        act = summed * sig
        r.act[:, cols] = act
        r.dact[:, cols] = sig * (1.0 + summed * (1.0 - sig))
        return act

    b = conv_tile(pl.ds(INNER, 128)).astype(BF16)
    c = conv_tile(pl.ds(INNER + 128, 128)).astype(BF16)

    def states(n, carry):
        i = own_group(n)
        wt = to_front(weight, i)
        for q in range(3):
            x = conv_tile(group_cols(i, q))
            scaled = (x * pair_cols(wt, q)[2]).astype(BF16)
            store_heads(r.ds, i, q, dot32(scaled, b, ((0,), (0,))).astype(BF16))
        ex.send(2 * i)
        ex.send(2 * i + 1)
        return carry

    lax.fori_loop(0, 8, states, 0)
    r.move("act", "dact")
    if rider:
        lax.fori_loop(early_tiles, HALF // 256, project_side, 0)
        r.move("side")
        ga.relay(0)
    if rider:
        ga.relay(1)
    for d in range(1, OWNERS):
        dec_copy(d).wait_recv()
    ex.scan(r.dec)
    if rider:
        ga.relay(3)
    r.cumt[...] = cum.T
    causal = tri_of(True)
    scores = dot32(c, b, ((1,), (1,)))
    lane = lax.broadcasted_iota(jnp.int32, (TOK, 128), 1)
    r.square[...] = jnp.zeros((TOK, 128), F32)

    def inside(i, carry):
        cum_i = to_front(cum, i)
        dt_i = to_front(dt, i)
        rows = r.cumt[pl.ds(pl.multiple_of(16 * i, 16), 16), :]
        for q in range(3):
            cols = group_cols(i, q)
            cum_a, cum_b, _ = pair_cols(cum_i, q)
            u = r.act[:, cols] * pair_cols(dt_i, q)[2]
            mixes = []
            for cum_h, off in ((cum_a, LANES[2 * q]), (cum_b, LANES[2 * q + 1])):
                gap = cum_h - rows[off : off + 1]
                mixes.append((scores * jnp.exp(jnp.where(causal, gap, -1e30))).astype(BF16))
            terms = jnp.concatenate(
                [jnp.where(lane < 64, u, 0.0).astype(BF16), jnp.where(lane < 64, 0.0, u).astype(BF16)], axis=0
            )
            r.raw[:, cols] = dot32(jnp.concatenate(mixes, axis=1), terms)
        return carry

    lax.fori_loop(0, 8, inside, 0)
    if rider:
        ga.relay(2)
    ex.finish()
    save = fetch(r.back, r.states, r.load.at[4])

    def across(i, carry):
        cum_i = to_front(cum, i)
        skip_i = pltpu.roll(heads, lax.rem(128 - 16 * i, 128), 1)[ROW_SKIP : ROW_SKIP + 1]
        for q in range(3):
            cols = group_cols(i, q)
            state = head_rows_at(r.back, i, q)
            raw = r.raw[:, cols] + jnp.exp(pair_cols(cum_i, q)[2]) * dot32(c, state, ((1,), (1,)))
            r.raw[:, cols] = raw
            y = (raw + pair_row(skip_i, q) * r.act[:, cols]).astype(BF16)
            r.y[:, cols] = y
            gate = r.side[:, gate_cols(i, q)]
            z = y.astype(F32) * (gate / (1.0 + jnp.exp(-gate)))
            r.z[:, cols] = z
            r.square[...] += z * z
        return carry

    lax.fori_loop(0, 8, across, 0)
    r.move("raw", "y")
    if rider:
        ga.last(0)
        ga.last(1)
    total = jnp.sum(r.square[...], axis=1, keepdims=True)
    inv = jnp.broadcast_to(lax.rsqrt(total / INNER + EPS), (TOK, 128))
    r.inv[...] = inv

    def scale(i, carry):
        cols = pl.ds(pl.multiple_of(i * 128, 128), 128)
        mid = r.taps[layer, ROW_MID : ROW_MID + 1, cols]
        r.gated[:, cols] = (r.z[:, cols] * inv * mid).astype(BF16)
        return carry

    lax.fori_loop(0, 24, scale, 0)
    pairs.append(net.go(r.gated, r.both_gated.at[section], sibling()))
    owns.append(fetch(r.gated, r.both_gated.at[section], r.load.at[5]))
    load_o.wait()
    for half in range(2):

        def project(n, carry):
            cols = pl.ds(pl.multiple_of(n * 256, 256), 256)
            full = pl.ds(pl.multiple_of(half * WALF + n * 256, 256), 256)
            branch = dot32(r.gated[...], r.wo_s[half, :, cols])
            r.result[:, full] = (x_ref[:, full].astype(F32) + live * branch).astype(BF16)
            return carry

        lax.fori_loop(0, WALF // 256, project, 0)
    if rider:
        for j in (3, 2):
            ga.last(j)
        ga.end()
        bulk.drain()
    r.moved("pre", "side", "act", "dact", "raw", "y")
    save.wait()
    for copy in owns:
        copy.wait()
    for copy in pairs:
        copy.wait_recv()
    net.drain()
    halo.drain()
    for d in range(1, OWNERS):
        dec_copy(d).wait_send()
    ex.drain()


def block_forward(layer, flags, x, given):
    rider = layer == 0
    inputs = {"flags": ("s", flags), "x": ("v", x)}
    if rider:
        for key, value in given.items():
            inputs[key] = ("v", value)
    else:
        w, wo, small = given
        inputs.update({
            "w": ("h", w), "wo": ("h", wo), "taps": ("v", small.taps), "gain": ("v", small.gain),
            "heads": ("v", small.heads),
        })
    outputs = {
        "act": saved(TOK, CONV), "dact": saved(TOK, CONV), "side": saved(TOK, HALF), "raw": saved(TOK, INNER),
        "dt": in_vmem(TOK, 128), "cum": in_vmem(TOK, 128), "inv": in_vmem(TOK, 128),
        "dec": in_vmem(OWNERS, 8, 128), "pre": saved(TOK, CONV, dtype=BF16), "halo": in_vmem(16, CONV, dtype=BF16),
        "y": saved(TOK, INNER, dtype=BF16), "result": in_vmem(TOK, D, dtype=BF16),
        "states": in_hbm(OWNERS, OWN, STATE), "both_hidden": in_hbm(2, TOK, D), "both_gated": in_hbm(2, TOK, INNER),
    }
    tile = pltpu.VMEM((TOK, 128), F32)
    edge = pltpu.VMEM((16, CONV), BF16)
    scratch = {
        "w_s": pltpu.VMEM((2, D, HALF), BF16), "wo_s": pltpu.VMEM((2, INNER, WALF), BF16),
        "hidden": pltpu.VMEM((TOK, D), BF16), "gated": pltpu.VMEM((TOK, INNER), BF16),
        "z": pltpu.VMEM((TOK, INNER), F32), "cumt": tile, "square": tile,
        "tail": edge, "halo_near": edge, "halo_far": edge, "halo_s": dma_sems(4),
        "dec_s": pltpu.VMEM((OWNERS, 8, 128), F32), "dec_send": dma_sems(OWNERS), "dec_recv": dma_sems(OWNERS),
        "load": dma_sems(6), "pair_send": dma_sems(2), "pair_recv": dma_sems(2),
        **exchange_scratch(),
    }
    if rider:
        outputs.update({
            "w0": in_hbm(2, 4, 4, 96, HALF), "wo0": in_hbm(2, 4, 4, 4, 48, WALF),
            "next_w": in_hbm(2, 4, 4, 96, HALF), "next_wo": in_hbm(2, 4, 4, 4, 48, WALF),
            "taps": in_vmem(2, 8, CONV), "gain": in_vmem(2, 8, D), "heads": in_vmem(2, 8, 128),
        })
        scratch.update({
            "mine": pltpu.VMEM((2, 48, CUT), BF16), "half": pltpu.VMEM((2, 48, CUT), BF16),
            "wide": pltpu.VMEM((24, 128), F32), "blob": pltpu.VMEM((16, 128), F32),
            "square_s": pltpu.VMEM((128, 128), F32),
            "half_o": pltpu.VMEM((2, 48, WALF), BF16), "cells": pltpu.VMEM((2, 4, 4, 4, 16, 128), F32),
            "net_send": dma_sems(400), "net_recv": dma_sems(400),
        })
        scratch.update({key + "0": value for key, value in gather_scratch().items()})
        scratch.update(gather_scratch())
    return call(
        functools.partial(forward_body, layer, rider), "block_forward", 2 + layer, inputs, outputs, scratch
    )


def add_rows(target, *parts):
    lead = target.shape[:-2]
    blocks = functools.reduce(lambda a, b: a * b, lead, 1)

    def body(b, carry):
        spot = (b,) if len(lead) == 1 else (b // lead[1], lax.rem(b, lead[1]))
        total = parts[0][spot].astype(F32)
        for ref in parts[1:]:
            total = total + ref[spot].astype(F32)
        target[spot] = total.astype(target.dtype)
        return carry

    lax.fori_loop(0, blocks, body, 0)


def fold_scratch(tag, cols, with_out):
    shapes = {"a": (4, 96, cols // 2), "b": (4, 96, cols // 2)}
    if with_out:
        shapes["o"] = (4, 4, 48, WALF)
    scratch = {}
    for key, shape in shapes.items():
        scratch[tag + "m" + key] = pltpu.VMEM(shape, BF16)
        scratch[tag + "s" + key] = pltpu.VMEM((2,) + shape, BF16)
    scratch[tag + "own"] = dma_sems(9)
    return scratch


def fold_targets(tag, cols, with_out, make):
    targets = {tag + "ha": make(4, 96, cols // 2), tag + "hb": make(4, 96, cols // 2)}
    if with_out:
        targets[tag + "ho"] = make(4, 4, 48, WALF)
    return targets


class Fold:
    def __init__(self, net, r, tag, cols, gi, go):
        self.net, self.gi, self.go_ref, self.cut = net, gi, go, cols // 2
        self.kinds = (0, 1, 2) if go is not None else (0, 1)
        keys = "abo"
        self.h = [getattr(r, tag + "h" + keys[n]) for n in self.kinds]
        self.m = [getattr(r, tag + "m" + keys[n]) for n in self.kinds]
        self.s = [getattr(r, tag + "s" + keys[n]) for n in self.kinds]
        self.own = getattr(r, tag + "own")
        self.place = places()
        self.peers = (y_peer, z_peer, x_peer)
        self.hops, self.direct, self.loads = {}, {}, {}

    def part(self, kind, t, half):
        _, y, z, x = self.place
        at = pl.ds(2 * half, 2) if half is not None else slice(None)
        if kind == 0:
            return self.gi.at[lax.rem(y + t, 4), at, :, pl.ds(0, self.cut)]
        if kind == 1:
            return self.gi.at[at, lax.rem(z + t, 4), :, pl.ds(self.cut, self.cut)]
        return self.go_ref.at[at, :, lax.rem(x + t, 4)]

    def begin(self, kinds):
        go = self.net.go
        for half, k in ((0, 1), (1, 3)):
            for kind in kinds:
                self.hops[kind, half] = go(
                    self.part(kind, 2, half), self.h[kind].at[pl.ds(2 * half, 2)], self.peers[kind](k)
                )
        for half, k in ((1, 1), (0, 3)):
            for kind in kinds:
                side = 0 if k == 1 else 1
                self.direct[kind, side] = go(
                    self.part(kind, k, half), self.s[kind].at[side, pl.ds(2 * half, 2)], self.peers[kind](k)
                )
        for kind in kinds:
            self.loads[kind] = [
                fetch(self.part(kind, 1, 0), self.m[kind].at[pl.ds(0, 2)], self.own.at[3 * kind]),
                fetch(self.part(kind, 3, 1), self.m[kind].at[pl.ds(2, 2)], self.own.at[3 * kind + 1]),
            ]

    def combine(self, kind):
        for copy in self.loads[kind]:
            copy.wait()
        for half in range(2):
            self.hops[kind, half].wait_recv()
        add_rows(self.m[kind], self.m[kind], self.h[kind])
        peer = self.peers[kind]
        for half, k in ((0, 1), (1, 3)):
            at = pl.ds(2 * half, 2)
            self.hops[kind, half] = self.net.go(self.m[kind].at[at], self.s[kind].at[half, at], peer(k))
        self.loads[kind] = [fetch(self.part(kind, 0, None), self.h[kind], self.own.at[3 * kind + 2])]

    def settle(self, kind):
        for copy in self.loads[kind]:
            copy.wait()
        for side in range(2):
            self.direct[kind, side].wait_recv()
            self.hops[kind, side].wait_recv()
        add_rows(self.h[kind], self.h[kind], self.s[kind].at[0], self.s[kind].at[1])


class Finish:
    def __init__(self, net, r, tag, cols, sums):
        self.net, self.sums, self.cut, self.cols = net, sums, cols // 2, cols
        for key in ("r2a", "r2b", "c3", "r3") + (("r2o", "o2", "r3o") if len(sums) > 2 else ()):
            setattr(self, key, getattr(r, tag + key))
        self.place = places()

    def second(self):
        _, y, z, _ = self.place
        go = self.net.go
        ha, hb = self.sums[:2]
        self.a, self.b, self.o = [], [], []
        for k in range(1, 4):
            self.a.append(go(ha.at[lax.rem(z + k, 4)], self.r2a.at[k], z_peer(k)))
            self.b.append(go(hb.at[lax.rem(y + k, 4)], self.r2b.at[k], y_peer(k)))
        self.r2a[0] = ha[z]
        self.r2b[0] = hb[y]
        if len(self.sums) > 2:
            ho = self.sums[2]
            one, two = pl.ds(0, WCUT), pl.ds(WCUT, WCUT)
            for k in range(1, 4):
                self.o.append(go(ho.at[lax.rem(y + k, 4), :, :, one], self.r2o.at[0, k], y_peer(k)))
                self.o.append(go(ho.at[:, lax.rem(z + k, 4), :, two], self.r2o.at[1, k], z_peer(k)))
            self.r2o[0, 0] = ho[y, :, :, :WCUT]
            for n in range(4):
                self.r2o[1, 0, n] = ho[n, z, :, WCUT:]

    def third(self):
        _, y, z, x = self.place
        go = self.net.go
        for copy in self.a + self.b:
            copy.wait_recv()
        for n in range(4):
            at = pl.ds(24 * n, 24)
            for parts, cols in ((self.r2a, pl.ds(0, self.cut)), (self.r2b, pl.ds(self.cut, self.cut))):
                total = parts[0, at, :].astype(F32)
                for k in range(1, 4):
                    total = total + parts[k, at, :].astype(F32)
                self.c3[n, :, cols] = total
        self.x = [go(self.c3.at[lax.rem(x + k, 4)], self.r3.at[x], x_peer(k)) for k in range(1, 4)]
        self.r3[x] = self.c3[x]
        if self.o:
            for copy in self.o:
                copy.wait_recv()
            for n in range(2):
                add_rows(self.o2.at[n], *[self.r2o.at[n, k] for k in range(4)])
            for k in range(1, 4):
                self.x.append(go(self.o2.at[0, lax.rem(z + k, 4)], self.r3o.at[0, k], z_peer(k)))
                self.x.append(go(self.o2.at[1, lax.rem(y + k, 4)], self.r3o.at[1, k], y_peer(k)))
            self.r3o[0, 0] = self.o2[0, z]
            self.r3o[1, 0] = self.o2[1, y]

    def last(self, in_ref, out_ref=None):
        for copy in self.x:
            copy.wait_recv()
        in_ref[...] = self.r3[0] + self.r3[1] + self.r3[2] + self.r3[3]
        if self.o:
            for n in range(2):
                total = self.r3o[n, 0].astype(F32)
                for k in range(1, 4):
                    total = total + self.r3o[n, k].astype(F32)
                out_ref[:, WCUT * n : WCUT * n + WCUT] = total


def finish_scratch(tag, cols, with_out):
    cut = cols // 2
    scratch = {
        tag + "r2a": pltpu.VMEM((4, 96, cut), BF16), tag + "r2b": pltpu.VMEM((4, 96, cut), BF16),
        tag + "c3": pltpu.VMEM((4, 24, cols), F32), tag + "r3": pltpu.VMEM((4, 24, cols), F32),
    }
    if with_out:
        scratch[tag + "r2o"] = pltpu.VMEM((2, 4, 4, 48, WCUT), BF16)
        scratch[tag + "o2"] = pltpu.VMEM((2, 4, 48, WCUT), BF16)
        scratch[tag + "r3o"] = pltpu.VMEM((2, 4, 48, WCUT), BF16)
    return scratch


def net_scratch(count):
    return {"net_send": dma_sems(count), "net_recv": dma_sems(count)}


def early_products(r, which):
    left, right, stage, target = (
        (r.gated2, r.gb2, r.stage_o, r.go) if which == 0 else (r.hid2, r.dg2, r.stage_e, r.ge)
    )
    tile = stage.shape[1]

    def body(i, carry):
        slot = lax.rem(i, 2)
        rows = pl.ds(pl.multiple_of(i * tile, tile), tile)
        copy = pltpu.make_async_copy(stage.at[slot], target.at[rows], r.stage_s.at[2 * which + slot])

        @pl.when(i >= 2)
        def _():
            copy.wait()

        stage[slot] = dot32(left[:, rows], right[...], ((0,), (0,))).astype(BF16)
        copy.start()
        return carry

    lax.fori_loop(0, target.shape[0] // tile, body, 0)
    for slot in range(2):
        pltpu.make_async_copy(stage.at[slot], target.at[pl.ds(0, tile)], r.stage_s.at[2 * which + slot]).wait()


def backward_body(layer, rider, r):
    section = lax.axis_index("section")
    slots_o, slots_w = r.wo_s.shape[0], r.w_s.shape[0]
    load_state = fetch(r.states, r.state_s, r.load.at[0])
    load_two = [fetch(r.both_hidden, r.hid2, r.load.at[3]), fetch(r.both_gated, r.gated2, r.load.at[4])]

    def wo_tile(i):
        rows = pl.ds(pl.multiple_of(i * 384, 384), 384)
        slot = lax.rem(i, slots_o)
        return pltpu.make_async_copy(r.wo.at[:, rows], r.wo_s.at[slot], r.wo_load.at[slot])

    def w_tile(n):
        slot = lax.rem(n, slots_w)
        rows = pl.ds(pl.multiple_of((n // 2) * 256, 256), 256)
        return pltpu.make_async_copy(r.w.at[lax.rem(n, 2), rows], r.w_s.at[slot], r.w_load.at[slot])

    for n in range(slots_o):
        wo_tile(n).start()
    r.move("side", "y", "act", "raw", "dact", "pre")
    for n in range(slots_w):
        w_tile(n).start()
    greet_layer(True, False)
    net = Net(r.pair_send, r.pair_recv)
    bulk = Net(r.net_send, r.net_recv)
    if rider:
        late = Fold(bulk, r, "l", LCOLS, r.gl, None)
        late.begin((0, 1))
        early_end = Finish(bulk, r, "e", ECOLS, (r.e1a, r.e1b, r.e1o))
        early_end.second()
        late_end = Finish(bulk, r, "l", LCOLS, late.h)
    early = Fold(
        bulk, r, "e", ECOLS, r.ge.reshape(4, 4, 96, ECOLS), r.go.reshape(4, 4, 4, 48, WALF)
    )
    ex = Exchange(True, r)
    flags = flags_of(r.flags)
    live = flags[0]
    heads = r.heads[layer]
    g_ref = r.g if rider else r.g.at[section]
    r.gb[...] = (g_ref[...].astype(F32) * live).astype(BF16)
    inv = r.inv[...]
    dt = r.dt[...]
    cum = r.cum[...]
    r.dots[...] = jnp.zeros((TOK, 128), F32)
    other_half = pl.ds(pl.multiple_of((1 - section) * WALF, 128), WALF)
    own_rows = pl.ds(pl.multiple_of(section * TOK, 128), TOK)
    pairs = [net.go(r.gb.at[:, other_half], r.gb2.at[own_rows], sibling())]
    r.gb2[own_rows, :] = jnp.where(section == 0, r.gb[:, :WALF], r.gb[:, WALF:])
    load_two[1].wait()
    pairs[0].wait_recv()
    early_products(r, 0)
    early.begin((2,))

    def first(i, carry):
        slot = lax.rem(i, slots_o)
        wo_tile(i).wait()
        gg = dot32(r.gb[:, :WALF], r.wo_s[slot, 0], ((1,), (1,)))
        gg = gg + dot32(r.gb[:, WALF:], r.wo_s[slot, 1], ((1,), (1,)))

        @pl.when(i + slots_o < 8)
        def _():
            wo_tile(i + slots_o).start()

        r.gg[:, pl.ds(pl.multiple_of(i * 384, 384), 384)] = gg
        for q in range(3):
            cols = group_cols(i, q)
            gate = r.side[:, gate_cols(i, q)]
            z = r.y[:, cols].astype(F32) * (gate / (1.0 + jnp.exp(-gate)))
            mid = r.taps[layer, ROW_MID : ROW_MID + 1, cols]
            r.dots[...] += gg[:, 128 * q : 128 * q + 128] * mid * z
        return carry

    r.moved("side", "y")
    lax.fori_loop(0, 8, first, 0)
    r.moved("act")
    b = r.act[:, INNER : INNER + 128].astype(BF16)
    c = r.act[:, INNER + 128 : CONV].astype(BF16)
    total = jnp.broadcast_to(jnp.sum(r.dots[...], axis=1, keepdims=True), (TOK, 128))
    shift = total * inv * inv * inv / INNER
    r.gtaps[...] = jnp.zeros_like(r.gtaps)

    def second(n, carry):
        i = own_group(n)
        cum_i = to_front(cum, i)
        for q in range(3):
            cols = group_cols(i, q)
            gate = r.side[:, gate_cols(i, q)]
            y = r.y[:, cols].astype(F32)
            gg = r.gg[:, cols]
            sig = 1.0 / (1.0 + jnp.exp(-gate))
            act = gate * sig
            z = y * act
            dz = gg * r.taps[layer, ROW_MID : ROW_MID + 1, cols] * inv - z * shift
            dy = (dz * act).astype(BF16)
            r.dy[:, cols] = dy
            r.gside[:, gate_cols(i, q)] = (dz * y * (sig * (1.0 + gate * (1.0 - sig)))).astype(BF16)
            r.gtaps[ROW_MID : ROW_MID + 1, cols] = jnp.sum(gg * z * inv, axis=0, keepdims=True)
            far = (dy.astype(F32) * jnp.exp(pair_cols(cum_i, q)[2])).astype(BF16)
            store_heads(r.ds, i, q, dot32(far, c, ((0,), (0,))).astype(BF16))
        ex.send(2 * i)
        ex.send(2 * i + 1)
        return carry

    lax.fori_loop(0, 8, second, 0)
    other_cols = pl.ds(pl.multiple_of(GATE0 + (1 - section) * ECOLS, 128), ECOLS)
    pairs.append(net.go(r.gside.at[:, other_cols], r.dg2.at[own_rows], sibling()))
    r.dg2[own_rows, :] = jnp.where(
        section == 0, r.gside[:, GATE0 : GATE0 + ECOLS], r.gside[:, GATE0 + ECOLS :]
    )
    if rider:
        late.combine(0)
        late.combine(1)
    load_two[0].wait()
    pairs[1].wait_recv()
    early_products(r, 1)
    ex.scan(r.dec)
    early.begin((0, 1))
    load_state.wait()
    r.cumt[...] = cum.T
    causal = tri_of(True)
    scores = dot32(c, b, ((1,), (1,)))
    lane = lax.broadcasted_iota(jnp.int32, (TOK, 128), 1)
    pick_row = lax.broadcasted_iota(jnp.int32, (128, 128), 0)
    pick_col = lax.broadcasted_iota(jnp.int32, (128, 128), 1)
    picks = []
    for q in range(3):
        target = jnp.where(pick_row < 64, LANES[2 * q], LANES[2 * q + 1])
        picks.append((pick_col == target).astype(F32).astype(BF16))
    for ref in (r.dscore, r.grad_b, r.grad_c, r.xdu, r.dyy, r.thin):
        ref[...] = jnp.zeros_like(ref)

    def inside(i, carry):
        cum_i = to_front(cum, i)
        dt_i = to_front(dt, i)
        rows = r.cumt[pl.ds(pl.multiple_of(16 * i, 16), 16), :]
        for q in range(3):
            cols = group_cols(i, q)
            cum_a, cum_b, cum_x = pair_cols(cum_i, q)
            u16 = (r.act[:, cols] * pair_cols(dt_i, q)[2]).astype(BF16)
            dy16 = r.dy[:, cols]
            nil = jnp.zeros_like(dy16)
            dys = jnp.concatenate([jnp.where(lane < 64, dy16, nil), jnp.where(lane < 64, nil, dy16)], axis=0)
            both = dot32(dys, u16, ((1,), (1,)))
            mixes = []
            for n, (cum_h, off) in enumerate(((cum_a, LANES[2 * q]), (cum_b, LANES[2 * q + 1]))):
                gap = cum_h - rows[off : off + 1]
                decay = jnp.exp(jnp.where(causal, gap, -1e30))
                mixes.append((scores * decay).astype(BF16))
                r.dscore[...] += both[n * TOK : n * TOK + TOK] * decay
            r.gg[:, cols] = dot32(jnp.concatenate(mixes, axis=0), dys, ((0,), (0,)))
            far = (dy16.astype(F32) * jnp.exp(cum_x)).astype(BF16)
            r.grad_c[...] += dot32(far, head_rows_at(r.state_s, i, q))
        return carry

    lax.fori_loop(0, 8, inside, 0)
    if rider:
        late.settle(0)
        late.settle(1)
        late_end.second()

    def conv_back(cols, gact):
        gsum = gact * r.dact[:, cols]
        r.gsum[:, cols] = gsum
        blk = r.pre[:, cols].astype(F32)
        cat = jnp.concatenate([r.halo[:, cols].astype(F32)[8:], blk], axis=0)
        sums = [jnp.sum(gsum * cat[5 + k : 5 + k + TOK], axis=0, keepdims=True) for k in range(4)]
        sums.append(jnp.sum(gsum, axis=0, keepdims=True))
        r.gtaps[0:5, cols] = jnp.concatenate(sums, axis=0)

    r.moved("raw", "dact", "pre")
    ex.finish()

    def across(i, carry):
        cum_i = to_front(cum, i)
        dt_i = to_front(dt, i)
        skip_i = pltpu.roll(heads, lax.rem(128 - 16 * i, 128), 1)[ROW_SKIP : ROW_SKIP + 1]
        x_du = jnp.zeros((TOK, 128), F32)
        dy_y = jnp.zeros((TOK, 128), F32)
        thin = jnp.zeros((16, 128), F32)
        edges = {}
        for q in range(3):
            cols = group_cols(i, q)
            x = r.act[:, cols]
            cum_x = pair_cols(cum_i, q)[2]
            dt_x = pair_cols(dt_i, q)[2]
            fade = jnp.exp(cum_x[TOK - 1 : TOK] - cum_x)
            u = x * dt_x
            dy = r.dy[:, cols].astype(F32)
            state16 = head_rows_at(r.state_s, i, q)
            dstate16 = head_rows_at(r.back, i, q)
            du_far = fade * dot32(b, dstate16, ((1,), (1,)))
            du = r.gg[:, cols] + du_far
            r.grad_b[...] += dot32((u * fade).astype(BF16), dstate16)
            overlap = state16.astype(F32) * dstate16.astype(F32)
            edges[LANES[2 * q]] = jnp.sum(overlap[:64], axis=0, keepdims=True)
            edges[LANES[2 * q + 1]] = jnp.sum(overlap[64:], axis=0, keepdims=True)
            x_du = x_du + split_right(x * du, picks[q], 2)
            dy_y = dy_y + split_right(dy * r.raw[:, cols], picks[q], 2)
            thin = thin + split_right(
                jnp.concatenate(
                    [
                        jnp.broadcast_to(jnp.sum(u * du_far, axis=0, keepdims=True), (8, 128)),
                        jnp.broadcast_to(jnp.sum(dy * x, axis=0, keepdims=True), (8, 128)),
                    ],
                    axis=0,
                ),
                picks[q],
                3,
            )
            conv_back(cols, du * dt_x + pair_row(skip_i, q) * dy)
        nothing = jnp.zeros((1, 128), F32)
        r.edge[pl.ds(pl.multiple_of(16 * i, 16), 16), :] = jnp.concatenate(
            [edges.get(k, nothing) for k in range(16)], axis=0
        )
        r.xdu[...] += pltpu.roll(x_du, 16 * i, 1)
        r.dyy[...] += pltpu.roll(dy_y, 16 * i, 1)
        r.thin[...] += pltpu.roll(thin, 16 * i, 1)
        return carry

    lax.fori_loop(0, 8, across, 0)
    early.combine(2)
    early.combine(0)
    early.combine(1)
    dscore16 = r.dscore[...].astype(BF16)
    conv_back(pl.ds(INNER, 128), r.grad_b[...] + dot32(dscore16, c, ((0,), (0,))))
    conv_back(pl.ds(INNER + 128, 128), r.grad_c[...] + dot32(dscore16, b))
    r.tail[...] = r.gsum[:8, :]
    halo = Halo(r.tail, r.halo_near, r.halo_far, r.halo_s, False)
    halo.start()
    ones = jnp.ones((128, 128), BF16)
    edge = split_right(r.edge[...], ones, 3).T[0:1] * jnp.exp(cum[TOK - 1 : TOK]) + r.thin[0:1]
    x_du = r.xdu[...]
    drate = split_left(tri_of(False).astype(F32).astype(BF16), r.dyy[...] - dt * x_du, 3) + edge
    speed = jnp.exp(heads[ROW_DECAY : ROW_DECAY + 1])
    ddt = x_du - drate * speed
    step = r.side[:, :128].astype(BF16).astype(F32) + heads[ROW_BIAS : ROW_BIAS + 1]
    dstep = jnp.where(head_lanes(), ddt / (1.0 + jnp.exp(-step)), 0.0) * live
    r.gside[:, :128] = dstep.astype(BF16)
    r.gside[:, 128:GATE0] = jnp.zeros((TOK, 128), BF16)
    r.ghead[...] = jnp.concatenate(
        [
            jnp.zeros((5, 128), F32),
            jnp.sum(dstep, axis=0, keepdims=True),
            jnp.sum(-drate * dt * speed, axis=0, keepdims=True),
            r.thin[8:9],
        ],
        axis=0,
    )
    halo.wait()
    after = jnp.where(flags[3] > 0.0, r.halo_far[...], r.halo_near[...])
    r.halo_near[...] = jnp.where(live > 0.0, after, jnp.zeros_like(after))

    def conv_tile(i, carry):
        cols = pl.ds(pl.multiple_of(i * 128, 128), 128)
        cat = jnp.concatenate([r.gsum[:, cols], r.halo_near[:, cols]], axis=0)
        taps = r.taps[layer, :, cols]
        total = taps[3:4] * cat[:TOK]
        for k in range(3):
            total = total + taps[k : k + 1] * cat[3 - k : 3 - k + TOK]
        r.gpre[:, cols] = total.astype(BF16)
        return carry

    lax.fori_loop(0, CONV // 128, conv_tile, 0)
    if rider:
        early_end.third()
        late_end.third()

    tail_cols = HALF - LCOLS
    side_cols = pl.ds(0, GATE0)
    both_gl = r.both_gl if rider else r.gl2
    moves = (
        net_copy(net, r.gpre.at[:, pl.ds(LCOLS, tail_cols)], both_gl.at[0, :, pl.ds(0, tail_cols)], 2),
        net_copy(net, r.gside.at[:, side_cols], both_gl.at[0, :, pl.ds(tail_cols, GATE0)], 3),
        net_copy(net, r.gpre.at[:, pl.ds(0, LCOLS)], both_gl.at[1], 2),
    )
    keeps = (
        pltpu.make_async_copy(r.gpre.at[:, pl.ds(LCOLS, tail_cols)], both_gl.at[1, :, pl.ds(0, tail_cols)], r.load.at[1]),
        pltpu.make_async_copy(r.gside.at[:, side_cols], both_gl.at[1, :, pl.ds(tail_cols, GATE0)], r.load.at[2]),
        pltpu.make_async_copy(r.gpre.at[:, pl.ds(0, LCOLS)], both_gl.at[0], r.load.at[1]),
    )

    @pl.when(section == 0)
    def _():
        moves[0].start()
        moves[1].start()
        keeps[2].start()

    @pl.when(section == 1)
    def _():
        moves[2].start()
        keeps[0].start()
        keeps[1].start()

    def project(n, carry):
        rows = pl.ds(pl.multiple_of(n * 256, 256), 256)
        w_tile(2 * n).wait()
        value = dot32(r.gpre[...], r.w_s[lax.rem(2 * n, slots_w)], ((1,), (1,)))

        @pl.when(2 * n + slots_w < 12)
        def _():
            w_tile(2 * n + slots_w).start()

        w_tile(2 * n + 1).wait()
        value = value + dot32(r.gside[...], r.w_s[lax.rem(2 * n + 1, slots_w)], ((1,), (1,)))

        @pl.when(2 * n + 1 + slots_w < 12)
        def _():
            w_tile(2 * n + 1 + slots_w).start()

        r.gg[:, rows] = value
        return carry

    lax.fori_loop(0, D // 256, project, 0)
    x = (r.x[section] if rider else r.x[...]).astype(F32)
    grad = r.gg[:, :D]
    inv_x = lax.rsqrt(jnp.sum(x * x, axis=1, keepdims=True) / D + EPS)
    scaled = grad * r.gain[layer, ROW_NORM : ROW_NORM + 1, :]
    dots = jnp.sum(scaled * x, axis=1, keepdims=True)
    dx = scaled * inv_x - x * (dots * inv_x * inv_x * inv_x / D)
    r.result[...] = (g_ref[...].astype(F32) + dx).astype(BF16)
    r.ggain[...] = jnp.broadcast_to(jnp.sum(grad * x * inv_x, axis=0, keepdims=True), (8, D))
    if rider:
        early_end.last(r.fin_e, r.fin_o)
        late_end.last(r.fin_l)

    @pl.when(section == 0)
    def _():
        moves[0].wait_send()
        moves[1].wait_send()
        keeps[2].wait()
        moves[2].wait_recv()

    @pl.when(section == 1)
    def _():
        moves[2].wait_send()
        keeps[0].wait()
        keeps[1].wait()
        moves[0].wait_recv()
        moves[1].wait_recv()

    if not rider:
        tile = r.stage_l.shape[1]
        late_grads = jnp.concatenate([r.gl2[0], r.gl2[1]], axis=0)
        writes = []
        for n in range(D // tile):
            rows = pl.ds(n * tile, tile)
            if n >= 2:
                writes[n - 2].wait()
            r.stage_l[n % 2] = dot32(r.hid2[:, rows], late_grads, ((0,), (0,))).astype(BF16)
            writes.append(fetch(r.stage_l.at[n % 2], r.glate.at[rows], r.late_s.at[n % 2]))
    for kind in range(3):
        early.settle(kind)
    if not rider:
        for copy in writes[-2:]:
            copy.wait()
    bulk.drain()
    net.drain()
    halo.drain()
    ex.drain()


def net_copy(net, src, dst, n):
    return pltpu.make_async_remote_copy(
        src_ref=src, dst_ref=dst, send_sem=net.send.at[n], recv_sem=net.recv.at[n],
        device_id=sibling(), device_id_type=MESH,
    )


def block_backward(layer, flags, g, x, w, wo, small, kept, grads):
    rider = grads is not None
    inputs = {
        "flags": ("s", flags), "g": ("v", g), "x": ("v", x), "w": ("h", w), "wo": ("h", wo), "taps": ("v", small.taps),
        "gain": ("v", small.gain), "heads": ("v", small.heads), "states": ("h", kept.states),
        "both_hidden": ("h", kept.both_hidden.reshape(2 * TOK, D)),
        "both_gated": ("h", kept.both_gated.reshape(2 * TOK, INNER)),
    }
    for key in ("dt", "cum", "inv", "dec", "halo"):
        inputs[key] = ("v", getattr(kept, key))
    for key in ("side", "y", "act", "raw", "dact", "pre"):
        inputs[key] = ("p", getattr(kept, key))
    outputs = {
        "result": in_vmem(TOK, D, dtype=BF16),
        "gtaps": in_vmem(8, CONV), "ggain": in_vmem(8, D), "ghead": in_vmem(8, 128),
        "ge": in_hbm(D, ECOLS), "go": in_hbm(INNER, WALF),
        **fold_targets("e", ECOLS, True, lambda *shape: in_vmem(*shape, dtype=BF16)),
    }
    tile = pltpu.VMEM((TOK, 128), F32)
    edge = pltpu.VMEM((8, CONV), F32)
    slots, tile_rows = (2, 128) if rider else (3, 512)
    scratch = {
        "wo_s": pltpu.VMEM((slots, 2, 384, WALF), BF16), "w_s": pltpu.VMEM((slots, 256, HALF), BF16),
        "wo_load": dma_sems(slots), "w_load": dma_sems(slots), "load": dma_sems(5),
        "hid2": pltpu.VMEM((2 * TOK, D), BF16), "gated2": pltpu.VMEM((2 * TOK, INNER), BF16),
        "gb2": pltpu.VMEM((2 * TOK, WALF), BF16), "dg2": pltpu.VMEM((2 * TOK, ECOLS), BF16),
        "stage_o": pltpu.VMEM((2, tile_rows, WALF), BF16), "stage_e": pltpu.VMEM((2, tile_rows, ECOLS), BF16), "stage_s": dma_sems(4),
        "state_s": pltpu.VMEM((OWNERS, OWN, STATE), BF16),
        "gb": pltpu.VMEM((TOK, D), BF16), "gg": pltpu.VMEM((TOK, INNER), F32), "dy": pltpu.VMEM((TOK, INNER), BF16),
        "gsum": pltpu.VMEM((TOK, CONV), F32), "gpre": pltpu.VMEM((TOK, HALF), BF16), "gside": pltpu.VMEM((TOK, HALF), BF16),
        "dots": tile, "cumt": tile, "edge": tile, "dscore": tile, "grad_b": tile, "grad_c": tile, "xdu": tile, "dyy": tile,
        "thin": pltpu.VMEM((16, 128), F32),
        "tail": edge, "halo_near": edge, "halo_far": edge, "halo_s": dma_sems(4),
        "pair_send": dma_sems(4), "pair_recv": dma_sems(4),
        **exchange_scratch(), **fold_scratch("e", ECOLS, True), **net_scratch(64),
    }
    if not rider:
        outputs["glate"] = in_hbm(D, LCOLS)
        scratch.update({
            "gl2": pltpu.VMEM((2, TOK, LCOLS), BF16), "stage_l": pltpu.VMEM((2, 256, LCOLS), BF16), "late_s": dma_sems(2),
        })
    if rider:
        outputs["both_gl"] = in_hbm(2, TOK, LCOLS)
        inputs.update({"gl": ("h", grads[0]), "e1a": ("v", grads[1]), "e1b": ("v", grads[2]), "e1o": ("v", grads[3])})
        outputs.update({"fin_e": in_vmem(24, ECOLS), "fin_l": in_vmem(24, LCOLS), "fin_o": in_vmem(48, WALF)})
        scratch.update(fold_scratch("l", LCOLS, False))
        scratch.update(fold_targets("l", LCOLS, False, lambda *shape: pltpu.VMEM(shape, BF16)))
        scratch.update(finish_scratch("e", ECOLS, True))
        scratch.update(finish_scratch("l", LCOLS, False))
    return call(
        functools.partial(backward_body, layer, rider), "block_backward", 4 + layer, inputs, outputs, scratch
    )


def reduce_body(r):
    c, y, z, x = places()
    greet_axes()
    net = Net(r.net_send, r.net_recv)
    late = Fold(net, r, "l", LCOLS, r.gl, None)
    late.begin((0, 1))
    early_end = Finish(net, r, "e", ECOLS, (r.e0a, r.e0b, r.e0o))
    early_end.second()
    late_end = Finish(net, r, "l", LCOLS, late.h)
    results = []
    for n, (first, second, target) in enumerate(((r.y0, r.y1, r.ys), (r.x0, r.x1, r.xs))):
        cross = [
            pltpu.make_async_remote_copy(
                src_ref=src, dst_ref=target.at[c], send_sem=r.final_s.at[3 * n], recv_sem=r.final_s.at[3 * n + 1],
                device_id=sibling(), device_id_type=MESH,
            )
            for src in (second, first)
        ]
        stay = [pltpu.make_async_copy(src, target.at[c], r.final_s.at[3 * n + 2]) for src in (first, second)]
        for core in range(2):

            @pl.when(c == core)
            def _():
                cross[core].start()
                stay[core].start()

        results.append((cross[0], stay[0]))
    row = lax.broadcasted_iota(jnp.int32, (8, 128), 0)
    lane = lane_at((8, 128))
    for layer in range(2):
        taps, gain, heads = (getattr(r, key + str(layer)) for key in ("gtaps", "ggain", "ghead"))
        for d in range(64):
            cell = (layer, d // 16, (d // 4) % 4, d % 4)
            first = jnp.where(lane < 48, take_chunk(taps, 0, 48, d), 0.0)
            norm = jnp.where(lane < 24, take_chunk(gain, 0, 24, d), 0.0)
            r.cells[cell + (slice(0, 8),)] = jnp.where(row == ROW_NORM, norm, first)
            second = jnp.where(lane < 4, take_chunk(taps, INNER, 4, d), 0.0)
            head = jnp.where(lane < 3, take_chunk(heads, 0, 8, d // 4), 0.0)
            r.cells[cell + (slice(8, 16),)] = jnp.where(row >= 5, head, second)
    pair = net.go(r.cells.at[1 - c], r.other, sibling())
    others = [
        net.go(r.far_e, r.got_far_e, sibling()),
        net.go(r.far_l, r.got_far_l, sibling()),
        net.go(r.far_o, r.got_far_o, sibling()),
    ]
    pair.wait_recv()
    r.sum0[...] = r.cells[c] + r.other[...]
    hops = [net.go(r.sum0.at[lax.rem(y + k, 4)], r.in_y.at[k], y_peer(k)) for k in range(1, 4)]
    late.combine(0)
    late.combine(1)
    early_end.third()
    for copy in hops:
        copy.wait_recv()
    r.sum1[...] = r.sum0[y] + r.in_y[1] + r.in_y[2] + r.in_y[3]
    hops = [net.go(r.sum1.at[lax.rem(z + k, 4)], r.in_z.at[k], z_peer(k)) for k in range(1, 4)]
    late.settle(0)
    late.settle(1)
    late_end.second()
    for copy in hops:
        copy.wait_recv()
    r.sum2[...] = r.sum1[z] + r.in_z[1] + r.in_z[2] + r.in_z[3]
    r.in_x[x] = r.sum2[x]
    hops = [net.go(r.sum2.at[lax.rem(x + k, 4)], r.in_x.at[x], x_peer(k)) for k in range(1, 4)]
    early_end.last(r.near_e, r.near_o)
    others.append(net.go(r.near_e, r.got_near_e, sibling()))
    others.append(net.go(r.near_o, r.got_near_o, sibling()))
    late_end.third()
    for copy in hops:
        copy.wait_recv()
    blob = r.in_x[0] + r.in_x[1] + r.in_x[2] + r.in_x[3]
    for n in range(5):
        r.conv_inner[n] = blob[n : n + 1, :48]
    r.mid[...] = blob[ROW_MID : ROW_MID + 1, :48]
    r.norm[...] = blob[ROW_NORM : ROW_NORM + 1, :24]
    r.square_s[...] = jnp.zeros_like(r.square_s)
    r.square_s[0:16, :] = blob
    r.conv_bc[0] = r.square_s[...].T[0:4, 8:13]
    for n in range(3):
        r.head[n] = blob[13 + n : 14 + n, :3]
    late_end.last(r.near_l)
    others.append(net.go(r.near_l, r.got_near_l, sibling()))
    for copy in others:
        copy.wait_recv()
    for cross, stay in results:
        cross.wait_recv()
        cross.wait_send()
        stay.wait()

    def put(first_l, second_l, first_e, second_e, first_o, second_o):
        r.inner[:, :LCOLS] = first_l[...]
        r.inner[:, LCOLS:] = second_l[:, : INNER - LCOLS]
        r.bc[...] = second_l[:, INNER - LCOLS : CONV - LCOLS]
        wide = second_l[:, CONV - LCOLS : CONV - LCOLS + 128]
        lane24 = lane_at((24, 128))
        steps = jnp.zeros((24, 128), F32)
        for n in range(OWNERS):
            moved = pltpu.roll(wide, 128 - 5 * n, 1) if n else wide
            steps = jnp.where((lane24 >= 3 * n) & (lane24 < 3 * n + 3), moved, steps)
        r.step[...] = steps[:, :HEADS]
        r.gate[:, :ECOLS] = first_e[...]
        r.gate[:, ECOLS:] = second_e[...]
        r.out[:, :WALF] = first_o[...]
        r.out[:, WALF:] = second_o[...]

    @pl.when(c == 0)
    def _():
        put(r.near_l, r.got_near_l, r.near_e, r.got_near_e, r.near_o, r.got_near_o)

    @pl.when(c == 1)
    def _():
        put(r.got_far_l, r.far_l, r.got_far_e, r.far_e, r.got_far_o, r.far_o)

    net.drain()


def reduce_all(grads, far, backs, outs):
    cell = (4, 4, 16, 128)
    return call(
        reduce_body, "reduce_grads", 6,
        {
            "gl": ("h", grads[0]), "e0a": ("v", grads[1]), "e0b": ("v", grads[2]), "e0o": ("v", grads[3]),
            "y0": ("v", outs[0]), "y1": ("v", outs[1]), "x0": ("v", backs[0].result), "x1": ("v", backs[1].result),
            "far_e": ("v", far[0]), "far_l": ("v", far[1]), "far_o": ("v", far[2]),
            **{
                key + str(n): ("v", getattr(backs[n], key)) for n in range(2) for key in ("gtaps", "ggain", "ghead")
            },
        },
        {
            "ys": in_hbm(2, TOK, D), "xs": in_hbm(2, TOK, D),
            "inner": in_vmem(24, INNER), "bc": in_vmem(24, 2 * STATE), "step": in_vmem(24, HEADS),
            "gate": in_vmem(24, INNER), "out": in_vmem(48, D), "conv_inner": in_vmem(5, 1, 48), "mid": in_vmem(1, 48),
            "norm": in_vmem(1, 24), "conv_bc": in_vmem(1, 4, 5), "head": in_vmem(3, 1, 3),
        },
        {
            **{
                name + part: pltpu.VMEM(shape, F32)
                for name in ("near_", "got_near_", "got_far_")
                for part, shape in (("e", (24, ECOLS)), ("l", (24, LCOLS)), ("o", (48, WALF)))
            },
            "final_s": dma_sems(6), "square_s": pltpu.VMEM((128, 128), F32),
            "cells": pltpu.VMEM((2, 4) + cell, F32), "other": pltpu.VMEM((4,) + cell, F32),
            "sum0": pltpu.VMEM((4,) + cell, F32), "in_y": pltpu.VMEM((4,) + cell, F32),
            "sum1": pltpu.VMEM(cell, F32), "in_z": pltpu.VMEM((4,) + cell[1:], F32),
            "sum2": pltpu.VMEM(cell[1:], F32), "in_x": pltpu.VMEM((4, 16, 128), F32),
            **fold_scratch("l", LCOLS, False),
            **fold_targets("l", LCOLS, False, lambda *shape: pltpu.VMEM(shape, BF16)),
            **finish_scratch("e", ECOLS, True), **finish_scratch("l", LCOLS, False), **net_scratch(64),
        },
    )


def deliver_body(*refs):
    count = len(refs) // 2
    for given, made in zip(refs[:count], refs[count:]):
        made[...] = given[...]


def deliver(*arrays):
    return pl.pallas_call(
        deliver_body,
        out_shape=tuple(jax.ShapeDtypeStruct(value.shape, value.dtype) for value in arrays),
        in_specs=[pl.BlockSpec(memory_space=pltpu.VMEM)] * len(arrays),
        out_specs=(pl.BlockSpec(memory_space=pltpu.VMEM),) * len(arrays),
        compiler_params=pltpu.CompilerParams(vmem_limit_bytes=VMEM_LIMIT),
        name="deliver",
    )(*arrays)


def per_device(
    block_input, cotangent, seg_groups, norm_gain, w_gate, w_inner, w_bc, w_step, conv_inner, conv_bc, head_params,
    inner_gain, w_out,
):
    shards = {
        "inner": w_inner[0], "bc": w_bc[0], "step": w_step[0], "gate": w_gate[0], "out": w_out[0],
        "norm": norm_gain, "mid": inner_gain, "conv_inner": conv_inner[0], "conv_bc": conv_bc.transpose(0, 2, 1),
        "head": head_params.transpose(1, 0, 2),
    }
    flags = seg_groups
    x = block_input[0]
    start = block_forward(0, flags, x, shards)
    weights = (
        (start.w0.reshape(2, D, HALF), start.wo0.reshape(2, INNER, WALF)),
        (start.next_w.reshape(2, D, HALF), start.next_wo.reshape(2, INNER, WALF)),
    )
    kept = [start, block_forward(1, flags, start.result, weights[1] + (start,))]
    inputs = [x, start.result]

    g = cotangent[0]
    grads = None
    backs = [None, None]
    for layer in (1, 0):
        w, wo = weights[layer]
        back = block_backward(layer, flags, g, inputs[layer], w, wo, start, kept[layer], grads)
        backs[layer] = back
        g = back.result
        if layer == 1:
            grad_late = back.glate
        else:
            hidden = kept[layer].both_hidden.reshape(2 * TOK, D)
            grad_late = dot32(hidden, back.both_gl.reshape(2 * TOK, LCOLS), ((0,), (0,))).astype(BF16)
        grads = (grad_late.reshape(4, 4, 96, LCOLS), back.eha, back.ehb, back.eho)

    final = reduce_all(
        grads, (backs[0].fin_e, backs[0].fin_l, backs[0].fin_o), backs, (kept[0].result, kept[1].result)
    )
    ys, xs, norm, gate, inner, bc, step, conv_inner_grad, conv_bc_grad, head, mid, out = deliver(
        final.ys[None, None], final.xs[None, None], final.norm, final.gate[None], final.inner[None], final.bc[None],
        final.step[None], final.conv_inner, final.conv_bc, final.head, final.mid, final.out[None],
    )
    return (
        ys, xs, norm, gate, inner, bc, step, conv_inner_grad.transpose(1, 0, 2), conv_bc_grad.transpose(0, 2, 1),
        head.transpose(1, 0, 2), mid, out,
    )


def solution(mesh):
    weight = P("section", ROWS_ALL, None)
    vector = P("section", ROWS_ALL)
    taps = P("section", None, ROWS_ALL)
    tokens = P("wsh", None, "seq", None)
    heads = P("section", None, "seq")
    result = P("section", "wsh", None, "seq", None)
    return jax.shard_map(
        per_device,
        mesh=mesh,
        in_specs=(
            tokens, tokens, P("wsh", None), vector, weight, weight, weight, weight, taps, taps, heads, vector, weight,
        ),
        out_specs=(
            result, result, vector, weight, weight, weight, weight, taps, taps, heads, vector, weight,
        ),
        check_vma=False,
    )
```
